32 devices in a mesh: grp: 2 (over y), ka: 4 (over z), ga: 2 (over x), ba: 2 (over core).
Axes of the slice: x: 2, y: 2, z: 4, core: 2. Of those that a mesh axis runs over, the one named last changes fastest.
Arguments:
- start_vector: float32 [8, 2, 2, 16], P(('grp', 'ka')), parts along dimension 0, may hold values from -250 to 250
- valence_density: bfloat16 [8, 4, 2, 4, 4, 1536], P(('grp', 'ka'), None, None, 'ba', None, 'ga'), parts along dimension 0, may hold values from -1 to 1
- conduction_density: bfloat16 [8, 4, 2, 4, 4, 1536], P(('grp', 'ka'), None, None, None, None, 'ga'), parts along dimension 0, may hold values from -0.0546875 to 0.0546875
- screening: bfloat16 [8, 2, 1536, 1536], P(('grp', 'ka'), None, 'ga'), parts along dimension 0, may hold values from -0.109375 to 0.109375
- qpoint_map: int32 [4, 4], replicated, may hold values from 0 to 3, as said below
- slot_owner: int32 [4], replicated, may hold values from 0 to 3, each once
- band_pairs: int32 [16], replicated, may hold values from 0 to 15, each once
- valence_energy: float32 [8, 4], P(('grp', 'ka')), parts along dimension 0, may hold values from -1.5 to -0.3
- conduction_energy: float32 [8, 4], P(('grp', 'ka')), parts along dimension 0, may hold values from 0.3 to 1.5
Outputs:
- next_vector: float32 [8, 2, 2, 16], P(('grp', 'ka')), parts along dimension 0
- coefficients: float32 [4, 6], P('grp'), parts along dimension 0
The draws below stay inside these ranges and needn't reach their ends.
There are 2 independent parts, one for each index of `grp`. The reference program is written for one: setup_inputs(seed, part) draws one part's arguments, and reference() takes and returns one part's arrays. A program takes and returns all parts, laid end to end along the dimension named above; an argument that names none is the same for every part. Nothing has to cross between parts.
Inputs may be any that keep to these rules, and one draw needn't show every extreme that they name: qpoint_map[k, k2] depends only on (k - k2) mod 4; each row names every q number once. `slot_owner`: every slot number appears exactly once. `band_pairs`: every code of the 4 x 4 band pairs appears exactly once.
All inputs are finite; a program needn't handle non-finite values.
Results may differ from the reference program's by a relative error of at most 0.0029.
Values may be sent and summed in bfloat16 or wider, within the bound.
No kernel may reach another device: no remote copies, remote signals or barrier semaphores. Data moves between devices by JAX's collectives and lax.ppermute only.
A program may use at most 64 MiB of HBM per device.

```python
import math
import jax
import jax.numpy as jnp
from jax import lax

NG = 1536
NV = 4
NC = 4
NPOL = 2
NBP = 16
NK = 4
NQ = 4


def draw_start_vector(key, part):
    key = jax.random.fold_in(key, 7)
    first_key, second_key = jax.random.split(key)
    shape = (NK, NPOL, 2, NBP)
    position = jnp.arange(NK, dtype=jnp.float32) / max(NK - 1, 1)
    columns = jnp.exp(jax.random.uniform(second_key, (NK, 1, 1, NBP), jnp.float32, 0.0, math.log(10.0)))
    values = jnp.clip(jax.random.normal(first_key, shape, jnp.float32), -4.0, 4.0)
    rising = jnp.exp(position * math.log(3.0))
    return values * rising[:, None, None, None] * columns


def draw_qpoint_map(key, part):
    key = jax.random.fold_in(key, 11)
    labels = jax.random.permutation(key, NQ).astype(jnp.int32)
    kpoints = jnp.arange(NK, dtype=jnp.int32)
    offsets = (kpoints[:, None] - kpoints[None, :]) % NK
    return jnp.take(labels, offsets).astype(jnp.int32)


def shard_levels(own_key, extent, cuts, low, top_value):
    def one(axis_at, parts):
        draws = jax.random.uniform(jax.random.fold_in(jax.random.fold_in(own_key, 6), axis_at), (parts,), jnp.float32, low / len(cuts), top_value / len(cuts))
        return jnp.repeat(jnp.exp(draws), extent[axis_at] // parts).reshape((-1,) + (1,) * (len(extent) - axis_at - 1))

    factor_of = one(*cuts[0])
    for cut in cuts[1:]:
        factor_of = factor_of * one(*cut)
    return factor_of


def normal_values(own_key, dims, spread, reach, shards=(), kind=jnp.bfloat16):
    loudness = shard_levels(own_key, dims, shards, -0.22, 0.18) if shards else 1.0
    array = jax.random.normal(own_key, dims, jnp.float32) * spread * loudness
    return jnp.minimum(jnp.maximum(array, -reach), reach).astype(kind)


def setup_inputs(seed: int = 0, part: int = 0) -> dict:
    seeds = jax.random.split(jax.random.key(seed), 10)
    own_keys = jax.random.split(jax.random.fold_in(seeds[9], part), 10)
    start_vector = draw_start_vector(jax.random.fold_in(jax.random.fold_in(seeds[9], part), 71), part)
    valence_density = normal_values(own_keys[1], (NK, NK, 2, NV, NV, NG), (2 * NK * NV) ** -0.5, 1.0, ((0, 4), (3, 2), (5, 2)))
    conduction_density = normal_values(own_keys[2], (NK, NK, 2, NC, NC, NG), (2 * NG * NC) ** -0.5, 0.0546875, ((0, 4), (5, 2)))
    screening = normal_values(own_keys[3], (NQ, 2, NG, NG), (2 * NG) ** -0.5, 0.109375, ((0, 4), (2, 2)))
    qpoint_map = draw_qpoint_map(jax.random.fold_in(seeds[9], 71), part)
    slot_owner = jax.random.permutation(seeds[5], NQ).astype(jnp.int32)
    band_pairs = jax.random.permutation(seeds[6], NBP).astype(jnp.int32)
    valence_energy = jnp.clip(-1.5 + 1.2 * jax.random.uniform(own_keys[7], (NK, NV), jnp.float32) ** shard_levels(own_keys[7], (NK, NV), ((0, 4),), -0.2, 0.2), -1.5, -0.3)
    conduction_energy = jnp.clip(0.3 + 1.2 * jax.random.uniform(own_keys[8], (NK, NC), jnp.float32) ** shard_levels(own_keys[8], (NK, NC), ((0, 4),), -0.2, 0.2), 0.3, 1.5)
    return dict(start_vector=start_vector, valence_density=valence_density, conduction_density=conduction_density, screening=screening, qpoint_map=qpoint_map, slot_owner=slot_owner, band_pairs=band_pairs, valence_energy=valence_energy, conduction_energy=conduction_energy)


exact_mode = lax.Precision.HIGHEST
epsilon = 1e-06

def transition_energy(valence_energy, conduction_energy, band_pairs):
    valence = (band_pairs // NC).astype(jnp.int32)
    conduction = (band_pairs % NC).astype(jnp.int32)
    return jnp.take(conduction_energy, conduction, axis=1) - jnp.take(valence_energy, valence, axis=1)

def apply_kernel(vector, valence_density, conduction_density, screening, slots, code_pick):
    pair_form = jnp.einsum('kpxb,bc->kpxc', vector, code_pick, precision=exact_mode).reshape(NK, NPOL, 2, NV, NC)
    kpoint_numbers = jnp.arange(NK, dtype=jnp.int32)

    def one_slot(running, slot_index):
        partner = lax.optimization_barrier(jnp.sum(jnp.where(slots == slot_index, kpoint_numbers[None, :], 0), axis=1)).astype(jnp.int32)
        val_rows = valence_density[kpoint_numbers, partner].astype(jnp.float32)
        chosen = jnp.take(pair_form, partner, axis=0)
        val_real = val_rows[:, 0]
        val_imag = val_rows[:, 1]
        vec_real = chosen[:, :, 0]
        vec_imag = chosen[:, :, 1]
        form = 'kvwg,kpwc->kpvcg'
        fold_real = jnp.einsum(form, val_real, vec_real, precision=exact_mode) - jnp.einsum(form, val_imag, vec_imag, precision=exact_mode)
        fold_imag = jnp.einsum(form, val_real, vec_imag, precision=exact_mode) + jnp.einsum(form, val_imag, vec_real, precision=exact_mode)
        folded = jnp.stack([fold_real, fold_imag], 4).astype(jnp.bfloat16)
        weights = lax.dynamic_index_in_dim(screening, slot_index, 0, keepdims=False).astype(jnp.float32).reshape(2 * NG, NG)
        images = lax.dot_general(folded.astype(jnp.float32).reshape(-1, NG), weights, (((1,), (1,)), ((), ())), precision=exact_mode)
        images = images.reshape(NK, NPOL, NV, NC, 2, 2, NG)
        scr_real = images[..., 0, 0, :] - images[..., 1, 1, :]
        scr_imag = images[..., 0, 1, :] + images[..., 1, 0, :]
        cond_rows = conduction_density[kpoint_numbers, partner].astype(jnp.float32)
        cond_real = cond_rows[:, 0]
        cond_imag = cond_rows[:, 1]
        project = 'kdeg,kpveg->kpvd'
        kern_real = jnp.einsum(project, cond_real, scr_real, precision=exact_mode) + jnp.einsum(project, cond_imag, scr_imag, precision=exact_mode)
        kern_imag = jnp.einsum(project, cond_real, scr_imag, precision=exact_mode) - jnp.einsum(project, cond_imag, scr_real, precision=exact_mode)
        return (running + jnp.stack([kern_real, kern_imag], 2), None)
    kernel = lax.scan(one_slot, jnp.zeros((NK, NPOL, 2, NV, NC), jnp.float32), jnp.arange(NQ, dtype=jnp.int32))[0]
    return jnp.einsum('kpxc,bc->kpxb', kernel.reshape(NK, NPOL, 2, NBP), code_pick, precision=exact_mode)

def mean_square(vector):
    return lax.optimization_barrier(jnp.sum(vector * vector, axis=(0, 2, 3))) / (NK * NBP)

def inner_product(left, right):
    real_part = lax.optimization_barrier(jnp.sum(left[:, :, 0] * right[:, :, 0] + left[:, :, 1] * right[:, :, 1], axis=(0, 2))) / (NK * NBP)
    imag_part = lax.optimization_barrier(jnp.sum(left[:, :, 0] * right[:, :, 1] - left[:, :, 1] * right[:, :, 0], axis=(0, 2))) / (NK * NBP)
    return (real_part, imag_part)

def scale_complex(coef_real, coef_imag, vector):
    vec_real = vector[:, :, 0]
    vec_imag = vector[:, :, 1]
    real_part = coef_real[None, :, None] * vec_real - coef_imag[None, :, None] * vec_imag
    imag_part = coef_real[None, :, None] * vec_imag + coef_imag[None, :, None] * vec_real
    return jnp.stack([real_part, imag_part], 2)

def reference(start_vector, valence_density, conduction_density, screening, qpoint_map, slot_owner, band_pairs, valence_energy, conduction_energy):
    energy = transition_energy(valence_energy, conduction_energy, band_pairs)[:, None, None, :]
    slots = jnp.take(slot_owner, qpoint_map).astype(jnp.int32)
    code_pick = (band_pairs[:, None] == jnp.arange(NBP, dtype=jnp.int32)[None, :]).astype(jnp.float32)

    def hamiltonian(vector):
        return energy * vector - apply_kernel(vector, valence_density, conduction_density, screening, slots, code_pick)
    norm_start = jnp.sqrt(mean_square(start_vector) + epsilon)
    first_vector = start_vector / norm_start[None, :, None, None]
    first_image = hamiltonian(first_vector)
    alpha_real, alpha_imag = inner_product(first_vector, first_image)
    first_resid = first_image - scale_complex(alpha_real, alpha_imag, first_vector)
    beta_one = jnp.sqrt(mean_square(first_resid) + epsilon)
    second_vector = first_resid / beta_one[None, :, None, None]
    second_image = hamiltonian(second_vector)
    gamma_real, gamma_imag = inner_product(second_vector, second_image)
    second_resid = second_image - scale_complex(gamma_real, gamma_imag, second_vector) - beta_one[None, :, None, None] * first_vector
    beta_two = jnp.sqrt(mean_square(second_resid) + epsilon)
    next_vector = second_resid / beta_two[None, :, None, None]
    coefficients = jnp.stack([alpha_real, alpha_imag, gamma_real, gamma_imag, beta_one, beta_two], 1)
    return (next_vector, coefficients)
```

```python
import functools

import jax
import jax.numpy as jnp
from jax import lax
from jax.experimental import pallas as pl
from jax.experimental.pallas import tpu as pltpu
from jax.sharding import PartitionSpec as P

EPSILON = 1e-06
EXACT = lax.Precision.HIGHEST
VMEM_LIMIT = 56 * 1024 * 1024

vmem = pl.BlockSpec(memory_space=pltpu.VMEM)
smem = pl.BlockSpec(memory_space=pltpu.SMEM)
anywhere = pl.BlockSpec(memory_space=pl.ANY)


def iota(shape, axis):
    return lax.broadcasted_iota(jnp.int32, shape, axis)


def split(values):
    high = values.astype(jnp.bfloat16)
    low = (values - high.astype(jnp.float32)).astype(jnp.bfloat16)
    return high, low


def route_kernel(ka, qmap, owner, valence, conduction, *rest):
    val_out, cond_out = rest[:ka], rest[ka : 2 * ka]
    partner, sems = rest[2 * ka :]
    me = lax.axis_index("ka")
    count = valence.shape[0]

    def note(k2, carry):
        partner[owner[qmap[me, k2]]] = k2
        return carry

    lax.fori_loop(0, count, note, 0)
    copies = []
    for j in range(ka):
        k2 = partner[lax.rem(me + j, ka)]
        copies.append(pltpu.make_async_copy(valence.at[k2], val_out[j], sems.at[0, j]))
        copies.append(pltpu.make_async_copy(conduction.at[k2], cond_out[j], sems.at[1, j]))
    for copy in copies:
        copy.start()
    for copy in copies:
        copy.wait()


def route(ka, qmap, owner, valence, conduction):
    val_shape = jax.ShapeDtypeStruct(valence.shape[1:], valence.dtype)
    cond_shape = jax.ShapeDtypeStruct(conduction.shape[1:], conduction.dtype)
    outs = pl.pallas_call(
        functools.partial(route_kernel, ka),
        out_shape=[val_shape] * ka + [cond_shape] * ka,
        in_specs=[smem, smem, anywhere, anywhere],
        out_specs=[anywhere] * (2 * ka),
        scratch_shapes=[pltpu.SMEM((owner.shape[0],), jnp.int32), pltpu.SemaphoreType.DMA((2, ka))],
        name="route",
    )(qmap, owner, valence, conduction)
    return outs[:ka], outs[ka:]


def screen_kernel(ka, ga, dims, *refs):
    vloc, val_count, cond_count = dims
    band_pairs, val_energy, cond_energy, start, screening = refs[:5]
    val_in = refs[5 : 5 + ka * ga]
    cond_in = refs[5 + ka * ga : 5 + ka * ga + ka]
    out = refs[5 + ka * ga + ka]
    near, far, cond = refs[5 + ka * ga + ka + 1 :]
    me = lax.axis_index("ka")
    mine = lax.axis_index("ga")
    half = lax.axis_index("ba")
    pairs = vloc * val_count
    block = 2 * pairs
    rows = ka * block
    codes = val_count * cond_count
    lanes = 2 * ka * codes
    cond_rows = cond_count * cond_count

    for r in range(ga):
        place = lax.rem(mine + ga - r, ga)
        for j in range(ka):
            piece = val_in[j * ga + r][...]
            wide = piece.astype(jnp.float32)
            turned = jnp.concatenate([-wide[pairs:], wide[:pairs]], 0).astype(jnp.bfloat16)
            near[place, j * block : (j + 1) * block, :] = piece
            near[place, rows + j * block : rows + (j + 1) * block, :] = turned
            far[place, j * block : (j + 1) * block, :] = turned
            far[place, rows + j * block : rows + (j + 1) * block, :] = -piece
    for j in range(ka):
        cond[j * 2 * cond_rows : (j + 1) * 2 * cond_rows, :] = cond_in[j][...]

    width = near.shape[2]
    fields = None
    for g in range(ga):
        for part, other in ((0, near), (1, far)):
            term = lax.dot_general(
                screening[part, :, g * width : (g + 1) * width],
                other[g],
                (((1,), (1,)), ((), ())),
                preferred_element_type=jnp.float32,
            )
            fields = term if fields is None else fields + term
    high, low = split(fields)
    cond_all = cond[...]
    crossed = jnp.dot(cond_all, high, preferred_element_type=jnp.float32) + jnp.dot(
        cond_all, low, preferred_element_type=jnp.float32
    )
    lane = iota((cond_rows, 2 * rows), 1)
    lane_j = lane % rows // block
    turned_lane = lane // rows
    kernel = jnp.zeros((cond_rows, 2 * rows), jnp.float32)
    for j in range(ka):
        base = j * 2 * cond_rows
        same = lane_j == j
        kernel = kernel + jnp.where(same & (turned_lane == 0), crossed[base : base + cond_rows], 0.0)
        kernel = kernel - jnp.where(
            same & (turned_lane == 1), crossed[base + cond_rows : base + 2 * cond_rows], 0.0
        )

    row = iota((2 * rows, lanes), 0)
    col = iota((2 * rows, lanes), 1)
    k_of_row = lax.rem(me + ka - row % rows // block, ka)
    want = (
        (row % block // pairs) * (ka * codes)
        + k_of_row * codes
        + (half * vloc + row % pairs // val_count) * cond_count
    )
    joined = (col - want >= 0) & (col - want < cond_count)
    kernel_high, kernel_low = split(kernel)
    stacked = jnp.concatenate([kernel_high, kernel_low], 0)
    same_c = iota((cond_rows, lanes), 0) // cond_count == iota((cond_rows, lanes), 1) % cond_count
    spread = []
    for v2 in range(val_count):
        pick = jnp.where(joined & (row % val_count == v2), 1.0, 0.0).astype(jnp.bfloat16)
        both = jnp.dot(stacked, pick, preferred_element_type=jnp.float32)
        spread.append(jnp.where(same_c, both[:cond_rows] + both[cond_rows:], 0.0))
    spread = jnp.concatenate(spread, 0)
    out_row = iota((codes, val_count * cond_rows), 0)
    out_col = iota((codes, val_count * cond_rows), 1)
    fold = (out_row // cond_count == out_col // cond_rows) & (
        out_row % cond_count == out_col % cond_count
    )
    fold = jnp.where(fold, 1.0, 0.0).astype(jnp.bfloat16)
    spread_high, spread_low = split(spread)
    out[0:codes, :] = jnp.dot(fold, spread_high, preferred_element_type=jnp.float32) + jnp.dot(
        fold, spread_low, preferred_element_type=jnp.float32
    )

    first = jnp.where((mine == 0) & (half == 0), 1.0, 0.0)
    band_row = iota((codes, lanes), 0)
    band_lane = iota((codes, lanes), 1)
    code = jnp.zeros((codes, lanes), jnp.int32)
    for b in range(codes):
        code = jnp.where(band_row == b, band_pairs[b], code)
    vectors = jnp.zeros((start.shape[1], lanes), jnp.float32)
    for part in range(2):
        spot = part * ka * codes + me * codes
        pick = jnp.where(band_lane == spot + code, first, 0.0)
        vectors = vectors + jnp.dot(start[0, :, part, :], pick, precision=EXACT)
    lane = iota((1, lanes), 1)
    energy = jnp.zeros((1, lanes), jnp.float32)
    for c in range(cond_count):
        energy = jnp.where(lane % cond_count == c, cond_energy[0, c], energy)
    for v in range(val_count):
        energy = energy - jnp.where(lane % codes // cond_count == v, val_energy[0, v], 0.0)
    energy = jnp.where(lane % (ka * codes) // codes == me, energy * first, 0.0)
    npol = start.shape[1]
    out[codes : codes + npol, :] = vectors
    out[codes + npol : codes + npol + 1, :] = energy


def screen(ka, ga, dims, band_pairs, val_energy, cond_energy, start, screening, val_blocks, cond_blocks):
    vloc, val_count, cond_count = dims
    codes = val_count * cond_count
    rows = ka * 2 * vloc * val_count
    width = screening.shape[2] // ga
    glocal = screening.shape[1]
    return pl.pallas_call(
        functools.partial(screen_kernel, ka, ga, dims),
        out_shape=jax.ShapeDtypeStruct((codes + 8, 2 * ka * codes), jnp.float32),
        in_specs=[smem, smem, smem] + [vmem] * (2 + len(val_blocks) + len(cond_blocks)),
        out_specs=vmem,
        scratch_shapes=[
            pltpu.VMEM((ga, 2 * rows, width), jnp.bfloat16),
            pltpu.VMEM((ga, 2 * rows, width), jnp.bfloat16),
            pltpu.VMEM((ka * 2 * cond_count * cond_count, glocal), jnp.bfloat16),
        ],
        compiler_params=pltpu.CompilerParams(vmem_limit_bytes=VMEM_LIMIT),
        name="screen",
    )(band_pairs, val_energy, cond_energy, start, screening, *val_blocks, *cond_blocks)


def haydock_kernel(ka, scale_count, npol, qmap, owner, band_pairs, pieces, next_out, coef_out, whole, matrix):
    me = lax.axis_index("ka")
    copies = pieces.shape[1]
    lanes = pieces.shape[3]
    codes = pieces.shape[2] - 8
    mid = lanes // 2
    for s in range(ka):
        total = pieces[s, 0]
        for other in range(1, copies):
            total = total + pieces[s, other]
        whole[s] = total
    extras = whole[0, codes:, :]
    for s in range(1, ka):
        extras = extras + whole[s, codes:, :]
    lane_k = iota((codes, lanes), 1) % mid // codes
    sign = jnp.where(iota((1, lanes), 1) < mid, -1.0, 1.0)
    for k2 in range(ka):
        block = jnp.zeros((codes, lanes), jnp.float32)
        for back in range(ka):
            slot = owner[qmap[0, back]]
            k = (k2 - back) % ka
            block = jnp.where(lane_k == k, whole[slot, :codes, :], block)
        matrix[k2 * codes : (k2 + 1) * codes, :] = block
        matrix[mid + k2 * codes : mid + (k2 + 1) * codes, :] = sign * pltpu.roll(block, mid, 1)
    full = matrix[...]
    energy = extras[npol : npol + 1]
    start = extras[:npol]

    def mean(values):
        return jnp.sum(values, axis=1, keepdims=True) / scale_count

    def norm(vector):
        return jnp.sqrt(mean(vector * vector) + EPSILON)

    def swap(vector):
        return pltpu.roll(vector, mid, 1)

    def hamiltonian(vector):
        return energy * vector - jnp.dot(vector, full, precision=EXACT)

    def inner(left, right):
        return mean(left * right), mean(-sign * left * swap(right))

    def times(real, imag, vector):
        return real * vector + imag * (sign * swap(vector))

    first = start / norm(start)
    first_image = hamiltonian(first)
    alpha_real, alpha_imag = inner(first, first_image)
    first_resid = first_image - times(alpha_real, alpha_imag, first)
    beta_one = norm(first_resid)
    second = first_resid / beta_one
    second_image = hamiltonian(second)
    gamma_real, gamma_imag = inner(second, second_image)
    second_resid = second_image - times(gamma_real, gamma_imag, second) - beta_one * first
    beta_two = norm(second_resid)
    following = second_resid / beta_two

    coef_lane = iota(coef_out.shape, 1)
    coefs = jnp.zeros(coef_out.shape, jnp.float32)
    for at, value in enumerate((alpha_real, alpha_imag, gamma_real, gamma_imag, beta_one, beta_two)):
        coefs = jnp.where(coef_lane == at, value, coefs)
    coef_out[...] = coefs
    band = iota((lanes, codes), 1)
    code = jnp.zeros((lanes, codes), jnp.int32)
    for b in range(codes):
        code = jnp.where(band == b, band_pairs[b], code)
    row = iota((lanes, codes), 0)
    for part in range(2):
        pick = jnp.where(row == part * mid + me * codes + code, 1.0, 0.0)
        next_out[0, :, part, :] = jnp.dot(following, pick, precision=EXACT)


def haydock(ka, scale_count, npol, qmap, owner, band_pairs, pieces):
    lanes = pieces.shape[3]
    codes = pieces.shape[2] - 8
    return pl.pallas_call(
        functools.partial(haydock_kernel, ka, scale_count, npol),
        out_shape=[
            jax.ShapeDtypeStruct((1, npol, 2, codes), jnp.float32),
            jax.ShapeDtypeStruct((npol, 6), jnp.float32),
        ],
        in_specs=[smem, smem, smem, vmem],
        out_specs=[vmem, vmem],
        scratch_shapes=[
            pltpu.VMEM((ka, codes + 8, lanes), jnp.float32),
            pltpu.VMEM((lanes, lanes), jnp.float32),
        ],
        compiler_params=pltpu.CompilerParams(vmem_limit_bytes=VMEM_LIMIT),
        name="haydock",
    )(qmap, owner, band_pairs, pieces)


def local(
    ka,
    ga,
    start_vector,
    valence_density,
    conduction_density,
    screening,
    qpoint_map,
    slot_owner,
    band_pairs,
    valence_energy,
    conduction_energy,
):
    npol = start_vector.shape[1]
    pair_count = start_vector.shape[3]
    kcount, vloc, val_count = qpoint_map.shape[0], valence_density.shape[3], valence_density.shape[4]
    cond_count = conduction_density.shape[3]
    glocal = valence_density.shape[5]
    valence = valence_density.reshape(kcount, 2 * vloc * val_count, glocal)
    conduction = conduction_density.reshape(kcount, 2 * cond_count * cond_count, glocal)
    val_out, cond_out = route(ka, qpoint_map, slot_owner, valence, conduction)

    def shifted(value, axis, size, by):
        if by == 0:
            return value
        return lax.ppermute(value, axis, [(i, (i + by) % size) for i in range(size)])

    arrived = [shifted(val_out[j], "ka", ka, j) for j in range(ka)]
    val_blocks = [shifted(arrived[j], "ga", ga, r) for j in range(ka) for r in range(ga)]
    cond_blocks = [shifted(cond_out[j], "ka", ka, j) for j in range(ka)]
    piece = screen(
        ka,
        ga,
        (vloc, val_count, cond_count),
        band_pairs,
        valence_energy,
        conduction_energy,
        start_vector,
        screening[0],
        val_blocks,
        cond_blocks,
    )
    pieces = lax.all_gather(piece, ("ka", "ga", "ba"), axis=0, tiled=False)
    pieces = pieces.reshape((ka, -1) + piece.shape)
    scale_count = float(kcount * pair_count)
    return tuple(haydock(ka, scale_count, npol, qpoint_map, slot_owner, band_pairs, pieces))


def solution(mesh):
    in_specs = (
        P(("grp", "ka"), None, None, None),
        P(("grp", "ka"), None, None, "ba", None, "ga"),
        P(("grp", "ka"), None, None, None, None, "ga"),
        P(("grp", "ka"), None, "ga", None),
        P(),
        P(),
        P(),
        P(("grp", "ka"), None),
        P(("grp", "ka"), None),
    )
    out_specs = (P(("grp", "ka"), None, None, None), P("grp", None))
    body = functools.partial(local, mesh.shape["ka"], mesh.shape["ga"])
    return jax.shard_map(body, mesh=mesh, in_specs=in_specs, out_specs=out_specs, check_vma=False)
```

```python
import functools
import math

import jax
import jax.numpy as jnp
from jax import lax
from jax.experimental import pallas as pl
from jax.experimental.pallas import tpu as pltpu
from jax.sharding import PartitionSpec as P

EPSILON = 1e-06
EXACT = lax.Precision.HIGHEST
VMEM_LEAST = 8 * 1024 * 1024
VMEM_MOST = 56 * 1024 * 1024

vmem = pl.BlockSpec(memory_space=pltpu.VMEM)
smem = pl.BlockSpec(memory_space=pltpu.SMEM)


def iota(shape, axis):
    return lax.broadcasted_iota(jnp.int32, shape, axis)


def split(values):
    high = values.astype(jnp.bfloat16)
    low = (values - high.astype(jnp.float32)).astype(jnp.bfloat16)
    return high, low


def in_vmem(shape, dtype):
    return pltpu.VMEM(shape, dtype)


def limits(*arrays):
    held = sum(math.prod(a.shape) * a.dtype.itemsize for a in arrays)
    return pltpu.CompilerParams(vmem_limit_bytes=min(VMEM_MOST, VMEM_LEAST + 4 * held))


def pack_kernel(ka, qmap, owner, valence, conduction, *rest):
    outs, partner = rest[:ka], rest[ka]
    me = lax.axis_index("ka")
    half = lax.axis_index("ba")
    count, width = valence.shape[1], valence.shape[5]
    cond_count = conduction.shape[3]
    share = cond_count // lax.axis_size("ba")
    val_rows = 2 * valence.shape[3] * valence.shape[4]
    cond_rows = 2 * share * cond_count

    def note(k2, carry):
        partner[owner[qmap[me, k2]]] = k2
        return carry

    lax.fori_loop(0, count, note, 0)
    for j in range(ka):
        k2 = partner[lax.rem(me + j, ka)]
        block = valence[0, k2].astype(jnp.float32).reshape(val_rows, width)
        outs[j][:val_rows, :] = block.astype(jnp.bfloat16)
        block = conduction[0, k2, :, pl.ds(half * share, share)].astype(jnp.float32)
        outs[j][val_rows:, :] = block.reshape(cond_rows, width).astype(jnp.bfloat16)


def pack(ka, ba, qmap, owner, valence, conduction):
    cond_count = conduction.shape[3]
    rows = 2 * valence.shape[3] * valence.shape[4] + 2 * cond_count // ba * cond_count
    shape = in_vmem((rows, valence.shape[5]), valence.dtype)
    return pl.pallas_call(
        functools.partial(pack_kernel, ka),
        out_shape=[shape] * ka,
        in_specs=[smem, smem, vmem, vmem],
        out_specs=[vmem] * ka,
        scratch_shapes=[pltpu.SMEM((owner.shape[0],), jnp.int32)],
        compiler_params=limits(valence, conduction),
        name="pack",
    )(qmap, owner, valence, conduction)


def regroup_kernel(ka, val_rows, *refs):
    blocks, val_all, cond_half = refs[:ka], refs[ka], refs[ka + 1]
    cond_rows = blocks[0].shape[0] - val_rows
    for j in range(ka):
        val_all[j * val_rows : (j + 1) * val_rows, :] = blocks[j][:val_rows, :]
        cond_half[j * cond_rows : (j + 1) * cond_rows, :] = blocks[j][val_rows:, :]


def regroup(ka, val_rows, blocks):
    rows, width = blocks[0].shape
    kind = blocks[0].dtype
    return pl.pallas_call(
        functools.partial(regroup_kernel, ka, val_rows),
        out_shape=[in_vmem((ka * val_rows, width), kind), in_vmem((ka * (rows - val_rows), width), kind)],
        in_specs=[vmem] * ka,
        out_specs=[vmem] * 2,
        compiler_params=limits(*blocks),
        name="regroup",
    )(*blocks)


def screened_block(screening, valence, pairs, place):
    wide = valence[...].astype(jnp.float32)
    parts = []
    for at in range(0, wide.shape[0], 2 * pairs):
        parts += [-wide[at + pairs : at + 2 * pairs], wide[at : at + pairs]]
    turned = jnp.concatenate(parts, 0)
    real = jnp.concatenate([wide, turned], 0).astype(jnp.bfloat16)
    imag = jnp.concatenate([turned, -wide], 0).astype(jnp.bfloat16)
    width = valence.shape[1]
    columns = pl.ds(pl.multiple_of(place * width, 128), width)
    form = (((1,), (1,)), ((), ()))
    return lax.dot_general(
        screening[0, 0, :, columns], real, form, preferred_element_type=jnp.float32
    ) + lax.dot_general(screening[0, 1, :, columns], imag, form, preferred_element_type=jnp.float32)


def near_kernel(pairs, screening, valence, out):
    out[...] = screened_block(screening, valence, pairs, lax.axis_index("ga"))


def near_field(pairs, screening, valence):
    rows, width = valence.shape
    glocal = screening.shape[2]
    return pl.pallas_call(
        functools.partial(near_kernel, pairs),
        out_shape=in_vmem((glocal, 2 * rows), jnp.float32),
        in_specs=[vmem, vmem],
        out_specs=vmem,
        cost_estimate=pl.CostEstimate(
            flops=8 * glocal * width * rows, bytes_accessed=screening.size, transcendentals=0
        ),
        compiler_params=limits(screening, valence),
        name="near_field",
    )(screening, valence)


def project_kernel(ka, ga, ba, dims, *refs):
    vloc, val_count, cond_count = dims
    band_pairs, val_energy, cond_energy, start, screening, near = refs[:6]
    val_in = refs[6 : 6 + ga - 1]
    cond_in = refs[6 + ga - 1 : 6 + ga - 1 + ba]
    out = refs[6 + ga - 1 + ba]
    me = lax.axis_index("ka")
    mine = lax.axis_index("ga")
    half = lax.axis_index("ba")
    pairs = vloc * val_count
    block = 2 * pairs
    rows = ka * block
    codes = val_count * cond_count
    lanes = 2 * ka * codes
    share = cond_count // ba
    cond_rows = cond_count * cond_count
    share_rows = share * cond_count

    fields = near[...]
    for r in range(1, ga):
        place = lax.rem(mine + ga - r, ga)
        fields = fields + screened_block(screening, val_in[r - 1], pairs, place)
    high, low = split(fields)
    lane = iota((share_rows, 2 * rows), 1)
    lane_j = lane % rows // block
    turned_lane = lane // rows
    kernel = []
    for h in range(ba):
        cond_all = cond_in[h][...]
        crossed = jnp.dot(cond_all, high, preferred_element_type=jnp.float32) + jnp.dot(
            cond_all, low, preferred_element_type=jnp.float32
        )
        total = jnp.zeros((share_rows, 2 * rows), jnp.float32)
        for j in range(ka):
            base = j * 2 * share_rows
            same = lane_j == j
            total = total + jnp.where(
                same & (turned_lane == 0), crossed[base : base + share_rows], 0.0
            )
            total = total - jnp.where(
                same & (turned_lane == 1), crossed[base + share_rows : base + 2 * share_rows], 0.0
            )
        kernel.append(total)
    kernel = jnp.concatenate(kernel, 0)

    row = iota((2 * rows, lanes), 0)
    col = iota((2 * rows, lanes), 1)
    k_of_row = lax.rem(me + ka - row % rows // block, ka)
    want = (
        (row % block // pairs) * (ka * codes)
        + k_of_row * codes
        + (half * vloc + row % pairs // val_count) * cond_count
    )
    joined = (col - want >= 0) & (col - want < cond_count)
    kernel_high, kernel_low = split(kernel)
    stacked = jnp.concatenate([kernel_high, kernel_low], 0)
    crow = iota((cond_rows, lanes), 0)
    c_of_row = lax.rem(half + ba - crow // share_rows, ba) * share + crow % share_rows // cond_count
    same_c = c_of_row == iota((cond_rows, lanes), 1) % cond_count
    spread = []
    for v2 in range(val_count):
        pick = jnp.where(joined & (row % val_count == v2), 1.0, 0.0).astype(jnp.bfloat16)
        both = jnp.dot(stacked, pick, preferred_element_type=jnp.float32)
        spread.append(jnp.where(same_c, both[:cond_rows] + both[cond_rows:], 0.0))
    spread = jnp.concatenate(spread, 0)
    out_row = iota((codes, val_count * cond_rows), 0)
    out_col = iota((codes, val_count * cond_rows), 1)
    fold = (out_row // cond_count == out_col // cond_rows) & (
        out_row % cond_count == out_col % cond_count
    )
    fold = jnp.where(fold, 1.0, 0.0).astype(jnp.bfloat16)
    spread_high, spread_low = split(spread)
    out[0:codes, :] = jnp.dot(fold, spread_high, preferred_element_type=jnp.float32) + jnp.dot(
        fold, spread_low, preferred_element_type=jnp.float32
    )

    first = jnp.where((mine == 0) & (half == 0), 1.0, 0.0)
    band_row = iota((codes, lanes), 0)
    band_lane = iota((codes, lanes), 1)
    code = jnp.zeros((codes, lanes), jnp.int32)
    for b in range(codes):
        code = jnp.where(band_row == b, band_pairs[b], code)
    npol = start.shape[1]
    vectors = jnp.zeros((npol, lanes), jnp.float32)
    for part in range(2):
        spot = part * ka * codes + me * codes
        pick = jnp.where(band_lane == spot + code, first, 0.0)
        vectors = vectors + jnp.dot(start[0, :, part, :], pick, precision=EXACT)
    lane = iota((1, lanes), 1)
    energy = jnp.zeros((1, lanes), jnp.float32)
    for c in range(cond_count):
        energy = jnp.where(lane % cond_count == c, cond_energy[0, c], energy)
    for v in range(val_count):
        energy = energy - jnp.where(lane % codes // cond_count == v, val_energy[0, v], 0.0)
    energy = jnp.where(lane % (ka * codes) // codes == me, energy * first, 0.0)
    rest = jnp.zeros((7 - npol, lanes), jnp.float32)
    out[codes:, :] = jnp.concatenate([vectors, energy, rest], 0)


def project(ka, ga, ba, dims, band_pairs, val_energy, cond_energy, start, screening, near, val_far, cond_all):
    vloc, val_count, cond_count = dims
    codes = val_count * cond_count
    return pl.pallas_call(
        functools.partial(project_kernel, ka, ga, ba, dims),
        out_shape=in_vmem((codes + 8, 2 * ka * codes), jnp.float32),
        in_specs=[smem, smem, smem] + [vmem] * (3 + len(val_far) + len(cond_all)),
        out_specs=vmem,
        compiler_params=limits(screening, near, *val_far, *cond_all),
        name="project",
    )(band_pairs, val_energy, cond_energy, start, screening, near, *val_far, *cond_all)


def haydock_kernel(ka, scale_count, npol, qmap, owner, band_pairs, *refs):
    pieces = refs[:ka]
    next_out, coef_out, whole, matrix = refs[ka:]
    me = lax.axis_index("ka")
    lanes = pieces[0].shape[1]
    codes = pieces[0].shape[0] - 8
    mid = lanes // 2
    for r in range(ka):
        whole[lax.rem(me + ka - r, ka)] = pieces[r][...]
    extras = whole[0, codes:, :]
    for s in range(1, ka):
        extras = extras + whole[s, codes:, :]
    lane_k = iota((codes, lanes), 1) % mid // codes
    sign = jnp.where(iota((1, lanes), 1) < mid, -1.0, 1.0)
    for k2 in range(ka):
        block = jnp.zeros((codes, lanes), jnp.float32)
        for back in range(ka):
            slot = owner[qmap[0, back]]
            k = (k2 - back) % ka
            block = jnp.where(lane_k == k, whole[slot, :codes, :], block)
        matrix[k2 * codes : (k2 + 1) * codes, :] = block
        matrix[mid + k2 * codes : mid + (k2 + 1) * codes, :] = sign * pltpu.roll(block, mid, 1)
    full = matrix[...]
    energy = extras[npol : npol + 1]
    start = extras[:npol]

    def mean(values):
        return jnp.sum(values, axis=1, keepdims=True) / scale_count

    def norm(vector):
        return jnp.sqrt(mean(vector * vector) + EPSILON)

    def swap(vector):
        return pltpu.roll(vector, mid, 1)

    def hamiltonian(vector):
        return energy * vector - jnp.dot(vector, full, precision=EXACT)

    def inner(left, right):
        return mean(left * right), mean(-sign * left * swap(right))

    def times(real, imag, vector):
        return real * vector + imag * (sign * swap(vector))

    first = start / norm(start)
    first_image = hamiltonian(first)
    alpha_real, alpha_imag = inner(first, first_image)
    first_resid = first_image - times(alpha_real, alpha_imag, first)
    beta_one = norm(first_resid)
    second = first_resid / beta_one
    second_image = hamiltonian(second)
    gamma_real, gamma_imag = inner(second, second_image)
    second_resid = second_image - times(gamma_real, gamma_imag, second) - beta_one * first
    beta_two = norm(second_resid)
    following = second_resid / beta_two

    coef_lane = iota(coef_out.shape, 1)
    coefs = jnp.zeros(coef_out.shape, jnp.float32)
    for at, value in enumerate((alpha_real, alpha_imag, gamma_real, gamma_imag, beta_one, beta_two)):
        coefs = jnp.where(coef_lane == at, value, coefs)
    coef_out[...] = coefs
    band = iota((lanes, codes), 1)
    code = jnp.zeros((lanes, codes), jnp.int32)
    for b in range(codes):
        code = jnp.where(band == b, band_pairs[b], code)
    row = iota((lanes, codes), 0)
    for part in range(2):
        pick = jnp.where(row == part * mid + me * codes + code, 1.0, 0.0)
        next_out[0, :, part, :] = jnp.dot(following, pick, precision=EXACT)


def haydock(ka, scale_count, npol, qmap, owner, band_pairs, pieces):
    lanes = pieces[0].shape[1]
    codes = pieces[0].shape[0] - 8
    return pl.pallas_call(
        functools.partial(haydock_kernel, ka, scale_count, npol),
        out_shape=[
            jax.ShapeDtypeStruct((1, npol, 2, codes), jnp.float32),
            jax.ShapeDtypeStruct((npol, 6), jnp.float32),
        ],
        in_specs=[smem, smem, smem] + [vmem] * ka,
        out_specs=[vmem, vmem],
        scratch_shapes=[
            pltpu.VMEM((ka, codes + 8, lanes), jnp.float32),
            pltpu.VMEM((lanes, lanes), jnp.float32),
        ],
        compiler_params=limits(*pieces, jax.ShapeDtypeStruct((lanes, lanes), jnp.float32)),
        name="haydock",
    )(qmap, owner, band_pairs, *pieces)


def shifted(value, axis, by):
    size = lax.axis_size(axis)
    return lax.ppermute(value, axis, [(i, (i + by) % size) for i in range(size)])


def summed(value, axis):
    size = lax.axis_size(axis)
    if size & (size - 1):
        return lax.psum(value, axis)
    step = 1
    while step < size:
        value = value + lax.ppermute(value, axis, [(i, i ^ step) for i in range(size)])
        step *= 2
    return value


def local(
    ka,
    ga,
    ba,
    start_vector,
    valence_density,
    conduction_density,
    screening,
    qpoint_map,
    slot_owner,
    band_pairs,
    valence_energy,
    conduction_energy,
):
    npol = start_vector.shape[1]
    pair_count = start_vector.shape[3]
    kcount, vloc, val_count = qpoint_map.shape[0], valence_density.shape[3], valence_density.shape[4]
    cond_count = conduction_density.shape[3]
    pairs = vloc * val_count
    screening = pltpu.with_memory_space_constraint(screening, pltpu.VMEM)
    packed = pack(ka, ba, qpoint_map, slot_owner, valence_density, conduction_density)
    blocks = [packed[0]] + [shifted(packed[j], "ka", j) for j in range(1, ka)]
    val_all, cond_half = regroup(ka, 2 * pairs, blocks)
    val_far = [shifted(val_all, "ga", r) for r in range(1, ga)]
    cond_all = [cond_half] + [shifted(cond_half, "ba", r) for r in range(1, ba)]
    near = near_field(pairs, screening, val_all)
    piece = project(
        ka,
        ga,
        ba,
        (vloc, val_count, cond_count),
        band_pairs,
        valence_energy,
        conduction_energy,
        start_vector,
        screening,
        near,
        val_far,
        cond_all,
    )
    piece = summed(summed(piece, "ba"), "ga")
    pieces = [piece] + [shifted(piece, "ka", j) for j in range(1, ka)]
    scale_count = float(kcount * pair_count)
    return tuple(haydock(ka, scale_count, npol, qpoint_map, slot_owner, band_pairs, pieces))


def solution(mesh):
    in_specs = (
        P(("grp", "ka"), None, None, None),
        P(("grp", "ka"), None, None, "ba", None, "ga"),
        P(("grp", "ka"), None, None, None, None, "ga"),
        P(("grp", "ka"), None, "ga", None),
        P(),
        P(),
        P(),
        P(("grp", "ka"), None),
        P(("grp", "ka"), None),
    )
    out_specs = (P(("grp", "ka"), None, None, None), P("grp", None))
    body = functools.partial(local, mesh.shape["ka"], mesh.shape["ga"], mesh.shape["ba"])
    return jax.shard_map(body, mesh=mesh, in_specs=in_specs, out_specs=out_specs, check_vma=False)
```

```python
import functools
import math

import jax
import jax.numpy as jnp
from jax import lax
from jax.experimental import pallas as pl
from jax.experimental.pallas import tpu as pltpu
from jax.sharding import PartitionSpec as P

EPSILON = 1e-06
EXACT = lax.Precision.HIGHEST
VMEM_LEAST = 8 * 1024 * 1024
VMEM_MOST = 56 * 1024 * 1024

vmem = pl.BlockSpec(memory_space=pltpu.VMEM)
anywhere = pl.BlockSpec(memory_space=pl.ANY)
EXTRA_ROWS = 8


def in_vmem(shape, dtype):
    return pltpu.VMEM(shape, dtype)


def placed(value, space):
    return pltpu.with_memory_space_constraint(value, space)


def iota(shape, axis):
    return lax.broadcasted_iota(jnp.int32, shape, axis)


def split(values):
    high = values.astype(jnp.bfloat16)
    low = (values - high.astype(jnp.float32)).astype(jnp.bfloat16)
    return high, low


def limits(*arrays):
    held = sum(math.prod(a.shape) * a.dtype.itemsize for a in arrays)
    return pltpu.CompilerParams(vmem_limit_bytes=min(VMEM_MOST, VMEM_LEAST + 4 * held))


def paired(me, step, size):
    if size & (size - 1):
        return lax.rem(me + step, size)
    return lax.bitwise_xor(me, step)


def origin(me, step, size):
    if size & (size - 1):
        return lax.rem(me + size - step, size)
    return lax.bitwise_xor(me, step)


def exchanged(value, axis, step):
    size = lax.axis_size(axis)
    if size & (size - 1):
        return lax.ppermute(value, axis, [(i, (i + step) % size) for i in range(size)])
    return lax.ppermute(value, axis, [(i, i ^ step) for i in range(size)])


def pack_kernel(ka, qmap_in, owner_in, valence_in, conduction_in, *rest):
    outs = rest[:ka]
    qmap, owner, partner, valence, conduction, sems = rest[ka:]
    copies = [
        pltpu.make_async_copy(src, dst, sems.at[at])
        for at, (src, dst) in enumerate(
            ((qmap_in, qmap), (owner_in, owner), (valence_in, valence), (conduction_in, conduction))
        )
    ]
    for copy in copies:
        copy.start()
    me = lax.axis_index("ka")
    half = lax.axis_index("ba")
    count, width = valence.shape[1], valence.shape[5]
    cond_count = conduction.shape[3]
    share = cond_count // lax.axis_size("ba")
    val_rows = 2 * valence.shape[3] * valence.shape[4]
    cond_rows = 2 * share * cond_count

    def note(k2, carry):
        partner[owner[qmap[me, k2]]] = k2
        return carry

    copies[0].wait()
    copies[1].wait()
    lax.fori_loop(0, count, note, 0)
    copies[2].wait()
    copies[3].wait()
    for j in range(ka):
        k2 = partner[paired(me, j, ka)]
        block = valence[0, k2].astype(jnp.float32).reshape(val_rows, width)
        outs[j][:val_rows, :] = block.astype(jnp.bfloat16)
        block = conduction[0, k2, :, pl.ds(half * share, share)].astype(jnp.float32)
        outs[j][val_rows:, :] = block.reshape(cond_rows, width).astype(jnp.bfloat16)


def pack(ka, ba, qmap, owner, valence, conduction):
    cond_count = conduction.shape[3]
    rows = 2 * valence.shape[3] * valence.shape[4] + 2 * cond_count // ba * cond_count
    shape = in_vmem((rows, valence.shape[5]), valence.dtype)
    operands = [placed(x, pltpu.HBM) for x in (qmap, owner, valence, conduction)]
    return pl.pallas_call(
        functools.partial(pack_kernel, ka),
        out_shape=[shape] * ka,
        in_specs=[anywhere] * 4,
        out_specs=[vmem] * ka,
        scratch_shapes=[
            pltpu.SMEM(qmap.shape, jnp.int32),
            pltpu.SMEM(owner.shape, jnp.int32),
            pltpu.SMEM(owner.shape, jnp.int32),
            pltpu.VMEM(valence.shape, valence.dtype),
            pltpu.VMEM(conduction.shape, conduction.dtype),
            pltpu.SemaphoreType.DMA((4,)),
        ],
        compiler_params=limits(valence, conduction),
        name="pack",
    )(*operands)


def prepare_kernel(ka, dims, *refs):
    vloc, val_count, cond_count, npol = dims
    ins, (screen_out, table, extras), scratch = refs[:7], refs[7:10], refs[10:]
    screen_in = ins[6]
    qmap, owner, band_pairs, val_energy, cond_energy, start, sems = scratch
    copies = [
        pltpu.make_async_copy(src, dst, sems.at[at])
        for at, (src, dst) in enumerate(
            zip(ins, (qmap, owner, band_pairs, val_energy, cond_energy, start, screen_out))
        )
    ]
    for copy in copies:
        copy.start()
    me = lax.axis_index("ka")
    half = lax.axis_index("ba")
    mine = lax.axis_index("ga")
    pairs = vloc * val_count
    block = 2 * pairs
    rows = ka * block
    codes = val_count * cond_count
    mid = ka * codes
    lanes = 2 * mid
    row = iota((2 * rows, lanes), 0)
    col = iota((2 * rows, lanes), 1)
    k_of_row = origin(me, row % rows // block, ka)
    want = (
        (row % block // pairs) * mid
        + k_of_row * codes
        + (half * vloc + row % pairs // val_count) * cond_count
    )
    joined = (col - want >= 0) & (col - want < cond_count)
    for v2 in range(val_count):
        pick = jnp.where(joined & (row % val_count == v2), 1.0, 0.0)
        table[:, v2 * lanes : (v2 + 1) * lanes] = pick.astype(jnp.bfloat16)

    for copy in copies[:6]:
        copy.wait()
    first = jnp.where((mine == 0) & (half == 0), 1.0, 0.0)
    lane = iota((1, lanes), 1)
    lane_k = lane % mid // codes
    band_row = iota((codes, lanes), 0)
    band_lane = iota((codes, lanes), 1)
    code = jnp.zeros((codes, lanes), jnp.int32)
    bands = jnp.full((1, lanes), -1.0, jnp.float32)
    for b in range(codes):
        code = jnp.where(band_row == b, band_pairs[b], code)
        bands = jnp.where(lane % codes == band_pairs[b], float(b), bands)
    vectors = jnp.zeros((npol, lanes), jnp.float32)
    for part in range(2):
        spot = part * mid + me * codes
        pick = jnp.where(band_lane == spot + code, first, 0.0)
        vectors = vectors + jnp.dot(start[0, :, part, :], pick, precision=EXACT)
    energy = jnp.zeros((1, lanes), jnp.float32)
    for c in range(cond_count):
        energy = jnp.where(lane % cond_count == c, cond_energy[0, c], energy)
    for v in range(val_count):
        energy = energy - jnp.where(lane % codes // cond_count == v, val_energy[0, v], 0.0)
    energy = jnp.where(lane_k == me, energy * first, 0.0)
    kcount = qmap.shape[0]

    def find(k2, found):
        return jnp.where(owner[qmap[0, k2]] == me, k2, found)

    back = lax.fori_loop(0, kcount, find, 0)
    second = lane_k + back
    second = jnp.where(second >= kcount, second - kcount, second).astype(jnp.float32) * first
    rest = jnp.zeros((EXTRA_ROWS - 3 - npol, lanes), jnp.float32)
    extras[...] = jnp.concatenate([vectors, energy, bands * first, second, rest], 0)
    copies[6].wait()


def prepare(ka, dims, qmap, owner, band_pairs, val_energy, cond_energy, start, screening):
    vloc, val_count, cond_count, npol = dims
    rows = 4 * ka * vloc * val_count
    lanes = 2 * ka * val_count * cond_count
    operands = (qmap, owner, band_pairs, val_energy, cond_energy, start, screening)
    table = jax.ShapeDtypeStruct((rows, val_count * lanes), jnp.bfloat16)
    return pl.pallas_call(
        functools.partial(prepare_kernel, ka, dims),
        out_shape=[
            in_vmem(screening.shape, screening.dtype),
            in_vmem(table.shape, table.dtype),
            in_vmem((EXTRA_ROWS, lanes), jnp.float32),
        ],
        in_specs=[anywhere] * 7,
        out_specs=[vmem] * 3,
        scratch_shapes=[pltpu.SMEM(x.shape, x.dtype) for x in operands[:5]]
        + [pltpu.VMEM(start.shape, start.dtype), pltpu.SemaphoreType.DMA((7,))],
        cost_estimate=pl.CostEstimate(
            flops=0, bytes_accessed=2 * screening.size * screening.dtype.itemsize, transcendentals=0
        ),
        compiler_params=limits(table),
        name="prepare",
    )(*[placed(x, pltpu.HBM) for x in operands])


def regroup_kernel(ka, val_rows, *refs):
    blocks, val_all, cond_half = refs[:ka], refs[ka], refs[ka + 1]
    cond_rows = blocks[0].shape[0] - val_rows
    for j in range(ka):
        val_all[j * val_rows : (j + 1) * val_rows, :] = blocks[j][:val_rows, :]
        cond_half[j * cond_rows : (j + 1) * cond_rows, :] = blocks[j][val_rows:, :]


def regroup(ka, val_rows, blocks):
    rows, width = blocks[0].shape
    kind = blocks[0].dtype
    return pl.pallas_call(
        functools.partial(regroup_kernel, ka, val_rows),
        out_shape=[in_vmem((ka * val_rows, width), kind), in_vmem((ka * (rows - val_rows), width), kind)],
        in_specs=[vmem] * ka,
        out_specs=[vmem] * 2,
        compiler_params=limits(*blocks),
        name="regroup",
    )(*blocks)


def screened_block(screening, valence, pairs, place):
    wide = valence[...].astype(jnp.float32)
    parts = []
    for at in range(0, wide.shape[0], 2 * pairs):
        parts += [-wide[at + pairs : at + 2 * pairs], wide[at : at + pairs]]
    turned = jnp.concatenate(parts, 0)
    real = jnp.concatenate([wide, turned], 0).astype(jnp.bfloat16)
    imag = jnp.concatenate([turned, -wide], 0).astype(jnp.bfloat16)
    width = valence.shape[1]
    columns = pl.ds(pl.multiple_of(place * width, 128), width)
    form = (((1,), (1,)), ((), ()))
    return lax.dot_general(
        screening[0, 0, :, columns], real, form, preferred_element_type=jnp.float32
    ) + lax.dot_general(screening[0, 1, :, columns], imag, form, preferred_element_type=jnp.float32)


def near_kernel(pairs, screening, valence, out):
    out[...] = screened_block(screening, valence, pairs, lax.axis_index("ga"))


def near_field(pairs, screening, valence):
    rows, width = valence.shape
    glocal = screening.shape[2]
    return pl.pallas_call(
        functools.partial(near_kernel, pairs),
        out_shape=in_vmem((glocal, 2 * rows), jnp.float32),
        in_specs=[vmem, vmem],
        out_specs=vmem,
        cost_estimate=pl.CostEstimate(
            flops=8 * glocal * width * rows, bytes_accessed=screening.size, transcendentals=0
        ),
        compiler_params=limits(screening, valence),
        name="near_field",
    )(screening, valence)


def project_kernel(ka, ga, ba, dims, *refs):
    vloc, val_count, cond_count, npol = dims
    screening, table, extras, near = refs[:4]
    val_in = refs[4 : 4 + ga - 1]
    cond_in = refs[4 + ga - 1 : 4 + ga - 1 + ba]
    out = refs[4 + ga - 1 + ba]
    mine = lax.axis_index("ga")
    half = lax.axis_index("ba")
    pairs = vloc * val_count
    block = 2 * pairs
    rows = ka * block
    codes = val_count * cond_count
    lanes = 2 * ka * codes
    share = cond_count // ba
    cond_rows = cond_count * cond_count
    share_rows = share * cond_count

    fields = near[...]
    for r in range(1, ga):
        fields = fields + screened_block(screening, val_in[r - 1], pairs, origin(mine, r, ga))
    high, low = split(fields)
    lane = iota((share_rows, 2 * rows), 1)
    lane_j = lane % rows // block
    turned_lane = lane // rows
    kernel = []
    for h in range(ba):
        cond_all = cond_in[h][...]
        crossed = jnp.dot(cond_all, high, preferred_element_type=jnp.float32) + jnp.dot(
            cond_all, low, preferred_element_type=jnp.float32
        )
        total = jnp.zeros((share_rows, 2 * rows), jnp.float32)
        for j in range(ka):
            base = j * 2 * share_rows
            same = lane_j == j
            total = total + jnp.where(
                same & (turned_lane == 0), crossed[base : base + share_rows], 0.0
            )
            total = total - jnp.where(
                same & (turned_lane == 1), crossed[base + share_rows : base + 2 * share_rows], 0.0
            )
        kernel.append(total)
    kernel = jnp.concatenate(kernel, 0)

    kernel_high, kernel_low = split(kernel)
    stacked = jnp.concatenate([kernel_high, kernel_low], 0)
    crow = iota((cond_rows, lanes), 0)
    c_of_row = origin(half, crow // share_rows, ba) * share + crow % share_rows // cond_count
    same_c = c_of_row == iota((cond_rows, lanes), 1) % cond_count
    spread = []
    for v2 in range(val_count):
        both = jnp.dot(
            stacked, table[:, v2 * lanes : (v2 + 1) * lanes], preferred_element_type=jnp.float32
        )
        spread.append(jnp.where(same_c, both[:cond_rows] + both[cond_rows:], 0.0))
    spread = jnp.concatenate(spread, 0)
    out_row = iota((codes, val_count * cond_rows), 0)
    out_col = iota((codes, val_count * cond_rows), 1)
    fold = (out_row // cond_count == out_col // cond_rows) & (
        out_row % cond_count == out_col % cond_count
    )
    fold = jnp.where(fold, 1.0, 0.0).astype(jnp.bfloat16)
    spread_high, spread_low = split(spread)
    out[:codes, :] = jnp.dot(fold, spread_high, preferred_element_type=jnp.float32) + jnp.dot(
        fold, spread_low, preferred_element_type=jnp.float32
    )
    out[codes:, :] = extras[...]


def project(ka, ga, ba, dims, screening, table, extras, near, val_far, cond_all):
    vloc, val_count, cond_count, npol = dims
    codes = val_count * cond_count
    operands = [screening, table, extras, near, *val_far, *cond_all]
    return pl.pallas_call(
        functools.partial(project_kernel, ka, ga, ba, dims),
        out_shape=in_vmem((codes + EXTRA_ROWS, 2 * ka * codes), jnp.float32),
        in_specs=[vmem] * len(operands),
        out_specs=vmem,
        compiler_params=limits(*operands[1:]),
        name="project",
    )(*operands)


def haydock_kernel(ka, codes, scale_count, npol, *refs):
    pieces = refs[:-3]
    next_out, coef_out, matrix = refs[-3:]
    lanes = pieces[0].shape[1]
    mid = lanes // 2
    height = codes + EXTRA_ROWS
    found = [(ref, at) for ref in pieces for at in range(0, ref.shape[0], height)]
    extras = None
    slots = []
    for ref, at in found:
        rows = ref[at + codes : at + height, :]
        extras = rows if extras is None else extras + rows
        slots.append((ref[at : at + codes, :], rows[npol + 2 : npol + 3]))
    own = pieces[0][codes:height, :]
    sign = jnp.where(iota((1, lanes), 1) < mid, -1.0, 1.0)
    for k2 in range(ka):
        block = jnp.zeros((codes, lanes), jnp.float32)
        for piece, second in slots:
            block = jnp.where(second == float(k2), piece, block)
        matrix[k2 * codes : (k2 + 1) * codes, :] = block
        matrix[mid + k2 * codes : mid + (k2 + 1) * codes, :] = sign * pltpu.roll(block, mid, 1)
    full = matrix[...]
    start = extras[:npol]
    energy = extras[npol : npol + 1]

    def mean(values):
        return jnp.sum(values, axis=1, keepdims=True) / scale_count

    def norm(vector):
        return jnp.sqrt(mean(vector * vector) + EPSILON)

    def swap(vector):
        return pltpu.roll(vector, mid, 1)

    def hamiltonian(vector):
        return energy * vector - jnp.dot(vector, full, precision=EXACT)

    def inner(left, right):
        return mean(left * right), mean(-sign * left * swap(right))

    def times(real, imag, vector):
        return real * vector + imag * (sign * swap(vector))

    first = start / norm(start)
    first_image = hamiltonian(first)
    alpha_real, alpha_imag = inner(first, first_image)
    first_resid = first_image - times(alpha_real, alpha_imag, first)
    beta_one = norm(first_resid)
    second = first_resid / beta_one
    second_image = hamiltonian(second)
    gamma_real, gamma_imag = inner(second, second_image)
    second_resid = second_image - times(gamma_real, gamma_imag, second) - beta_one * first
    beta_two = norm(second_resid)
    following = second_resid / beta_two

    coef_lane = iota(coef_out.shape, 1)
    coefs = jnp.zeros(coef_out.shape, jnp.float32)
    for at, value in enumerate((alpha_real, alpha_imag, gamma_real, gamma_imag, beta_one, beta_two)):
        coefs = jnp.where(coef_lane == at, value, coefs)
    coef_out[...] = coefs
    band = iota((codes, lanes), 0).astype(jnp.float32)
    here = iota((codes, lanes), 1) % mid // codes == lax.axis_index("ka")
    for part in range(2):
        half = iota((codes, lanes), 1) // mid == part
        pick = jnp.where(here & half & (own[npol + 1 : npol + 2] == band), 1.0, 0.0)
        next_out[0, :, part, :] = lax.dot_general(
            following, pick, (((1,), (1,)), ((), ())), precision=EXACT
        )


def haydock(ka, codes, scale_count, npol, pieces):
    lanes = pieces[0].shape[1]
    square = jax.ShapeDtypeStruct((lanes, lanes), jnp.float32)
    return pl.pallas_call(
        functools.partial(haydock_kernel, ka, codes, scale_count, npol),
        out_shape=[
            jax.ShapeDtypeStruct((1, npol, 2, codes), jnp.float32),
            jax.ShapeDtypeStruct((npol, 6), jnp.float32),
        ],
        in_specs=[vmem] * len(pieces),
        out_specs=[vmem, vmem],
        scratch_shapes=[pltpu.VMEM(square.shape, square.dtype)],
        compiler_params=limits(*pieces, square),
        name="haydock",
    )(*pieces)


def summed(value, axis):
    size = lax.axis_size(axis)
    if size & (size - 1):
        return lax.psum(value, axis)
    step = 1
    while step < size:
        value = value + exchanged(value, axis, step)
        step *= 2
    return value


def gathered(value, axis):
    size = lax.axis_size(axis)
    if size & (size - 1):
        return [value] + [exchanged(value, axis, j) for j in range(1, size)]
    step = 1
    while True:
        other = exchanged(value, axis, step)
        step *= 2
        if step >= size:
            return [value, other]
        value = jnp.concatenate([value, other], 0)


def local(
    ka,
    ga,
    ba,
    start_vector,
    valence_density,
    conduction_density,
    screening,
    qpoint_map,
    slot_owner,
    band_pairs,
    valence_energy,
    conduction_energy,
):
    npol = start_vector.shape[1]
    pair_count = start_vector.shape[3]
    kcount, vloc, val_count = qpoint_map.shape[0], valence_density.shape[3], valence_density.shape[4]
    cond_count = conduction_density.shape[3]
    pairs = vloc * val_count
    dims = (vloc, val_count, cond_count, npol)
    packed = pack(ka, ba, qpoint_map, slot_owner, valence_density, conduction_density)
    blocks = [packed[0]] + [exchanged(packed[j], "ka", j) for j in range(1, ka)]
    screening, table, extras = prepare(
        ka,
        dims,
        qpoint_map,
        slot_owner,
        band_pairs,
        valence_energy,
        conduction_energy,
        start_vector,
        screening,
    )
    val_all, cond_half = regroup(ka, 2 * pairs, blocks)
    cond_all = [cond_half] + [exchanged(cond_half, "ba", r) for r in range(1, ba)]
    val_far = [exchanged(val_all, "ga", r) for r in range(1, ga)]
    near = near_field(pairs, screening, val_all)
    piece = project(ka, ga, ba, dims, screening, table, extras, near, val_far, cond_all)
    piece = summed(summed(piece, "ba"), "ga")
    pieces = gathered(piece, "ka") if ka > 1 else [piece]
    scale_count = float(kcount * pair_count)
    return tuple(haydock(ka, pair_count, scale_count, npol, pieces))


def solution(mesh):
    in_specs = (
        P(("grp", "ka"), None, None, None),
        P(("grp", "ka"), None, None, "ba", None, "ga"),
        P(("grp", "ka"), None, None, None, None, "ga"),
        P(("grp", "ka"), None, "ga", None),
        P(),
        P(),
        P(),
        P(("grp", "ka"), None),
        P(("grp", "ka"), None),
    )
    out_specs = (P(("grp", "ka"), None, None, None), P("grp", None))
    body = functools.partial(local, mesh.shape["ka"], mesh.shape["ga"], mesh.shape["ba"])
    return jax.shard_map(body, mesh=mesh, in_specs=in_specs, out_specs=out_specs, check_vma=False)
```

```python
import functools
import math

import jax
import jax.numpy as jnp
from jax import lax
from jax.experimental import pallas as pl
from jax.experimental.pallas import tpu as pltpu
from jax.sharding import PartitionSpec as P

EPSILON = 1e-06
EXACT = lax.Precision.HIGHEST
VMEM_LEAST = 8 * 1024 * 1024
VMEM_MOST = 56 * 1024 * 1024

vmem = pl.BlockSpec(memory_space=pltpu.VMEM)
anywhere = pl.BlockSpec(memory_space=pl.ANY)
EXTRA_ROWS = 8


def in_vmem(shape, dtype):
    return pltpu.VMEM(shape, dtype)


def placed(value, space):
    return pltpu.with_memory_space_constraint(value, space)


def iota(shape, axis):
    return lax.broadcasted_iota(jnp.int32, shape, axis)


def split(values):
    high = values.astype(jnp.bfloat16)
    low = (values - high.astype(jnp.float32)).astype(jnp.bfloat16)
    return high, low


def limits(*arrays):
    held = sum(math.prod(a.shape) * a.dtype.itemsize for a in arrays)
    return pltpu.CompilerParams(vmem_limit_bytes=min(VMEM_MOST, VMEM_LEAST + 4 * held))


def paired(me, step, size):
    if size & (size - 1):
        return lax.rem(me + step, size)
    return lax.bitwise_xor(me, step)


def origin(me, step, size):
    if size & (size - 1):
        return lax.rem(me + size - step, size)
    return lax.bitwise_xor(me, step)


def exchanged(value, axis, step):
    size = lax.axis_size(axis)
    if size & (size - 1):
        return lax.ppermute(value, axis, [(i, (i + step) % size) for i in range(size)])
    return lax.ppermute(value, axis, [(i, i ^ step) for i in range(size)])


def pack_kernel(ka, qmap_in, owner_in, valence_in, conduction_in, *rest):
    outs = rest[:1] + rest[1:ka][::-1]
    qmap, owner, partner, valence, conduction, sems = rest[ka:]
    copies = [
        pltpu.make_async_copy(src, dst, sems.at[at])
        for at, (src, dst) in enumerate(
            ((qmap_in, qmap), (owner_in, owner), (valence_in, valence), (conduction_in, conduction))
        )
    ]
    for copy in copies:
        copy.start()
    me = lax.axis_index("ka")
    half = lax.axis_index("ba")
    count, width = valence.shape[1], valence.shape[5]
    cond_count = conduction.shape[3]
    share = cond_count // lax.axis_size("ba")
    val_rows = 2 * valence.shape[3] * valence.shape[4]
    cond_rows = 2 * share * cond_count

    def note(k2, carry):
        partner[owner[qmap[me, k2]]] = k2
        return carry

    copies[0].wait()
    copies[1].wait()
    lax.fori_loop(0, count, note, 0)
    copies[2].wait()
    copies[3].wait()
    for j in range(ka):
        k2 = partner[paired(me, j, ka)]
        block = valence[0, k2].astype(jnp.float32).reshape(val_rows, width)
        outs[j][:val_rows, :] = block.astype(jnp.bfloat16)
        block = conduction[0, k2, :, pl.ds(half * share, share)].astype(jnp.float32)
        outs[j][val_rows:, :] = block.reshape(cond_rows, width).astype(jnp.bfloat16)


def pack(ka, ba, qmap, owner, valence, conduction):
    cond_count = conduction.shape[3]
    rows = 2 * valence.shape[3] * valence.shape[4] + 2 * cond_count // ba * cond_count
    shape = in_vmem((rows, valence.shape[5]), valence.dtype)
    operands = [placed(x, pltpu.HBM) for x in (qmap, owner, valence, conduction)]
    outs = pl.pallas_call(
        functools.partial(pack_kernel, ka),
        out_shape=[shape] * ka,
        in_specs=[anywhere] * 4,
        out_specs=[vmem] * ka,
        scratch_shapes=[
            pltpu.SMEM(qmap.shape, jnp.int32),
            pltpu.SMEM(owner.shape, jnp.int32),
            pltpu.SMEM(owner.shape, jnp.int32),
            pltpu.VMEM(valence.shape, valence.dtype),
            pltpu.VMEM(conduction.shape, conduction.dtype),
            pltpu.SemaphoreType.DMA((4,)),
        ],
        compiler_params=limits(valence, conduction),
        name="pack",
    )(*operands)
    return outs[:1] + outs[1:][::-1]


def prepare_kernel(ka, dims, *refs):
    vloc, val_count, cond_count, npol = dims
    ins, (screen_out, table, extras), scratch = refs[:7], refs[7:10], refs[10:]
    screen_in = ins[6]
    qmap, owner, band_pairs, val_energy, cond_energy, start, sems = scratch
    copies = [
        pltpu.make_async_copy(src, dst, sems.at[at])
        for at, (src, dst) in enumerate(
            zip(ins, (qmap, owner, band_pairs, val_energy, cond_energy, start, screen_out))
        )
    ]
    for copy in copies:
        copy.start()
    me = lax.axis_index("ka")
    half = lax.axis_index("ba")
    mine = lax.axis_index("ga")
    pairs = vloc * val_count
    block = 2 * pairs
    rows = ka * block
    codes = val_count * cond_count
    mid = ka * codes
    lanes = 2 * mid
    row = iota((2 * rows, lanes), 0)
    col = iota((2 * rows, lanes), 1)
    k_of_row = origin(me, row % rows // block, ka)
    want = (
        (row % block // pairs) * mid
        + k_of_row * codes
        + (half * vloc + row % pairs // val_count) * cond_count
    )
    joined = (col - want >= 0) & (col - want < cond_count)
    for v2 in range(val_count):
        pick = jnp.where(joined & (row % val_count == v2), 1.0, 0.0)
        table[:, v2 * lanes : (v2 + 1) * lanes] = pick.astype(jnp.bfloat16)

    for copy in copies[:6]:
        copy.wait()
    first = jnp.where((mine == 0) & (half == 0), 1.0, 0.0)
    lane = iota((1, lanes), 1)
    lane_k = lane % mid // codes
    band_row = iota((codes, lanes), 0)
    band_lane = iota((codes, lanes), 1)
    code = jnp.zeros((codes, lanes), jnp.int32)
    bands = jnp.full((1, lanes), -1.0, jnp.float32)
    for b in range(codes):
        code = jnp.where(band_row == b, band_pairs[b], code)
        bands = jnp.where(lane % codes == band_pairs[b], float(b), bands)
    vectors = jnp.zeros((npol, lanes), jnp.float32)
    for part in range(2):
        spot = part * mid + me * codes
        pick = jnp.where(band_lane == spot + code, first, 0.0)
        vectors = vectors + jnp.dot(start[0, :, part, :], pick, precision=EXACT)
    energy = jnp.zeros((1, lanes), jnp.float32)
    for c in range(cond_count):
        energy = jnp.where(lane % cond_count == c, cond_energy[0, c], energy)
    for v in range(val_count):
        energy = energy - jnp.where(lane % codes // cond_count == v, val_energy[0, v], 0.0)
    energy = jnp.where(lane_k == me, energy * first, 0.0)
    kcount = qmap.shape[0]

    def find(k2, found):
        return jnp.where(owner[qmap[0, k2]] == me, k2, found)

    back = lax.fori_loop(0, kcount, find, 0)
    second = lane_k + back
    second = jnp.where(second >= kcount, second - kcount, second).astype(jnp.float32) * first
    rest = jnp.zeros((EXTRA_ROWS - 3 - npol, lanes), jnp.float32)
    extras[...] = jnp.concatenate([vectors, energy, bands * first, second, rest], 0)
    copies[6].wait()


def prepare(ka, dims, qmap, owner, band_pairs, val_energy, cond_energy, start, screening):
    vloc, val_count, cond_count, npol = dims
    rows = 4 * ka * vloc * val_count
    lanes = 2 * ka * val_count * cond_count
    operands = (qmap, owner, band_pairs, val_energy, cond_energy, start, screening)
    table = jax.ShapeDtypeStruct((rows, val_count * lanes), jnp.bfloat16)
    return pl.pallas_call(
        functools.partial(prepare_kernel, ka, dims),
        out_shape=[
            in_vmem(screening.shape, screening.dtype),
            in_vmem(table.shape, table.dtype),
            in_vmem((EXTRA_ROWS, lanes), jnp.float32),
        ],
        in_specs=[anywhere] * 7,
        out_specs=[vmem] * 3,
        scratch_shapes=[pltpu.SMEM(x.shape, x.dtype) for x in operands[:5]]
        + [pltpu.VMEM(start.shape, start.dtype), pltpu.SemaphoreType.DMA((7,))],
        cost_estimate=pl.CostEstimate(
            flops=0, bytes_accessed=2 * screening.size * screening.dtype.itemsize, transcendentals=0
        ),
        compiler_params=limits(table),
        name="prepare",
    )(*[placed(x, pltpu.HBM) for x in operands])


def regroup_kernel(ka, val_rows, *refs):
    blocks, (val_all, cond_half) = refs[:ka], refs[-2:]
    cond_rows = blocks[0].shape[0] - val_rows
    for j in range(ka):
        val_all[j * val_rows : (j + 1) * val_rows, :] = blocks[j][:val_rows, :]
        cond_half[j * cond_rows : (j + 1) * cond_rows, :] = blocks[j][val_rows:, :]


def regroup(ka, val_rows, blocks, after):
    rows, width = blocks[0].shape
    kind = blocks[0].dtype
    return pl.pallas_call(
        functools.partial(regroup_kernel, ka, val_rows),
        out_shape=[in_vmem((ka * val_rows, width), kind), in_vmem((ka * (rows - val_rows), width), kind)],
        in_specs=[vmem] * (ka + 1),
        out_specs=[vmem] * 2,
        compiler_params=limits(*blocks),
        name="regroup",
    )(*blocks, after)


def screened_block(screening, valence, pairs, place):
    wide = valence[...].astype(jnp.float32)
    parts = []
    for at in range(0, wide.shape[0], 2 * pairs):
        parts += [-wide[at + pairs : at + 2 * pairs], wide[at : at + pairs]]
    turned = jnp.concatenate(parts, 0)
    real = jnp.concatenate([wide, turned], 0).astype(jnp.bfloat16)
    imag = jnp.concatenate([turned, -wide], 0).astype(jnp.bfloat16)
    width = valence.shape[1]
    columns = pl.ds(pl.multiple_of(place * width, 128), width)
    form = (((1,), (1,)), ((), ()))
    return lax.dot_general(
        screening[0, 0, :, columns], real, form, preferred_element_type=jnp.float32
    ) + lax.dot_general(screening[0, 1, :, columns], imag, form, preferred_element_type=jnp.float32)


def near_kernel(pairs, screening, valence, out):
    out[...] = screened_block(screening, valence, pairs, lax.axis_index("ga"))


def near_field(pairs, screening, valence):
    rows, width = valence.shape
    glocal = screening.shape[2]
    return pl.pallas_call(
        functools.partial(near_kernel, pairs),
        out_shape=in_vmem((glocal, 2 * rows), jnp.float32),
        in_specs=[vmem, vmem],
        out_specs=vmem,
        cost_estimate=pl.CostEstimate(
            flops=8 * glocal * width * rows, bytes_accessed=screening.size, transcendentals=0
        ),
        compiler_params=limits(screening, valence),
        name="near_field",
    )(screening, valence)


def project_kernel(ka, ga, ba, dims, *refs):
    vloc, val_count, cond_count, npol = dims
    screening, table, extras, near = refs[:4]
    val_in = refs[4 : 4 + ga - 1]
    cond_in = refs[4 + ga - 1 : 4 + ga - 1 + ba]
    out = refs[4 + ga - 1 + ba]
    mine = lax.axis_index("ga")
    half = lax.axis_index("ba")
    pairs = vloc * val_count
    block = 2 * pairs
    rows = ka * block
    codes = val_count * cond_count
    lanes = 2 * ka * codes
    share = cond_count // ba
    cond_rows = cond_count * cond_count
    share_rows = share * cond_count

    fields = near[...]
    for r in range(1, ga):
        fields = fields + screened_block(screening, val_in[r - 1], pairs, origin(mine, r, ga))
    high, low = split(fields)
    lane = iota((share_rows, 2 * rows), 1)
    lane_j = lane % rows // block
    turned_lane = lane // rows
    kernel = []
    for h in range(ba):
        cond_all = cond_in[h][...]
        crossed = jnp.dot(cond_all, high, preferred_element_type=jnp.float32) + jnp.dot(
            cond_all, low, preferred_element_type=jnp.float32
        )
        total = jnp.zeros((share_rows, 2 * rows), jnp.float32)
        for j in range(ka):
            base = j * 2 * share_rows
            same = lane_j == j
            total = total + jnp.where(
                same & (turned_lane == 0), crossed[base : base + share_rows], 0.0
            )
            total = total - jnp.where(
                same & (turned_lane == 1), crossed[base + share_rows : base + 2 * share_rows], 0.0
            )
        kernel.append(total)
    kernel = jnp.concatenate(kernel, 0)

    kernel_high, kernel_low = split(kernel)
    stacked = jnp.concatenate([kernel_high, kernel_low], 0)
    crow = iota((cond_rows, lanes), 0)
    c_of_row = origin(half, crow // share_rows, ba) * share + crow % share_rows // cond_count
    same_c = c_of_row == iota((cond_rows, lanes), 1) % cond_count
    spread = []
    for v2 in range(val_count):
        both = jnp.dot(
            stacked, table[:, v2 * lanes : (v2 + 1) * lanes], preferred_element_type=jnp.float32
        )
        spread.append(jnp.where(same_c, both[:cond_rows] + both[cond_rows:], 0.0))
    spread = jnp.concatenate(spread, 0)
    out_row = iota((codes, val_count * cond_rows), 0)
    out_col = iota((codes, val_count * cond_rows), 1)
    fold = (out_row // cond_count == out_col // cond_rows) & (
        out_row % cond_count == out_col % cond_count
    )
    fold = jnp.where(fold, 1.0, 0.0).astype(jnp.bfloat16)
    spread_high, spread_low = split(spread)
    out[:codes, :] = jnp.dot(fold, spread_high, preferred_element_type=jnp.float32) + jnp.dot(
        fold, spread_low, preferred_element_type=jnp.float32
    )
    out[codes:, :] = extras[...]


def project(ka, ga, ba, dims, screening, table, extras, near, val_far, cond_all):
    vloc, val_count, cond_count, npol = dims
    codes = val_count * cond_count
    operands = [screening, table, extras, near, *val_far, *cond_all]
    return pl.pallas_call(
        functools.partial(project_kernel, ka, ga, ba, dims),
        out_shape=in_vmem((codes + EXTRA_ROWS, 2 * ka * codes), jnp.float32),
        in_specs=[vmem] * len(operands),
        out_specs=vmem,
        compiler_params=limits(*operands[1:]),
        name="project",
    )(*operands)


def haydock_kernel(ka, codes, scale_count, npol, *refs):
    pieces = refs[:-3]
    next_out, coef_out, matrix = refs[-3:]
    lanes = pieces[0].shape[1]
    mid = lanes // 2
    height = codes + EXTRA_ROWS
    found = [(ref, at) for ref in pieces for at in range(0, ref.shape[0], height)]
    extras = None
    slots = []
    for ref, at in found:
        rows = ref[at + codes : at + height, :]
        extras = rows if extras is None else extras + rows
        slots.append((ref[at : at + codes, :], rows[npol + 2 : npol + 3]))
    own = pieces[0][codes:height, :]
    sign = jnp.where(iota((1, lanes), 1) < mid, -1.0, 1.0)
    for k2 in range(ka):
        block = jnp.zeros((codes, lanes), jnp.float32)
        for piece, second in slots:
            block = jnp.where(second == float(k2), piece, block)
        matrix[k2 * codes : (k2 + 1) * codes, :] = block
        matrix[mid + k2 * codes : mid + (k2 + 1) * codes, :] = sign * pltpu.roll(block, mid, 1)
    full = matrix[...]
    start = extras[:npol]
    energy = extras[npol : npol + 1]

    def mean(values):
        return jnp.sum(values, axis=1, keepdims=True) / scale_count

    def norm(vector):
        return jnp.sqrt(mean(vector * vector) + EPSILON)

    def swap(vector):
        return pltpu.roll(vector, mid, 1)

    def hamiltonian(vector):
        return energy * vector - jnp.dot(vector, full, precision=EXACT)

    def inner(left, right):
        return mean(left * right), mean(-sign * left * swap(right))

    def times(real, imag, vector):
        return real * vector + imag * (sign * swap(vector))

    first = start / norm(start)
    first_image = hamiltonian(first)
    alpha_real, alpha_imag = inner(first, first_image)
    first_resid = first_image - times(alpha_real, alpha_imag, first)
    beta_one = norm(first_resid)
    second = first_resid / beta_one
    second_image = hamiltonian(second)
    gamma_real, gamma_imag = inner(second, second_image)
    second_resid = second_image - times(gamma_real, gamma_imag, second) - beta_one * first
    beta_two = norm(second_resid)
    following = second_resid / beta_two

    coef_lane = iota(coef_out.shape, 1)
    coefs = jnp.zeros(coef_out.shape, jnp.float32)
    for at, value in enumerate((alpha_real, alpha_imag, gamma_real, gamma_imag, beta_one, beta_two)):
        coefs = jnp.where(coef_lane == at, value, coefs)
    coef_out[...] = coefs
    band = iota((codes, lanes), 0).astype(jnp.float32)
    here = iota((codes, lanes), 1) % mid // codes == lax.axis_index("ka")
    for part in range(2):
        half = iota((codes, lanes), 1) // mid == part
        pick = jnp.where(here & half & (own[npol + 1 : npol + 2] == band), 1.0, 0.0)
        next_out[0, :, part, :] = lax.dot_general(
            following, pick, (((1,), (1,)), ((), ())), precision=EXACT
        )


def haydock(ka, codes, scale_count, npol, pieces):
    lanes = pieces[0].shape[1]
    square = jax.ShapeDtypeStruct((lanes, lanes), jnp.float32)
    return pl.pallas_call(
        functools.partial(haydock_kernel, ka, codes, scale_count, npol),
        out_shape=[
            jax.ShapeDtypeStruct((1, npol, 2, codes), jnp.float32),
            jax.ShapeDtypeStruct((npol, 6), jnp.float32),
        ],
        in_specs=[vmem] * len(pieces),
        out_specs=[vmem, vmem],
        scratch_shapes=[pltpu.VMEM(square.shape, square.dtype)],
        compiler_params=limits(*pieces, square),
        name="haydock",
    )(*pieces)


def summed(value, axis):
    size = lax.axis_size(axis)
    if size & (size - 1):
        return lax.psum(value, axis)
    step = 1
    while step < size:
        value = value + exchanged(value, axis, step)
        step *= 2
    return value


def spread(values, axis):
    steps = range(lax.axis_size(axis) - 1, 0, -1)
    return [exchanged(values[step], axis, step) for step in steps][::-1]


def combined(value, first, second):
    if lax.axis_size(first) != 2 or lax.axis_size(second) != 2:
        return summed(summed(value, first), second)
    other = exchanged(value, second, 1)
    cross = lax.ppermute(value, (second, first), [(i, 3 - i) for i in range(4)])
    return (value + exchanged(value, first, 1)) + (other + cross)


def local(
    ka,
    ga,
    ba,
    start_vector,
    valence_density,
    conduction_density,
    screening,
    qpoint_map,
    slot_owner,
    band_pairs,
    valence_energy,
    conduction_energy,
):
    npol = start_vector.shape[1]
    pair_count = start_vector.shape[3]
    kcount, vloc, val_count = qpoint_map.shape[0], valence_density.shape[3], valence_density.shape[4]
    cond_count = conduction_density.shape[3]
    pairs = vloc * val_count
    dims = (vloc, val_count, cond_count, npol)
    packed = pack(ka, ba, qpoint_map, slot_owner, valence_density, conduction_density)
    blocks = [packed[0]] + spread(packed, "ka")
    screening, table, extras = prepare(
        ka,
        dims,
        qpoint_map,
        slot_owner,
        band_pairs,
        valence_energy,
        conduction_energy,
        start_vector,
        screening,
    )
    val_all, cond_half = regroup(ka, 2 * pairs, blocks, extras)
    cond_all = [cond_half] + [exchanged(cond_half, "ba", r) for r in range(1, ba)]
    val_far = [exchanged(val_all, "ga", r) for r in range(1, ga)]
    near = near_field(pairs, screening, val_all)
    piece = project(ka, ga, ba, dims, screening, table, extras, near, val_far, cond_all)
    piece = combined(piece, "ba", "ga")
    pieces = [piece] + spread([piece] * ka, "ka")
    scale_count = float(kcount * pair_count)
    return tuple(haydock(ka, pair_count, scale_count, npol, pieces))


def solution(mesh):
    in_specs = (
        P(("grp", "ka"), None, None, None),
        P(("grp", "ka"), None, None, "ba", None, "ga"),
        P(("grp", "ka"), None, None, None, None, "ga"),
        P(("grp", "ka"), None, "ga", None),
        P(),
        P(),
        P(),
        P(("grp", "ka"), None),
        P(("grp", "ka"), None),
    )
    out_specs = (P(("grp", "ka"), None, None, None), P("grp", None))
    body = functools.partial(local, mesh.shape["ka"], mesh.shape["ga"], mesh.shape["ba"])
    return jax.shard_map(body, mesh=mesh, in_specs=in_specs, out_specs=out_specs, check_vma=False)
```

```python
import functools
import math

import jax
import jax.numpy as jnp
from jax import lax
from jax.experimental import pallas as pl
from jax.experimental.pallas import tpu as pltpu
from jax.sharding import PartitionSpec as P

EPSILON = 1e-06
EXACT = lax.Precision.HIGHEST
VMEM_LEAST = 8 * 1024 * 1024
VMEM_MOST = 56 * 1024 * 1024

vmem = pl.BlockSpec(memory_space=pltpu.VMEM)
anywhere = pl.BlockSpec(memory_space=pl.ANY)
EXTRA_ROWS = 8
CHUNKS = 4


def in_vmem(shape, dtype):
    return pltpu.VMEM(shape, dtype)


def placed(value, space):
    return pltpu.with_memory_space_constraint(value, space)


def iota(shape, axis):
    return lax.broadcasted_iota(jnp.int32, shape, axis)


def split(values):
    high = values.astype(jnp.bfloat16)
    low = (values - high.astype(jnp.float32)).astype(jnp.bfloat16)
    return high, low


def limits(*arrays):
    held = sum(math.prod(a.shape) * a.dtype.itemsize for a in arrays)
    return pltpu.CompilerParams(vmem_limit_bytes=min(VMEM_MOST, VMEM_LEAST + 4 * held))


def order(size):
    return [0] + list(range(size - 1, 0, -1))


def paired(me, step, size):
    if size & (size - 1):
        return lax.rem(me + step, size)
    return lax.bitwise_xor(me, step)


def origin(me, step, size):
    if size & (size - 1):
        return lax.rem(me + size - step, size)
    return lax.bitwise_xor(me, step)


def exchanged(value, axis, step):
    size = lax.axis_size(axis)
    if size & (size - 1):
        return lax.ppermute(value, axis, [(i, (i + step) % size) for i in range(size)])
    return lax.ppermute(value, axis, [(i, i ^ step) for i in range(size)])


def pack_kernel(ka, qmap_in, owner_in, valence_in, conduction_in, *rest):
    outs = rest[:ka]
    qmap, owner, partner, valence, conduction, sems = rest[ka:]
    copies = [
        pltpu.make_async_copy(src, dst, sems.at[at])
        for at, (src, dst) in enumerate(
            ((qmap_in, qmap), (owner_in, owner), (valence_in, valence), (conduction_in, conduction))
        )
    ]
    for copy in copies:
        copy.start()
    me = lax.axis_index("ka")
    half = lax.axis_index("ba")
    count, width = valence.shape[1], valence.shape[5]
    cond_count = conduction.shape[3]
    share = cond_count // lax.axis_size("ba")
    val_rows = 2 * valence.shape[3] * valence.shape[4]
    cond_rows = 2 * share * cond_count

    def note(k2, carry):
        partner[owner[qmap[me, k2]]] = k2
        return carry

    copies[0].wait()
    copies[1].wait()
    lax.fori_loop(0, count, note, 0)
    copies[2].wait()
    copies[3].wait()
    for at, step in enumerate(order(ka)):
        k2 = partner[paired(me, step, ka)]
        block = valence[0, k2].astype(jnp.float32).reshape(val_rows, width)
        outs[at][:val_rows, :] = block.astype(jnp.bfloat16)
        block = conduction[0, k2, :, pl.ds(half * share, share)].astype(jnp.float32)
        outs[at][val_rows:, :] = block.reshape(cond_rows, width).astype(jnp.bfloat16)


def pack(ka, ba, qmap, owner, valence, conduction):
    cond_count = conduction.shape[3]
    rows = 2 * valence.shape[3] * valence.shape[4] + 2 * cond_count // ba * cond_count
    shape = in_vmem((rows, valence.shape[5]), valence.dtype)
    operands = [placed(x, pltpu.HBM) for x in (qmap, owner, valence, conduction)]
    return pl.pallas_call(
        functools.partial(pack_kernel, ka),
        out_shape=[shape] * ka,
        in_specs=[anywhere] * 4,
        out_specs=[vmem] * ka,
        scratch_shapes=[
            pltpu.SMEM(qmap.shape, jnp.int32),
            pltpu.SMEM(owner.shape, jnp.int32),
            pltpu.SMEM(owner.shape, jnp.int32),
            pltpu.VMEM(valence.shape, valence.dtype),
            pltpu.VMEM(conduction.shape, conduction.dtype),
            pltpu.SemaphoreType.DMA((4,)),
        ],
        compiler_params=limits(valence, conduction),
        name="pack",
    )(*operands)


def step_of(position, size):
    return lax.rem(size - position, size)


def column_copies(screening, out, place, sems):
    width, height = out.shape[2], out.shape[1] // CHUNKS
    columns = pl.ds(pl.multiple_of(place * width, 128), width)
    return [
        pltpu.make_async_copy(
            screening.at[0, part, pl.ds(c * height, height), columns],
            out.at[part, pl.ds(c * height, height)],
            sems.at[part, c],
        )
        for part in range(2)
        for c in range(CHUNKS)
    ]


def prepare_kernel(ka, dims, *refs):
    vloc, val_count, cond_count, npol = dims
    ins, screening, (screen_out, table, extras), scratch = refs[:6], refs[6], refs[8:11], refs[11:]
    qmap, owner, band_pairs, val_energy, cond_energy, start, sems, screen_sems = scratch
    me = lax.axis_index("ka")
    half = lax.axis_index("ba")
    mine = lax.axis_index("ga")
    copies = [
        pltpu.make_async_copy(src, dst, sems.at[at])
        for at, (src, dst) in enumerate(
            zip(ins, (qmap, owner, band_pairs, val_energy, cond_energy, start))
        )
    ]
    columns = column_copies(screening, screen_out, mine, screen_sems)
    for copy in copies + columns:
        copy.start()
    pairs = vloc * val_count
    block = 2 * pairs
    rows = ka * block
    codes = val_count * cond_count
    mid = ka * codes
    lanes = 2 * mid
    row = iota((2 * rows, lanes), 0)
    col = iota((2 * rows, lanes), 1)
    k_of_row = origin(me, step_of(row % rows // block, ka), ka)
    want = (
        (row % block // pairs) * mid
        + k_of_row * codes
        + (half * vloc + row % pairs // val_count) * cond_count
    )
    joined = (col - want >= 0) & (col - want < cond_count)
    for v2 in range(val_count):
        pick = jnp.where(joined & (row % val_count == v2), 1.0, 0.0)
        table[:, v2 * lanes : (v2 + 1) * lanes] = pick.astype(jnp.bfloat16)

    for copy in copies:
        copy.wait()
    first = jnp.where((mine == 0) & (half == 0), 1.0, 0.0)
    lane = iota((1, lanes), 1)
    lane_k = lane % mid // codes
    band_row = iota((codes, lanes), 0)
    band_lane = iota((codes, lanes), 1)
    code = jnp.zeros((codes, lanes), jnp.int32)
    bands = jnp.full((1, lanes), -1.0, jnp.float32)
    for b in range(codes):
        code = jnp.where(band_row == b, band_pairs[b], code)
        bands = jnp.where(lane % codes == band_pairs[b], float(b), bands)
    vectors = jnp.zeros((npol, lanes), jnp.float32)
    for part in range(2):
        spot = part * mid + me * codes
        pick = jnp.where(band_lane == spot + code, first, 0.0)
        vectors = vectors + jnp.dot(start[0, :, part, :], pick, precision=EXACT)
    energy = jnp.zeros((1, lanes), jnp.float32)
    for c in range(cond_count):
        energy = jnp.where(lane % cond_count == c, cond_energy[0, c], energy)
    for v in range(val_count):
        energy = energy - jnp.where(lane % codes // cond_count == v, val_energy[0, v], 0.0)
    energy = jnp.where(lane_k == me, energy * first, 0.0)
    kcount = qmap.shape[0]

    def find(k2, found):
        return jnp.where(owner[qmap[0, k2]] == me, k2, found)

    back = lax.fori_loop(0, kcount, find, 0)
    second = lane_k + back
    second = jnp.where(second >= kcount, second - kcount, second).astype(jnp.float32) * first
    rest = jnp.zeros((EXTRA_ROWS - 3 - npol, lanes), jnp.float32)
    extras[...] = jnp.concatenate([vectors, energy, bands * first, second, rest], 0)
    for copy in columns:
        copy.wait()


def prepare(ka, dims, qmap, owner, band_pairs, val_energy, cond_energy, start, screening, after):
    vloc, val_count, cond_count, npol = dims
    rows = 4 * ka * vloc * val_count
    lanes = 2 * ka * val_count * cond_count
    operands = (qmap, owner, band_pairs, val_energy, cond_energy, start, screening)
    block = (2, screening.shape[2], after.shape[1])
    table = jax.ShapeDtypeStruct((rows, val_count * lanes), jnp.bfloat16)
    return pl.pallas_call(
        functools.partial(prepare_kernel, ka, dims),
        out_shape=[
            in_vmem(block, screening.dtype),
            in_vmem(table.shape, table.dtype),
            in_vmem((EXTRA_ROWS, lanes), jnp.float32),
        ],
        in_specs=[anywhere] * 8,
        out_specs=[vmem] * 3,
        scratch_shapes=[pltpu.SMEM(x.shape, x.dtype) for x in operands[:5]]
        + [
            pltpu.VMEM(start.shape, start.dtype),
            pltpu.SemaphoreType.DMA((6,)),
            pltpu.SemaphoreType.DMA((2, CHUNKS)),
        ],
        cost_estimate=pl.CostEstimate(
            flops=0, bytes_accessed=4 * math.prod(block), transcendentals=0
        ),
        compiler_params=limits(table),
        name="prepare",
    )(*[placed(x, pltpu.HBM) for x in operands], after)


def hold_kernel(value, token, out):
    out[...] = value[...]


def hold(value, token):
    return pl.pallas_call(
        hold_kernel,
        out_shape=in_vmem(value.shape, value.dtype),
        in_specs=[vmem, anywhere],
        out_specs=vmem,
        compiler_params=limits(value),
        name="hold",
    )(value, token)


def regroup_kernel(count, first, last, *refs):
    blocks, out = refs[:count], refs[-1]
    rows = last - first
    for at in range(count):
        out[at * rows : (at + 1) * rows, :] = blocks[at][first:last, :]


def regroup(blocks, first, last, after=()):
    shape = (len(blocks) * (last - first), blocks[0].shape[1])
    return pl.pallas_call(
        functools.partial(regroup_kernel, len(blocks), first, last),
        out_shape=in_vmem(shape, blocks[0].dtype),
        in_specs=[vmem] * len(blocks) + [anywhere] * len(after),
        out_specs=vmem,
        compiler_params=limits(*blocks),
        name="regroup",
    )(*blocks, *after)


def screened_block(screening, blocks, pairs):
    wide = jnp.concatenate([block[...].astype(jnp.float32) for block in blocks], 0)
    parts = []
    for at in range(0, wide.shape[0], 2 * pairs):
        parts += [-wide[at + pairs : at + 2 * pairs], wide[at : at + pairs]]
    turned = jnp.concatenate(parts, 0)
    real = jnp.concatenate([wide, turned], 0).astype(jnp.bfloat16)
    imag = jnp.concatenate([turned, -wide], 0).astype(jnp.bfloat16)
    form = (((1,), (1,)), ((), ()))
    return lax.dot_general(
        screening[0], real, form, preferred_element_type=jnp.float32
    ) + lax.dot_general(screening[1], imag, form, preferred_element_type=jnp.float32)


def near_kernel(ka, ga, pairs, *refs):
    screening, near = refs[:2]
    blocks = refs[2 : 2 + ka]
    out, sems = refs[2 + ka], refs[-1]
    far = refs[3 + ka : -1]
    mine = lax.axis_index("ga")
    copies = []
    for r in range(1, ga):
        copies += column_copies(screening, far[r - 1], origin(mine, r, ga), sems.at[r - 1])
    for copy in copies:
        copy.start()
    out[...] = screened_block(near, [block.at[: 2 * pairs, :] for block in blocks], pairs)
    for copy in copies:
        copy.wait()


def near_field(ga, pairs, screening, near, blocks):
    ka, width = len(blocks), blocks[0].shape[1]
    rows = 2 * pairs * ka
    glocal = near.shape[1]
    outs = pl.pallas_call(
        functools.partial(near_kernel, ka, ga, pairs),
        out_shape=[in_vmem((glocal, 2 * rows), jnp.float32)] + [in_vmem(near.shape, near.dtype)] * (ga - 1),
        in_specs=[anywhere] + [vmem] * (ka + 1),
        out_specs=[vmem] * ga,
        scratch_shapes=[pltpu.SemaphoreType.DMA((max(ga - 1, 1), 2, CHUNKS))],
        cost_estimate=pl.CostEstimate(
            flops=8 * glocal * width * rows, bytes_accessed=near.size * 4, transcendentals=0
        ),
        compiler_params=limits(near, *blocks),
        name="near_field",
    )(placed(screening, pltpu.HBM), near, *blocks)
    return outs[0], outs[1:]


def project_kernel(ka, ga, ba, dims, *refs):
    vloc, val_count, cond_count, npol = dims
    table, extras, near = refs[:3]
    screens = refs[3 : 2 + ga]
    val_in = refs[2 + ga : 2 + ga + 2 * (ga - 1)]
    cond_in = refs[-1 - ba : -1]
    out = refs[-1]
    half = lax.axis_index("ba")
    pairs = vloc * val_count
    block = 2 * pairs
    rows = ka * block
    codes = val_count * cond_count
    lanes = 2 * ka * codes
    share = cond_count // ba
    cond_rows = cond_count * cond_count
    share_rows = share * cond_count

    fields = near[...]
    for r in range(ga - 1):
        fields = fields + screened_block(screens[r], val_in[2 * r : 2 * r + 2], pairs)
    high, low = split(fields)
    lane = iota((share_rows, 2 * rows), 1)
    lane_j = lane % rows // block
    turned_lane = lane // rows
    kernel = []
    for h in range(ba):
        cond_all = cond_in[h][...]
        crossed = jnp.dot(cond_all, high, preferred_element_type=jnp.float32) + jnp.dot(
            cond_all, low, preferred_element_type=jnp.float32
        )
        total = jnp.zeros((share_rows, 2 * rows), jnp.float32)
        for j in range(ka):
            base = j * 2 * share_rows
            same = lane_j == j
            total = total + jnp.where(
                same & (turned_lane == 0), crossed[base : base + share_rows], 0.0
            )
            total = total - jnp.where(
                same & (turned_lane == 1), crossed[base + share_rows : base + 2 * share_rows], 0.0
            )
        kernel.append(total)
    kernel = jnp.concatenate(kernel, 0)

    kernel_high, kernel_low = split(kernel)
    stacked = jnp.concatenate([kernel_high, kernel_low], 0)
    crow = iota((cond_rows, lanes), 0)
    c_of_row = origin(half, crow // share_rows, ba) * share + crow % share_rows // cond_count
    same_c = c_of_row == iota((cond_rows, lanes), 1) % cond_count
    spread = []
    for v2 in range(val_count):
        both = jnp.dot(
            stacked, table[:, v2 * lanes : (v2 + 1) * lanes], preferred_element_type=jnp.float32
        )
        spread.append(jnp.where(same_c, both[:cond_rows] + both[cond_rows:], 0.0))
    spread = jnp.concatenate(spread, 0)
    out_row = iota((codes, val_count * cond_rows), 0)
    out_col = iota((codes, val_count * cond_rows), 1)
    fold = (out_row // cond_count == out_col // cond_rows) & (
        out_row % cond_count == out_col % cond_count
    )
    fold = jnp.where(fold, 1.0, 0.0).astype(jnp.bfloat16)
    spread_high, spread_low = split(spread)
    out[:codes, :] = jnp.dot(fold, spread_high, preferred_element_type=jnp.float32) + jnp.dot(
        fold, spread_low, preferred_element_type=jnp.float32
    )
    out[codes:, :] = extras[...]


def project(ka, ga, ba, dims, table, extras, near, screens, val_far, cond_all):
    vloc, val_count, cond_count, npol = dims
    codes = val_count * cond_count
    operands = [table, extras, near, *screens, *val_far, *cond_all]
    return pl.pallas_call(
        functools.partial(project_kernel, ka, ga, ba, dims),
        out_shape=in_vmem((codes + EXTRA_ROWS, 2 * ka * codes), jnp.float32),
        in_specs=[vmem] * len(operands),
        out_specs=vmem,
        compiler_params=limits(*operands),
        name="project",
    )(*operands)


def haydock_kernel(ka, codes, scale_count, npol, *refs):
    pieces = refs[:-3]
    next_out, coef_out, matrix = refs[-3:]
    lanes = pieces[0].shape[1]
    mid = lanes // 2
    height = codes + EXTRA_ROWS
    found = [(ref, at) for ref in pieces for at in range(0, ref.shape[0], height)]
    extras = None
    slots = []
    for ref, at in found:
        rows = ref[at + codes : at + height, :]
        extras = rows if extras is None else extras + rows
        slots.append((ref[at : at + codes, :], rows[npol + 2 : npol + 3]))
    own = pieces[0][codes:height, :]
    sign = jnp.where(iota((1, lanes), 1) < mid, -1.0, 1.0)
    for k2 in range(ka):
        block = jnp.zeros((codes, lanes), jnp.float32)
        for piece, second in slots:
            block = jnp.where(second == float(k2), piece, block)
        matrix[k2 * codes : (k2 + 1) * codes, :] = block
        matrix[mid + k2 * codes : mid + (k2 + 1) * codes, :] = sign * pltpu.roll(block, mid, 1)
    high, low = split(matrix[...])
    full = jnp.concatenate([high, low], 1)
    start = extras[:npol]
    energy = extras[npol : npol + 1]

    def halves(vector):
        top = vector.astype(jnp.bfloat16).astype(jnp.float32)
        return jnp.concatenate([top, vector - top], 0).astype(jnp.bfloat16)

    def mean(values):
        return jnp.sum(values, axis=1, keepdims=True) / scale_count

    def norm(vector):
        return jnp.sqrt(mean(vector * vector) + EPSILON)

    def swap(vector):
        return pltpu.roll(vector, mid, 1)

    def hamiltonian(vector):
        product = jnp.dot(halves(vector), full, preferred_element_type=jnp.float32)
        main = product[:npol, :lanes] + product[npol:, :lanes]
        return energy * vector - (main + product[:npol, lanes:])

    def inner(left, right):
        return mean(left * right), mean(-sign * left * swap(right))

    def times(real, imag, vector):
        return real * vector + imag * (sign * swap(vector))

    first = start / norm(start)
    first_image = hamiltonian(first)
    alpha_real, alpha_imag = inner(first, first_image)
    first_resid = first_image - times(alpha_real, alpha_imag, first)
    beta_one = norm(first_resid)
    second = first_resid / beta_one
    second_image = hamiltonian(second)
    gamma_real, gamma_imag = inner(second, second_image)
    second_resid = second_image - times(gamma_real, gamma_imag, second) - beta_one * first
    beta_two = norm(second_resid)
    following = second_resid / beta_two

    coef_lane = iota(coef_out.shape, 1)
    coefs = jnp.zeros(coef_out.shape, jnp.float32)
    for at, value in enumerate((alpha_real, alpha_imag, gamma_real, gamma_imag, beta_one, beta_two)):
        coefs = jnp.where(coef_lane == at, value, coefs)
    coef_out[...] = coefs
    row = iota((2 * codes, lanes), 0)
    lane = iota((2 * codes, lanes), 1)
    here = (lane % mid // codes == lax.axis_index("ka")) & (lane // mid == row // codes)
    band = (row % codes).astype(jnp.float32)
    pick = jnp.where(here & (own[npol + 1 : npol + 2] == band), 1.0, 0.0).astype(jnp.bfloat16)
    picked = lax.dot_general(
        halves(following), pick, (((1,), (1,)), ((), ())), preferred_element_type=jnp.float32
    )
    picked = picked[:npol] + picked[npol:]
    next_out[0, :, 0, :] = picked[:, :codes]
    next_out[0, :, 1, :] = picked[:, codes:]


def haydock(ka, codes, scale_count, npol, pieces):
    lanes = pieces[0].shape[1]
    square = jax.ShapeDtypeStruct((lanes, lanes), jnp.float32)
    return pl.pallas_call(
        functools.partial(haydock_kernel, ka, codes, scale_count, npol),
        out_shape=[
            jax.ShapeDtypeStruct((1, npol, 2, codes), jnp.float32),
            jax.ShapeDtypeStruct((npol, 6), jnp.float32),
        ],
        in_specs=[vmem] * len(pieces),
        out_specs=[vmem, vmem],
        scratch_shapes=[pltpu.VMEM(square.shape, square.dtype)],
        compiler_params=limits(*pieces, square),
        name="haydock",
    )(*pieces)


def summed(value, axis):
    size = lax.axis_size(axis)
    if size & (size - 1):
        return lax.psum(value, axis)
    step = 1
    while step < size:
        value = value + exchanged(value, axis, step)
        step *= 2
    return value


def sent(values, axis):
    found, token = [values[0]], None
    for step, value in zip(order(lax.axis_size(axis))[1:], values[1:]):
        token = value if token is None else hold(value, token)
        found.append(exchanged(token, axis, step))
    return found


def local(
    ka,
    ga,
    ba,
    start_vector,
    valence_density,
    conduction_density,
    screening,
    qpoint_map,
    slot_owner,
    band_pairs,
    valence_energy,
    conduction_energy,
):
    npol = start_vector.shape[1]
    pair_count = start_vector.shape[3]
    kcount, vloc, val_count = qpoint_map.shape[0], valence_density.shape[3], valence_density.shape[4]
    cond_count = conduction_density.shape[3]
    pairs = vloc * val_count
    dims = (vloc, val_count, cond_count, npol)
    packed = pack(ka, ba, qpoint_map, slot_owner, valence_density, conduction_density)
    blocks = sent(packed, "ka")
    early = ka // 2
    val_early = regroup(blocks[:early], 0, 2 * pairs)
    far_early = [exchanged(val_early, "ga", r) for r in range(1, ga)]
    screen_near, table, extras = prepare(
        ka,
        dims,
        qpoint_map,
        slot_owner,
        band_pairs,
        valence_energy,
        conduction_energy,
        start_vector,
        screening,
        val_early,
    )
    val_late = regroup(blocks[early:], 0, 2 * pairs, (extras, *far_early))
    far_late = [exchanged(val_late, "ga", r) for r in range(1, ga)]
    cond_half = regroup(blocks, 2 * pairs, blocks[0].shape[0], (val_late,))
    cond_all = [cond_half] + [exchanged(cond_half, "ba", r) for r in range(1, ba)]
    near, screens = near_field(ga, pairs, screening, screen_near, blocks)
    val_far = [x for both in zip(far_early, far_late) for x in both]
    piece = project(ka, ga, ba, dims, table, extras, near, screens, val_far, cond_all)
    piece = summed(summed(piece, "ba"), "ga")
    pieces = sent([piece] * ka, "ka")
    scale_count = float(kcount * pair_count)
    return tuple(haydock(ka, pair_count, scale_count, npol, pieces))


def solution(mesh):
    in_specs = (
        P(("grp", "ka"), None, None, None),
        P(("grp", "ka"), None, None, "ba", None, "ga"),
        P(("grp", "ka"), None, None, None, None, "ga"),
        P(("grp", "ka"), None, "ga", None),
        P(),
        P(),
        P(),
        P(("grp", "ka"), None),
        P(("grp", "ka"), None),
    )
    out_specs = (P(("grp", "ka"), None, None, None), P("grp", None))
    body = functools.partial(local, mesh.shape["ka"], mesh.shape["ga"], mesh.shape["ba"])
    return jax.shard_map(body, mesh=mesh, in_specs=in_specs, out_specs=out_specs, check_vma=False)
```

```python
import functools
import math

import jax
import jax.numpy as jnp
from jax import lax
from jax.experimental import pallas as pl
from jax.experimental.pallas import tpu as pltpu
from jax.sharding import PartitionSpec as P

EPSILON = 1e-06
EXACT = lax.Precision.HIGHEST
VMEM_LEAST = 8 * 1024 * 1024
VMEM_MOST = 56 * 1024 * 1024

vmem = pl.BlockSpec(memory_space=pltpu.VMEM)
anywhere = pl.BlockSpec(memory_space=pl.ANY)
EXTRA_ROWS = 8
CHUNKS = 4


def in_vmem(shape, dtype):
    return pltpu.VMEM(shape, dtype)


def placed(value, space):
    return pltpu.with_memory_space_constraint(value, space)


def iota(shape, axis):
    return lax.broadcasted_iota(jnp.int32, shape, axis)


def split(values):
    high = values.astype(jnp.bfloat16)
    low = (values - high.astype(jnp.float32)).astype(jnp.bfloat16)
    return high, low


def limits(*arrays):
    held = sum(math.prod(a.shape) * a.dtype.itemsize for a in arrays)
    return pltpu.CompilerParams(vmem_limit_bytes=min(VMEM_MOST, VMEM_LEAST + 4 * held))


def target(me, step, size):
    return lax.rem(me + step, size)


def origin(me, step, size):
    return lax.rem(me + size - step, size)


def exchanged(value, axis, step):
    size = lax.axis_size(axis)
    return lax.ppermute(value, axis, [(i, (i + step) % size) for i in range(size)])


def pack_kernel(ka, qmap_in, owner_in, valence_in, conduction_in, *rest):
    outs = rest[:ka]
    qmap, owner, partner, valence, conduction, sems = rest[ka:]
    copies = [
        pltpu.make_async_copy(src, dst, sems.at[at])
        for at, (src, dst) in enumerate(
            ((qmap_in, qmap), (owner_in, owner), (valence_in, valence), (conduction_in, conduction))
        )
    ]
    for copy in copies:
        copy.start()
    me = lax.axis_index("ka")
    half = lax.axis_index("ba")
    count, width = valence.shape[1], valence.shape[5]
    cond_count = conduction.shape[3]
    share = cond_count // lax.axis_size("ba")
    val_rows = 2 * valence.shape[3] * valence.shape[4]
    cond_rows = 2 * share * cond_count

    def note(k2, carry):
        partner[owner[qmap[me, k2]]] = k2
        return carry

    copies[0].wait()
    copies[1].wait()
    lax.fori_loop(0, count, note, 0)
    copies[2].wait()
    copies[3].wait()
    for at in range(ka):
        k2 = partner[target(me, at, ka)]
        block = valence[0, k2].astype(jnp.float32).reshape(val_rows, width)
        outs[at][:val_rows, :] = block.astype(jnp.bfloat16)
        block = conduction[0, k2, :, pl.ds(half * share, share)].astype(jnp.float32)
        outs[at][val_rows:, :] = block.reshape(cond_rows, width).astype(jnp.bfloat16)


def pack(ka, ba, qmap, owner, valence, conduction):
    cond_count = conduction.shape[3]
    rows = 2 * valence.shape[3] * valence.shape[4] + 2 * cond_count // ba * cond_count
    shape = in_vmem((rows, valence.shape[5]), valence.dtype)
    operands = [placed(x, pltpu.HBM) for x in (qmap, owner, valence, conduction)]
    return pl.pallas_call(
        functools.partial(pack_kernel, ka),
        out_shape=[shape] * ka,
        in_specs=[anywhere] * 4,
        out_specs=[vmem] * ka,
        scratch_shapes=[
            pltpu.SMEM(qmap.shape, jnp.int32),
            pltpu.SMEM(owner.shape, jnp.int32),
            pltpu.SMEM(owner.shape, jnp.int32),
            pltpu.VMEM(valence.shape, valence.dtype),
            pltpu.VMEM(conduction.shape, conduction.dtype),
            pltpu.SemaphoreType.DMA((4,)),
        ],
        compiler_params=limits(valence, conduction),
        name="pack",
    )(*operands)


def prepare_kernel(ka, dims, *refs):
    vloc, val_count, cond_count, npol = dims
    ins, screening, (screen_out, table, extras), scratch = refs[:6], refs[6], refs[8:11], refs[11:]
    qmap, owner, band_pairs, val_energy, cond_energy, start, sems, screen_sems = scratch
    me = lax.axis_index("ka")
    half = lax.axis_index("ba")
    mine = lax.axis_index("ga")
    copies = [
        pltpu.make_async_copy(src, dst, sems.at[at])
        for at, (src, dst) in enumerate(
            zip(ins, (qmap, owner, band_pairs, val_energy, cond_energy, start))
        )
    ]
    height = screening.shape[2] // CHUNKS
    chunks = [
        pltpu.make_async_copy(
            screening.at[0, part, pl.ds(c * height, height)],
            screen_out.at[part, pl.ds(c * height, height)],
            screen_sems.at[part, c],
        )
        for part in range(2)
        for c in range(CHUNKS)
    ]
    for copy in copies + chunks:
        copy.start()
    pairs = vloc * val_count
    block = 2 * pairs
    rows = ka * block
    codes = val_count * cond_count
    mid = ka * codes
    lanes = 2 * mid
    row = iota((2 * rows, lanes), 0)
    col = iota((2 * rows, lanes), 1)
    k_of_row = origin(me, row % rows // block, ka)
    want = (
        (row % block // pairs) * mid
        + k_of_row * codes
        + (half * vloc + row % pairs // val_count) * cond_count
    )
    joined = (col - want >= 0) & (col - want < cond_count)
    for v2 in range(val_count):
        pick = jnp.where(joined & (row % val_count == v2), 1.0, 0.0)
        table[:, v2 * lanes : (v2 + 1) * lanes] = pick.astype(jnp.bfloat16)

    for copy in copies:
        copy.wait()
    first = jnp.where((mine == 0) & (half == 0), 1.0, 0.0)
    lane = iota((1, lanes), 1)
    lane_k = lane % mid // codes
    band_row = iota((codes, lanes), 0)
    band_lane = iota((codes, lanes), 1)
    code = jnp.zeros((codes, lanes), jnp.int32)
    bands = jnp.full((1, lanes), -1.0, jnp.float32)
    for b in range(codes):
        code = jnp.where(band_row == b, band_pairs[b], code)
        bands = jnp.where(lane % codes == band_pairs[b], float(b), bands)
    vectors = jnp.zeros((npol, lanes), jnp.float32)
    for part in range(2):
        spot = part * mid + me * codes
        pick = jnp.where(band_lane == spot + code, first, 0.0)
        vectors = vectors + jnp.dot(start[0, :, part, :], pick, precision=EXACT)
    energy = jnp.zeros((1, lanes), jnp.float32)
    for c in range(cond_count):
        energy = jnp.where(lane % cond_count == c, cond_energy[0, c], energy)
    for v in range(val_count):
        energy = energy - jnp.where(lane % codes // cond_count == v, val_energy[0, v], 0.0)
    energy = jnp.where(lane_k == me, energy * first, 0.0)
    kcount = qmap.shape[0]

    def find(k2, found):
        return jnp.where(owner[qmap[0, k2]] == me, k2, found)

    back = lax.fori_loop(0, kcount, find, 0)
    second = lane_k + back
    second = jnp.where(second >= kcount, second - kcount, second).astype(jnp.float32) * first
    rest = jnp.zeros((EXTRA_ROWS - 3 - npol, lanes), jnp.float32)
    extras[...] = jnp.concatenate([vectors, energy, bands * first, second, rest], 0)
    for copy in chunks:
        copy.wait()


def prepare(ka, dims, qmap, owner, band_pairs, val_energy, cond_energy, start, screening, after):
    vloc, val_count, cond_count, npol = dims
    rows = 4 * ka * vloc * val_count
    lanes = 2 * ka * val_count * cond_count
    operands = (qmap, owner, band_pairs, val_energy, cond_energy, start, screening)
    table = jax.ShapeDtypeStruct((rows, val_count * lanes), jnp.bfloat16)
    return pl.pallas_call(
        functools.partial(prepare_kernel, ka, dims),
        out_shape=[
            in_vmem(screening.shape[1:], screening.dtype),
            in_vmem(table.shape, table.dtype),
            in_vmem((EXTRA_ROWS, lanes), jnp.float32),
        ],
        in_specs=[anywhere] * 8,
        out_specs=[vmem] * 3,
        scratch_shapes=[pltpu.SMEM(x.shape, x.dtype) for x in operands[:5]]
        + [
            pltpu.VMEM(start.shape, start.dtype),
            pltpu.SemaphoreType.DMA((6,)),
            pltpu.SemaphoreType.DMA((2, CHUNKS)),
        ],
        cost_estimate=pl.CostEstimate(
            flops=0, bytes_accessed=4 * screening.size, transcendentals=0
        ),
        compiler_params=limits(table),
        name="prepare",
    )(*[placed(x, pltpu.HBM) for x in operands], after)


def regroup_kernel(count, first, last, *refs):
    blocks, out = refs[:count], refs[-1]
    rows = last - first
    for at in range(count):
        out[at * rows : (at + 1) * rows, :] = blocks[at][first:last, :]


def regroup(blocks, first, last, after=()):
    shape = (len(blocks) * (last - first), blocks[0].shape[1])
    return pl.pallas_call(
        functools.partial(regroup_kernel, len(blocks), first, last),
        out_shape=in_vmem(shape, blocks[0].dtype),
        in_specs=[vmem] * len(blocks) + [anywhere] * len(after),
        out_specs=vmem,
        compiler_params=limits(*blocks),
        name="regroup",
    )(*blocks, *after)


def screened_block(screening, blocks, pairs, place):
    wide = jnp.concatenate([block[...].astype(jnp.float32) for block in blocks], 0)
    parts = []
    for at in range(0, wide.shape[0], 2 * pairs):
        parts += [-wide[at + pairs : at + 2 * pairs], wide[at : at + pairs]]
    turned = jnp.concatenate(parts, 0)
    real = jnp.concatenate([wide, turned], 0).astype(jnp.bfloat16)
    imag = jnp.concatenate([turned, -wide], 0).astype(jnp.bfloat16)
    width = wide.shape[1]
    columns = pl.ds(pl.multiple_of(place * width, 128), width)
    form = (((1,), (1,)), ((), ()))
    return lax.dot_general(
        screening[0, :, columns], real, form, preferred_element_type=jnp.float32
    ) + lax.dot_general(screening[1, :, columns], imag, form, preferred_element_type=jnp.float32)


def near_kernel(pairs, screening, *refs):
    refs[-1][...] = screened_block(screening, refs[:-1], pairs, lax.axis_index("ga"))


def near_field(pairs, screening, blocks):
    rows = sum(block.shape[0] for block in blocks)
    glocal, width = screening.shape[1], blocks[0].shape[1]
    return pl.pallas_call(
        functools.partial(near_kernel, pairs),
        out_shape=in_vmem((glocal, 2 * rows), jnp.float32),
        in_specs=[vmem] * (1 + len(blocks)),
        out_specs=vmem,
        cost_estimate=pl.CostEstimate(
            flops=8 * glocal * width * rows, bytes_accessed=screening.size, transcendentals=0
        ),
        compiler_params=limits(screening, *blocks),
        name="near_field",
    )(screening, *blocks)


def project_kernel(ka, ga, ba, dims, *refs):
    vloc, val_count, cond_count, npol = dims
    screening, table, extras, near = refs[:4]
    val_in = refs[4 : 4 + 2 * (ga - 1)]
    cond_in = refs[-1 - ba : -1]
    out = refs[-1]
    mine = lax.axis_index("ga")
    half = lax.axis_index("ba")
    pairs = vloc * val_count
    block = 2 * pairs
    rows = ka * block
    codes = val_count * cond_count
    lanes = 2 * ka * codes
    share = cond_count // ba
    cond_rows = cond_count * cond_count
    share_rows = share * cond_count

    fields = near[...]
    for r in range(1, ga):
        halves = val_in[2 * r - 2 : 2 * r]
        fields = fields + screened_block(screening, halves, pairs, origin(mine, r, ga))
    high, low = split(fields)
    lane = iota((share_rows, 2 * rows), 1)
    lane_j = lane % rows // block
    turned_lane = lane // rows
    kernel = []
    for h in range(ba):
        cond_all = cond_in[h][...]
        crossed = jnp.dot(cond_all, high, preferred_element_type=jnp.float32) + jnp.dot(
            cond_all, low, preferred_element_type=jnp.float32
        )
        total = jnp.zeros((share_rows, 2 * rows), jnp.float32)
        for j in range(ka):
            base = j * 2 * share_rows
            same = lane_j == j
            total = total + jnp.where(
                same & (turned_lane == 0), crossed[base : base + share_rows], 0.0
            )
            total = total - jnp.where(
                same & (turned_lane == 1), crossed[base + share_rows : base + 2 * share_rows], 0.0
            )
        kernel.append(total)
    kernel = jnp.concatenate(kernel, 0)

    kernel_high, kernel_low = split(kernel)
    stacked = jnp.concatenate([kernel_high, kernel_low], 0)
    crow = iota((cond_rows, lanes), 0)
    c_of_row = origin(half, crow // share_rows, ba) * share + crow % share_rows // cond_count
    same_c = c_of_row == iota((cond_rows, lanes), 1) % cond_count
    spread = []
    for v2 in range(val_count):
        both = jnp.dot(
            stacked, table[:, v2 * lanes : (v2 + 1) * lanes], preferred_element_type=jnp.float32
        )
        spread.append(jnp.where(same_c, both[:cond_rows] + both[cond_rows:], 0.0))
    spread = jnp.concatenate(spread, 0)
    out_row = iota((codes, val_count * cond_rows), 0)
    out_col = iota((codes, val_count * cond_rows), 1)
    fold = (out_row // cond_count == out_col // cond_rows) & (
        out_row % cond_count == out_col % cond_count
    )
    fold = jnp.where(fold, 1.0, 0.0).astype(jnp.bfloat16)
    spread_high, spread_low = split(spread)
    out[:codes, :] = jnp.dot(fold, spread_high, preferred_element_type=jnp.float32) + jnp.dot(
        fold, spread_low, preferred_element_type=jnp.float32
    )
    out[codes:, :] = extras[...]


def project(ka, ga, ba, dims, screening, table, extras, near, val_far, cond_all):
    vloc, val_count, cond_count, npol = dims
    codes = val_count * cond_count
    operands = [screening, table, extras, near, *val_far, *cond_all]
    return pl.pallas_call(
        functools.partial(project_kernel, ka, ga, ba, dims),
        out_shape=in_vmem((codes + EXTRA_ROWS, 2 * ka * codes), jnp.float32),
        in_specs=[vmem] * len(operands),
        out_specs=vmem,
        compiler_params=limits(*operands),
        name="project",
    )(*operands)


def haydock_kernel(ka, codes, scale_count, npol, *refs):
    pieces = refs[:-3]
    next_out, coef_out, matrix = refs[-3:]
    lanes = pieces[0].shape[1]
    mid = lanes // 2
    height = codes + EXTRA_ROWS
    found = [(ref, at) for ref in pieces for at in range(0, ref.shape[0], height)]
    extras = None
    slots = []
    for ref, at in found:
        rows = ref[at + codes : at + height, :]
        extras = rows if extras is None else extras + rows
        slots.append((ref[at : at + codes, :], rows[npol + 2 : npol + 3]))
    own = pieces[0][codes:height, :]
    sign = jnp.where(iota((1, lanes), 1) < mid, -1.0, 1.0)
    for k2 in range(ka):
        block = jnp.zeros((codes, lanes), jnp.float32)
        for piece, second in slots:
            block = jnp.where(second == float(k2), piece, block)
        matrix[k2 * codes : (k2 + 1) * codes, :] = block
        matrix[mid + k2 * codes : mid + (k2 + 1) * codes, :] = sign * pltpu.roll(block, mid, 1)
    high, low = split(matrix[...])
    full = jnp.concatenate([high, low], 1)
    start = extras[:npol]
    energy = extras[npol : npol + 1]

    def halves(vector):
        top = vector.astype(jnp.bfloat16).astype(jnp.float32)
        return jnp.concatenate([top, vector - top], 0).astype(jnp.bfloat16)

    def mean(values):
        return jnp.sum(values, axis=1, keepdims=True) / scale_count

    def norm(vector):
        return jnp.sqrt(mean(vector * vector) + EPSILON)

    def swap(vector):
        return pltpu.roll(vector, mid, 1)

    def hamiltonian(vector):
        product = jnp.dot(halves(vector), full, preferred_element_type=jnp.float32)
        main = product[:npol, :lanes] + product[npol:, :lanes]
        return energy * vector - (main + product[:npol, lanes:])

    def inner(left, right):
        return mean(left * right), mean(-sign * left * swap(right))

    def times(real, imag, vector):
        return real * vector + imag * (sign * swap(vector))

    first = start / norm(start)
    first_image = hamiltonian(first)
    alpha_real, alpha_imag = inner(first, first_image)
    first_resid = first_image - times(alpha_real, alpha_imag, first)
    beta_one = norm(first_resid)
    second = first_resid / beta_one
    second_image = hamiltonian(second)
    gamma_real, gamma_imag = inner(second, second_image)
    second_resid = second_image - times(gamma_real, gamma_imag, second) - beta_one * first
    beta_two = norm(second_resid)
    following = second_resid / beta_two

    coef_lane = iota(coef_out.shape, 1)
    coefs = jnp.zeros(coef_out.shape, jnp.float32)
    for at, value in enumerate((alpha_real, alpha_imag, gamma_real, gamma_imag, beta_one, beta_two)):
        coefs = jnp.where(coef_lane == at, value, coefs)
    coef_out[...] = coefs
    row = iota((2 * codes, lanes), 0)
    lane = iota((2 * codes, lanes), 1)
    here = (lane % mid // codes == lax.axis_index("ka")) & (lane // mid == row // codes)
    band = (row % codes).astype(jnp.float32)
    pick = jnp.where(here & (own[npol + 1 : npol + 2] == band), 1.0, 0.0).astype(jnp.bfloat16)
    picked = lax.dot_general(
        halves(following), pick, (((1,), (1,)), ((), ())), preferred_element_type=jnp.float32
    )
    picked = picked[:npol] + picked[npol:]
    next_out[0, :, 0, :] = picked[:, :codes]
    next_out[0, :, 1, :] = picked[:, codes:]


def haydock(ka, codes, scale_count, npol, pieces):
    lanes = pieces[0].shape[1]
    square = jax.ShapeDtypeStruct((lanes, lanes), jnp.float32)
    return pl.pallas_call(
        functools.partial(haydock_kernel, ka, codes, scale_count, npol),
        out_shape=[
            jax.ShapeDtypeStruct((1, npol, 2, codes), jnp.float32),
            jax.ShapeDtypeStruct((npol, 6), jnp.float32),
        ],
        in_specs=[vmem] * len(pieces),
        out_specs=[vmem, vmem],
        scratch_shapes=[pltpu.VMEM(square.shape, square.dtype)],
        compiler_params=limits(*pieces, square),
        name="haydock",
    )(*pieces)


def summed(value, axis):
    size = lax.axis_size(axis)
    if size & (size - 1):
        return lax.psum(value, axis)
    step = 1
    while step < size:
        value = value + lax.ppermute(value, axis, [(i, i ^ step) for i in range(size)])
        step *= 2
    return value


def sent(values, axis):
    return [values[0]] + [exchanged(values[j], axis, j) for j in range(1, lax.axis_size(axis))]


def local(
    ka,
    ga,
    ba,
    start_vector,
    valence_density,
    conduction_density,
    screening,
    qpoint_map,
    slot_owner,
    band_pairs,
    valence_energy,
    conduction_energy,
):
    npol = start_vector.shape[1]
    pair_count = start_vector.shape[3]
    kcount, vloc, val_count = qpoint_map.shape[0], valence_density.shape[3], valence_density.shape[4]
    cond_count = conduction_density.shape[3]
    pairs = vloc * val_count
    dims = (vloc, val_count, cond_count, npol)
    packed = pack(ka, ba, qpoint_map, slot_owner, valence_density, conduction_density)
    blocks = sent(packed, "ka")
    early = ka // 2
    val_early = regroup(blocks[:early], 0, 2 * pairs)
    far_early = [exchanged(val_early, "ga", r) for r in range(1, ga)]
    whole, table, extras = prepare(
        ka,
        dims,
        qpoint_map,
        slot_owner,
        band_pairs,
        valence_energy,
        conduction_energy,
        start_vector,
        screening,
        val_early,
    )
    val_late = regroup(blocks[early:], 0, 2 * pairs, (extras,))
    far_late = [exchanged(val_late, "ga", r) for r in range(1, ga)]
    cond_half = regroup(blocks, 2 * pairs, blocks[0].shape[0], (val_late, *far_early))
    cond_all = [cond_half] + [exchanged(cond_half, "ba", r) for r in range(1, ba)]
    near = near_field(pairs, whole, [val_early, val_late])
    val_far = [x for both in zip(far_early, far_late) for x in both]
    piece = project(ka, ga, ba, dims, whole, table, extras, near, val_far, cond_all)
    piece = summed(summed(piece, "ba"), "ga")
    pieces = sent([piece] * ka, "ka")
    scale_count = float(kcount * pair_count)
    return tuple(haydock(ka, pair_count, scale_count, npol, pieces))


def solution(mesh):
    in_specs = (
        P(("grp", "ka"), None, None, None),
        P(("grp", "ka"), None, None, "ba", None, "ga"),
        P(("grp", "ka"), None, None, None, None, "ga"),
        P(("grp", "ka"), None, "ga", None),
        P(),
        P(),
        P(),
        P(("grp", "ka"), None),
        P(("grp", "ka"), None),
    )
    out_specs = (P(("grp", "ka"), None, None, None), P("grp", None))
    body = functools.partial(local, mesh.shape["ka"], mesh.shape["ga"], mesh.shape["ba"])
    return jax.shard_map(body, mesh=mesh, in_specs=in_specs, out_specs=out_specs, check_vma=False)
```

```python
import functools
import math

import jax
import jax.numpy as jnp
from jax import lax
from jax.experimental import pallas as pl
from jax.experimental.pallas import tpu as pltpu
from jax.sharding import PartitionSpec as P

EPSILON = 1e-06
EXACT = lax.Precision.HIGHEST
VMEM_LEAST = 8 * 1024 * 1024
VMEM_MOST = 56 * 1024 * 1024

vmem = pl.BlockSpec(memory_space=pltpu.VMEM)
anywhere = pl.BlockSpec(memory_space=pl.ANY)
EXTRA_ROWS = 8
CHUNKS = 4


def in_vmem(shape, dtype):
    return pltpu.VMEM(shape, dtype)


def placed(value, space):
    return pltpu.with_memory_space_constraint(value, space)


def iota(shape, axis):
    return lax.broadcasted_iota(jnp.int32, shape, axis)


def split(values):
    high = values.astype(jnp.bfloat16)
    low = (values - high.astype(jnp.float32)).astype(jnp.bfloat16)
    return high, low


def limits(*arrays):
    held = sum(math.prod(a.shape) * a.dtype.itemsize for a in arrays)
    return pltpu.CompilerParams(vmem_limit_bytes=min(VMEM_MOST, VMEM_LEAST + 4 * held))


def target(me, step, size):
    return lax.rem(me + step, size)


def origin(me, step, size):
    return lax.rem(me + size - step, size)


def exchanged(value, axis, step):
    size = lax.axis_size(axis)
    return lax.ppermute(value, axis, [(i, (i + step) % size) for i in range(size)])


def pack_kernel(ka, qmap_in, owner_in, valence_in, conduction_in, *rest):
    outs = rest[:ka]
    qmap, owner, partner, valence, conduction, sems = rest[ka:]
    copies = [
        pltpu.make_async_copy(src, dst, sems.at[at])
        for at, (src, dst) in enumerate(
            ((qmap_in, qmap), (owner_in, owner), (valence_in, valence), (conduction_in, conduction))
        )
    ]
    for copy in copies:
        copy.start()
    me = lax.axis_index("ka")
    half = lax.axis_index("ba")
    count, width = valence.shape[1], valence.shape[5]
    cond_count = conduction.shape[3]
    share = cond_count // lax.axis_size("ba")
    val_rows = 2 * valence.shape[3] * valence.shape[4]
    cond_rows = 2 * share * cond_count

    def note(k2, carry):
        partner[owner[qmap[me, k2]]] = k2
        return carry

    copies[0].wait()
    copies[1].wait()
    lax.fori_loop(0, count, note, 0)
    copies[2].wait()
    copies[3].wait()
    for at in range(ka):
        k2 = partner[target(me, at, ka)]
        block = valence[0, k2].astype(jnp.float32).reshape(val_rows, width)
        outs[at][:val_rows, :] = block.astype(jnp.bfloat16)
        block = conduction[0, k2, :, pl.ds(half * share, share)].astype(jnp.float32)
        outs[at][val_rows:, :] = block.reshape(cond_rows, width).astype(jnp.bfloat16)


def pack(ka, ba, qmap, owner, valence, conduction):
    cond_count = conduction.shape[3]
    rows = 2 * valence.shape[3] * valence.shape[4] + 2 * cond_count // ba * cond_count
    shape = in_vmem((rows, valence.shape[5]), valence.dtype)
    operands = [placed(x, pltpu.HBM) for x in (qmap, owner, valence, conduction)]
    return pl.pallas_call(
        functools.partial(pack_kernel, ka),
        out_shape=[shape] * ka,
        in_specs=[anywhere] * 4,
        out_specs=[vmem] * ka,
        scratch_shapes=[
            pltpu.SMEM(qmap.shape, jnp.int32),
            pltpu.SMEM(owner.shape, jnp.int32),
            pltpu.SMEM(owner.shape, jnp.int32),
            pltpu.VMEM(valence.shape, valence.dtype),
            pltpu.VMEM(conduction.shape, conduction.dtype),
            pltpu.SemaphoreType.DMA((4,)),
        ],
        compiler_params=limits(valence, conduction),
        name="pack",
    )(*operands)


def prepare_kernel(ka, dims, *refs):
    vloc, val_count, cond_count, npol = dims
    ins, screening, (screen_out, table, extras), scratch = refs[:6], refs[6], refs[8:11], refs[11:]
    qmap, owner, band_pairs, val_energy, cond_energy, start, sems, screen_sems = scratch
    me = lax.axis_index("ka")
    half = lax.axis_index("ba")
    mine = lax.axis_index("ga")
    copies = [
        pltpu.make_async_copy(src, dst, sems.at[at])
        for at, (src, dst) in enumerate(
            zip(ins, (qmap, owner, band_pairs, val_energy, cond_energy, start))
        )
    ]
    height = screening.shape[2] // CHUNKS
    chunks = [
        pltpu.make_async_copy(
            screening.at[0, part, pl.ds(c * height, height)],
            screen_out.at[part, pl.ds(c * height, height)],
            screen_sems.at[part, c],
        )
        for part in range(2)
        for c in range(CHUNKS)
    ]
    for copy in copies + chunks:
        copy.start()
    pairs = vloc * val_count
    block = 2 * pairs
    rows = ka * block
    codes = val_count * cond_count
    mid = ka * codes
    lanes = 2 * mid
    row = iota((2 * rows, lanes), 0)
    col = iota((2 * rows, lanes), 1)
    k_of_row = origin(me, row % rows // block, ka)
    want = (
        (row % block // pairs) * mid
        + k_of_row * codes
        + (half * vloc + row % pairs // val_count) * cond_count
    )
    joined = (col - want >= 0) & (col - want < cond_count)
    for v2 in range(val_count):
        pick = jnp.where(joined & (row % val_count == v2), 1.0, 0.0)
        table[:, v2 * lanes : (v2 + 1) * lanes] = pick.astype(jnp.bfloat16)

    for copy in copies:
        copy.wait()
    first = jnp.where((mine == 0) & (half == 0), 1.0, 0.0)
    lane = iota((1, lanes), 1)
    lane_k = lane % mid // codes
    band_row = iota((codes, lanes), 0)
    band_lane = iota((codes, lanes), 1)
    code = jnp.zeros((codes, lanes), jnp.int32)
    bands = jnp.full((1, lanes), -1.0, jnp.float32)
    for b in range(codes):
        code = jnp.where(band_row == b, band_pairs[b], code)
        bands = jnp.where(lane % codes == band_pairs[b], float(b), bands)
    vectors = jnp.zeros((npol, lanes), jnp.float32)
    for part in range(2):
        spot = part * mid + me * codes
        pick = jnp.where(band_lane == spot + code, first, 0.0)
        vectors = vectors + jnp.dot(start[0, :, part, :], pick, precision=EXACT)
    energy = jnp.zeros((1, lanes), jnp.float32)
    for c in range(cond_count):
        energy = jnp.where(lane % cond_count == c, cond_energy[0, c], energy)
    for v in range(val_count):
        energy = energy - jnp.where(lane % codes // cond_count == v, val_energy[0, v], 0.0)
    energy = jnp.where(lane_k == me, energy * first, 0.0)
    kcount = qmap.shape[0]

    def find(k2, found):
        return jnp.where(owner[qmap[0, k2]] == me, k2, found)

    back = lax.fori_loop(0, kcount, find, 0)
    second = lane_k + back
    second = jnp.where(second >= kcount, second - kcount, second).astype(jnp.float32) * first
    rest = jnp.zeros((EXTRA_ROWS - 3 - npol, lanes), jnp.float32)
    extras[...] = jnp.concatenate([vectors, energy, bands * first, second, rest], 0)
    for copy in chunks:
        copy.wait()


def prepare(ka, dims, qmap, owner, band_pairs, val_energy, cond_energy, start, screening, after):
    vloc, val_count, cond_count, npol = dims
    rows = 4 * ka * vloc * val_count
    lanes = 2 * ka * val_count * cond_count
    operands = (qmap, owner, band_pairs, val_energy, cond_energy, start, screening)
    table = jax.ShapeDtypeStruct((rows, val_count * lanes), jnp.bfloat16)
    return pl.pallas_call(
        functools.partial(prepare_kernel, ka, dims),
        out_shape=[
            in_vmem(screening.shape[1:], screening.dtype),
            in_vmem(table.shape, table.dtype),
            in_vmem((EXTRA_ROWS, lanes), jnp.float32),
        ],
        in_specs=[anywhere] * 8,
        out_specs=[vmem] * 3,
        scratch_shapes=[pltpu.SMEM(x.shape, x.dtype) for x in operands[:5]]
        + [
            pltpu.VMEM(start.shape, start.dtype),
            pltpu.SemaphoreType.DMA((6,)),
            pltpu.SemaphoreType.DMA((2, CHUNKS)),
        ],
        cost_estimate=pl.CostEstimate(
            flops=0, bytes_accessed=4 * screening.size, transcendentals=0
        ),
        compiler_params=limits(table),
        name="prepare",
    )(*[placed(x, pltpu.HBM) for x in operands], after)


def regroup_kernel(ka, val_rows, *refs):
    blocks, (val_all, cond_half) = refs[:ka], refs[-2:]
    cond_rows = blocks[0].shape[0] - val_rows
    for j in range(ka):
        val_all[j * val_rows : (j + 1) * val_rows, :] = blocks[j][:val_rows, :]
        cond_half[j * cond_rows : (j + 1) * cond_rows, :] = blocks[j][val_rows:, :]


def regroup(ka, val_rows, blocks, after):
    rows, width = blocks[0].shape
    kind = blocks[0].dtype
    return pl.pallas_call(
        functools.partial(regroup_kernel, ka, val_rows),
        out_shape=[in_vmem((ka * val_rows, width), kind), in_vmem((ka * (rows - val_rows), width), kind)],
        in_specs=[vmem] * ka + [anywhere],
        out_specs=[vmem] * 2,
        compiler_params=limits(*blocks),
        name="regroup",
    )(*blocks, after)


def screened_block(screening, valence, pairs, place):
    wide = valence[...].astype(jnp.float32)
    parts = []
    for at in range(0, wide.shape[0], 2 * pairs):
        parts += [-wide[at + pairs : at + 2 * pairs], wide[at : at + pairs]]
    turned = jnp.concatenate(parts, 0)
    real = jnp.concatenate([wide, turned], 0).astype(jnp.bfloat16)
    imag = jnp.concatenate([turned, -wide], 0).astype(jnp.bfloat16)
    width = wide.shape[1]
    columns = pl.ds(pl.multiple_of(place * width, 128), width)
    form = (((1,), (1,)), ((), ()))
    return lax.dot_general(
        screening[0, :, columns], real, form, preferred_element_type=jnp.float32
    ) + lax.dot_general(screening[1, :, columns], imag, form, preferred_element_type=jnp.float32)


def near_kernel(pairs, screening, valence, out):
    out[...] = screened_block(screening, valence, pairs, lax.axis_index("ga"))


def near_field(pairs, screening, valence):
    rows, width = valence.shape
    glocal = screening.shape[1]
    return pl.pallas_call(
        functools.partial(near_kernel, pairs),
        out_shape=in_vmem((glocal, 2 * rows), jnp.float32),
        in_specs=[vmem, vmem],
        out_specs=vmem,
        cost_estimate=pl.CostEstimate(
            flops=8 * glocal * width * rows, bytes_accessed=screening.size, transcendentals=0
        ),
        compiler_params=limits(screening, valence),
        name="near_field",
    )(screening, valence)


def project_kernel(ka, ga, ba, dims, *refs):
    vloc, val_count, cond_count, npol = dims
    screening, table, extras, near = refs[:4]
    val_in = refs[4 : 4 + ga - 1]
    cond_in = refs[-1 - ba : -1]
    out = refs[-1]
    mine = lax.axis_index("ga")
    half = lax.axis_index("ba")
    pairs = vloc * val_count
    block = 2 * pairs
    rows = ka * block
    codes = val_count * cond_count
    lanes = 2 * ka * codes
    share = cond_count // ba
    cond_rows = cond_count * cond_count
    share_rows = share * cond_count

    fields = near[...]
    for r in range(1, ga):
        fields = fields + screened_block(screening, val_in[r - 1], pairs, origin(mine, r, ga))
    both = jnp.concatenate(split(fields), 1)
    cond_all = jnp.concatenate([ref[...] for ref in cond_in], 0)
    crossed = jnp.dot(cond_all, both, preferred_element_type=jnp.float32)
    crossed = crossed[:, : 2 * rows] + crossed[:, 2 * rows :]
    lane = iota((share_rows, 2 * rows), 1)
    lane_j = lane % rows // block
    turned_lane = lane // rows
    kernel = []
    for h in range(ba):
        total = jnp.zeros((share_rows, 2 * rows), jnp.float32)
        for j in range(ka):
            base = (h * ka + j) * 2 * share_rows
            real = crossed[base : base + share_rows]
            imag = crossed[base + share_rows : base + 2 * share_rows]
            value = jnp.where(turned_lane == 0, real, -imag)
            total = jnp.where(lane_j == j, value, total)
        kernel.append(total)
    kernel = jnp.concatenate(kernel, 0)

    spread = jnp.dot(
        jnp.concatenate(split(kernel), 0), table[...], preferred_element_type=jnp.float32
    )
    spread = spread[:cond_rows] + spread[cond_rows:]
    crow = iota((cond_rows, lanes), 0)
    c_of_row = origin(half, crow // share_rows, ba) * share + crow % share_rows // cond_count
    same_c = c_of_row == iota((cond_rows, lanes), 1) % cond_count
    spread = jnp.concatenate(
        [
            jnp.where(same_c, spread[:, v2 * lanes : (v2 + 1) * lanes], 0.0)
            for v2 in range(val_count)
        ],
        0,
    )
    out_row = iota((codes, val_count * cond_rows), 0)
    out_col = iota((codes, val_count * cond_rows), 1)
    fold = (out_row // cond_count == out_col // cond_rows) & (
        out_row % cond_count == out_col % cond_count
    )
    fold = jnp.where(fold, 1.0, 0.0).astype(jnp.bfloat16)
    piece = jnp.dot(fold, jnp.concatenate(split(spread), 1), preferred_element_type=jnp.float32)
    out[:codes, :] = piece[:, :lanes] + piece[:, lanes:]
    out[codes:, :] = extras[...]


def project(ka, ga, ba, dims, screening, table, extras, near, val_far, cond_all):
    vloc, val_count, cond_count, npol = dims
    codes = val_count * cond_count
    operands = [screening, table, extras, near, *val_far, *cond_all]
    return pl.pallas_call(
        functools.partial(project_kernel, ka, ga, ba, dims),
        out_shape=in_vmem((codes + EXTRA_ROWS, 2 * ka * codes), jnp.float32),
        in_specs=[vmem] * len(operands),
        out_specs=vmem,
        compiler_params=limits(*operands),
        name="project",
    )(*operands)


def haydock_kernel(ka, codes, scale_count, npol, *refs):
    pieces = refs[:-3]
    next_out, coef_out, matrix = refs[-3:]
    lanes = pieces[0].shape[1]
    mid = lanes // 2
    height = codes + EXTRA_ROWS
    found = [(ref, at) for ref in pieces for at in range(0, ref.shape[0], height)]
    extras = None
    slots = []
    for ref, at in found:
        rows = ref[at + codes : at + height, :]
        extras = rows if extras is None else extras + rows
        slots.append((ref[at : at + codes, :], rows[npol + 2 : npol + 3]))
    own = pieces[0][codes:height, :]
    sign = jnp.where(iota((1, lanes), 1) < mid, -1.0, 1.0)
    for k2 in range(ka):
        block = jnp.zeros((codes, lanes), jnp.float32)
        for piece, second in slots:
            block = jnp.where(second == float(k2), piece, block)
        matrix[k2 * codes : (k2 + 1) * codes, :] = block
        matrix[mid + k2 * codes : mid + (k2 + 1) * codes, :] = sign * pltpu.roll(block, mid, 1)
    high, low = split(matrix[...])
    full = jnp.concatenate([high, low], 1)
    start = extras[:npol]
    energy = extras[npol : npol + 1]

    def halves(vector):
        top = vector.astype(jnp.bfloat16).astype(jnp.float32)
        return jnp.concatenate([top, vector - top], 0).astype(jnp.bfloat16)

    def mean(values):
        return jnp.sum(values, axis=1, keepdims=True) / scale_count

    def norm(vector):
        return jnp.sqrt(mean(vector * vector) + EPSILON)

    def swap(vector):
        return pltpu.roll(vector, mid, 1)

    def hamiltonian(vector):
        product = jnp.dot(halves(vector), full, preferred_element_type=jnp.float32)
        main = product[:npol, :lanes] + product[npol:, :lanes]
        return energy * vector - (main + product[:npol, lanes:])

    def inner(left, right):
        return mean(left * right), mean(-sign * left * swap(right))

    def times(real, imag, vector):
        return real * vector + imag * (sign * swap(vector))

    start_image = hamiltonian(start)
    scale = 1.0 / norm(start)
    first = start * scale
    first_image = start_image * scale
    alpha_real, alpha_imag = inner(first, first_image)
    first_resid = first_image - times(alpha_real, alpha_imag, first)
    resid_image = hamiltonian(first_resid)
    beta_one = norm(first_resid)
    scale = 1.0 / beta_one
    second = first_resid * scale
    second_image = resid_image * scale
    gamma_real, gamma_imag = inner(second, second_image)
    second_resid = second_image - times(gamma_real, gamma_imag, second) - beta_one * first
    beta_two = norm(second_resid)

    coef_lane = iota(coef_out.shape, 1)
    coefs = jnp.zeros(coef_out.shape, jnp.float32)
    for at, value in enumerate((alpha_real, alpha_imag, gamma_real, gamma_imag, beta_one, beta_two)):
        coefs = jnp.where(coef_lane == at, value, coefs)
    coef_out[...] = coefs
    row = iota((2 * codes, lanes), 0)
    lane = iota((2 * codes, lanes), 1)
    here = (lane % mid // codes == lax.axis_index("ka")) & (lane // mid == row // codes)
    band = (row % codes).astype(jnp.float32)
    pick = jnp.where(here & (own[npol + 1 : npol + 2] == band), 1.0, 0.0).astype(jnp.bfloat16)
    picked = lax.dot_general(
        halves(second_resid), pick, (((1,), (1,)), ((), ())), preferred_element_type=jnp.float32
    )
    picked = (picked[:npol] + picked[npol:]) / beta_two
    next_out[0, :, 0, :] = picked[:, :codes]
    next_out[0, :, 1, :] = picked[:, codes:]


def haydock(ka, codes, scale_count, npol, pieces):
    lanes = pieces[0].shape[1]
    square = jax.ShapeDtypeStruct((lanes, lanes), jnp.float32)
    return pl.pallas_call(
        functools.partial(haydock_kernel, ka, codes, scale_count, npol),
        out_shape=[
            jax.ShapeDtypeStruct((1, npol, 2, codes), jnp.float32),
            jax.ShapeDtypeStruct((npol, 6), jnp.float32),
        ],
        in_specs=[vmem] * len(pieces),
        out_specs=[vmem, vmem],
        scratch_shapes=[pltpu.VMEM(square.shape, square.dtype)],
        compiler_params=limits(*pieces, square),
        name="haydock",
    )(*pieces)


def summed(value, axis):
    size = lax.axis_size(axis)
    if size & (size - 1):
        return lax.psum(value, axis)
    step = 1
    while step < size:
        value = value + lax.ppermute(value, axis, [(i, i ^ step) for i in range(size)])
        step *= 2
    return value


def sent(values, axis):
    return [values[0]] + [exchanged(values[j], axis, j) for j in range(1, lax.axis_size(axis))]


def local(
    ka,
    ga,
    ba,
    start_vector,
    valence_density,
    conduction_density,
    screening,
    qpoint_map,
    slot_owner,
    band_pairs,
    valence_energy,
    conduction_energy,
):
    npol = start_vector.shape[1]
    pair_count = start_vector.shape[3]
    kcount, vloc, val_count = qpoint_map.shape[0], valence_density.shape[3], valence_density.shape[4]
    cond_count = conduction_density.shape[3]
    pairs = vloc * val_count
    dims = (vloc, val_count, cond_count, npol)
    packed = pack(ka, ba, qpoint_map, slot_owner, valence_density, conduction_density)
    blocks = sent(packed, "ka")
    whole, table, extras = prepare(
        ka,
        dims,
        qpoint_map,
        slot_owner,
        band_pairs,
        valence_energy,
        conduction_energy,
        start_vector,
        screening,
        packed[0],
    )
    val_all, cond_half = regroup(ka, 2 * pairs, blocks, extras)
    val_far = [exchanged(val_all, "ga", r) for r in range(1, ga)]
    cond_all = [cond_half] + [exchanged(cond_half, "ba", r) for r in range(1, ba)]
    near = near_field(pairs, whole, val_all)
    piece = project(ka, ga, ba, dims, whole, table, extras, near, val_far, cond_all)
    piece = summed(summed(piece, "ba"), "ga")
    pieces = sent([piece] * ka, "ka")
    scale_count = float(kcount * pair_count)
    return tuple(haydock(ka, pair_count, scale_count, npol, pieces))


def solution(mesh):
    in_specs = (
        P(("grp", "ka"), None, None, None),
        P(("grp", "ka"), None, None, "ba", None, "ga"),
        P(("grp", "ka"), None, None, None, None, "ga"),
        P(("grp", "ka"), None, "ga", None),
        P(),
        P(),
        P(),
        P(("grp", "ka"), None),
        P(("grp", "ka"), None),
    )
    out_specs = (P(("grp", "ka"), None, None, None), P("grp", None))
    body = functools.partial(local, mesh.shape["ka"], mesh.shape["ga"], mesh.shape["ba"])
    return jax.shard_map(body, mesh=mesh, in_specs=in_specs, out_specs=out_specs, check_vma=False)
```

```python
import functools
import math

import jax
import jax.numpy as jnp
from jax import lax
from jax.experimental import pallas as pl
from jax.experimental.pallas import tpu as pltpu
from jax.sharding import PartitionSpec as P

EPSILON = 1e-06
EXACT = lax.Precision.HIGHEST
VMEM_LEAST = 8 * 1024 * 1024
VMEM_MOST = 56 * 1024 * 1024

vmem = pl.BlockSpec(memory_space=pltpu.VMEM)
anywhere = pl.BlockSpec(memory_space=pl.ANY)
EXTRA_ROWS = 8
CHUNKS = 4
TOGETHER = 4


def in_vmem(shape, dtype):
    return pltpu.VMEM(shape, dtype)


def placed(value, space):
    return pltpu.with_memory_space_constraint(value, space)


def iota(shape, axis):
    return lax.broadcasted_iota(jnp.int32, shape, axis)


def split(values):
    high = values.astype(jnp.bfloat16)
    low = (values - high.astype(jnp.float32)).astype(jnp.bfloat16)
    return high, low


def limits(*arrays):
    held = sum(math.prod(a.shape) * a.dtype.itemsize for a in arrays)
    return pltpu.CompilerParams(vmem_limit_bytes=min(VMEM_MOST, VMEM_LEAST + 4 * held))


def target(me, step, size):
    return lax.rem(me + step, size)


def origin(me, step, size):
    return lax.rem(me + size - step, size)


def exchanged(value, axis, move):
    size, cores = lax.axis_size(axis), lax.axis_size("ba")
    pairs = [(i * cores + cores - 1, move(i, size) * cores + cores - 1) for i in range(size)]
    return lax.ppermute(value, (axis, "ba"), pairs)


def shifted(value, axis, step):
    return exchanged(value, axis, lambda i, size: (i + step) % size)


def sort_kernel(ka, qmap_in, owner_in, valence_in, conduction_in, *rest):
    own, cond, chosen = rest[:3]
    qmap, owner, partner, valence, conduction, sems = rest[3:]
    copies = [
        pltpu.make_async_copy(src, dst, sems.at[at])
        for at, (src, dst) in enumerate(
            ((qmap_in, qmap), (owner_in, owner), (valence_in, valence), (conduction_in, conduction))
        )
    ]
    for copy in copies:
        copy.start()
    me = lax.axis_index("ka")
    count, width = valence.shape[1], valence.shape[5]
    val_rows = own.shape[0] // ka
    cond_rows = cond.shape[0] // ka

    def note(k2, carry):
        partner[owner[qmap[me, k2]]] = k2
        return carry

    copies[0].wait()
    copies[1].wait()
    lax.fori_loop(0, count, note, 0)
    copies[2].wait()
    copies[3].wait()
    for j in range(ka):
        k2 = partner[target(me, j, ka)]
        block = valence[0, k2].astype(jnp.float32).reshape(val_rows, width)
        own[j * val_rows : (j + 1) * val_rows, :] = block.astype(jnp.bfloat16)
        block = conduction[0, k2].astype(jnp.float32).reshape(cond_rows, width)
        cond[j * cond_rows : (j + 1) * cond_rows, :] = block.astype(jnp.bfloat16)
        chosen[j * 8 : (j + 1) * 8, :] = jnp.full((8, 128), k2.astype(jnp.float32))


def sort(ka, qmap, owner, valence, conduction):
    width = valence.shape[5]
    val_rows = math.prod(valence.shape[2:5])
    cond_rows = math.prod(conduction.shape[2:5])
    return pl.pallas_call(
        functools.partial(sort_kernel, ka),
        out_shape=[
            in_vmem((ka * val_rows, width), valence.dtype),
            in_vmem((ka * cond_rows, width), conduction.dtype),
            in_vmem((ka * 8, 128), jnp.float32),
        ],
        in_specs=[anywhere] * 4,
        out_specs=[vmem] * 3,
        scratch_shapes=[
            pltpu.SMEM(qmap.shape, jnp.int32),
            pltpu.SMEM(owner.shape, jnp.int32),
            pltpu.SMEM(owner.shape, jnp.int32),
            pltpu.VMEM(valence.shape, valence.dtype),
            pltpu.VMEM(conduction.shape, conduction.dtype),
            pltpu.SemaphoreType.DMA((4,)),
        ],
        cost_estimate=pl.CostEstimate(
            flops=0, bytes_accessed=4 * (valence.size + conduction.size), transcendentals=0
        ),
        compiler_params=limits(valence, conduction),
        name="sort",
    )(*[placed(x, pltpu.HBM) for x in (qmap, owner, valence, conduction)])


def merge_kernel(ka, *refs):
    own, cond, chosen = refs[:3]
    received, outs = refs[3:-ka], refs[-ka:]
    width = own.shape[1]
    val_rows = own.shape[0] // ka
    cond_rows = cond.shape[0] // ka
    half = val_rows // 2
    count = received[0].shape[1] if received else 0
    others = [
        [ref[0, k2].astype(jnp.float32).reshape(val_rows, width) for k2 in range(count)]
        for ref in received
    ]
    for j in range(ka):
        here = chosen[j * 8 : j * 8 + 1, 0:1]
        shares = []
        for blocks in others:
            block = blocks[0]
            for k2 in range(1, count):
                block = jnp.where(here == float(k2), blocks[k2], block)
            shares.append(block)
        shares.append(own[j * val_rows : (j + 1) * val_rows, :].astype(jnp.float32))
        rows = [x[part * half : (part + 1) * half] for part in range(2) for x in shares]
        rows = jnp.concatenate(rows, 0)
        outs[j][: rows.shape[0], :] = rows.astype(jnp.bfloat16)
        outs[j][rows.shape[0] :, :] = cond[j * cond_rows : (j + 1) * cond_rows, :]


def merge(ka, own, cond, chosen, received):
    rows = (own.shape[0] * (1 + len(received)) + cond.shape[0]) // ka
    shape = in_vmem((rows, own.shape[1]), own.dtype)
    operands = [own, cond, chosen, *received]
    return pl.pallas_call(
        functools.partial(merge_kernel, ka),
        out_shape=[shape] * ka,
        in_specs=[vmem] * len(operands),
        out_specs=[vmem] * ka,
        compiler_params=limits(*operands),
        name="merge",
    )(*operands)


def prepare_kernel(ka, dims, *refs):
    val_count, cond_count, npol = dims
    ins, screening, (screen_out, table, extras), scratch = refs[:6], refs[6], refs[8:11], refs[11:]
    qmap, owner, band_pairs, val_energy, cond_energy, start, sems, screen_sems = scratch
    me = lax.axis_index("ka")
    mine = lax.axis_index("ga")
    copies = [
        pltpu.make_async_copy(src, dst, sems.at[at])
        for at, (src, dst) in enumerate(
            zip(ins, (qmap, owner, band_pairs, val_energy, cond_energy, start))
        )
    ]
    height = screening.shape[2] // CHUNKS
    chunks = [
        pltpu.make_async_copy(
            screening.at[0, part, pl.ds(c * height, height)],
            screen_out.at[part, pl.ds(c * height, height)],
            screen_sems.at[part, c],
        )
        for part in range(2)
        for c in range(CHUNKS)
    ]
    for copy in copies + chunks:
        copy.start()
    pairs = val_count * val_count
    block = 2 * pairs
    codes = val_count * cond_count
    mid = ka * codes
    lanes = 2 * mid
    row = iota((block, val_count * lanes), 0)
    col = iota((block, val_count * lanes), 1)
    same = (row // pairs == col % lanes // mid) & (row % val_count == col // lanes)
    same = same & (row % pairs // val_count == col % codes // cond_count)
    col_k = col % mid // codes

    def fill(j, carry):
        pick = jnp.where(same & (col_k == origin(me, j, ka)), 1.0, 0.0)
        table[pl.ds(pl.multiple_of(j * block, block), block), :] = pick.astype(jnp.bfloat16)
        return carry

    lax.fori_loop(0, ka, fill, 0)
    for copy in copies:
        copy.wait()
    first = jnp.where(mine == 0, 1.0, 0.0)
    lane = iota((1, lanes), 1)
    lane_k = lane % mid // codes
    band_row = iota((codes, lanes), 0)
    band_lane = iota((codes, lanes), 1)
    code = jnp.zeros((codes, lanes), jnp.int32)
    bands = jnp.full((1, lanes), -1.0, jnp.float32)
    for b in range(codes):
        code = jnp.where(band_row == b, band_pairs[b], code)
        bands = jnp.where(lane % codes == band_pairs[b], float(b), bands)
    vectors = jnp.zeros((npol, lanes), jnp.float32)
    for part in range(2):
        spot = part * mid + me * codes
        pick = jnp.where(band_lane == spot + code, first, 0.0)
        vectors = vectors + jnp.dot(start[0, :, part, :], pick, precision=EXACT)
    energy = jnp.zeros((1, lanes), jnp.float32)
    for c in range(cond_count):
        energy = jnp.where(lane % cond_count == c, cond_energy[0, c], energy)
    for v in range(val_count):
        energy = energy - jnp.where(lane % codes // cond_count == v, val_energy[0, v], 0.0)
    energy = jnp.where(lane_k == me, energy * first, 0.0)
    kcount = qmap.shape[0]

    def find(k2, found):
        return jnp.where(owner[qmap[0, k2]] == me, k2, found)

    back = lax.fori_loop(0, kcount, find, 0)
    second = lane_k + back
    second = jnp.where(second >= kcount, second - kcount, second).astype(jnp.float32) * first
    rest = jnp.zeros((EXTRA_ROWS - 3 - npol, lanes), jnp.float32)
    extras[...] = jnp.concatenate([vectors, energy, bands * first, second, rest], 0)
    for copy in chunks:
        copy.wait()


def prepare(ka, dims, qmap, owner, band_pairs, val_energy, cond_energy, start, screening, after):
    val_count, cond_count, npol = dims
    rows = 2 * ka * val_count * val_count
    lanes = 2 * ka * val_count * cond_count
    operands = (qmap, owner, band_pairs, val_energy, cond_energy, start, screening)
    table = jax.ShapeDtypeStruct((rows, val_count * lanes), jnp.bfloat16)
    return pl.pallas_call(
        functools.partial(prepare_kernel, ka, dims),
        out_shape=[
            in_vmem(screening.shape[1:], screening.dtype),
            in_vmem(table.shape, table.dtype),
            in_vmem((EXTRA_ROWS, lanes), jnp.float32),
        ],
        in_specs=[anywhere] * 8,
        out_specs=[vmem] * 3,
        scratch_shapes=[pltpu.SMEM(x.shape, x.dtype) for x in operands[:5]]
        + [
            pltpu.VMEM(start.shape, start.dtype),
            pltpu.SemaphoreType.DMA((6,)),
            pltpu.SemaphoreType.DMA((2, CHUNKS)),
        ],
        cost_estimate=pl.CostEstimate(
            flops=0, bytes_accessed=4 * screening.size, transcendentals=0
        ),
        compiler_params=limits(table),
        name="prepare",
    )(*[placed(x, pltpu.HBM) for x in operands], after)


def regroup_kernel(ka, val_rows, *refs):
    blocks, (val_all, cond_half) = refs[:ka], refs[-2:]
    cond_rows = blocks[0].shape[0] - val_rows
    for j in range(ka):
        val_all[j * val_rows : (j + 1) * val_rows, :] = blocks[j][:val_rows, :]
        cond_half[j * cond_rows : (j + 1) * cond_rows, :] = blocks[j][val_rows:, :]


def regroup(ka, val_rows, blocks, after):
    rows, width = blocks[0].shape
    kind = blocks[0].dtype
    return pl.pallas_call(
        functools.partial(regroup_kernel, ka, val_rows),
        out_shape=[in_vmem((ka * val_rows, width), kind), in_vmem((ka * (rows - val_rows), width), kind)],
        in_specs=[vmem] * ka + [anywhere],
        out_specs=[vmem] * 2,
        compiler_params=limits(*blocks),
        name="regroup",
    )(*blocks, after)


def screened_block(screening, valence, pairs, place):
    wide = valence[...].astype(jnp.float32)
    parts = []
    for at in range(0, wide.shape[0], 2 * pairs):
        parts += [-wide[at + pairs : at + 2 * pairs], wide[at : at + pairs]]
    turned = jnp.concatenate(parts, 0)
    real = jnp.concatenate([wide, turned], 0).astype(jnp.bfloat16)
    imag = jnp.concatenate([turned, -wide], 0).astype(jnp.bfloat16)
    width = wide.shape[1]
    columns = pl.ds(pl.multiple_of(place * width, 128), width)
    form = (((1,), (1,)), ((), ()))
    return lax.dot_general(
        screening[0, :, columns], real, form, preferred_element_type=jnp.float32
    ) + lax.dot_general(screening[1, :, columns], imag, form, preferred_element_type=jnp.float32)


def near_kernel(pairs, screening, valence, out):
    out[...] = screened_block(screening, valence, pairs, lax.axis_index("ga"))


def near_field(pairs, screening, valence):
    rows, width = valence.shape
    glocal = screening.shape[1]
    return pl.pallas_call(
        functools.partial(near_kernel, pairs),
        out_shape=in_vmem((glocal, 2 * rows), jnp.float32),
        in_specs=[vmem, vmem],
        out_specs=vmem,
        cost_estimate=pl.CostEstimate(
            flops=8 * glocal * width * rows, bytes_accessed=screening.size, transcendentals=0
        ),
        compiler_params=limits(screening, valence),
        name="near_field",
    )(screening, valence)


def project_kernel(ka, ga, dims, *refs):
    val_count, cond_count, npol = dims
    screening, table, extras, near = refs[:4]
    val_in = refs[4 : 4 + ga - 1]
    cond_in, out = refs[-2:]
    mine = lax.axis_index("ga")
    pairs = val_count * val_count
    block = 2 * pairs
    rows = ka * block
    codes = val_count * cond_count
    lanes = 2 * ka * codes
    cond_rows = cond_count * cond_count

    fields = near[...]
    for r in range(1, ga):
        fields = fields + screened_block(screening, val_in[r - 1], pairs, origin(mine, r, ga))
    both = jnp.concatenate(split(fields), 1)
    lane_j = iota((cond_rows, rows), 1) // block
    kernel = jnp.zeros((cond_rows, rows), jnp.float32)
    for start in range(0, ka, TOGETHER):
        end = min(start + TOGETHER, ka)
        cond = cond_in[start * 2 * cond_rows : end * 2 * cond_rows, :]
        crossed = jnp.dot(cond, both, preferred_element_type=jnp.float32)
        crossed = crossed[:, : 2 * rows] + crossed[:, 2 * rows :]
        for j in range(start, end):
            base = (j - start) * 2 * cond_rows
            real = crossed[base : base + cond_rows, :rows]
            imag = crossed[base + cond_rows : base + 2 * cond_rows, rows:]
            kernel = jnp.where(lane_j == j, real - imag, kernel)

    spread = jnp.dot(
        jnp.concatenate(split(kernel), 0), table[...], preferred_element_type=jnp.float32
    )
    spread = spread[:cond_rows] + spread[cond_rows:]
    crow = iota((cond_rows, lanes), 0)
    same_c = crow // cond_count == iota((cond_rows, lanes), 1) % cond_count
    spread = jnp.concatenate(
        [
            jnp.where(same_c, spread[:, v2 * lanes : (v2 + 1) * lanes], 0.0)
            for v2 in range(val_count)
        ],
        0,
    )
    out_row = iota((codes, val_count * cond_rows), 0)
    out_col = iota((codes, val_count * cond_rows), 1)
    fold = (out_row // cond_count == out_col // cond_rows) & (
        out_row % cond_count == out_col % cond_count
    )
    fold = jnp.where(fold, 1.0, 0.0).astype(jnp.bfloat16)
    piece = jnp.dot(fold, jnp.concatenate(split(spread), 1), preferred_element_type=jnp.float32)
    out[:codes, :] = piece[:, :lanes] + piece[:, lanes:]
    out[codes:, :] = extras[...]


def project(ka, ga, dims, screening, table, extras, near, val_far, cond_all):
    val_count, cond_count, npol = dims
    codes = val_count * cond_count
    operands = [screening, table, extras, near, *val_far, cond_all]
    return pl.pallas_call(
        functools.partial(project_kernel, ka, ga, dims),
        out_shape=in_vmem((codes + EXTRA_ROWS, 2 * ka * codes), jnp.float32),
        in_specs=[vmem] * len(operands),
        out_specs=vmem,
        compiler_params=limits(*operands),
        name="project",
    )(*operands)


def haydock_kernel(ka, codes, scale_count, npol, *refs):
    versions = refs[:-3]
    next_out, coef_out, matrix = refs[-3:]
    cores = lax.axis_size("ba")
    gathered = versions[0][...]
    for h in range(cores - 1):
        gathered = jnp.where(lax.axis_index("ba") == h, versions[1 + h][...], gathered)
    lanes = gathered.shape[1]
    mid = lanes // 2
    height = codes + EXTRA_ROWS
    extras = None
    slots = []
    for at in range(0, gathered.shape[0], height):
        rows = gathered[at + codes : at + height]
        extras = rows if extras is None else extras + rows
        slots.append((gathered[at : at + codes], rows[npol + 2 : npol + 3]))
    own = gathered[codes:height]
    sign = jnp.where(iota((1, lanes), 1) < mid, -1.0, 1.0)
    for k2 in range(ka):
        block = jnp.zeros((codes, lanes), jnp.float32)
        for piece, second in slots:
            block = jnp.where(second == float(k2), piece, block)
        matrix[k2 * codes : (k2 + 1) * codes, :] = block
        matrix[mid + k2 * codes : mid + (k2 + 1) * codes, :] = sign * pltpu.roll(block, mid, 1)
    high, low = split(matrix[...])
    full = jnp.concatenate([high, low], 1)
    start = extras[:npol]
    energy = extras[npol : npol + 1]

    def halves(vector):
        top = vector.astype(jnp.bfloat16).astype(jnp.float32)
        return jnp.concatenate([top, vector - top], 0).astype(jnp.bfloat16)

    def mean(values):
        return jnp.sum(values, axis=1, keepdims=True) / scale_count

    def norm(vector):
        return jnp.sqrt(mean(vector * vector) + EPSILON)

    def swap(vector):
        return pltpu.roll(vector, mid, 1)

    def hamiltonian(vector):
        product = jnp.dot(halves(vector), full, preferred_element_type=jnp.float32)
        main = product[:npol, :lanes] + product[npol:, :lanes]
        return energy * vector - (main + product[:npol, lanes:])

    def inner(left, right):
        return mean(left * right), mean(-sign * left * swap(right))

    def times(real, imag, vector):
        return real * vector + imag * (sign * swap(vector))

    start_image = hamiltonian(start)
    scale = 1.0 / norm(start)
    first = start * scale
    first_image = start_image * scale
    alpha_real, alpha_imag = inner(first, first_image)
    first_resid = first_image - times(alpha_real, alpha_imag, first)
    resid_image = hamiltonian(first_resid)
    beta_one = norm(first_resid)
    scale = 1.0 / beta_one
    second = first_resid * scale
    second_image = resid_image * scale
    gamma_real, gamma_imag = inner(second, second_image)
    second_resid = second_image - times(gamma_real, gamma_imag, second) - beta_one * first
    beta_two = norm(second_resid)

    coef_lane = iota(coef_out.shape, 1)
    coefs = jnp.zeros(coef_out.shape, jnp.float32)
    for at, value in enumerate((alpha_real, alpha_imag, gamma_real, gamma_imag, beta_one, beta_two)):
        coefs = jnp.where(coef_lane == at, value, coefs)
    coef_out[...] = coefs
    row = iota((2 * codes, lanes), 0)
    lane = iota((2 * codes, lanes), 1)
    here = (lane % mid // codes == lax.axis_index("ka")) & (lane // mid == row // codes)
    band = (row % codes).astype(jnp.float32)
    pick = jnp.where(here & (own[npol + 1 : npol + 2] == band), 1.0, 0.0).astype(jnp.bfloat16)
    picked = lax.dot_general(
        halves(second_resid), pick, (((1,), (1,)), ((), ())), preferred_element_type=jnp.float32
    )
    picked = (picked[:npol] + picked[npol:]) / beta_two
    next_out[0, :, 0, :] = picked[:, :codes]
    next_out[0, :, 1, :] = picked[:, codes:]


def haydock(ka, codes, scale_count, npol, versions):
    lanes = versions[0].shape[1]
    square = jax.ShapeDtypeStruct((lanes, lanes), jnp.float32)
    return pl.pallas_call(
        functools.partial(haydock_kernel, ka, codes, scale_count, npol),
        out_shape=[
            jax.ShapeDtypeStruct((1, npol, 2, codes), jnp.float32),
            jax.ShapeDtypeStruct((npol, 6), jnp.float32),
        ],
        in_specs=[vmem] * len(versions),
        out_specs=[vmem, vmem],
        scratch_shapes=[pltpu.VMEM(square.shape, square.dtype)],
        compiler_params=limits(*versions, square),
        name="haydock",
    )(*versions)


def summed(value, axis):
    size = lax.axis_size(axis)
    if size & (size - 1):
        return value + sum(shifted(value, axis, step) for step in range(1, size))
    step = 1
    while step < size:
        value = value + exchanged(value, axis, lambda i, size: i ^ step)
        step *= 2
    return value


def local(
    ka,
    ga,
    ba,
    start_vector,
    valence_density,
    conduction_density,
    screening,
    qpoint_map,
    slot_owner,
    band_pairs,
    valence_energy,
    conduction_energy,
):
    npol = start_vector.shape[1]
    pair_count = start_vector.shape[3]
    kcount, val_count = qpoint_map.shape[0], valence_density.shape[4]
    cond_count = conduction_density.shape[3]
    pairs = val_count * val_count
    dims = (val_count, cond_count, npol)
    last = ba - 1
    received = [lax.ppermute(valence_density, "ba", [(h, last)]) for h in range(last)]
    own, cond, chosen = sort(ka, qpoint_map, slot_owner, valence_density, conduction_density)
    packed = merge(ka, own, cond, chosen, received)
    blocks = [packed[0]] + [shifted(packed[j], "ka", j) for j in range(1, ka)]
    whole, table, extras = prepare(
        ka,
        dims,
        qpoint_map,
        slot_owner,
        band_pairs,
        valence_energy,
        conduction_energy,
        start_vector,
        screening,
        packed[0],
    )
    val_all, cond_all = regroup(ka, 2 * pairs, blocks, extras)
    val_far = [shifted(val_all, "ga", r) for r in range(1, ga)]
    near = near_field(pairs, whole, val_all)
    piece = project(ka, ga, dims, whole, table, extras, near, val_far, cond_all)
    piece = summed(piece, "ga")
    pieces = [piece] + [shifted(piece, "ka", j) for j in range(1, ka)]
    gathered = jnp.concatenate(pieces, 0)
    versions = [gathered] + [lax.ppermute(gathered, "ba", [(last, h)]) for h in range(last)]
    scale_count = float(kcount * pair_count)
    return tuple(haydock(ka, pair_count, scale_count, npol, versions))


def solution(mesh):
    in_specs = (
        P(("grp", "ka"), None, None, None),
        P(("grp", "ka"), None, None, "ba", None, "ga"),
        P(("grp", "ka"), None, None, None, None, "ga"),
        P(("grp", "ka"), None, "ga", None),
        P(),
        P(),
        P(),
        P(("grp", "ka"), None),
        P(("grp", "ka"), None),
    )
    out_specs = (P(("grp", "ka"), None, None, None), P("grp", None))
    body = functools.partial(local, mesh.shape["ka"], mesh.shape["ga"], mesh.shape["ba"])
    return jax.shard_map(body, mesh=mesh, in_specs=in_specs, out_specs=out_specs, check_vma=False)
```

```python
import functools
import math

import jax
import jax.numpy as jnp
from jax import lax
from jax.experimental import pallas as pl
from jax.experimental.pallas import tpu as pltpu
from jax.sharding import PartitionSpec as P

EPSILON = 1e-06
EXACT = lax.Precision.HIGHEST
VMEM_LEAST = 8 * 1024 * 1024
VMEM_MOST = 56 * 1024 * 1024

vmem = pl.BlockSpec(memory_space=pltpu.VMEM)
anywhere = pl.BlockSpec(memory_space=pl.ANY)
EXTRA_ROWS = 8
CHUNKS = 4
TOGETHER = 4


def in_vmem(shape, dtype):
    return pltpu.VMEM(shape, dtype)


def placed(value, space):
    return pltpu.with_memory_space_constraint(value, space)


def iota(shape, axis):
    return lax.broadcasted_iota(jnp.int32, shape, axis)


def split(values):
    high = values.astype(jnp.bfloat16)
    low = (values - high.astype(jnp.float32)).astype(jnp.bfloat16)
    return high, low


def limits(*arrays):
    held = sum(math.prod(a.shape) * a.dtype.itemsize for a in arrays)
    return pltpu.CompilerParams(vmem_limit_bytes=min(VMEM_MOST, VMEM_LEAST + 4 * held))


def target(me, step, size):
    return lax.rem(me + step, size)


def origin(me, step, size):
    return lax.rem(me + size - step, size)


def exchanged(value, axis, move):
    size, cores = lax.axis_size(axis), lax.axis_size("ba")
    pairs = []
    for i in range(size):
        pairs += [(i * cores + h, i * cores + h) for h in range(cores - 1)]
        pairs.append((i * cores + cores - 1, move(i, size) * cores + cores - 1))
    return lax.ppermute(value, (axis, "ba"), pairs)


def handed(value, step):
    size = lax.axis_size("ba")
    return lax.ppermute(value, "ba", [(h, (h + step) % size) for h in range(size)])


def shifted(value, axis, step):
    return exchanged(value, axis, lambda i, size: (i + step) % size)


def sort_kernel(ka, qmap_in, owner_in, valence_in, conduction_in, *rest):
    own, cond, chosen = rest[:3]
    qmap, owner, partner, valence, conduction, sems = rest[3:]
    copies = [
        pltpu.make_async_copy(src, dst, sems.at[at])
        for at, (src, dst) in enumerate(
            ((qmap_in, qmap), (owner_in, owner), (valence_in, valence), (conduction_in, conduction))
        )
    ]
    for copy in copies:
        copy.start()
    me = lax.axis_index("ka")
    count, width = valence.shape[1], valence.shape[5]
    val_rows = own.shape[0] // ka
    cond_rows = cond.shape[0] // ka

    def note(k2, carry):
        partner[owner[qmap[me, k2]]] = k2
        return carry

    copies[0].wait()
    copies[1].wait()
    lax.fori_loop(0, count, note, 0)
    copies[2].wait()
    copies[3].wait()
    for j in range(ka):
        k2 = partner[target(me, j, ka)]
        block = valence[0, k2].astype(jnp.float32).reshape(val_rows, width)
        own[j * val_rows : (j + 1) * val_rows, :] = block.astype(jnp.bfloat16)
        block = conduction[0, k2].astype(jnp.float32).reshape(cond_rows, width)
        cond[j * cond_rows : (j + 1) * cond_rows, :] = block.astype(jnp.bfloat16)
        chosen[j * 8 : (j + 1) * 8, :] = jnp.full((8, 128), k2.astype(jnp.float32))


def sort(ka, qmap, owner, valence, conduction):
    width = valence.shape[5]
    val_rows = math.prod(valence.shape[2:5])
    cond_rows = math.prod(conduction.shape[2:5])
    return pl.pallas_call(
        functools.partial(sort_kernel, ka),
        out_shape=[
            in_vmem((ka * val_rows, width), valence.dtype),
            in_vmem((ka * cond_rows, width), conduction.dtype),
            in_vmem((ka * 8, 128), jnp.float32),
        ],
        in_specs=[anywhere] * 4,
        out_specs=[vmem] * 3,
        scratch_shapes=[
            pltpu.SMEM(qmap.shape, jnp.int32),
            pltpu.SMEM(owner.shape, jnp.int32),
            pltpu.SMEM(owner.shape, jnp.int32),
            pltpu.VMEM(valence.shape, valence.dtype),
            pltpu.VMEM(conduction.shape, conduction.dtype),
            pltpu.SemaphoreType.DMA((4,)),
        ],
        cost_estimate=pl.CostEstimate(
            flops=0, bytes_accessed=4 * (valence.size + conduction.size), transcendentals=0
        ),
        compiler_params=limits(valence, conduction),
        name="sort",
    )(*[placed(x, pltpu.HBM) for x in (qmap, owner, valence, conduction)])


def merge_kernel(ka, *refs):
    own, cond, chosen = refs[:3]
    received, outs = refs[3:-ka], refs[-ka:]
    width = own.shape[1]
    val_rows = own.shape[0] // ka
    cond_rows = cond.shape[0] // ka
    half = val_rows // 2
    count = received[0].shape[1] if received else 0
    others = [
        [ref[0, k2].astype(jnp.float32).reshape(val_rows, width) for k2 in range(count)]
        for ref in received
    ]
    for j in range(ka):
        here = chosen[j * 8 : j * 8 + 1, 0:1]
        shares = []
        for blocks in others:
            block = blocks[0]
            for k2 in range(1, count):
                block = jnp.where(here == float(k2), blocks[k2], block)
            shares.append(block)
        shares.append(own[j * val_rows : (j + 1) * val_rows, :].astype(jnp.float32))
        rows = [x[part * half : (part + 1) * half] for part in range(2) for x in shares]
        rows = jnp.concatenate(rows, 0)
        outs[j][: rows.shape[0], :] = rows.astype(jnp.bfloat16)
        outs[j][rows.shape[0] :, :] = cond[j * cond_rows : (j + 1) * cond_rows, :]


def merge(ka, own, cond, chosen, received):
    rows = (own.shape[0] * (1 + len(received)) + cond.shape[0]) // ka
    shape = in_vmem((rows, own.shape[1]), own.dtype)
    operands = [own, cond, chosen, *received]
    return pl.pallas_call(
        functools.partial(merge_kernel, ka),
        out_shape=[shape] * ka,
        in_specs=[vmem] * len(operands),
        out_specs=[vmem] * ka,
        compiler_params=limits(*operands),
        name="merge",
    )(*operands)


def prepare_kernel(ka, dims, *refs):
    val_count, cond_count, npol = dims
    ins, screening, (screen_out, table, extras), scratch = refs[:6], refs[6], refs[8:11], refs[11:]
    qmap, owner, band_pairs, val_energy, cond_energy, start, sems, screen_sems = scratch
    me = lax.axis_index("ka")
    mine = lax.axis_index("ga")
    copies = [
        pltpu.make_async_copy(src, dst, sems.at[at])
        for at, (src, dst) in enumerate(
            zip(ins, (qmap, owner, band_pairs, val_energy, cond_energy, start))
        )
    ]
    height = screening.shape[2] // CHUNKS
    chunks = [
        pltpu.make_async_copy(
            screening.at[0, part, pl.ds(c * height, height)],
            screen_out.at[part, pl.ds(c * height, height)],
            screen_sems.at[part, c],
        )
        for part in range(2)
        for c in range(CHUNKS)
    ]
    for copy in copies + chunks:
        copy.start()
    pairs = val_count * val_count
    block = 2 * pairs
    codes = val_count * cond_count
    mid = ka * codes
    lanes = 2 * mid
    row = iota((block, val_count * lanes), 0)
    col = iota((block, val_count * lanes), 1)
    same = (row // pairs == col % lanes // mid) & (row % val_count == col // lanes)
    same = same & (row % pairs // val_count == col % codes // cond_count)
    col_k = col % mid // codes

    def fill(j, carry):
        pick = jnp.where(same & (col_k == origin(me, j, ka)), 1.0, 0.0)
        table[pl.ds(pl.multiple_of(j * block, block), block), :] = pick.astype(jnp.bfloat16)
        return carry

    lax.fori_loop(0, ka, fill, 0)
    for copy in copies:
        copy.wait()
    first = jnp.where(mine == 0, 1.0, 0.0)
    lane = iota((1, lanes), 1)
    lane_k = lane % mid // codes
    band_row = iota((codes, lanes), 0)
    band_lane = iota((codes, lanes), 1)
    code = jnp.zeros((codes, lanes), jnp.int32)
    bands = jnp.full((1, lanes), -1.0, jnp.float32)
    for b in range(codes):
        code = jnp.where(band_row == b, band_pairs[b], code)
        bands = jnp.where(lane % codes == band_pairs[b], float(b), bands)
    vectors = jnp.zeros((npol, lanes), jnp.float32)
    for part in range(2):
        spot = part * mid + me * codes
        pick = jnp.where(band_lane == spot + code, first, 0.0)
        vectors = vectors + jnp.dot(start[0, :, part, :], pick, precision=EXACT)
    energy = jnp.zeros((1, lanes), jnp.float32)
    for c in range(cond_count):
        energy = jnp.where(lane % cond_count == c, cond_energy[0, c], energy)
    for v in range(val_count):
        energy = energy - jnp.where(lane % codes // cond_count == v, val_energy[0, v], 0.0)
    energy = jnp.where(lane_k == me, energy * first, 0.0)
    kcount = qmap.shape[0]

    def find(k2, found):
        return jnp.where(owner[qmap[0, k2]] == me, k2, found)

    back = lax.fori_loop(0, kcount, find, 0)
    second = lane_k + back
    second = jnp.where(second >= kcount, second - kcount, second).astype(jnp.float32) * first
    rest = jnp.zeros((EXTRA_ROWS - 3 - npol, lanes), jnp.float32)
    extras[...] = jnp.concatenate([vectors, energy, bands * first, second, rest], 0)
    for copy in chunks:
        copy.wait()


def prepare(ka, dims, qmap, owner, band_pairs, val_energy, cond_energy, start, screening, after):
    val_count, cond_count, npol = dims
    rows = 2 * ka * val_count * val_count
    lanes = 2 * ka * val_count * cond_count
    operands = (qmap, owner, band_pairs, val_energy, cond_energy, start, screening)
    table = jax.ShapeDtypeStruct((rows, val_count * lanes), jnp.bfloat16)
    return pl.pallas_call(
        functools.partial(prepare_kernel, ka, dims),
        out_shape=[
            in_vmem(screening.shape[1:], screening.dtype),
            in_vmem(table.shape, table.dtype),
            in_vmem((EXTRA_ROWS, lanes), jnp.float32),
        ],
        in_specs=[anywhere] * 8,
        out_specs=[vmem] * 3,
        scratch_shapes=[pltpu.SMEM(x.shape, x.dtype) for x in operands[:5]]
        + [
            pltpu.VMEM(start.shape, start.dtype),
            pltpu.SemaphoreType.DMA((6,)),
            pltpu.SemaphoreType.DMA((2, CHUNKS)),
        ],
        cost_estimate=pl.CostEstimate(
            flops=0, bytes_accessed=4 * screening.size, transcendentals=0
        ),
        compiler_params=limits(table),
        name="prepare",
    )(*[placed(x, pltpu.HBM) for x in operands], after)


def regroup_kernel(ka, val_rows, *refs):
    blocks, (val_all, cond_half) = refs[:ka], refs[-2:]
    cond_rows = blocks[0].shape[0] - val_rows
    for j in range(ka):
        val_all[j * val_rows : (j + 1) * val_rows, :] = blocks[j][:val_rows, :]
        cond_half[j * cond_rows : (j + 1) * cond_rows, :] = blocks[j][val_rows:, :]


def regroup(ka, val_rows, blocks, after):
    rows, width = blocks[0].shape
    kind = blocks[0].dtype
    return pl.pallas_call(
        functools.partial(regroup_kernel, ka, val_rows),
        out_shape=[in_vmem((ka * val_rows, width), kind), in_vmem((ka * (rows - val_rows), width), kind)],
        in_specs=[vmem] * ka + [anywhere],
        out_specs=[vmem] * 2,
        compiler_params=limits(*blocks),
        name="regroup",
    )(*blocks, after)


def screened_block(screening, valence, pairs, place):
    wide = valence[...].astype(jnp.float32)
    parts = []
    for at in range(0, wide.shape[0], 2 * pairs):
        parts += [-wide[at + pairs : at + 2 * pairs], wide[at : at + pairs]]
    turned = jnp.concatenate(parts, 0)
    real = jnp.concatenate([wide, turned], 0).astype(jnp.bfloat16)
    imag = jnp.concatenate([turned, -wide], 0).astype(jnp.bfloat16)
    width = wide.shape[1]
    columns = pl.ds(pl.multiple_of(place * width, 128), width)
    form = (((1,), (1,)), ((), ()))
    return lax.dot_general(
        screening[0, :, columns], real, form, preferred_element_type=jnp.float32
    ) + lax.dot_general(screening[1, :, columns], imag, form, preferred_element_type=jnp.float32)


def near_kernel(pairs, screening, valence, out):
    out[...] = screened_block(screening, valence, pairs, lax.axis_index("ga"))


def near_field(pairs, screening, valence):
    rows, width = valence.shape
    glocal = screening.shape[1]
    return pl.pallas_call(
        functools.partial(near_kernel, pairs),
        out_shape=in_vmem((glocal, 2 * rows), jnp.float32),
        in_specs=[vmem, vmem],
        out_specs=vmem,
        cost_estimate=pl.CostEstimate(
            flops=8 * glocal * width * rows, bytes_accessed=screening.size, transcendentals=0
        ),
        compiler_params=limits(screening, valence),
        name="near_field",
    )(screening, valence)


def project_kernel(ka, ga, dims, *refs):
    val_count, cond_count, npol = dims
    screening, table, extras, near = refs[:4]
    val_in = refs[4 : 4 + ga - 1]
    cond_in, out = refs[-2:]
    mine = lax.axis_index("ga")
    pairs = val_count * val_count
    block = 2 * pairs
    rows = ka * block
    codes = val_count * cond_count
    lanes = 2 * ka * codes
    cond_rows = cond_count * cond_count

    fields = near[...]
    for r in range(1, ga):
        fields = fields + screened_block(screening, val_in[r - 1], pairs, origin(mine, r, ga))
    both = jnp.concatenate(split(fields), 1)
    lane_j = iota((cond_rows, rows), 1) // block
    kernel = jnp.zeros((cond_rows, rows), jnp.float32)
    for start in range(0, ka, TOGETHER):
        end = min(start + TOGETHER, ka)
        cond = cond_in[start * 2 * cond_rows : end * 2 * cond_rows, :]
        crossed = jnp.dot(cond, both, preferred_element_type=jnp.float32)
        crossed = crossed[:, : 2 * rows] + crossed[:, 2 * rows :]
        for j in range(start, end):
            base = (j - start) * 2 * cond_rows
            real = crossed[base : base + cond_rows, :rows]
            imag = crossed[base + cond_rows : base + 2 * cond_rows, rows:]
            kernel = jnp.where(lane_j == j, real - imag, kernel)

    spread = jnp.dot(
        jnp.concatenate(split(kernel), 0), table[...], preferred_element_type=jnp.float32
    )
    spread = spread[:cond_rows] + spread[cond_rows:]
    crow = iota((cond_rows, lanes), 0)
    same_c = crow // cond_count == iota((cond_rows, lanes), 1) % cond_count
    spread = jnp.concatenate(
        [
            jnp.where(same_c, spread[:, v2 * lanes : (v2 + 1) * lanes], 0.0)
            for v2 in range(val_count)
        ],
        0,
    )
    out_row = iota((codes, val_count * cond_rows), 0)
    out_col = iota((codes, val_count * cond_rows), 1)
    fold = (out_row // cond_count == out_col // cond_rows) & (
        out_row % cond_count == out_col % cond_count
    )
    fold = jnp.where(fold, 1.0, 0.0).astype(jnp.bfloat16)
    piece = jnp.dot(fold, jnp.concatenate(split(spread), 1), preferred_element_type=jnp.float32)
    out[:codes, :] = piece[:, :lanes] + piece[:, lanes:]
    out[codes:, :] = extras[...]


def project(ka, ga, dims, screening, table, extras, near, val_far, cond_all):
    val_count, cond_count, npol = dims
    codes = val_count * cond_count
    operands = [screening, table, extras, near, *val_far, cond_all]
    return pl.pallas_call(
        functools.partial(project_kernel, ka, ga, dims),
        out_shape=in_vmem((codes + EXTRA_ROWS, 2 * ka * codes), jnp.float32),
        in_specs=[vmem] * len(operands),
        out_specs=vmem,
        compiler_params=limits(*operands),
        name="project",
    )(*operands)


def haydock_kernel(ka, codes, scale_count, npol, *refs):
    versions = refs[:-3]
    next_out, coef_out, matrix = refs[-3:]
    cores = lax.axis_size("ba")
    gathered = versions[0][...]
    for h in range(cores - 1):
        gathered = jnp.where(lax.axis_index("ba") == h, versions[1 + h][...], gathered)
    lanes = gathered.shape[1]
    mid = lanes // 2
    height = codes + EXTRA_ROWS
    extras = None
    slots = []
    for at in range(0, gathered.shape[0], height):
        rows = gathered[at + codes : at + height]
        extras = rows if extras is None else extras + rows
        slots.append((gathered[at : at + codes], rows[npol + 2 : npol + 3]))
    own = gathered[codes:height]
    sign = jnp.where(iota((1, lanes), 1) < mid, -1.0, 1.0)
    for k2 in range(ka):
        block = jnp.zeros((codes, lanes), jnp.float32)
        for piece, second in slots:
            block = jnp.where(second == float(k2), piece, block)
        matrix[k2 * codes : (k2 + 1) * codes, :] = block
        matrix[mid + k2 * codes : mid + (k2 + 1) * codes, :] = sign * pltpu.roll(block, mid, 1)
    high, low = split(matrix[...])
    full = jnp.concatenate([high, low], 1)
    start = extras[:npol]
    energy = extras[npol : npol + 1]

    def halves(vector):
        top = vector.astype(jnp.bfloat16).astype(jnp.float32)
        return jnp.concatenate([top, vector - top], 0).astype(jnp.bfloat16)

    def mean(values):
        return jnp.sum(values, axis=1, keepdims=True) / scale_count

    def norm(vector):
        return jnp.sqrt(mean(vector * vector) + EPSILON)

    def swap(vector):
        return pltpu.roll(vector, mid, 1)

    def hamiltonian(vector):
        product = jnp.dot(halves(vector), full, preferred_element_type=jnp.float32)
        main = product[:npol, :lanes] + product[npol:, :lanes]
        return energy * vector - (main + product[:npol, lanes:])

    def inner(left, right):
        return mean(left * right), mean(-sign * left * swap(right))

    def times(real, imag, vector):
        return real * vector + imag * (sign * swap(vector))

    start_image = hamiltonian(start)
    scale = 1.0 / norm(start)
    first = start * scale
    first_image = start_image * scale
    alpha_real, alpha_imag = inner(first, first_image)
    first_resid = first_image - times(alpha_real, alpha_imag, first)
    resid_image = hamiltonian(first_resid)
    beta_one = norm(first_resid)
    scale = 1.0 / beta_one
    second = first_resid * scale
    second_image = resid_image * scale
    gamma_real, gamma_imag = inner(second, second_image)
    second_resid = second_image - times(gamma_real, gamma_imag, second) - beta_one * first
    beta_two = norm(second_resid)

    coef_lane = iota(coef_out.shape, 1)
    coefs = jnp.zeros(coef_out.shape, jnp.float32)
    for at, value in enumerate((alpha_real, alpha_imag, gamma_real, gamma_imag, beta_one, beta_two)):
        coefs = jnp.where(coef_lane == at, value, coefs)
    coef_out[...] = coefs
    row = iota((2 * codes, lanes), 0)
    lane = iota((2 * codes, lanes), 1)
    here = (lane % mid // codes == lax.axis_index("ka")) & (lane // mid == row // codes)
    band = (row % codes).astype(jnp.float32)
    pick = jnp.where(here & (own[npol + 1 : npol + 2] == band), 1.0, 0.0).astype(jnp.bfloat16)
    picked = lax.dot_general(
        halves(second_resid), pick, (((1,), (1,)), ((), ())), preferred_element_type=jnp.float32
    )
    picked = (picked[:npol] + picked[npol:]) / beta_two
    next_out[0, :, 0, :] = picked[:, :codes]
    next_out[0, :, 1, :] = picked[:, codes:]


def haydock(ka, codes, scale_count, npol, versions):
    lanes = versions[0].shape[1]
    square = jax.ShapeDtypeStruct((lanes, lanes), jnp.float32)
    return pl.pallas_call(
        functools.partial(haydock_kernel, ka, codes, scale_count, npol),
        out_shape=[
            jax.ShapeDtypeStruct((1, npol, 2, codes), jnp.float32),
            jax.ShapeDtypeStruct((npol, 6), jnp.float32),
        ],
        in_specs=[vmem] * len(versions),
        out_specs=[vmem, vmem],
        scratch_shapes=[pltpu.VMEM(square.shape, square.dtype)],
        compiler_params=limits(*versions, square),
        name="haydock",
    )(*versions)


def summed(value, axis):
    size = lax.axis_size(axis)
    if size & (size - 1):
        return value + sum(shifted(value, axis, step) for step in range(1, size))
    step = 1
    while step < size:
        value = value + exchanged(value, axis, lambda i, size: i ^ step)
        step *= 2
    return value


def local(
    ka,
    ga,
    ba,
    start_vector,
    valence_density,
    conduction_density,
    screening,
    qpoint_map,
    slot_owner,
    band_pairs,
    valence_energy,
    conduction_energy,
):
    npol = start_vector.shape[1]
    pair_count = start_vector.shape[3]
    kcount, val_count = qpoint_map.shape[0], valence_density.shape[4]
    cond_count = conduction_density.shape[3]
    pairs = val_count * val_count
    dims = (val_count, cond_count, npol)
    last = ba - 1
    received = [handed(valence_density, last - h) for h in range(last)]
    own, cond, chosen = sort(ka, qpoint_map, slot_owner, valence_density, conduction_density)
    packed = merge(ka, own, cond, chosen, received)
    blocks = [packed[0]] + [shifted(packed[j], "ka", j) for j in range(1, ka)]
    whole, table, extras = prepare(
        ka,
        dims,
        qpoint_map,
        slot_owner,
        band_pairs,
        valence_energy,
        conduction_energy,
        start_vector,
        screening,
        packed[0],
    )
    val_all, cond_all = regroup(ka, 2 * pairs, blocks, extras)
    val_far = [shifted(val_all, "ga", r) for r in range(1, ga)]
    near = near_field(pairs, whole, val_all)
    piece = project(ka, ga, dims, whole, table, extras, near, val_far, cond_all)
    piece = summed(piece, "ga")
    pieces = [piece] + [shifted(piece, "ka", j) for j in range(1, ka)]
    gathered = jnp.concatenate(pieces, 0)
    versions = [gathered] + [handed(gathered, h + 1) for h in range(last)]
    scale_count = float(kcount * pair_count)
    return tuple(haydock(ka, pair_count, scale_count, npol, versions))


def solution(mesh):
    in_specs = (
        P(("grp", "ka"), None, None, None),
        P(("grp", "ka"), None, None, "ba", None, "ga"),
        P(("grp", "ka"), None, None, None, None, "ga"),
        P(("grp", "ka"), None, "ga", None),
        P(),
        P(),
        P(),
        P(("grp", "ka"), None),
        P(("grp", "ka"), None),
    )
    out_specs = (P(("grp", "ka"), None, None, None), P("grp", None))
    body = functools.partial(local, mesh.shape["ka"], mesh.shape["ga"], mesh.shape["ba"])
    return jax.shard_map(body, mesh=mesh, in_specs=in_specs, out_specs=out_specs, check_vma=False)
```

```python
import functools
import math

import jax
import jax.numpy as jnp
from jax import lax
from jax.experimental import pallas as pl
from jax.experimental.pallas import tpu as pltpu
from jax.sharding import PartitionSpec as P

EPSILON = 1e-06
EXACT = lax.Precision.HIGHEST
VMEM_LEAST = 8 * 1024 * 1024
VMEM_MOST = 56 * 1024 * 1024

vmem = pl.BlockSpec(memory_space=pltpu.VMEM)
anywhere = pl.BlockSpec(memory_space=pl.ANY)
EXTRA_ROWS = 8
CHUNKS = 4


def in_vmem(shape, dtype):
    return pltpu.VMEM(shape, dtype)


def placed(value, space):
    return pltpu.with_memory_space_constraint(value, space)


def iota(shape, axis):
    return lax.broadcasted_iota(jnp.int32, shape, axis)


def split(values):
    high = values.astype(jnp.bfloat16)
    low = (values - high.astype(jnp.float32)).astype(jnp.bfloat16)
    return high, low


def limits(*arrays):
    held = sum(math.prod(a.shape) * a.dtype.itemsize for a in arrays)
    return pltpu.CompilerParams(vmem_limit_bytes=min(VMEM_MOST, VMEM_LEAST + 4 * held))


def target(me, step, size):
    return lax.rem(me + step, size)


def origin(me, step, size):
    return lax.rem(me + size - step, size)


def exchanged(value, axis, move):
    size, cores = lax.axis_size(axis), lax.axis_size("ba")
    pairs = [
        (i * cores + h, move(i, size) * cores + (h + 1) % cores)
        for i in range(size)
        for h in range(cores)
    ]
    return lax.ppermute(value, (axis, "ba"), pairs)


def shifted(value, axis, step):
    return exchanged(value, axis, lambda i, size: (i + step) % size)


def handed(value, step):
    size = lax.axis_size("ba")
    return lax.ppermute(value, "ba", [(h, (h + step) % size) for h in range(size)])


def pack_kernel(ka, qmap_in, owner_in, valence_in, conduction_in, *rest):
    outs = rest[:ka]
    qmap, owner, partner, valence, conduction, sems = rest[ka:]
    copies = [
        pltpu.make_async_copy(src, dst, sems.at[at])
        for at, (src, dst) in enumerate(
            ((qmap_in, qmap), (owner_in, owner), (valence_in, valence), (conduction_in, conduction))
        )
    ]
    for copy in copies:
        copy.start()
    me = lax.axis_index("ka")
    half = lax.axis_index("ba")
    count, width = valence.shape[1], valence.shape[5]
    cond_count = conduction.shape[3]
    share = cond_count // lax.axis_size("ba")
    val_rows = 2 * valence.shape[3] * valence.shape[4]
    cond_rows = 2 * share * cond_count

    def note(k2, carry):
        partner[owner[qmap[me, k2]]] = k2
        return carry

    copies[0].wait()
    copies[1].wait()
    lax.fori_loop(0, count, note, 0)
    copies[2].wait()
    copies[3].wait()
    for at in range(ka):
        k2 = partner[target(me, at, ka)]
        block = valence[0, k2].astype(jnp.float32).reshape(val_rows, width)
        outs[at][:val_rows, :] = block.astype(jnp.bfloat16)
        to = lax.rem(half + min(at, 1), lax.axis_size("ba"))
        block = conduction[0, k2, :, pl.ds(to * share, share)].astype(jnp.float32)
        outs[at][val_rows:, :] = block.reshape(cond_rows, width).astype(jnp.bfloat16)


def pack(ka, ba, qmap, owner, valence, conduction):
    cond_count = conduction.shape[3]
    rows = 2 * valence.shape[3] * valence.shape[4] + 2 * cond_count // ba * cond_count
    shape = in_vmem((rows, valence.shape[5]), valence.dtype)
    operands = [placed(x, pltpu.HBM) for x in (qmap, owner, valence, conduction)]
    return pl.pallas_call(
        functools.partial(pack_kernel, ka),
        out_shape=[shape] * ka,
        in_specs=[anywhere] * 4,
        out_specs=[vmem] * ka,
        scratch_shapes=[
            pltpu.SMEM(qmap.shape, jnp.int32),
            pltpu.SMEM(owner.shape, jnp.int32),
            pltpu.SMEM(owner.shape, jnp.int32),
            pltpu.VMEM(valence.shape, valence.dtype),
            pltpu.VMEM(conduction.shape, conduction.dtype),
            pltpu.SemaphoreType.DMA((4,)),
        ],
        compiler_params=limits(valence, conduction),
        name="pack",
    )(*operands)


def prepare_kernel(ka, dims, *refs):
    vloc, val_count, cond_count, npol = dims
    ins, screening, (screen_out, near_table, far_table, extras), scratch = refs[:6], refs[6], refs[8:12], refs[12:]
    qmap, owner, band_pairs, val_energy, cond_energy, start, sems, screen_sems = scratch
    me = lax.axis_index("ka")
    half = lax.axis_index("ba")
    mine = lax.axis_index("ga")
    copies = [
        pltpu.make_async_copy(src, dst, sems.at[at])
        for at, (src, dst) in enumerate(
            zip(ins, (qmap, owner, band_pairs, val_energy, cond_energy, start))
        )
    ]
    height = screening.shape[2] // CHUNKS
    chunks = [
        pltpu.make_async_copy(
            screening.at[0, part, pl.ds(c * height, height)],
            screen_out.at[part, pl.ds(c * height, height)],
            screen_sems.at[part, c],
        )
        for part in range(2)
        for c in range(CHUNKS)
    ]
    for copy in copies + chunks:
        copy.start()
    pairs = vloc * val_count
    block = 2 * pairs
    rows = ka * block
    codes = val_count * cond_count
    mid = ka * codes
    lanes = 2 * mid
    row = iota((2 * rows, lanes), 0)
    col = iota((2 * rows, lanes), 1)
    j_of_row = row % rows // block
    cores = lax.axis_size("ba")
    for moves, table in enumerate((near_table, far_table)):
        share = lax.rem(half + 2 * cores - moves - jnp.where(j_of_row == 0, 0, 1), cores)
        want = (
            (row % block // pairs) * mid
            + origin(me, j_of_row, ka) * codes
            + (share * vloc + row % pairs // val_count) * cond_count
        )
        joined = (col - want >= 0) & (col - want < cond_count)
        for v2 in range(val_count):
            pick = jnp.where(joined & (row % val_count == v2), 1.0, 0.0)
            table[:, v2 * lanes : (v2 + 1) * lanes] = pick.astype(jnp.bfloat16)

    for copy in copies:
        copy.wait()
    first = jnp.where((mine == 0) & (half == 0), 1.0, 0.0)
    lane = iota((1, lanes), 1)
    lane_k = lane % mid // codes
    band_row = iota((codes, lanes), 0)
    band_lane = iota((codes, lanes), 1)
    code = jnp.zeros((codes, lanes), jnp.int32)
    bands = jnp.full((1, lanes), -1.0, jnp.float32)
    for b in range(codes):
        code = jnp.where(band_row == b, band_pairs[b], code)
        bands = jnp.where(lane % codes == band_pairs[b], float(b), bands)
    vectors = jnp.zeros((npol, lanes), jnp.float32)
    for part in range(2):
        spot = part * mid + me * codes
        pick = jnp.where(band_lane == spot + code, first, 0.0)
        vectors = vectors + jnp.dot(start[0, :, part, :], pick, precision=EXACT)
    energy = jnp.zeros((1, lanes), jnp.float32)
    for c in range(cond_count):
        energy = jnp.where(lane % cond_count == c, cond_energy[0, c], energy)
    for v in range(val_count):
        energy = energy - jnp.where(lane % codes // cond_count == v, val_energy[0, v], 0.0)
    energy = jnp.where(lane_k == me, energy * first, 0.0)
    kcount = qmap.shape[0]

    def find(k2, found):
        return jnp.where(owner[qmap[0, k2]] == me, k2, found)

    back = lax.fori_loop(0, kcount, find, 0)
    second = lane_k + back
    second = jnp.where(second >= kcount, second - kcount, second).astype(jnp.float32) * first
    rest = jnp.zeros((EXTRA_ROWS - 3 - npol, lanes), jnp.float32)
    extras[...] = jnp.concatenate([vectors, energy, bands * first, second, rest], 0)
    for copy in chunks:
        copy.wait()


def prepare(ka, dims, qmap, owner, band_pairs, val_energy, cond_energy, start, screening, after):
    vloc, val_count, cond_count, npol = dims
    rows = 4 * ka * vloc * val_count
    lanes = 2 * ka * val_count * cond_count
    operands = (qmap, owner, band_pairs, val_energy, cond_energy, start, screening)
    table = jax.ShapeDtypeStruct((rows, val_count * lanes), jnp.bfloat16)
    return pl.pallas_call(
        functools.partial(prepare_kernel, ka, dims),
        out_shape=[
            in_vmem(screening.shape[1:], screening.dtype),
            in_vmem(table.shape, table.dtype),
            in_vmem(table.shape, table.dtype),
            in_vmem((EXTRA_ROWS, lanes), jnp.float32),
        ],
        in_specs=[anywhere] * 8,
        out_specs=[vmem] * 4,
        scratch_shapes=[pltpu.SMEM(x.shape, x.dtype) for x in operands[:5]]
        + [
            pltpu.VMEM(start.shape, start.dtype),
            pltpu.SemaphoreType.DMA((6,)),
            pltpu.SemaphoreType.DMA((2, CHUNKS)),
        ],
        cost_estimate=pl.CostEstimate(
            flops=0, bytes_accessed=4 * screening.size, transcendentals=0
        ),
        compiler_params=limits(table),
        name="prepare",
    )(*[placed(x, pltpu.HBM) for x in operands], after)


def regroup_kernel(ka, val_rows, *refs):
    blocks, (val_all, cond_half) = refs[:ka], refs[-2:]
    cond_rows = blocks[0].shape[0] - val_rows
    for j in range(ka):
        val_all[j * val_rows : (j + 1) * val_rows, :] = blocks[j][:val_rows, :]
        cond_half[j * cond_rows : (j + 1) * cond_rows, :] = blocks[j][val_rows:, :]


def regroup(ka, val_rows, blocks, after):
    rows, width = blocks[0].shape
    kind = blocks[0].dtype
    return pl.pallas_call(
        functools.partial(regroup_kernel, ka, val_rows),
        out_shape=[in_vmem((ka * val_rows, width), kind), in_vmem((ka * (rows - val_rows), width), kind)],
        in_specs=[vmem] * ka + [anywhere],
        out_specs=[vmem] * 2,
        compiler_params=limits(*blocks),
        name="regroup",
    )(*blocks, after)


def screened_block(screening, valence, pairs, place):
    wide = valence[...].astype(jnp.float32)
    parts = []
    for at in range(0, wide.shape[0], 2 * pairs):
        parts += [-wide[at + pairs : at + 2 * pairs], wide[at : at + pairs]]
    turned = jnp.concatenate(parts, 0)
    real = jnp.concatenate([wide, turned], 0).astype(jnp.bfloat16)
    imag = jnp.concatenate([turned, -wide], 0).astype(jnp.bfloat16)
    width = wide.shape[1]
    columns = pl.ds(pl.multiple_of(place * width, 128), width)
    form = (((1,), (1,)), ((), ()))
    return lax.dot_general(
        screening[0, :, columns], real, form, preferred_element_type=jnp.float32
    ) + lax.dot_general(screening[1, :, columns], imag, form, preferred_element_type=jnp.float32)


def project_kernel(ka, ba, far, dims, *refs):
    vloc, val_count, cond_count, npol = dims
    screening, table, held = refs[:3]
    val_in, cond_in, out = refs[3 : -1 - ba], refs[-1 - ba : -1], refs[-1]
    ga = lax.axis_size("ga")
    mine = lax.axis_index("ga")
    half = lax.axis_index("ba")
    pairs = vloc * val_count
    block = 2 * pairs
    rows = ka * block
    codes = val_count * cond_count
    lanes = 2 * ka * codes
    share = cond_count // ba
    cond_rows = cond_count * cond_count
    share_rows = share * cond_count

    fields = None
    for r, valence in enumerate(val_in, far):
        term = screened_block(screening, valence, pairs, origin(mine, r, ga))
        fields = term if fields is None else fields + term
    both = jnp.concatenate(split(fields), 1)
    cond_all = jnp.concatenate([ref[...] for ref in cond_in], 0)
    crossed = jnp.dot(cond_all, both, preferred_element_type=jnp.float32)
    crossed = crossed[:, : 2 * rows] + crossed[:, 2 * rows :]
    lane = iota((share_rows, 2 * rows), 1)
    lane_j = lane % rows // block
    turned_lane = lane // rows
    kernel = []
    for h in range(ba):
        total = jnp.zeros((share_rows, 2 * rows), jnp.float32)
        for j in range(ka):
            base = (h * ka + j) * 2 * share_rows
            real = crossed[base : base + share_rows]
            imag = crossed[base + share_rows : base + 2 * share_rows]
            value = jnp.where(turned_lane == 0, real, -imag)
            total = jnp.where(lane_j == j, value, total)
        kernel.append(total)
    kernel = jnp.concatenate(kernel, 0)

    spread = jnp.dot(
        jnp.concatenate(split(kernel), 0), table[...], preferred_element_type=jnp.float32
    )
    spread = spread[:cond_rows] + spread[cond_rows:]
    crow = iota((cond_rows, lanes), 0)
    c_of_row = origin(half, crow // share_rows, ba) * share + crow % share_rows // cond_count
    same_c = c_of_row == iota((cond_rows, lanes), 1) % cond_count
    spread = jnp.concatenate(
        [
            jnp.where(same_c, spread[:, v2 * lanes : (v2 + 1) * lanes], 0.0)
            for v2 in range(val_count)
        ],
        0,
    )
    out_row = iota((codes, val_count * cond_rows), 0)
    out_col = iota((codes, val_count * cond_rows), 1)
    fold = (out_row // cond_count == out_col // cond_rows) & (
        out_row % cond_count == out_col % cond_count
    )
    fold = jnp.where(fold, 1.0, 0.0).astype(jnp.bfloat16)
    piece = jnp.dot(fold, jnp.concatenate(split(spread), 1), preferred_element_type=jnp.float32)
    piece = piece[:, :lanes] + piece[:, lanes:]
    out[:codes, :] = piece + held[:codes, :] if far else piece
    out[codes:, :] = held[codes:, :] if far else held[...]


def project(ka, ba, far, dims, screening, table, base, val_in, cond_all):
    vloc, val_count, cond_count, npol = dims
    codes = val_count * cond_count
    operands = [screening, table, base, *val_in, *cond_all]
    rows, width = val_in[0].shape
    return pl.pallas_call(
        functools.partial(project_kernel, ka, ba, far, dims),
        out_shape=in_vmem((codes + EXTRA_ROWS, 2 * ka * codes), jnp.float32),
        in_specs=[vmem] * len(operands),
        out_specs=vmem,
        cost_estimate=pl.CostEstimate(
            flops=8 * screening.shape[1] * width * rows, bytes_accessed=screening.size, transcendentals=0
        ),
        compiler_params=limits(*operands),
        name="project_far" if far else "project_near",
    )(*operands)


def haydock_kernel(ka, codes, scale_count, npol, *refs):
    pieces = refs[:-3]
    next_out, coef_out, matrix = refs[-3:]
    lanes = pieces[0].shape[1]
    mid = lanes // 2
    height = codes + EXTRA_ROWS
    found = [(ref, at) for ref in pieces for at in range(0, ref.shape[0], height)]
    extras = None
    slots = []
    for ref, at in found:
        rows = ref[at + codes : at + height, :]
        extras = rows if extras is None else extras + rows
        slots.append((ref[at : at + codes, :], rows[npol + 2 : npol + 3]))
    own = pieces[0][codes:height, :]
    sign = jnp.where(iota((1, lanes), 1) < mid, -1.0, 1.0)
    for k2 in range(ka):
        block = jnp.zeros((codes, lanes), jnp.float32)
        for piece, second in slots:
            block = jnp.where(second == float(k2), piece, block)
        matrix[k2 * codes : (k2 + 1) * codes, :] = block
        matrix[mid + k2 * codes : mid + (k2 + 1) * codes, :] = sign * pltpu.roll(block, mid, 1)
    high, low = split(matrix[...])
    full = jnp.concatenate([high, low], 1)
    start = extras[:npol]
    energy = extras[npol : npol + 1]

    def halves(vector):
        top = vector.astype(jnp.bfloat16).astype(jnp.float32)
        return jnp.concatenate([top, vector - top], 0).astype(jnp.bfloat16)

    def mean(values):
        return jnp.sum(values, axis=1, keepdims=True) / scale_count

    def norm(vector):
        return jnp.sqrt(mean(vector * vector) + EPSILON)

    def swap(vector):
        return pltpu.roll(vector, mid, 1)

    def hamiltonian(vector):
        product = jnp.dot(halves(vector), full, preferred_element_type=jnp.float32)
        main = product[:npol, :lanes] + product[npol:, :lanes]
        return energy * vector - (main + product[:npol, lanes:])

    def inner(left, right):
        return mean(left * right), mean(-sign * left * swap(right))

    def times(real, imag, vector):
        return real * vector + imag * (sign * swap(vector))

    start_image = hamiltonian(start)
    scale = 1.0 / norm(start)
    first = start * scale
    first_image = start_image * scale
    alpha_real, alpha_imag = inner(first, first_image)
    first_resid = first_image - times(alpha_real, alpha_imag, first)
    resid_image = hamiltonian(first_resid)
    beta_one = norm(first_resid)
    scale = 1.0 / beta_one
    second = first_resid * scale
    second_image = resid_image * scale
    gamma_real, gamma_imag = inner(second, second_image)
    second_resid = second_image - times(gamma_real, gamma_imag, second) - beta_one * first
    beta_two = norm(second_resid)

    coef_lane = iota(coef_out.shape, 1)
    coefs = jnp.zeros(coef_out.shape, jnp.float32)
    for at, value in enumerate((alpha_real, alpha_imag, gamma_real, gamma_imag, beta_one, beta_two)):
        coefs = jnp.where(coef_lane == at, value, coefs)
    coef_out[...] = coefs
    row = iota((2 * codes, lanes), 0)
    lane = iota((2 * codes, lanes), 1)
    here = (lane % mid // codes == lax.axis_index("ka")) & (lane // mid == row // codes)
    band = (row % codes).astype(jnp.float32)
    pick = jnp.where(here & (own[npol + 1 : npol + 2] == band), 1.0, 0.0).astype(jnp.bfloat16)
    picked = lax.dot_general(
        halves(second_resid), pick, (((1,), (1,)), ((), ())), preferred_element_type=jnp.float32
    )
    picked = (picked[:npol] + picked[npol:]) / beta_two
    next_out[0, :, 0, :] = picked[:, :codes]
    next_out[0, :, 1, :] = picked[:, codes:]


def haydock(ka, codes, scale_count, npol, pieces):
    lanes = pieces[0].shape[1]
    square = jax.ShapeDtypeStruct((lanes, lanes), jnp.float32)
    return pl.pallas_call(
        functools.partial(haydock_kernel, ka, codes, scale_count, npol),
        out_shape=[
            jax.ShapeDtypeStruct((1, npol, 2, codes), jnp.float32),
            jax.ShapeDtypeStruct((npol, 6), jnp.float32),
        ],
        in_specs=[vmem] * len(pieces),
        out_specs=[vmem, vmem],
        scratch_shapes=[pltpu.VMEM(square.shape, square.dtype)],
        compiler_params=limits(*pieces, square),
        name="haydock",
    )(*pieces)


def summed(value, axis):
    size = lax.axis_size(axis)
    if size & (size - 1):
        return value + sum(shifted(value, axis, step) for step in range(1, size))
    step = 1
    while step < size:
        value = value + exchanged(value, axis, lambda i, size: i ^ step)
        step *= 2
    return value


def local(
    ka,
    ga,
    ba,
    start_vector,
    valence_density,
    conduction_density,
    screening,
    qpoint_map,
    slot_owner,
    band_pairs,
    valence_energy,
    conduction_energy,
):
    npol = start_vector.shape[1]
    pair_count = start_vector.shape[3]
    kcount, vloc, val_count = qpoint_map.shape[0], valence_density.shape[3], valence_density.shape[4]
    cond_count = conduction_density.shape[3]
    pairs = vloc * val_count
    dims = (vloc, val_count, cond_count, npol)
    packed = pack(ka, ba, qpoint_map, slot_owner, valence_density, conduction_density)
    blocks = [packed[0]] + [shifted(packed[j], "ka", j) for j in range(1, ka)]
    whole, near_table, far_table, extras = prepare(
        ka,
        dims,
        qpoint_map,
        slot_owner,
        band_pairs,
        valence_energy,
        conduction_energy,
        start_vector,
        screening,
        packed[0],
    )
    val_all, cond_half = regroup(ka, 2 * pairs, blocks, extras)
    val_far = [shifted(val_all, "ga", r) for r in range(1, ga)]
    cond_all = [cond_half] + [handed(cond_half, r) for r in range(1, ba)]
    piece = project(ka, ba, 0, dims, whole, near_table, extras, [val_all], cond_all)
    if val_far:
        piece = project(ka, ba, 1, dims, whole, far_table, piece, val_far, cond_all)
    piece = piece + sum(handed(piece, r) for r in range(1, ba))
    piece = summed(piece, "ga")
    pieces = [piece] + [shifted(piece, "ka", j) for j in range(1, ka)]
    scale_count = float(kcount * pair_count)
    return tuple(haydock(ka, pair_count, scale_count, npol, pieces))


def solution(mesh):
    in_specs = (
        P(("grp", "ka"), None, None, None),
        P(("grp", "ka"), None, None, "ba", None, "ga"),
        P(("grp", "ka"), None, None, None, None, "ga"),
        P(("grp", "ka"), None, "ga", None),
        P(),
        P(),
        P(),
        P(("grp", "ka"), None),
        P(("grp", "ka"), None),
    )
    out_specs = (P(("grp", "ka"), None, None, None), P("grp", None))
    body = functools.partial(local, mesh.shape["ka"], mesh.shape["ga"], mesh.shape["ba"])
    return jax.shard_map(body, mesh=mesh, in_specs=in_specs, out_specs=out_specs, check_vma=False)
```

```python
import functools
import math

import jax
import jax.numpy as jnp
from jax import lax
from jax.experimental import pallas as pl
from jax.experimental.pallas import tpu as pltpu
from jax.sharding import PartitionSpec as P

EPSILON = 1e-06
EXACT = lax.Precision.HIGHEST
VMEM_LEAST = 8 * 1024 * 1024
VMEM_MOST = 56 * 1024 * 1024

vmem = pl.BlockSpec(memory_space=pltpu.VMEM)
anywhere = pl.BlockSpec(memory_space=pl.ANY)
EXTRA_ROWS = 8
CHUNKS = 4


def in_vmem(shape, dtype):
    return pltpu.VMEM(shape, dtype)


def placed(value, space):
    return pltpu.with_memory_space_constraint(value, space)


def iota(shape, axis):
    return lax.broadcasted_iota(jnp.int32, shape, axis)


def split(values):
    high = values.astype(jnp.bfloat16)
    low = (values - high.astype(jnp.float32)).astype(jnp.bfloat16)
    return high, low


def limits(*arrays):
    held = sum(math.prod(a.shape) * a.dtype.itemsize for a in arrays)
    return pltpu.CompilerParams(vmem_limit_bytes=min(VMEM_MOST, VMEM_LEAST + 4 * held))


def target(me, step, size):
    return lax.rem(me + step, size)


def origin(me, step, size):
    return lax.rem(me + size - step, size)


def exchanged(value, axis, move):
    size, cores = lax.axis_size(axis), lax.axis_size("ba")
    pairs = [
        (i * cores + h, move(i, size) * cores + (h + 1) % cores)
        for i in range(size)
        for h in range(cores)
    ]
    return lax.ppermute(value, (axis, "ba"), pairs)


def shifted(value, axis, step):
    return exchanged(value, axis, lambda i, size: (i + step) % size)


def handed(value, step):
    size = lax.axis_size("ba")
    return lax.ppermute(value, "ba", [(h, (h + step) % size) for h in range(size)])


def pack_kernel(ka, qmap_in, owner_in, valence_in, conduction_in, *rest):
    outs = rest[:ka]
    qmap, owner, partner, valence, conduction, sems = rest[ka:]
    copies = [
        pltpu.make_async_copy(src, dst, sems.at[at])
        for at, (src, dst) in enumerate(
            ((qmap_in, qmap), (owner_in, owner), (valence_in, valence), (conduction_in, conduction))
        )
    ]
    for copy in copies:
        copy.start()
    me = lax.axis_index("ka")
    half = lax.axis_index("ba")
    count, width = valence.shape[1], valence.shape[5]
    cond_count = conduction.shape[3]
    share = cond_count // lax.axis_size("ba")
    val_rows = 2 * valence.shape[3] * valence.shape[4]
    cond_rows = 2 * share * cond_count

    def note(k2, carry):
        partner[owner[qmap[me, k2]]] = k2
        return carry

    copies[0].wait()
    copies[1].wait()
    lax.fori_loop(0, count, note, 0)
    copies[2].wait()
    copies[3].wait()
    for at in range(ka):
        k2 = partner[target(me, at, ka)]
        block = valence[0, k2].astype(jnp.float32).reshape(val_rows, width)
        outs[at][:val_rows, :] = block.astype(jnp.bfloat16)
        to = lax.rem(half + min(at, 1), lax.axis_size("ba"))
        block = conduction[0, k2, :, pl.ds(to * share, share)].astype(jnp.float32)
        outs[at][val_rows:, :] = block.reshape(cond_rows, width).astype(jnp.bfloat16)


def pack(ka, ba, qmap, owner, valence, conduction):
    cond_count = conduction.shape[3]
    rows = 2 * valence.shape[3] * valence.shape[4] + 2 * cond_count // ba * cond_count
    shape = in_vmem((rows, valence.shape[5]), valence.dtype)
    operands = [placed(x, pltpu.HBM) for x in (qmap, owner, valence, conduction)]
    return pl.pallas_call(
        functools.partial(pack_kernel, ka),
        out_shape=[shape] * ka,
        in_specs=[anywhere] * 4,
        out_specs=[vmem] * ka,
        scratch_shapes=[
            pltpu.SMEM(qmap.shape, jnp.int32),
            pltpu.SMEM(owner.shape, jnp.int32),
            pltpu.SMEM(owner.shape, jnp.int32),
            pltpu.VMEM(valence.shape, valence.dtype),
            pltpu.VMEM(conduction.shape, conduction.dtype),
            pltpu.SemaphoreType.DMA((4,)),
        ],
        compiler_params=limits(valence, conduction),
        name="pack",
    )(*operands)


def prepare_kernel(ka, dims, *refs):
    vloc, val_count, cond_count, npol = dims
    ins, screening, (screen_out, near_table, far_table, extras), scratch = refs[:6], refs[6], refs[8:12], refs[12:]
    qmap, owner, band_pairs, val_energy, cond_energy, start, sems, screen_sems = scratch
    me = lax.axis_index("ka")
    half = lax.axis_index("ba")
    mine = lax.axis_index("ga")
    copies = [
        pltpu.make_async_copy(src, dst, sems.at[at])
        for at, (src, dst) in enumerate(
            zip(ins, (qmap, owner, band_pairs, val_energy, cond_energy, start))
        )
    ]
    height = screening.shape[2] // CHUNKS
    chunks = [
        pltpu.make_async_copy(
            screening.at[0, part, pl.ds(c * height, height)],
            screen_out.at[part, pl.ds(c * height, height)],
            screen_sems.at[part, c],
        )
        for part in range(2)
        for c in range(CHUNKS)
    ]
    for copy in copies + chunks:
        copy.start()
    pairs = vloc * val_count
    block = 2 * pairs
    rows = ka * block
    codes = val_count * cond_count
    mid = ka * codes
    lanes = 2 * mid
    row = iota((2 * rows, lanes), 0)
    col = iota((2 * rows, lanes), 1)
    j_of_row = row % rows // block
    cores = lax.axis_size("ba")
    for moves, table in enumerate((near_table, far_table)):
        share = lax.rem(half + 2 * cores - moves - jnp.where(j_of_row == 0, 0, 1), cores)
        want = (
            (row % block // pairs) * mid
            + origin(me, j_of_row, ka) * codes
            + (share * vloc + row % pairs // val_count) * cond_count
        )
        joined = (col - want >= 0) & (col - want < cond_count)
        for v2 in range(val_count):
            pick = jnp.where(joined & (row % val_count == v2), 1.0, 0.0)
            table[:, v2 * lanes : (v2 + 1) * lanes] = pick.astype(jnp.bfloat16)

    for copy in copies:
        copy.wait()
    first = jnp.where((mine == 0) & (half == 0), 1.0, 0.0)
    lane = iota((1, lanes), 1)
    lane_k = lane % mid // codes
    band_row = iota((codes, lanes), 0)
    band_lane = iota((codes, lanes), 1)
    code = jnp.zeros((codes, lanes), jnp.int32)
    bands = jnp.full((1, lanes), -1.0, jnp.float32)
    for b in range(codes):
        code = jnp.where(band_row == b, band_pairs[b], code)
        bands = jnp.where(lane % codes == band_pairs[b], float(b), bands)
    vectors = jnp.zeros((npol, lanes), jnp.float32)
    for part in range(2):
        spot = part * mid + me * codes
        pick = jnp.where(band_lane == spot + code, first, 0.0)
        vectors = vectors + jnp.dot(start[0, :, part, :], pick, precision=EXACT)
    energy = jnp.zeros((1, lanes), jnp.float32)
    for c in range(cond_count):
        energy = jnp.where(lane % cond_count == c, cond_energy[0, c], energy)
    for v in range(val_count):
        energy = energy - jnp.where(lane % codes // cond_count == v, val_energy[0, v], 0.0)
    energy = jnp.where(lane_k == me, energy * first, 0.0)
    kcount = qmap.shape[0]

    def find(k2, found):
        return jnp.where(owner[qmap[0, k2]] == me, k2, found)

    back = lax.fori_loop(0, kcount, find, 0)
    second = lane_k + back
    second = jnp.where(second >= kcount, second - kcount, second).astype(jnp.float32) * first
    rest = jnp.zeros((EXTRA_ROWS - 3 - npol, lanes), jnp.float32)
    extras[...] = jnp.concatenate([vectors, energy, bands * first, second, rest], 0)
    for copy in chunks:
        copy.wait()


def prepare(ka, dims, qmap, owner, band_pairs, val_energy, cond_energy, start, screening, after):
    vloc, val_count, cond_count, npol = dims
    rows = 4 * ka * vloc * val_count
    lanes = 2 * ka * val_count * cond_count
    operands = (qmap, owner, band_pairs, val_energy, cond_energy, start, screening)
    table = jax.ShapeDtypeStruct((rows, val_count * lanes), jnp.bfloat16)
    return pl.pallas_call(
        functools.partial(prepare_kernel, ka, dims),
        out_shape=[
            in_vmem(screening.shape[1:], screening.dtype),
            in_vmem(table.shape, table.dtype),
            in_vmem(table.shape, table.dtype),
            in_vmem((EXTRA_ROWS, lanes), jnp.float32),
        ],
        in_specs=[anywhere] * 8,
        out_specs=[vmem] * 4,
        scratch_shapes=[pltpu.SMEM(x.shape, x.dtype) for x in operands[:5]]
        + [
            pltpu.VMEM(start.shape, start.dtype),
            pltpu.SemaphoreType.DMA((6,)),
            pltpu.SemaphoreType.DMA((2, CHUNKS)),
        ],
        cost_estimate=pl.CostEstimate(
            flops=0, bytes_accessed=4 * screening.size, transcendentals=0
        ),
        compiler_params=limits(table),
        name="prepare",
    )(*[placed(x, pltpu.HBM) for x in operands], after)


def regroup_kernel(ka, val_rows, *refs):
    blocks, (val_all, cond_half) = refs[:ka], refs[-2:]
    cond_rows = blocks[0].shape[0] - val_rows
    for j in range(ka):
        val_all[j * val_rows : (j + 1) * val_rows, :] = blocks[j][:val_rows, :]
        cond_half[j * cond_rows : (j + 1) * cond_rows, :] = blocks[j][val_rows:, :]


def regroup(ka, val_rows, blocks, after):
    rows, width = blocks[0].shape
    kind = blocks[0].dtype
    return pl.pallas_call(
        functools.partial(regroup_kernel, ka, val_rows),
        out_shape=[in_vmem((ka * val_rows, width), kind), in_vmem((ka * (rows - val_rows), width), kind)],
        in_specs=[vmem] * ka + [anywhere],
        out_specs=[vmem] * 2,
        compiler_params=limits(*blocks),
        name="regroup",
    )(*blocks, after)


def with_turned(valence, pairs):
    wide = valence[...].astype(jnp.float32)
    parts = []
    for at in range(0, wide.shape[0], 2 * pairs):
        parts += [-wide[at + pairs : at + 2 * pairs], wide[at : at + pairs]]
    return wide, jnp.concatenate(parts, 0)


def columns_of(place, width):
    return pl.ds(pl.multiple_of(place * width, 128), width)


def placed_piece(kernel, table, dims, ba):
    vloc, val_count, cond_count, npol = dims
    half = lax.axis_index("ba")
    codes = val_count * cond_count
    lanes = table.shape[1] // val_count
    share = cond_count // ba
    cond_rows = cond_count * cond_count
    spread = jnp.dot(
        jnp.concatenate(split(kernel), 0), table[...], preferred_element_type=jnp.float32
    )
    spread = spread[:cond_rows] + spread[cond_rows:]
    crow = iota((cond_rows, lanes), 0)
    share_rows = share * cond_count
    c_of_row = origin(half, crow // share_rows, ba) * share + crow % share_rows // cond_count
    same_c = c_of_row == iota((cond_rows, lanes), 1) % cond_count
    spread = jnp.concatenate(
        [
            jnp.where(same_c, spread[:, v2 * lanes : (v2 + 1) * lanes], 0.0)
            for v2 in range(val_count)
        ],
        0,
    )
    out_row = iota((codes, val_count * cond_rows), 0)
    out_col = iota((codes, val_count * cond_rows), 1)
    fold = (out_row // cond_count == out_col // cond_rows) & (
        out_row % cond_count == out_col % cond_count
    )
    fold = jnp.where(fold, 1.0, 0.0).astype(jnp.bfloat16)
    piece = jnp.dot(fold, jnp.concatenate(split(spread), 1), preferred_element_type=jnp.float32)
    return piece[:, :lanes] + piece[:, lanes:]


def diagonal(crossed, ka, ba, share_rows, sign):
    rows = crossed.shape[1] // 2
    lane = iota((share_rows, 2 * rows), 1)
    lane_j = lane % rows // (rows // ka)
    straight = lane < rows
    kernel = []
    for h in range(ba):
        total = jnp.zeros((share_rows, 2 * rows), jnp.float32)
        for j in range(ka):
            at = (h * ka + j) * 2 * share_rows
            real = crossed[at : at + share_rows]
            imag = crossed[at + share_rows : at + 2 * share_rows]
            total = jnp.where(lane_j == j, jnp.where(straight, real, sign * imag), total)
        kernel.append(total)
    return jnp.concatenate(kernel, 0)


def near_kernel(ka, ba, dims, *refs):
    vloc, val_count, cond_count, npol = dims
    screening, table, extras, valence = refs[:4]
    cond_in, out = refs[4 : 4 + ba], refs[-1]
    codes = val_count * cond_count
    columns = columns_of(lax.axis_index("ga"), valence.shape[1])
    wide, turned = with_turned(valence, vloc * val_count)
    real = jnp.concatenate([wide, turned], 0).astype(jnp.bfloat16)
    imag = jnp.concatenate([turned, -wide], 0).astype(jnp.bfloat16)
    form = (((1,), (1,)), ((), ()))
    fields = lax.dot_general(
        screening[0, :, columns], real, form, preferred_element_type=jnp.float32
    ) + lax.dot_general(screening[1, :, columns], imag, form, preferred_element_type=jnp.float32)
    both = jnp.concatenate(split(fields), 1)
    cond = jnp.concatenate([ref[...] for ref in cond_in], 0)
    crossed = jnp.dot(cond, both, preferred_element_type=jnp.float32)
    half = crossed.shape[1] // 2
    crossed = crossed[:, :half] + crossed[:, half:]
    kernel = diagonal(crossed, ka, ba, cond_count // ba * cond_count, -1.0)
    out[:codes, :] = placed_piece(kernel, table, dims, ba)
    out[codes:, :] = extras[...]


def near(ka, ba, dims, screening, table, extras, valence, cond_all):
    vloc, val_count, cond_count, npol = dims
    codes = val_count * cond_count
    operands = [screening, table, extras, valence, *cond_all]
    rows, width = valence.shape
    return pl.pallas_call(
        functools.partial(near_kernel, ka, ba, dims),
        out_shape=in_vmem((codes + EXTRA_ROWS, 2 * ka * codes), jnp.float32),
        in_specs=[vmem] * len(operands),
        out_specs=vmem,
        cost_estimate=pl.CostEstimate(
            flops=8 * screening.shape[1] * width * rows, bytes_accessed=screening.size, transcendentals=0
        ),
        compiler_params=limits(*operands),
        name="near",
    )(*operands)


def couple_kernel(ka, ga, ba, share_rows, screening, *refs):
    cond_in, outs = refs[:ba], refs[ba:]
    mine = lax.axis_index("ga")
    wide = jnp.concatenate([ref[...].astype(jnp.float32) for ref in cond_in], 0)
    straight, turned = [], []
    for at in range(0, wide.shape[0], 2 * share_rows):
        real, imag = wide[at : at + share_rows], wide[at + share_rows : at + 2 * share_rows]
        straight += [real, -imag]
        turned += [imag, real]
    straight = jnp.concatenate(straight, 0).astype(jnp.bfloat16)
    turned = jnp.concatenate(turned, 0).astype(jnp.bfloat16)
    width = screening.shape[2] // ga
    for r in range(1, ga):
        columns = columns_of(origin(mine, r, ga), width)
        coupled = jnp.dot(
            straight, screening[0, :, columns], preferred_element_type=jnp.float32
        ) + jnp.dot(turned, screening[1, :, columns], preferred_element_type=jnp.float32)
        high, low = split(coupled)
        outs[r - 1][: coupled.shape[0], :] = high
        outs[r - 1][coupled.shape[0] :, :] = low


def couple(ka, ga, ba, dims, screening, cond_all):
    share_rows = dims[2] // ba * dims[2]
    rows = 2 * sum(x.shape[0] for x in cond_all)
    width = screening.shape[2] // ga
    operands = [screening, *cond_all]
    return pl.pallas_call(
        functools.partial(couple_kernel, ka, ga, ba, share_rows),
        out_shape=[in_vmem((rows, width), jnp.bfloat16)] * (ga - 1),
        in_specs=[vmem] * len(operands),
        out_specs=[vmem] * (ga - 1),
        cost_estimate=pl.CostEstimate(
            flops=2 * screening.size * rows, bytes_accessed=screening.size, transcendentals=0
        ),
        compiler_params=limits(*operands),
        name="couple",
    )(*operands)


def far_kernel(ka, ba, dims, *refs):
    vloc, val_count, cond_count, npol = dims
    table, held, out = refs[0], refs[1], refs[-1]
    count = (len(refs) - 3) // 2
    codes = val_count * cond_count
    crossed = None
    for coupled, valence in zip(refs[2 : 2 + count], refs[2 + count : -1]):
        rows = jnp.concatenate(with_turned(valence, vloc * val_count), 0).astype(jnp.bfloat16)
        term = lax.dot_general(
            coupled[...], rows, (((1,), (1,)), ((), ())), preferred_element_type=jnp.float32
        )
        crossed = term if crossed is None else crossed + term
    half = crossed.shape[0] // 2
    crossed = crossed[:half] + crossed[half:]
    kernel = diagonal(crossed, ka, ba, cond_count // ba * cond_count, 1.0)
    out[:codes, :] = held[:codes, :] + placed_piece(kernel, table, dims, ba)
    out[codes:, :] = held[codes:, :]


def far(ka, ba, dims, table, held, coupled, val_far):
    operands = [table, held, *coupled, *val_far]
    return pl.pallas_call(
        functools.partial(far_kernel, ka, ba, dims),
        out_shape=in_vmem(held.shape, jnp.float32),
        in_specs=[vmem] * len(operands),
        out_specs=vmem,
        compiler_params=limits(*operands),
        name="far",
    )(*operands)


def haydock_kernel(ka, codes, scale_count, npol, *refs):
    pieces = refs[:-3]
    next_out, coef_out, matrix = refs[-3:]
    lanes = pieces[0].shape[1]
    mid = lanes // 2
    height = codes + EXTRA_ROWS
    found = [(ref, at) for ref in pieces for at in range(0, ref.shape[0], height)]
    extras = None
    slots = []
    for ref, at in found:
        rows = ref[at + codes : at + height, :]
        extras = rows if extras is None else extras + rows
        slots.append((ref[at : at + codes, :], rows[npol + 2 : npol + 3]))
    own = pieces[0][codes:height, :]
    sign = jnp.where(iota((1, lanes), 1) < mid, -1.0, 1.0)
    for k2 in range(ka):
        block = jnp.zeros((codes, lanes), jnp.float32)
        for piece, second in slots:
            block = jnp.where(second == float(k2), piece, block)
        matrix[k2 * codes : (k2 + 1) * codes, :] = block
        matrix[mid + k2 * codes : mid + (k2 + 1) * codes, :] = sign * pltpu.roll(block, mid, 1)
    high, low = split(matrix[...])
    full = jnp.concatenate([high, low], 1)
    start = extras[:npol]
    energy = extras[npol : npol + 1]

    def halves(vector):
        top = vector.astype(jnp.bfloat16).astype(jnp.float32)
        return jnp.concatenate([top, vector - top], 0).astype(jnp.bfloat16)

    def mean(values):
        return jnp.sum(values, axis=1, keepdims=True) / scale_count

    def norm(vector):
        return jnp.sqrt(mean(vector * vector) + EPSILON)

    def swap(vector):
        return pltpu.roll(vector, mid, 1)

    def hamiltonian(vector):
        product = jnp.dot(halves(vector), full, preferred_element_type=jnp.float32)
        main = product[:npol, :lanes] + product[npol:, :lanes]
        return energy * vector - (main + product[:npol, lanes:])

    def inner(left, right):
        return mean(left * right), mean(-sign * left * swap(right))

    def times(real, imag, vector):
        return real * vector + imag * (sign * swap(vector))

    start_image = hamiltonian(start)
    scale = 1.0 / norm(start)
    first = start * scale
    first_image = start_image * scale
    alpha_real, alpha_imag = inner(first, first_image)
    first_resid = first_image - times(alpha_real, alpha_imag, first)
    resid_image = hamiltonian(first_resid)
    beta_one = norm(first_resid)
    scale = 1.0 / beta_one
    second = first_resid * scale
    second_image = resid_image * scale
    gamma_real, gamma_imag = inner(second, second_image)
    second_resid = second_image - times(gamma_real, gamma_imag, second) - beta_one * first
    beta_two = norm(second_resid)

    coef_lane = iota(coef_out.shape, 1)
    coefs = jnp.zeros(coef_out.shape, jnp.float32)
    for at, value in enumerate((alpha_real, alpha_imag, gamma_real, gamma_imag, beta_one, beta_two)):
        coefs = jnp.where(coef_lane == at, value, coefs)
    coef_out[...] = coefs
    row = iota((2 * codes, lanes), 0)
    lane = iota((2 * codes, lanes), 1)
    here = (lane % mid // codes == lax.axis_index("ka")) & (lane // mid == row // codes)
    band = (row % codes).astype(jnp.float32)
    pick = jnp.where(here & (own[npol + 1 : npol + 2] == band), 1.0, 0.0).astype(jnp.bfloat16)
    picked = lax.dot_general(
        halves(second_resid), pick, (((1,), (1,)), ((), ())), preferred_element_type=jnp.float32
    )
    picked = (picked[:npol] + picked[npol:]) / beta_two
    next_out[0, :, 0, :] = picked[:, :codes]
    next_out[0, :, 1, :] = picked[:, codes:]


def haydock(ka, codes, scale_count, npol, pieces):
    lanes = pieces[0].shape[1]
    square = jax.ShapeDtypeStruct((lanes, lanes), jnp.float32)
    return pl.pallas_call(
        functools.partial(haydock_kernel, ka, codes, scale_count, npol),
        out_shape=[
            jax.ShapeDtypeStruct((1, npol, 2, codes), jnp.float32),
            jax.ShapeDtypeStruct((npol, 6), jnp.float32),
        ],
        in_specs=[vmem] * len(pieces),
        out_specs=[vmem, vmem],
        scratch_shapes=[pltpu.VMEM(square.shape, square.dtype)],
        compiler_params=limits(*pieces, square),
        name="haydock",
    )(*pieces)


def summed(value, axis):
    size = lax.axis_size(axis)
    if size & (size - 1):
        return value + sum(shifted(value, axis, step) for step in range(1, size))
    step = 1
    while step < size:
        value = value + exchanged(value, axis, lambda i, size: i ^ step)
        step *= 2
    return value


def local(
    ka,
    ga,
    ba,
    start_vector,
    valence_density,
    conduction_density,
    screening,
    qpoint_map,
    slot_owner,
    band_pairs,
    valence_energy,
    conduction_energy,
):
    npol = start_vector.shape[1]
    pair_count = start_vector.shape[3]
    kcount, vloc, val_count = qpoint_map.shape[0], valence_density.shape[3], valence_density.shape[4]
    cond_count = conduction_density.shape[3]
    pairs = vloc * val_count
    dims = (vloc, val_count, cond_count, npol)
    packed = pack(ka, ba, qpoint_map, slot_owner, valence_density, conduction_density)
    blocks = [packed[0]] + [shifted(packed[j], "ka", j) for j in range(1, ka)]
    whole, near_table, far_table, extras = prepare(
        ka,
        dims,
        qpoint_map,
        slot_owner,
        band_pairs,
        valence_energy,
        conduction_energy,
        start_vector,
        screening,
        packed[0],
    )
    val_all, cond_half = regroup(ka, 2 * pairs, blocks, extras)
    val_far = [shifted(val_all, "ga", r) for r in range(1, ga)]
    cond_all = [cond_half] + [handed(cond_half, r) for r in range(1, ba)]
    piece = near(ka, ba, dims, whole, near_table, extras, val_all, cond_all)
    if val_far:
        coupled = couple(ka, ga, ba, dims, whole, cond_all)
        piece = far(ka, ba, dims, far_table, piece, coupled, val_far)
    piece = piece + sum(handed(piece, r) for r in range(1, ba))
    piece = summed(piece, "ga")
    pieces = [piece] + [shifted(piece, "ka", j) for j in range(1, ka)]
    scale_count = float(kcount * pair_count)
    return tuple(haydock(ka, pair_count, scale_count, npol, pieces))


def solution(mesh):
    in_specs = (
        P(("grp", "ka"), None, None, None),
        P(("grp", "ka"), None, None, "ba", None, "ga"),
        P(("grp", "ka"), None, None, None, None, "ga"),
        P(("grp", "ka"), None, "ga", None),
        P(),
        P(),
        P(),
        P(("grp", "ka"), None),
        P(("grp", "ka"), None),
    )
    out_specs = (P(("grp", "ka"), None, None, None), P("grp", None))
    body = functools.partial(local, mesh.shape["ka"], mesh.shape["ga"], mesh.shape["ba"])
    return jax.shard_map(body, mesh=mesh, in_specs=in_specs, out_specs=out_specs, check_vma=False)
```

```python
import functools
import math

import jax
import jax.numpy as jnp
from jax import lax
from jax.experimental import pallas as pl
from jax.experimental.pallas import tpu as pltpu
from jax.sharding import PartitionSpec as P

EPSILON = 1e-06
EXACT = lax.Precision.HIGHEST
VMEM_LEAST = 8 * 1024 * 1024
VMEM_MOST = 56 * 1024 * 1024

vmem = pl.BlockSpec(memory_space=pltpu.VMEM)
anywhere = pl.BlockSpec(memory_space=pl.ANY)
EXTRA_ROWS = 8
CHUNKS = 4


def in_vmem(shape, dtype):
    return pltpu.VMEM(shape, dtype)


def placed(value, space):
    return pltpu.with_memory_space_constraint(value, space)


def iota(shape, axis):
    return lax.broadcasted_iota(jnp.int32, shape, axis)


def split(values):
    high = values.astype(jnp.bfloat16)
    low = (values - high.astype(jnp.float32)).astype(jnp.bfloat16)
    return high, low


def limits(*arrays):
    held = sum(math.prod(a.shape) * a.dtype.itemsize for a in arrays)
    return pltpu.CompilerParams(vmem_limit_bytes=min(VMEM_MOST, VMEM_LEAST + 4 * held))


def target(me, step, size):
    return lax.rem(me + step, size)


def origin(me, step, size):
    return lax.rem(me + size - step, size)


def exchanged(value, axis, move):
    size, cores = lax.axis_size(axis), lax.axis_size("ba")
    pairs = [
        (i * cores + h, move(i, size) * cores + (h + 1) % cores)
        for i in range(size)
        for h in range(cores)
    ]
    return lax.ppermute(value, (axis, "ba"), pairs)


def shifted(value, axis, step):
    return exchanged(value, axis, lambda i, size: (i + step) % size)


def handed(value, step):
    size = lax.axis_size("ba")
    return lax.ppermute(value, "ba", [(h, (h + step) % size) for h in range(size)])


def pack_kernel(ka, qmap_in, owner_in, valence_in, conduction_in, *rest):
    outs = rest[:ka]
    qmap, owner, partner, valence, conduction, sems = rest[ka:]
    copies = [
        pltpu.make_async_copy(src, dst, sems.at[at])
        for at, (src, dst) in enumerate(
            ((qmap_in, qmap), (owner_in, owner), (valence_in, valence), (conduction_in, conduction))
        )
    ]
    for copy in copies:
        copy.start()
    me = lax.axis_index("ka")
    half = lax.axis_index("ba")
    count, width = valence.shape[1], valence.shape[5]
    cond_count = conduction.shape[3]
    share = cond_count // lax.axis_size("ba")
    val_rows = 2 * valence.shape[3] * valence.shape[4]
    cond_rows = 2 * share * cond_count

    def note(k2, carry):
        partner[owner[qmap[me, k2]]] = k2
        return carry

    copies[0].wait()
    copies[1].wait()
    lax.fori_loop(0, count, note, 0)
    copies[2].wait()
    copies[3].wait()
    for at in range(ka):
        k2 = partner[target(me, at, ka)]
        block = valence[0, k2].astype(jnp.float32).reshape(val_rows, width)
        outs[at][:val_rows, :] = block.astype(jnp.bfloat16)
        to = lax.rem(half + min(at, 1), lax.axis_size("ba"))
        block = conduction[0, k2, :, pl.ds(to * share, share)].astype(jnp.float32)
        outs[at][val_rows:, :] = block.reshape(cond_rows, width).astype(jnp.bfloat16)


def pack(ka, ba, qmap, owner, valence, conduction):
    cond_count = conduction.shape[3]
    rows = 2 * valence.shape[3] * valence.shape[4] + 2 * cond_count // ba * cond_count
    shape = in_vmem((rows, valence.shape[5]), valence.dtype)
    operands = [placed(x, pltpu.HBM) for x in (qmap, owner, valence, conduction)]
    return pl.pallas_call(
        functools.partial(pack_kernel, ka),
        out_shape=[shape] * ka,
        in_specs=[anywhere] * 4,
        out_specs=[vmem] * ka,
        scratch_shapes=[
            pltpu.SMEM(qmap.shape, jnp.int32),
            pltpu.SMEM(owner.shape, jnp.int32),
            pltpu.SMEM(owner.shape, jnp.int32),
            pltpu.VMEM(valence.shape, valence.dtype),
            pltpu.VMEM(conduction.shape, conduction.dtype),
            pltpu.SemaphoreType.DMA((4,)),
        ],
        compiler_params=limits(valence, conduction),
        name="pack",
    )(*operands)


def prepare_kernel(ka, dims, *refs):
    vloc, val_count, cond_count, npol = dims
    ins, screening, (screen_out, near_table, far_table, extras), scratch = refs[:6], refs[6], refs[8:12], refs[12:]
    qmap, owner, band_pairs, val_energy, cond_energy, start, sems, screen_sems = scratch
    me = lax.axis_index("ka")
    half = lax.axis_index("ba")
    mine = lax.axis_index("ga")
    copies = [
        pltpu.make_async_copy(src, dst, sems.at[at])
        for at, (src, dst) in enumerate(
            zip(ins, (qmap, owner, band_pairs, val_energy, cond_energy, start))
        )
    ]
    height = screening.shape[2] // CHUNKS
    chunks = [
        pltpu.make_async_copy(
            screening.at[0, part, pl.ds(c * height, height)],
            screen_out.at[part, pl.ds(c * height, height)],
            screen_sems.at[part, c],
        )
        for part in range(2)
        for c in range(CHUNKS)
    ]
    for copy in copies + chunks:
        copy.start()
    pairs = vloc * val_count
    block = 2 * pairs
    rows = ka * block
    codes = val_count * cond_count
    mid = ka * codes
    lanes = 2 * mid
    row = iota((2 * rows, lanes), 0)
    col = iota((2 * rows, lanes), 1)
    j_of_row = row % rows // block
    cores = lax.axis_size("ba")
    for moves, table in enumerate((near_table, far_table)):
        share = lax.rem(half + 2 * cores - moves - jnp.where(j_of_row == 0, 0, 1), cores)
        want = (
            (row % block // pairs) * mid
            + origin(me, j_of_row, ka) * codes
            + (share * vloc + row % pairs // val_count) * cond_count
        )
        joined = (col - want >= 0) & (col - want < cond_count)
        for v2 in range(val_count):
            pick = jnp.where(joined & (row % val_count == v2), 1.0, 0.0)
            table[:, v2 * lanes : (v2 + 1) * lanes] = pick.astype(jnp.bfloat16)

    for copy in copies:
        copy.wait()
    first = jnp.where((mine == 0) & (half == 0), 1.0, 0.0)
    lane = iota((1, lanes), 1)
    lane_k = lane % mid // codes
    band_row = iota((codes, lanes), 0)
    band_lane = iota((codes, lanes), 1)
    code = jnp.zeros((codes, lanes), jnp.int32)
    bands = jnp.full((1, lanes), -1.0, jnp.float32)
    for b in range(codes):
        code = jnp.where(band_row == b, band_pairs[b], code)
        bands = jnp.where(lane % codes == band_pairs[b], float(b), bands)
    vectors = jnp.zeros((npol, lanes), jnp.float32)
    for part in range(2):
        spot = part * mid + me * codes
        pick = jnp.where(band_lane == spot + code, first, 0.0)
        vectors = vectors + jnp.dot(start[0, :, part, :], pick, precision=EXACT)
    energy = jnp.zeros((1, lanes), jnp.float32)
    for c in range(cond_count):
        energy = jnp.where(lane % cond_count == c, cond_energy[0, c], energy)
    for v in range(val_count):
        energy = energy - jnp.where(lane % codes // cond_count == v, val_energy[0, v], 0.0)
    energy = jnp.where(lane_k == me, energy * first, 0.0)
    kcount = qmap.shape[0]

    def find(k2, found):
        return jnp.where(owner[qmap[0, k2]] == me, k2, found)

    back = lax.fori_loop(0, kcount, find, 0)
    second = lane_k + back
    second = jnp.where(second >= kcount, second - kcount, second).astype(jnp.float32) * first
    rest = jnp.zeros((EXTRA_ROWS - 3 - npol, lanes), jnp.float32)
    extras[...] = jnp.concatenate([vectors, energy, bands * first, second, rest], 0)
    for copy in chunks:
        copy.wait()


def prepare(ka, dims, qmap, owner, band_pairs, val_energy, cond_energy, start, screening, after):
    vloc, val_count, cond_count, npol = dims
    rows = 4 * ka * vloc * val_count
    lanes = 2 * ka * val_count * cond_count
    operands = (qmap, owner, band_pairs, val_energy, cond_energy, start, screening)
    table = jax.ShapeDtypeStruct((rows, val_count * lanes), jnp.bfloat16)
    return pl.pallas_call(
        functools.partial(prepare_kernel, ka, dims),
        out_shape=[
            in_vmem(screening.shape[1:], screening.dtype),
            in_vmem(table.shape, table.dtype),
            in_vmem(table.shape, table.dtype),
            in_vmem((EXTRA_ROWS, lanes), jnp.float32),
        ],
        in_specs=[anywhere] * 8,
        out_specs=[vmem] * 4,
        scratch_shapes=[pltpu.SMEM(x.shape, x.dtype) for x in operands[:5]]
        + [
            pltpu.VMEM(start.shape, start.dtype),
            pltpu.SemaphoreType.DMA((6,)),
            pltpu.SemaphoreType.DMA((2, CHUNKS)),
        ],
        cost_estimate=pl.CostEstimate(
            flops=0, bytes_accessed=4 * screening.size, transcendentals=0
        ),
        compiler_params=limits(table),
        name="prepare",
    )(*[placed(x, pltpu.HBM) for x in operands], after)


def hold_kernel(value, token, out):
    out[...] = value[...]


def hold(value, token):
    return pl.pallas_call(
        hold_kernel,
        out_shape=in_vmem(value.shape, value.dtype),
        in_specs=[vmem, anywhere],
        out_specs=vmem,
        compiler_params=limits(value),
        name="hold",
    )(value, token)


def regroup_kernel(count, first, last, *refs):
    blocks, out = refs[:count], refs[-1]
    rows = last - first
    for at in range(count):
        out[at * rows : (at + 1) * rows, :] = blocks[at][first:last, :]


def regroup(blocks, first, last, after=()):
    shape = (len(blocks) * (last - first), blocks[0].shape[1])
    return pl.pallas_call(
        functools.partial(regroup_kernel, len(blocks), first, last),
        out_shape=in_vmem(shape, blocks[0].dtype),
        in_specs=[vmem] * len(blocks) + [anywhere] * len(after),
        out_specs=vmem,
        compiler_params=limits(*blocks),
        name="regroup",
    )(*blocks, *after)


def with_turned(halves, pairs):
    wide = jnp.concatenate([half[...].astype(jnp.float32) for half in halves], 0)
    parts = []
    for at in range(0, wide.shape[0], 2 * pairs):
        parts += [-wide[at + pairs : at + 2 * pairs], wide[at : at + pairs]]
    return wide, jnp.concatenate(parts, 0)


def columns_of(place, width):
    return pl.ds(pl.multiple_of(place * width, 128), width)


def placed_piece(kernel, table, dims, ba):
    vloc, val_count, cond_count, npol = dims
    half = lax.axis_index("ba")
    codes = val_count * cond_count
    lanes = table.shape[1] // val_count
    share = cond_count // ba
    cond_rows = cond_count * cond_count
    spread = jnp.dot(
        jnp.concatenate(split(kernel), 0), table[...], preferred_element_type=jnp.float32
    )
    spread = spread[:cond_rows] + spread[cond_rows:]
    crow = iota((cond_rows, lanes), 0)
    share_rows = share * cond_count
    c_of_row = origin(half, crow // share_rows, ba) * share + crow % share_rows // cond_count
    same_c = c_of_row == iota((cond_rows, lanes), 1) % cond_count
    spread = jnp.concatenate(
        [
            jnp.where(same_c, spread[:, v2 * lanes : (v2 + 1) * lanes], 0.0)
            for v2 in range(val_count)
        ],
        0,
    )
    out_row = iota((codes, val_count * cond_rows), 0)
    out_col = iota((codes, val_count * cond_rows), 1)
    fold = (out_row // cond_count == out_col // cond_rows) & (
        out_row % cond_count == out_col % cond_count
    )
    fold = jnp.where(fold, 1.0, 0.0).astype(jnp.bfloat16)
    piece = jnp.dot(fold, jnp.concatenate(split(spread), 1), preferred_element_type=jnp.float32)
    return piece[:, :lanes] + piece[:, lanes:]


def diagonal(crossed, ka, ba, share_rows, sign):
    rows = crossed.shape[1] // 2
    lane = iota((share_rows, 2 * rows), 1)
    lane_j = lane % rows // (rows // ka)
    straight = lane < rows
    kernel = []
    for h in range(ba):
        total = jnp.zeros((share_rows, 2 * rows), jnp.float32)
        for j in range(ka):
            at = (h * ka + j) * 2 * share_rows
            real = crossed[at : at + share_rows]
            imag = crossed[at + share_rows : at + 2 * share_rows]
            total = jnp.where(lane_j == j, jnp.where(straight, real, sign * imag), total)
        kernel.append(total)
    return jnp.concatenate(kernel, 0)


def near_kernel(ka, ba, dims, *refs):
    vloc, val_count, cond_count, npol = dims
    screening, table, extras = refs[:3]
    halves, cond_in, out = refs[3 : -1 - ba], refs[-1 - ba : -1], refs[-1]
    codes = val_count * cond_count
    columns = columns_of(lax.axis_index("ga"), halves[0].shape[1])
    wide, turned = with_turned(halves, vloc * val_count)
    real = jnp.concatenate([wide, turned], 0).astype(jnp.bfloat16)
    imag = jnp.concatenate([turned, -wide], 0).astype(jnp.bfloat16)
    form = (((1,), (1,)), ((), ()))
    fields = lax.dot_general(
        screening[0, :, columns], real, form, preferred_element_type=jnp.float32
    ) + lax.dot_general(screening[1, :, columns], imag, form, preferred_element_type=jnp.float32)
    both = jnp.concatenate(split(fields), 1)
    cond = jnp.concatenate([ref[...] for ref in cond_in], 0)
    crossed = jnp.dot(cond, both, preferred_element_type=jnp.float32)
    half = crossed.shape[1] // 2
    crossed = crossed[:, :half] + crossed[:, half:]
    kernel = diagonal(crossed, ka, ba, cond_count // ba * cond_count, -1.0)
    out[:codes, :] = placed_piece(kernel, table, dims, ba)
    out[codes:, :] = extras[...]


def near(ka, ba, dims, screening, table, extras, halves, cond_all):
    vloc, val_count, cond_count, npol = dims
    codes = val_count * cond_count
    operands = [screening, table, extras, *halves, *cond_all]
    rows, width = sum(half.shape[0] for half in halves), halves[0].shape[1]
    return pl.pallas_call(
        functools.partial(near_kernel, ka, ba, dims),
        out_shape=in_vmem((codes + EXTRA_ROWS, 2 * ka * codes), jnp.float32),
        in_specs=[vmem] * len(operands),
        out_specs=vmem,
        cost_estimate=pl.CostEstimate(
            flops=8 * screening.shape[1] * width * rows, bytes_accessed=screening.size, transcendentals=0
        ),
        compiler_params=limits(*operands),
        name="near",
    )(*operands)


def couple_kernel(ka, ga, ba, share_rows, screening, *refs):
    cond_in, outs = refs[:ba], refs[ba:]
    mine = lax.axis_index("ga")
    wide = jnp.concatenate([ref[...].astype(jnp.float32) for ref in cond_in], 0)
    straight, turned = [], []
    for at in range(0, wide.shape[0], 2 * share_rows):
        real, imag = wide[at : at + share_rows], wide[at + share_rows : at + 2 * share_rows]
        straight += [real, -imag]
        turned += [imag, real]
    straight = jnp.concatenate(straight, 0).astype(jnp.bfloat16)
    turned = jnp.concatenate(turned, 0).astype(jnp.bfloat16)
    width = screening.shape[2] // ga
    for r in range(1, ga):
        columns = columns_of(origin(mine, r, ga), width)
        coupled = jnp.dot(
            straight, screening[0, :, columns], preferred_element_type=jnp.float32
        ) + jnp.dot(turned, screening[1, :, columns], preferred_element_type=jnp.float32)
        high, low = split(coupled)
        outs[r - 1][: coupled.shape[0], :] = high
        outs[r - 1][coupled.shape[0] :, :] = low


def couple(ka, ga, ba, dims, screening, cond_all):
    share_rows = dims[2] // ba * dims[2]
    rows = 2 * sum(x.shape[0] for x in cond_all)
    width = screening.shape[2] // ga
    operands = [screening, *cond_all]
    return pl.pallas_call(
        functools.partial(couple_kernel, ka, ga, ba, share_rows),
        out_shape=[in_vmem((rows, width), jnp.bfloat16)] * (ga - 1),
        in_specs=[vmem] * len(operands),
        out_specs=[vmem] * (ga - 1),
        cost_estimate=pl.CostEstimate(
            flops=2 * screening.size * rows, bytes_accessed=screening.size, transcendentals=0
        ),
        compiler_params=limits(*operands),
        name="couple",
    )(*operands)


def far_kernel(ka, ba, dims, *refs):
    vloc, val_count, cond_count, npol = dims
    table, held, out = refs[0], refs[1], refs[-1]
    count = lax.axis_size("ga") - 1
    each = (len(refs) - 3 - count) // count
    codes = val_count * cond_count
    crossed = None
    for r in range(count):
        coupled = refs[2 + r]
        halves = refs[2 + count + r * each : 2 + count + (r + 1) * each]
        rows = jnp.concatenate(with_turned(halves, vloc * val_count), 0).astype(jnp.bfloat16)
        term = lax.dot_general(
            coupled[...], rows, (((1,), (1,)), ((), ())), preferred_element_type=jnp.float32
        )
        crossed = term if crossed is None else crossed + term
    half = crossed.shape[0] // 2
    crossed = crossed[:half] + crossed[half:]
    kernel = diagonal(crossed, ka, ba, cond_count // ba * cond_count, 1.0)
    out[:codes, :] = held[:codes, :] + placed_piece(kernel, table, dims, ba)
    out[codes:, :] = held[codes:, :]


def far(ka, ba, dims, table, held, coupled, val_far):
    operands = [table, held, *coupled, *val_far]
    return pl.pallas_call(
        functools.partial(far_kernel, ka, ba, dims),
        out_shape=in_vmem(held.shape, jnp.float32),
        in_specs=[vmem] * len(operands),
        out_specs=vmem,
        compiler_params=limits(*operands),
        name="far",
    )(*operands)


def haydock_kernel(ka, codes, scale_count, npol, *refs):
    pieces = refs[:-3]
    next_out, coef_out, matrix = refs[-3:]
    lanes = pieces[0].shape[1]
    mid = lanes // 2
    height = codes + EXTRA_ROWS
    found = [(ref, at) for ref in pieces for at in range(0, ref.shape[0], height)]
    extras = None
    slots = []
    for ref, at in found:
        rows = ref[at + codes : at + height, :]
        extras = rows if extras is None else extras + rows
        slots.append((ref[at : at + codes, :], rows[npol + 2 : npol + 3]))
    own = pieces[0][codes:height, :]
    sign = jnp.where(iota((1, lanes), 1) < mid, -1.0, 1.0)
    for k2 in range(ka):
        block = jnp.zeros((codes, lanes), jnp.float32)
        for piece, second in slots:
            block = jnp.where(second == float(k2), piece, block)
        matrix[k2 * codes : (k2 + 1) * codes, :] = block
        matrix[mid + k2 * codes : mid + (k2 + 1) * codes, :] = sign * pltpu.roll(block, mid, 1)
    high, low = split(matrix[...])
    full = jnp.concatenate([high, low], 1)
    start = extras[:npol]
    energy = extras[npol : npol + 1]

    def halves(vector):
        top = vector.astype(jnp.bfloat16).astype(jnp.float32)
        return jnp.concatenate([top, vector - top], 0).astype(jnp.bfloat16)

    def mean(values):
        return jnp.sum(values, axis=1, keepdims=True) / scale_count

    def norm(vector):
        return jnp.sqrt(mean(vector * vector) + EPSILON)

    def swap(vector):
        return pltpu.roll(vector, mid, 1)

    def hamiltonian(vector):
        product = jnp.dot(halves(vector), full, preferred_element_type=jnp.float32)
        main = product[:npol, :lanes] + product[npol:, :lanes]
        return energy * vector - (main + product[:npol, lanes:])

    def inner(left, right):
        return mean(left * right), mean(-sign * left * swap(right))

    def times(real, imag, vector):
        return real * vector + imag * (sign * swap(vector))

    start_image = hamiltonian(start)
    scale = 1.0 / norm(start)
    first = start * scale
    first_image = start_image * scale
    alpha_real, alpha_imag = inner(first, first_image)
    first_resid = first_image - times(alpha_real, alpha_imag, first)
    resid_image = hamiltonian(first_resid)
    beta_one = norm(first_resid)
    scale = 1.0 / beta_one
    second = first_resid * scale
    second_image = resid_image * scale
    gamma_real, gamma_imag = inner(second, second_image)
    second_resid = second_image - times(gamma_real, gamma_imag, second) - beta_one * first
    beta_two = norm(second_resid)

    coef_lane = iota(coef_out.shape, 1)
    coefs = jnp.zeros(coef_out.shape, jnp.float32)
    for at, value in enumerate((alpha_real, alpha_imag, gamma_real, gamma_imag, beta_one, beta_two)):
        coefs = jnp.where(coef_lane == at, value, coefs)
    coef_out[...] = coefs
    row = iota((2 * codes, lanes), 0)
    lane = iota((2 * codes, lanes), 1)
    here = (lane % mid // codes == lax.axis_index("ka")) & (lane // mid == row // codes)
    band = (row % codes).astype(jnp.float32)
    pick = jnp.where(here & (own[npol + 1 : npol + 2] == band), 1.0, 0.0).astype(jnp.bfloat16)
    picked = lax.dot_general(
        halves(second_resid), pick, (((1,), (1,)), ((), ())), preferred_element_type=jnp.float32
    )
    picked = (picked[:npol] + picked[npol:]) / beta_two
    next_out[0, :, 0, :] = picked[:, :codes]
    next_out[0, :, 1, :] = picked[:, codes:]


def haydock(ka, codes, scale_count, npol, pieces):
    lanes = pieces[0].shape[1]
    square = jax.ShapeDtypeStruct((lanes, lanes), jnp.float32)
    return pl.pallas_call(
        functools.partial(haydock_kernel, ka, codes, scale_count, npol),
        out_shape=[
            jax.ShapeDtypeStruct((1, npol, 2, codes), jnp.float32),
            jax.ShapeDtypeStruct((npol, 6), jnp.float32),
        ],
        in_specs=[vmem] * len(pieces),
        out_specs=[vmem, vmem],
        scratch_shapes=[pltpu.VMEM(square.shape, square.dtype)],
        compiler_params=limits(*pieces, square),
        name="haydock",
    )(*pieces)


def summed(value, axis):
    size = lax.axis_size(axis)
    if size & (size - 1):
        return value + sum(shifted(value, axis, step) for step in range(1, size))
    step = 1
    while step < size:
        value = value + exchanged(value, axis, lambda i, size: i ^ step)
        step *= 2
    return value


def local(
    ka,
    ga,
    ba,
    start_vector,
    valence_density,
    conduction_density,
    screening,
    qpoint_map,
    slot_owner,
    band_pairs,
    valence_energy,
    conduction_energy,
):
    npol = start_vector.shape[1]
    pair_count = start_vector.shape[3]
    kcount, vloc, val_count = qpoint_map.shape[0], valence_density.shape[3], valence_density.shape[4]
    cond_count = conduction_density.shape[3]
    pairs = vloc * val_count
    dims = (vloc, val_count, cond_count, npol)
    packed = pack(ka, ba, qpoint_map, slot_owner, valence_density, conduction_density)
    blocks = [packed[0]] + [shifted(packed[j], "ka", j) for j in range(1, ka)]
    early = ka // 2
    val_early = regroup(blocks[:early], 0, 2 * pairs)
    far_early = [shifted(val_early, "ga", r) for r in range(1, ga)]
    whole, near_table, far_table, extras = prepare(
        ka,
        dims,
        qpoint_map,
        slot_owner,
        band_pairs,
        valence_energy,
        conduction_energy,
        start_vector,
        screening,
        val_early,
    )
    val_late = regroup(blocks[early:], 0, 2 * pairs, (extras,))
    far_late = [shifted(val_late, "ga", r) for r in range(1, ga)]
    cond_half = regroup(blocks, 2 * pairs, blocks[0].shape[0], (val_late, *far_early))
    cond_all = [cond_half] + [handed(cond_half, r) for r in range(1, ba)]
    piece = near(ka, ba, dims, whole, near_table, extras, [val_early, val_late], cond_all)
    if ga > 1:
        coupled = couple(ka, ga, ba, dims, whole, cond_all)
        val_far = [half for both in zip(far_early, far_late) for half in both]
        piece = far(ka, ba, dims, far_table, piece, coupled, val_far)
    piece = piece + sum(handed(piece, r) for r in range(1, ba))
    piece = summed(piece, "ga")
    pieces, token = [piece], piece
    for j in range(1, ka):
        pieces.append(shifted(token, "ka", j))
        token = hold(piece, token)
    scale_count = float(kcount * pair_count)
    return tuple(haydock(ka, pair_count, scale_count, npol, pieces))


def solution(mesh):
    in_specs = (
        P(("grp", "ka"), None, None, None),
        P(("grp", "ka"), None, None, "ba", None, "ga"),
        P(("grp", "ka"), None, None, None, None, "ga"),
        P(("grp", "ka"), None, "ga", None),
        P(),
        P(),
        P(),
        P(("grp", "ka"), None),
        P(("grp", "ka"), None),
    )
    out_specs = (P(("grp", "ka"), None, None, None), P("grp", None))
    body = functools.partial(local, mesh.shape["ka"], mesh.shape["ga"], mesh.shape["ba"])
    return jax.shard_map(body, mesh=mesh, in_specs=in_specs, out_specs=out_specs, check_vma=False)
```

```python
import functools
import math

import jax
import jax.numpy as jnp
from jax import lax
from jax.experimental import pallas as pl
from jax.experimental.pallas import tpu as pltpu
from jax.sharding import PartitionSpec as P

EPSILON = 1e-06
EXACT = lax.Precision.HIGHEST
VMEM_LEAST = 8 * 1024 * 1024
VMEM_MOST = 56 * 1024 * 1024

vmem = pl.BlockSpec(memory_space=pltpu.VMEM)
anywhere = pl.BlockSpec(memory_space=pl.ANY)
EXTRA_ROWS = 8


def in_vmem(shape, dtype):
    return pltpu.VMEM(shape, dtype)


def placed(value, space):
    return pltpu.with_memory_space_constraint(value, space)


def iota(shape, axis):
    return lax.broadcasted_iota(jnp.int32, shape, axis)


def split(values):
    high = values.astype(jnp.bfloat16)
    low = (values - high.astype(jnp.float32)).astype(jnp.bfloat16)
    return high, low


def limits(*arrays):
    held = sum(math.prod(a.shape) * a.dtype.itemsize for a in arrays)
    return pltpu.CompilerParams(vmem_limit_bytes=min(VMEM_MOST, VMEM_LEAST + 4 * held))


def target(me, step, size):
    return lax.rem(me + step, size)


def origin(me, step, size):
    return lax.rem(me + size - step, size)


def exchanged(value, axis, move):
    size, cores = lax.axis_size(axis), lax.axis_size("ba")
    pairs = [
        (i * cores + h, move(i, size) * cores + (h + 1) % cores)
        for i in range(size)
        for h in range(cores)
    ]
    return lax.ppermute(value, (axis, "ba"), pairs)


def shifted(value, axis, step):
    return exchanged(value, axis, lambda i, size: (i + step) % size)


def handed(value, step):
    size = lax.axis_size("ba")
    return lax.ppermute(value, "ba", [(h, (h + step) % size) for h in range(size)])


def pack_kernel(ka, qmap_in, owner_in, valence_in, conduction_in, *rest):
    outs = rest[:ka]
    qmap, owner, partner, valence, conduction, sems = rest[ka:]
    copies = [
        pltpu.make_async_copy(src, dst, sems.at[at])
        for at, (src, dst) in enumerate(
            ((qmap_in, qmap), (owner_in, owner), (valence_in, valence), (conduction_in, conduction))
        )
    ]
    for copy in copies:
        copy.start()
    me = lax.axis_index("ka")
    half = lax.axis_index("ba")
    count, width = valence.shape[1], valence.shape[5]
    cond_count = conduction.shape[3]
    share = cond_count // lax.axis_size("ba")
    val_rows = 2 * valence.shape[3] * valence.shape[4]
    cond_rows = 2 * share * cond_count

    def note(k2, carry):
        partner[owner[qmap[me, k2]]] = k2
        return carry

    copies[0].wait()
    copies[1].wait()
    lax.fori_loop(0, count, note, 0)
    copies[2].wait()
    copies[3].wait()
    for at in range(ka):
        k2 = partner[target(me, at, ka)]
        block = valence[0, k2].astype(jnp.float32).reshape(val_rows, width)
        outs[at][:val_rows, :] = block.astype(jnp.bfloat16)
        to = lax.rem(half + min(at, 1), lax.axis_size("ba"))
        block = conduction[0, k2, :, pl.ds(to * share, share)].astype(jnp.float32)
        outs[at][val_rows:, :] = block.reshape(cond_rows, width).astype(jnp.bfloat16)


def pack(ka, ba, qmap, owner, valence, conduction):
    cond_count = conduction.shape[3]
    rows = 2 * valence.shape[3] * valence.shape[4] + 2 * cond_count // ba * cond_count
    shape = in_vmem((rows, valence.shape[5]), valence.dtype)
    operands = [placed(x, pltpu.HBM) for x in (qmap, owner, valence, conduction)]
    return pl.pallas_call(
        functools.partial(pack_kernel, ka),
        out_shape=[shape] * ka,
        in_specs=[anywhere] * 4,
        out_specs=[vmem] * ka,
        scratch_shapes=[
            pltpu.SMEM(qmap.shape, jnp.int32),
            pltpu.SMEM(owner.shape, jnp.int32),
            pltpu.SMEM(owner.shape, jnp.int32),
            pltpu.VMEM(valence.shape, valence.dtype),
            pltpu.VMEM(conduction.shape, conduction.dtype),
            pltpu.SemaphoreType.DMA((4,)),
        ],
        compiler_params=limits(valence, conduction),
        name="pack",
    )(*operands)


def prepare_kernel(ka, dims, *refs):
    vloc, val_count, cond_count, npol = dims
    ins, screening, (screen_out, near_table, far_table, extras), scratch = refs[:6], refs[6], refs[8:12], refs[12:]
    qmap, owner, band_pairs, val_energy, cond_energy, start, sems, screen_sem = scratch
    me = lax.axis_index("ka")
    half = lax.axis_index("ba")
    mine = lax.axis_index("ga")
    copies = [
        pltpu.make_async_copy(src, dst, sems.at[at])
        for at, (src, dst) in enumerate(
            zip(ins, (qmap, owner, band_pairs, val_energy, cond_energy, start))
        )
    ]
    load = pltpu.make_async_copy(screening.at[0, 0], screen_out, screen_sem)
    for copy in copies + [load]:
        copy.start()
    pairs = vloc * val_count
    block = 2 * pairs
    rows = ka * block
    codes = val_count * cond_count
    mid = ka * codes
    lanes = 2 * mid
    row = iota((2 * rows, lanes), 0)
    col = iota((2 * rows, lanes), 1)
    j_of_row = row % rows // block
    cores = lax.axis_size("ba")
    for moves, table in enumerate((near_table, far_table)):
        share = lax.rem(half + 2 * cores - moves - jnp.where(j_of_row == 0, 0, 1), cores)
        want = (
            (row % block // pairs) * mid
            + origin(me, j_of_row, ka) * codes
            + (share * vloc + row % pairs // val_count) * cond_count
        )
        joined = (col - want >= 0) & (col - want < cond_count)
        for v2 in range(val_count):
            pick = jnp.where(joined & (row % val_count == v2), 1.0, 0.0)
            table[:, v2 * lanes : (v2 + 1) * lanes] = pick.astype(jnp.bfloat16)

    for copy in copies:
        copy.wait()
    first = jnp.where((mine == 0) & (half == 0), 1.0, 0.0)
    lane = iota((1, lanes), 1)
    lane_k = lane % mid // codes
    band_row = iota((codes, lanes), 0)
    band_lane = iota((codes, lanes), 1)
    code = jnp.zeros((codes, lanes), jnp.int32)
    bands = jnp.full((1, lanes), -1.0, jnp.float32)
    for b in range(codes):
        code = jnp.where(band_row == b, band_pairs[b], code)
        bands = jnp.where(lane % codes == band_pairs[b], float(b), bands)
    vectors = jnp.zeros((npol, lanes), jnp.float32)
    for part in range(2):
        spot = part * mid + me * codes
        pick = jnp.where(band_lane == spot + code, first, 0.0)
        vectors = vectors + jnp.dot(start[0, :, part, :], pick, precision=EXACT)
    energy = jnp.zeros((1, lanes), jnp.float32)
    for c in range(cond_count):
        energy = jnp.where(lane % cond_count == c, cond_energy[0, c], energy)
    for v in range(val_count):
        energy = energy - jnp.where(lane % codes // cond_count == v, val_energy[0, v], 0.0)
    energy = jnp.where(lane_k == me, energy * first, 0.0)
    kcount = qmap.shape[0]

    def find(k2, found):
        return jnp.where(owner[qmap[0, k2]] == me, k2, found)

    back = lax.fori_loop(0, kcount, find, 0)
    second = lane_k + back
    second = jnp.where(second >= kcount, second - kcount, second).astype(jnp.float32) * first
    rest = jnp.zeros((EXTRA_ROWS - 3 - npol, lanes), jnp.float32)
    extras[...] = jnp.concatenate([vectors, energy, bands * first, second, rest], 0)
    load.wait()


def prepare(ka, dims, qmap, owner, band_pairs, val_energy, cond_energy, start, screening, after):
    vloc, val_count, cond_count, npol = dims
    rows = 4 * ka * vloc * val_count
    lanes = 2 * ka * val_count * cond_count
    operands = (qmap, owner, band_pairs, val_energy, cond_energy, start, screening)
    table = jax.ShapeDtypeStruct((rows, val_count * lanes), jnp.bfloat16)
    return pl.pallas_call(
        functools.partial(prepare_kernel, ka, dims),
        out_shape=[
            in_vmem(screening.shape[2:], screening.dtype),
            in_vmem(table.shape, table.dtype),
            in_vmem(table.shape, table.dtype),
            in_vmem((EXTRA_ROWS, lanes), jnp.float32),
        ],
        in_specs=[anywhere] * 8,
        out_specs=[vmem] * 4,
        scratch_shapes=[pltpu.SMEM(x.shape, x.dtype) for x in operands[:5]]
        + [
            pltpu.VMEM(start.shape, start.dtype),
            pltpu.SemaphoreType.DMA((6,)),
            pltpu.SemaphoreType.DMA,
        ],
        cost_estimate=pl.CostEstimate(
            flops=0, bytes_accessed=2 * screening.size, transcendentals=0
        ),
        compiler_params=limits(table),
        name="prepare",
    )(*[placed(x, pltpu.HBM) for x in operands], after)


def load_kernel(screening, after, out, sem):
    load = pltpu.make_async_copy(screening.at[0, 1], out, sem)
    load.start()
    load.wait()


def load_imaginary(screening, after):
    return pl.pallas_call(
        load_kernel,
        out_shape=in_vmem(screening.shape[2:], screening.dtype),
        in_specs=[anywhere, anywhere],
        out_specs=vmem,
        scratch_shapes=[pltpu.SemaphoreType.DMA],
        cost_estimate=pl.CostEstimate(
            flops=0, bytes_accessed=2 * screening.size, transcendentals=0
        ),
        compiler_params=limits(),
        name="load_imaginary",
    )(placed(screening, pltpu.HBM), after)


def regroup_kernel(count, first, last, *refs):
    blocks, out = refs[:count], refs[-1]
    rows = last - first
    for at in range(count):
        out[at * rows : (at + 1) * rows, :] = blocks[at][first:last, :]


def regroup(blocks, first, last, after=()):
    shape = (len(blocks) * (last - first), blocks[0].shape[1])
    return pl.pallas_call(
        functools.partial(regroup_kernel, len(blocks), first, last),
        out_shape=in_vmem(shape, blocks[0].dtype),
        in_specs=[vmem] * len(blocks) + [anywhere] * len(after),
        out_specs=vmem,
        compiler_params=limits(*blocks),
        name="regroup",
    )(*blocks, *after)


def with_turned(halves, pairs):
    wide = jnp.concatenate([half[...].astype(jnp.float32) for half in halves], 0)
    parts = []
    for at in range(0, wide.shape[0], 2 * pairs):
        parts += [-wide[at + pairs : at + 2 * pairs], wide[at : at + pairs]]
    return wide, jnp.concatenate(parts, 0)


def columns_of(place, width):
    return pl.ds(pl.multiple_of(place * width, 128), width)


def placed_piece(kernel, table, dims, ba):
    vloc, val_count, cond_count, npol = dims
    half = lax.axis_index("ba")
    codes = val_count * cond_count
    lanes = table.shape[1] // val_count
    share = cond_count // ba
    cond_rows = cond_count * cond_count
    spread = jnp.dot(
        jnp.concatenate(split(kernel), 0), table[...], preferred_element_type=jnp.float32
    )
    spread = spread[:cond_rows] + spread[cond_rows:]
    crow = iota((cond_rows, lanes), 0)
    share_rows = share * cond_count
    c_of_row = origin(half, crow // share_rows, ba) * share + crow % share_rows // cond_count
    same_c = c_of_row == iota((cond_rows, lanes), 1) % cond_count
    spread = jnp.concatenate(
        [
            jnp.where(same_c, spread[:, v2 * lanes : (v2 + 1) * lanes], 0.0)
            for v2 in range(val_count)
        ],
        0,
    )
    out_row = iota((codes, val_count * cond_rows), 0)
    out_col = iota((codes, val_count * cond_rows), 1)
    fold = (out_row // cond_count == out_col // cond_rows) & (
        out_row % cond_count == out_col % cond_count
    )
    fold = jnp.where(fold, 1.0, 0.0).astype(jnp.bfloat16)
    piece = jnp.dot(fold, jnp.concatenate(split(spread), 1), preferred_element_type=jnp.float32)
    return piece[:, :lanes] + piece[:, lanes:]


def diagonal(crossed, ka, ba, share_rows, sign):
    rows = crossed.shape[1] // 2
    lane = iota((share_rows, 2 * rows), 1)
    lane_j = lane % rows // (rows // ka)
    straight = lane < rows
    kernel = []
    for h in range(ba):
        total = jnp.zeros((share_rows, 2 * rows), jnp.float32)
        for j in range(ka):
            at = (h * ka + j) * 2 * share_rows
            real = crossed[at : at + share_rows]
            imag = crossed[at + share_rows : at + 2 * share_rows]
            total = jnp.where(lane_j == j, jnp.where(straight, real, sign * imag), total)
        kernel.append(total)
    return jnp.concatenate(kernel, 0)


def near_kernel(ka, ba, dims, *refs):
    vloc, val_count, cond_count, npol = dims
    screen_real, screen_imag, table, extras = refs[:4]
    halves, cond_in, out = refs[4 : -1 - ba], refs[-1 - ba : -1], refs[-1]
    codes = val_count * cond_count
    columns = columns_of(lax.axis_index("ga"), halves[0].shape[1])
    wide, turned = with_turned(halves, vloc * val_count)
    real = jnp.concatenate([wide, turned], 0).astype(jnp.bfloat16)
    imag = jnp.concatenate([turned, -wide], 0).astype(jnp.bfloat16)
    form = (((1,), (1,)), ((), ()))
    fields = lax.dot_general(
        screen_real[:, columns], real, form, preferred_element_type=jnp.float32
    ) + lax.dot_general(screen_imag[:, columns], imag, form, preferred_element_type=jnp.float32)
    both = jnp.concatenate(split(fields), 1)
    cond = jnp.concatenate([ref[...] for ref in cond_in], 0)
    crossed = jnp.dot(cond, both, preferred_element_type=jnp.float32)
    half = crossed.shape[1] // 2
    crossed = crossed[:, :half] + crossed[:, half:]
    kernel = diagonal(crossed, ka, ba, cond_count // ba * cond_count, -1.0)
    out[:codes, :] = placed_piece(kernel, table, dims, ba)
    out[codes:, :] = extras[...]


def near(ka, ba, dims, screening, table, extras, halves, cond_all):
    vloc, val_count, cond_count, npol = dims
    codes = val_count * cond_count
    operands = [*screening, table, extras, *halves, *cond_all]
    rows, width = sum(half.shape[0] for half in halves), halves[0].shape[1]
    return pl.pallas_call(
        functools.partial(near_kernel, ka, ba, dims),
        out_shape=in_vmem((codes + EXTRA_ROWS, 2 * ka * codes), jnp.float32),
        in_specs=[vmem] * len(operands),
        out_specs=vmem,
        cost_estimate=pl.CostEstimate(
            flops=8 * screening[0].shape[0] * width * rows, bytes_accessed=screening[0].size, transcendentals=0
        ),
        compiler_params=limits(*operands),
        name="near",
    )(*operands)


def couple_kernel(ka, ga, ba, share_rows, screen_real, screen_imag, *refs):
    cond_in, outs = refs[:ba], refs[ba:]
    mine = lax.axis_index("ga")
    wide = jnp.concatenate([ref[...].astype(jnp.float32) for ref in cond_in], 0)
    straight, turned = [], []
    for at in range(0, wide.shape[0], 2 * share_rows):
        real, imag = wide[at : at + share_rows], wide[at + share_rows : at + 2 * share_rows]
        straight += [real, -imag]
        turned += [imag, real]
    straight = jnp.concatenate(straight, 0).astype(jnp.bfloat16)
    turned = jnp.concatenate(turned, 0).astype(jnp.bfloat16)
    width = screen_real.shape[1] // ga
    for r in range(1, ga):
        columns = columns_of(origin(mine, r, ga), width)
        coupled = jnp.dot(
            straight, screen_real[:, columns], preferred_element_type=jnp.float32
        ) + jnp.dot(turned, screen_imag[:, columns], preferred_element_type=jnp.float32)
        high, low = split(coupled)
        outs[r - 1][: coupled.shape[0], :] = high
        outs[r - 1][coupled.shape[0] :, :] = low


def couple(ka, ga, ba, dims, screening, cond_all):
    share_rows = dims[2] // ba * dims[2]
    rows = 2 * sum(x.shape[0] for x in cond_all)
    width = screening[0].shape[1] // ga
    operands = [*screening, *cond_all]
    return pl.pallas_call(
        functools.partial(couple_kernel, ka, ga, ba, share_rows),
        out_shape=[in_vmem((rows, width), jnp.bfloat16)] * (ga - 1),
        in_specs=[vmem] * len(operands),
        out_specs=[vmem] * (ga - 1),
        cost_estimate=pl.CostEstimate(
            flops=4 * screening[0].size * rows, bytes_accessed=screening[0].size, transcendentals=0
        ),
        compiler_params=limits(*operands),
        name="couple",
    )(*operands)


def far_kernel(ka, ba, dims, *refs):
    vloc, val_count, cond_count, npol = dims
    table, held, out = refs[0], refs[1], refs[-1]
    count = lax.axis_size("ga") - 1
    each = (len(refs) - 3 - count) // count
    codes = val_count * cond_count
    crossed = None
    for r in range(count):
        coupled = refs[2 + r]
        halves = refs[2 + count + r * each : 2 + count + (r + 1) * each]
        rows = jnp.concatenate(with_turned(halves, vloc * val_count), 0).astype(jnp.bfloat16)
        term = lax.dot_general(
            coupled[...], rows, (((1,), (1,)), ((), ())), preferred_element_type=jnp.float32
        )
        crossed = term if crossed is None else crossed + term
    half = crossed.shape[0] // 2
    crossed = crossed[:half] + crossed[half:]
    kernel = diagonal(crossed, ka, ba, cond_count // ba * cond_count, 1.0)
    out[:codes, :] = held[:codes, :] + placed_piece(kernel, table, dims, ba)
    out[codes:, :] = held[codes:, :]


def far(ka, ba, dims, table, held, coupled, val_far):
    operands = [table, held, *coupled, *val_far]
    return pl.pallas_call(
        functools.partial(far_kernel, ka, ba, dims),
        out_shape=in_vmem(held.shape, jnp.float32),
        in_specs=[vmem] * len(operands),
        out_specs=vmem,
        compiler_params=limits(*operands),
        name="far",
    )(*operands)


def haydock_kernel(ka, codes, scale_count, npol, *refs):
    pieces = refs[:-3]
    next_out, coef_out, matrix = refs[-3:]
    lanes = pieces[0].shape[1]
    mid = lanes // 2
    height = codes + EXTRA_ROWS
    found = [(ref, at) for ref in pieces for at in range(0, ref.shape[0], height)]
    extras = None
    slots = []
    for ref, at in found:
        rows = ref[at + codes : at + height, :]
        extras = rows if extras is None else extras + rows
        slots.append((ref[at : at + codes, :], rows[npol + 2 : npol + 3]))
    own = pieces[0][codes:height, :]
    sign = jnp.where(iota((1, lanes), 1) < mid, -1.0, 1.0)
    for k2 in range(ka):
        block = jnp.zeros((codes, lanes), jnp.float32)
        for piece, second in slots:
            block = jnp.where(second == float(k2), piece, block)
        matrix[k2 * codes : (k2 + 1) * codes, :] = block
        matrix[mid + k2 * codes : mid + (k2 + 1) * codes, :] = sign * pltpu.roll(block, mid, 1)
    high, low = split(matrix[...])
    full = jnp.concatenate([high, low], 1)
    start = extras[:npol]
    energy = extras[npol : npol + 1]

    def halves(vector):
        top = vector.astype(jnp.bfloat16).astype(jnp.float32)
        return jnp.concatenate([top, vector - top], 0).astype(jnp.bfloat16)

    def mean(values):
        return jnp.sum(values, axis=1, keepdims=True) / scale_count

    def norm(vector):
        return jnp.sqrt(mean(vector * vector) + EPSILON)

    def swap(vector):
        return pltpu.roll(vector, mid, 1)

    def hamiltonian(vector):
        product = jnp.dot(halves(vector), full, preferred_element_type=jnp.float32)
        main = product[:npol, :lanes] + product[npol:, :lanes]
        return energy * vector - (main + product[:npol, lanes:])

    def inner(left, right):
        return mean(left * right), mean(-sign * left * swap(right))

    def times(real, imag, vector):
        return real * vector + imag * (sign * swap(vector))

    start_image = hamiltonian(start)
    scale = 1.0 / norm(start)
    first = start * scale
    first_image = start_image * scale
    alpha_real, alpha_imag = inner(first, first_image)
    first_resid = first_image - times(alpha_real, alpha_imag, first)
    resid_image = hamiltonian(first_resid)
    beta_one = norm(first_resid)
    scale = 1.0 / beta_one
    second = first_resid * scale
    second_image = resid_image * scale
    gamma_real, gamma_imag = inner(second, second_image)
    second_resid = second_image - times(gamma_real, gamma_imag, second) - beta_one * first
    beta_two = norm(second_resid)

    coef_lane = iota(coef_out.shape, 1)
    coefs = jnp.zeros(coef_out.shape, jnp.float32)
    for at, value in enumerate((alpha_real, alpha_imag, gamma_real, gamma_imag, beta_one, beta_two)):
        coefs = jnp.where(coef_lane == at, value, coefs)
    coef_out[...] = coefs
    row = iota((2 * codes, lanes), 0)
    lane = iota((2 * codes, lanes), 1)
    here = (lane % mid // codes == lax.axis_index("ka")) & (lane // mid == row // codes)
    band = (row % codes).astype(jnp.float32)
    pick = jnp.where(here & (own[npol + 1 : npol + 2] == band), 1.0, 0.0).astype(jnp.bfloat16)
    picked = lax.dot_general(
        halves(second_resid), pick, (((1,), (1,)), ((), ())), preferred_element_type=jnp.float32
    )
    picked = (picked[:npol] + picked[npol:]) / beta_two
    next_out[0, :, 0, :] = picked[:, :codes]
    next_out[0, :, 1, :] = picked[:, codes:]


def haydock(ka, codes, scale_count, npol, pieces):
    lanes = pieces[0].shape[1]
    square = jax.ShapeDtypeStruct((lanes, lanes), jnp.float32)
    return pl.pallas_call(
        functools.partial(haydock_kernel, ka, codes, scale_count, npol),
        out_shape=[
            jax.ShapeDtypeStruct((1, npol, 2, codes), jnp.float32),
            jax.ShapeDtypeStruct((npol, 6), jnp.float32),
        ],
        in_specs=[vmem] * len(pieces),
        out_specs=[vmem, vmem],
        scratch_shapes=[pltpu.VMEM(square.shape, square.dtype)],
        compiler_params=limits(*pieces, square),
        name="haydock",
    )(*pieces)


def summed(value, axis):
    size = lax.axis_size(axis)
    if size & (size - 1):
        return value + sum(shifted(value, axis, step) for step in range(1, size))
    step = 1
    while step < size:
        value = value + exchanged(value, axis, lambda i, size: i ^ step)
        step *= 2
    return value


def local(
    ka,
    ga,
    ba,
    start_vector,
    valence_density,
    conduction_density,
    screening,
    qpoint_map,
    slot_owner,
    band_pairs,
    valence_energy,
    conduction_energy,
):
    npol = start_vector.shape[1]
    pair_count = start_vector.shape[3]
    kcount, vloc, val_count = qpoint_map.shape[0], valence_density.shape[3], valence_density.shape[4]
    cond_count = conduction_density.shape[3]
    pairs = vloc * val_count
    dims = (vloc, val_count, cond_count, npol)
    packed = pack(ka, ba, qpoint_map, slot_owner, valence_density, conduction_density)
    blocks = [packed[0]] + [shifted(packed[j], "ka", j) for j in range(1, ka)]
    real, near_table, far_table, extras = prepare(
        ka,
        dims,
        qpoint_map,
        slot_owner,
        band_pairs,
        valence_energy,
        conduction_energy,
        start_vector,
        screening,
        packed[0],
    )
    early = ka // 2
    val_early = regroup(blocks[:early], 0, 2 * pairs, (extras,))
    far_early = [shifted(val_early, "ga", r) for r in range(1, ga)]
    imag = load_imaginary(screening, val_early)
    whole = (real, imag)
    val_late = regroup(blocks[early:], 0, 2 * pairs, (imag,))
    far_late = [shifted(val_late, "ga", r) for r in range(1, ga)]
    cond_half = regroup(blocks, 2 * pairs, blocks[0].shape[0], (val_late, *far_early))
    cond_all = [cond_half] + [handed(cond_half, r) for r in range(1, ba)]
    piece = near(ka, ba, dims, whole, near_table, extras, [val_early, val_late], cond_all)
    if ga > 1:
        coupled = couple(ka, ga, ba, dims, whole, cond_all)
        val_far = [half for both in zip(far_early, far_late) for half in both]
        piece = far(ka, ba, dims, far_table, piece, coupled, val_far)
    piece = piece + sum(handed(piece, r) for r in range(1, ba))
    piece = summed(piece, "ga")
    pieces = [piece] + [shifted(piece, "ka", j) for j in reversed(range(1, ka))]
    scale_count = float(kcount * pair_count)
    return tuple(haydock(ka, pair_count, scale_count, npol, pieces))


def solution(mesh):
    in_specs = (
        P(("grp", "ka"), None, None, None),
        P(("grp", "ka"), None, None, "ba", None, "ga"),
        P(("grp", "ka"), None, None, None, None, "ga"),
        P(("grp", "ka"), None, "ga", None),
        P(),
        P(),
        P(),
        P(("grp", "ka"), None),
        P(("grp", "ka"), None),
    )
    out_specs = (P(("grp", "ka"), None, None, None), P("grp", None))
    body = functools.partial(local, mesh.shape["ka"], mesh.shape["ga"], mesh.shape["ba"])
    return jax.shard_map(body, mesh=mesh, in_specs=in_specs, out_specs=out_specs, check_vma=False)
```

```python
import functools
import math

import jax
import jax.numpy as jnp
from jax import lax
from jax.experimental import pallas as pl
from jax.experimental.pallas import tpu as pltpu
from jax.sharding import PartitionSpec as P

EPSILON = 1e-06
EXACT = lax.Precision.HIGHEST
VMEM_LEAST = 8 * 1024 * 1024
VMEM_MOST = 56 * 1024 * 1024

vmem = pl.BlockSpec(memory_space=pltpu.VMEM)
anywhere = pl.BlockSpec(memory_space=pl.ANY)
EXTRA_ROWS = 8
LIGHT = pl.CostEstimate(flops=1, bytes_accessed=1, transcendentals=0)
CHUNKS = 4


def in_vmem(shape, dtype):
    return pltpu.VMEM(shape, dtype)


def placed(value, space):
    return pltpu.with_memory_space_constraint(value, space)


def iota(shape, axis):
    return lax.broadcasted_iota(jnp.int32, shape, axis)


def split(values):
    high = values.astype(jnp.bfloat16)
    low = (values - high.astype(jnp.float32)).astype(jnp.bfloat16)
    return high, low


def limits(*arrays):
    held = sum(math.prod(a.shape) * a.dtype.itemsize for a in arrays)
    return pltpu.CompilerParams(vmem_limit_bytes=min(VMEM_MOST, VMEM_LEAST + 4 * held))


def target(me, step, size):
    return lax.rem(me + step, size)


def origin(me, step, size):
    return lax.rem(me + size - step, size)


def exchanged(value, axis, move):
    size, cores = lax.axis_size(axis), lax.axis_size("ba")
    pairs = [
        (i * cores + h, move(i, size) * cores + (h + 1) % cores)
        for i in range(size)
        for h in range(cores)
    ]
    return lax.ppermute(value, (axis, "ba"), pairs)


def shifted(value, axis, step):
    return exchanged(value, axis, lambda i, size: (i + step) % size)


def handed(value, step):
    size = lax.axis_size("ba")
    return lax.ppermute(value, "ba", [(h, (h + step) % size) for h in range(size)])


def pack_kernel(ka, qmap_in, owner_in, valence_in, conduction_in, *rest):
    outs = rest[:ka]
    qmap, owner, partner, valence, conduction, sems = rest[ka:]
    copies = [
        pltpu.make_async_copy(src, dst, sems.at[at])
        for at, (src, dst) in enumerate(
            ((qmap_in, qmap), (owner_in, owner), (valence_in, valence), (conduction_in, conduction))
        )
    ]
    for copy in copies:
        copy.start()
    me = lax.axis_index("ka")
    half = lax.axis_index("ba")
    count, width = valence.shape[1], valence.shape[5]
    cond_count = conduction.shape[3]
    share = cond_count // lax.axis_size("ba")
    val_rows = 2 * valence.shape[3] * valence.shape[4]
    cond_rows = 2 * share * cond_count

    def note(k2, carry):
        partner[owner[qmap[me, k2]]] = k2
        return carry

    copies[0].wait()
    copies[1].wait()
    lax.fori_loop(0, count, note, 0)
    copies[2].wait()
    copies[3].wait()
    for at in range(ka):
        k2 = partner[target(me, at, ka)]
        block = valence[0, k2].astype(jnp.float32).reshape(val_rows, width)
        outs[at][:val_rows, :] = block.astype(jnp.bfloat16)
        to = lax.rem(half + min(at, 1), lax.axis_size("ba"))
        block = conduction[0, k2, :, pl.ds(to * share, share)].astype(jnp.float32)
        outs[at][val_rows:, :] = block.reshape(cond_rows, width).astype(jnp.bfloat16)


def pack(ka, ba, qmap, owner, valence, conduction):
    cond_count = conduction.shape[3]
    rows = 2 * valence.shape[3] * valence.shape[4] + 2 * cond_count // ba * cond_count
    shape = in_vmem((rows, valence.shape[5]), valence.dtype)
    operands = [placed(x, pltpu.HBM) for x in (qmap, owner, valence, conduction)]
    return pl.pallas_call(
        functools.partial(pack_kernel, ka),
        out_shape=[shape] * ka,
        in_specs=[anywhere] * 4,
        out_specs=[vmem] * ka,
        scratch_shapes=[
            pltpu.SMEM(qmap.shape, jnp.int32),
            pltpu.SMEM(owner.shape, jnp.int32),
            pltpu.SMEM(owner.shape, jnp.int32),
            pltpu.VMEM(valence.shape, valence.dtype),
            pltpu.VMEM(conduction.shape, conduction.dtype),
            pltpu.SemaphoreType.DMA((4,)),
        ],
        compiler_params=limits(valence, conduction),
        name="pack",
    )(*operands)


def prepare_kernel(ka, dims, *refs):
    vloc, val_count, cond_count, npol = dims
    ins, screening, (screen_out, near_table, far_table, extras), scratch = refs[:6], refs[6], refs[8:12], refs[12:]
    qmap, owner, band_pairs, val_energy, cond_energy, start, sems, screen_sems = scratch
    me = lax.axis_index("ka")
    half = lax.axis_index("ba")
    mine = lax.axis_index("ga")
    copies = [
        pltpu.make_async_copy(src, dst, sems.at[at])
        for at, (src, dst) in enumerate(
            zip(ins, (qmap, owner, band_pairs, val_energy, cond_energy, start))
        )
    ]
    height = screening.shape[2] // CHUNKS
    chunks = [
        pltpu.make_async_copy(
            screening.at[0, part, pl.ds(c * height, height)],
            screen_out.at[part, pl.ds(c * height, height)],
            screen_sems.at[part, c],
        )
        for part in range(2)
        for c in range(CHUNKS)
    ]
    for copy in copies + chunks:
        copy.start()
    pairs = vloc * val_count
    block = 2 * pairs
    rows = ka * block
    codes = val_count * cond_count
    mid = ka * codes
    lanes = 2 * mid
    row = iota((2 * rows, lanes), 0)
    col = iota((2 * rows, lanes), 1)
    j_of_row = row % rows // block
    cores = lax.axis_size("ba")
    for moves, table in enumerate((near_table, far_table)):
        share = lax.rem(half + 2 * cores - moves - jnp.where(j_of_row == 0, 0, 1), cores)
        want = (
            (row % block // pairs) * mid
            + origin(me, j_of_row, ka) * codes
            + (share * vloc + row % pairs // val_count) * cond_count
        )
        joined = (col - want >= 0) & (col - want < cond_count)
        for v2 in range(val_count):
            pick = jnp.where(joined & (row % val_count == v2), 1.0, 0.0)
            table[:, v2 * lanes : (v2 + 1) * lanes] = pick.astype(jnp.bfloat16)

    for copy in copies:
        copy.wait()
    first = jnp.where((mine == 0) & (half == 0), 1.0, 0.0)
    lane = iota((1, lanes), 1)
    lane_k = lane % mid // codes
    band_row = iota((codes, lanes), 0)
    band_lane = iota((codes, lanes), 1)
    code = jnp.zeros((codes, lanes), jnp.int32)
    bands = jnp.full((1, lanes), -1.0, jnp.float32)
    for b in range(codes):
        code = jnp.where(band_row == b, band_pairs[b], code)
        bands = jnp.where(lane % codes == band_pairs[b], float(b), bands)
    vectors = jnp.zeros((npol, lanes), jnp.float32)
    for part in range(2):
        spot = part * mid + me * codes
        pick = jnp.where(band_lane == spot + code, first, 0.0)
        vectors = vectors + jnp.dot(start[0, :, part, :], pick, precision=EXACT)
    energy = jnp.zeros((1, lanes), jnp.float32)
    for c in range(cond_count):
        energy = jnp.where(lane % cond_count == c, cond_energy[0, c], energy)
    for v in range(val_count):
        energy = energy - jnp.where(lane % codes // cond_count == v, val_energy[0, v], 0.0)
    energy = jnp.where(lane_k == me, energy * first, 0.0)
    kcount = qmap.shape[0]

    def find(k2, found):
        return jnp.where(owner[qmap[0, k2]] == me, k2, found)

    back = lax.fori_loop(0, kcount, find, 0)
    second = lane_k + back
    second = jnp.where(second >= kcount, second - kcount, second).astype(jnp.float32) * first
    rest = jnp.zeros((EXTRA_ROWS - 3 - npol, lanes), jnp.float32)
    extras[...] = jnp.concatenate([vectors, energy, bands * first, second, rest], 0)
    for copy in chunks:
        copy.wait()


def prepare(ka, dims, qmap, owner, band_pairs, val_energy, cond_energy, start, screening, after):
    vloc, val_count, cond_count, npol = dims
    rows = 4 * ka * vloc * val_count
    lanes = 2 * ka * val_count * cond_count
    operands = (qmap, owner, band_pairs, val_energy, cond_energy, start, screening)
    table = jax.ShapeDtypeStruct((rows, val_count * lanes), jnp.bfloat16)
    return pl.pallas_call(
        functools.partial(prepare_kernel, ka, dims),
        out_shape=[
            in_vmem(screening.shape[1:], screening.dtype),
            in_vmem(table.shape, table.dtype),
            in_vmem(table.shape, table.dtype),
            in_vmem((EXTRA_ROWS, lanes), jnp.float32),
        ],
        in_specs=[anywhere] * 8,
        out_specs=[vmem] * 4,
        scratch_shapes=[pltpu.SMEM(x.shape, x.dtype) for x in operands[:5]]
        + [
            pltpu.VMEM(start.shape, start.dtype),
            pltpu.SemaphoreType.DMA((6,)),
            pltpu.SemaphoreType.DMA((2, CHUNKS)),
        ],
        cost_estimate=pl.CostEstimate(
            flops=0, bytes_accessed=4 * screening.size, transcendentals=0
        ),
        compiler_params=limits(table),
        name="prepare",
    )(*[placed(x, pltpu.HBM) for x in operands], after)


def regroup_kernel(count, first, last, *refs):
    blocks, out = refs[:count], refs[-1]
    rows = last - first
    for at in range(count):
        out[at * rows : (at + 1) * rows, :] = blocks[at][first:last, :]


def regroup(blocks, first, last, after=()):
    shape = (len(blocks) * (last - first), blocks[0].shape[1])
    return pl.pallas_call(
        functools.partial(regroup_kernel, len(blocks), first, last),
        out_shape=in_vmem(shape, blocks[0].dtype),
        in_specs=[vmem] * len(blocks) + [anywhere] * len(after),
        out_specs=vmem,
        compiler_params=limits(*blocks),
        name="regroup",
    )(*blocks, *after)


def with_turned(halves, pairs):
    wide = jnp.concatenate([half[...].astype(jnp.float32) for half in halves], 0)
    parts = []
    for at in range(0, wide.shape[0], 2 * pairs):
        parts += [-wide[at + pairs : at + 2 * pairs], wide[at : at + pairs]]
    return wide, jnp.concatenate(parts, 0)


def columns_of(place, width):
    return pl.ds(pl.multiple_of(place * width, 128), width)


def placed_piece(kernel, table, dims, ba):
    vloc, val_count, cond_count, npol = dims
    half = lax.axis_index("ba")
    codes = val_count * cond_count
    lanes = table.shape[1] // val_count
    share = cond_count // ba
    cond_rows = cond_count * cond_count
    spread = jnp.dot(
        jnp.concatenate(split(kernel), 0), table[...], preferred_element_type=jnp.float32
    )
    spread = spread[:cond_rows] + spread[cond_rows:]
    crow = iota((cond_rows, lanes), 0)
    share_rows = share * cond_count
    c_of_row = origin(half, crow // share_rows, ba) * share + crow % share_rows // cond_count
    same_c = c_of_row == iota((cond_rows, lanes), 1) % cond_count
    spread = jnp.concatenate(
        [
            jnp.where(same_c, spread[:, v2 * lanes : (v2 + 1) * lanes], 0.0)
            for v2 in range(val_count)
        ],
        0,
    )
    out_row = iota((codes, val_count * cond_rows), 0)
    out_col = iota((codes, val_count * cond_rows), 1)
    fold = (out_row // cond_count == out_col // cond_rows) & (
        out_row % cond_count == out_col % cond_count
    )
    fold = jnp.where(fold, 1.0, 0.0).astype(jnp.bfloat16)
    piece = jnp.dot(fold, jnp.concatenate(split(spread), 1), preferred_element_type=jnp.float32)
    return piece[:, :lanes] + piece[:, lanes:]


def diagonal(crossed, ka, ba, share_rows, sign):
    rows = crossed.shape[1] // 2
    lane = iota((share_rows, 2 * rows), 1)
    lane_j = lane % rows // (rows // ka)
    straight = lane < rows
    kernel = []
    for h in range(ba):
        total = jnp.zeros((share_rows, 2 * rows), jnp.float32)
        for j in range(ka):
            at = (h * ka + j) * 2 * share_rows
            real = crossed[at : at + share_rows]
            imag = crossed[at + share_rows : at + 2 * share_rows]
            total = jnp.where(lane_j == j, jnp.where(straight, real, sign * imag), total)
        kernel.append(total)
    return jnp.concatenate(kernel, 0)


def near_kernel(ka, ba, dims, *refs):
    vloc, val_count, cond_count, npol = dims
    screening, table, extras = refs[:3]
    halves, cond_in, out = refs[3 : -1 - ba], refs[-1 - ba : -1], refs[-1]
    codes = val_count * cond_count
    columns = columns_of(lax.axis_index("ga"), halves[0].shape[1])
    wide, turned = with_turned(halves, vloc * val_count)
    real = jnp.concatenate([wide, turned], 0).astype(jnp.bfloat16)
    imag = jnp.concatenate([turned, -wide], 0).astype(jnp.bfloat16)
    form = (((1,), (1,)), ((), ()))
    fields = lax.dot_general(
        screening[0, :, columns], real, form, preferred_element_type=jnp.float32
    ) + lax.dot_general(screening[1, :, columns], imag, form, preferred_element_type=jnp.float32)
    both = jnp.concatenate(split(fields), 1)
    cond = jnp.concatenate([ref[...] for ref in cond_in], 0)
    crossed = jnp.dot(cond, both, preferred_element_type=jnp.float32)
    half = crossed.shape[1] // 2
    crossed = crossed[:, :half] + crossed[:, half:]
    kernel = diagonal(crossed, ka, ba, cond_count // ba * cond_count, -1.0)
    out[:codes, :] = placed_piece(kernel, table, dims, ba)
    out[codes:, :] = extras[...]


def near(ka, ba, dims, screening, table, extras, halves, cond_all):
    vloc, val_count, cond_count, npol = dims
    codes = val_count * cond_count
    operands = [screening, table, extras, *halves, *cond_all]
    return pl.pallas_call(
        functools.partial(near_kernel, ka, ba, dims),
        out_shape=in_vmem((codes + EXTRA_ROWS, 2 * ka * codes), jnp.float32),
        in_specs=[vmem] * len(operands),
        out_specs=vmem,
        cost_estimate=LIGHT,
        compiler_params=limits(*operands),
        name="near",
    )(*operands)


def couple_kernel(ka, ga, ba, share_rows, screening, *refs):
    cond_in, outs = refs[:ba], refs[ba:]
    mine = lax.axis_index("ga")
    wide = jnp.concatenate([ref[...].astype(jnp.float32) for ref in cond_in], 0)
    straight, turned = [], []
    for at in range(0, wide.shape[0], 2 * share_rows):
        real, imag = wide[at : at + share_rows], wide[at + share_rows : at + 2 * share_rows]
        straight += [real, -imag]
        turned += [imag, real]
    straight = jnp.concatenate(straight, 0).astype(jnp.bfloat16)
    turned = jnp.concatenate(turned, 0).astype(jnp.bfloat16)
    width = screening.shape[2] // ga
    for r in range(1, ga):
        columns = columns_of(origin(mine, r, ga), width)
        coupled = jnp.dot(
            straight, screening[0, :, columns], preferred_element_type=jnp.float32
        ) + jnp.dot(turned, screening[1, :, columns], preferred_element_type=jnp.float32)
        high, low = split(coupled)
        outs[r - 1][: coupled.shape[0], :] = high
        outs[r - 1][coupled.shape[0] :, :] = low


def couple(ka, ga, ba, dims, screening, cond_all):
    share_rows = dims[2] // ba * dims[2]
    rows = 2 * sum(x.shape[0] for x in cond_all)
    width = screening.shape[2] // ga
    operands = [screening, *cond_all]
    return pl.pallas_call(
        functools.partial(couple_kernel, ka, ga, ba, share_rows),
        out_shape=[in_vmem((rows, width), jnp.bfloat16)] * (ga - 1),
        in_specs=[vmem] * len(operands),
        out_specs=[vmem] * (ga - 1),
        cost_estimate=LIGHT,
        compiler_params=limits(*operands),
        name="couple",
    )(*operands)


def far_kernel(ka, ba, dims, *refs):
    vloc, val_count, cond_count, npol = dims
    table, held, out = refs[0], refs[1], refs[-1]
    count = lax.axis_size("ga") - 1
    each = (len(refs) - 3 - count) // count
    codes = val_count * cond_count
    crossed = None
    for r in range(count):
        coupled = refs[2 + r]
        halves = refs[2 + count + r * each : 2 + count + (r + 1) * each]
        rows = jnp.concatenate(with_turned(halves, vloc * val_count), 0).astype(jnp.bfloat16)
        term = lax.dot_general(
            coupled[...], rows, (((1,), (1,)), ((), ())), preferred_element_type=jnp.float32
        )
        crossed = term if crossed is None else crossed + term
    half = crossed.shape[0] // 2
    crossed = crossed[:half] + crossed[half:]
    kernel = diagonal(crossed, ka, ba, cond_count // ba * cond_count, 1.0)
    out[:codes, :] = held[:codes, :] + placed_piece(kernel, table, dims, ba)
    out[codes:, :] = held[codes:, :]


def far(ka, ba, dims, table, held, coupled, val_far):
    operands = [table, held, *coupled, *val_far]
    return pl.pallas_call(
        functools.partial(far_kernel, ka, ba, dims),
        out_shape=in_vmem(held.shape, jnp.float32),
        in_specs=[vmem] * len(operands),
        out_specs=vmem,
        compiler_params=limits(*operands),
        name="far",
    )(*operands)


def haydock_kernel(ka, codes, scale_count, npol, *refs):
    pieces = refs[:-3]
    next_out, coef_out, matrix = refs[-3:]
    lanes = pieces[0].shape[1]
    mid = lanes // 2
    height = codes + EXTRA_ROWS
    found = [(ref, at) for ref in pieces for at in range(0, ref.shape[0], height)]
    extras = None
    slots = []
    for ref, at in found:
        rows = ref[at + codes : at + height, :]
        extras = rows if extras is None else extras + rows
        slots.append((ref[at : at + codes, :], rows[npol + 2 : npol + 3]))
    own = pieces[0][codes:height, :]
    sign = jnp.where(iota((1, lanes), 1) < mid, -1.0, 1.0)
    for k2 in range(ka):
        block = jnp.zeros((codes, lanes), jnp.float32)
        for piece, second in slots:
            block = jnp.where(second == float(k2), piece, block)
        matrix[k2 * codes : (k2 + 1) * codes, :] = block
        matrix[mid + k2 * codes : mid + (k2 + 1) * codes, :] = sign * pltpu.roll(block, mid, 1)
    high, low = split(matrix[...])
    full = jnp.concatenate([high, low], 1)
    start = extras[:npol]
    energy = extras[npol : npol + 1]

    def halves(vector):
        top = vector.astype(jnp.bfloat16).astype(jnp.float32)
        return jnp.concatenate([top, vector - top], 0).astype(jnp.bfloat16)

    def mean(values):
        return jnp.sum(values, axis=1, keepdims=True) / scale_count

    def norm(vector):
        return jnp.sqrt(mean(vector * vector) + EPSILON)

    def swap(vector):
        return pltpu.roll(vector, mid, 1)

    def hamiltonian(vector):
        product = jnp.dot(halves(vector), full, preferred_element_type=jnp.float32)
        main = product[:npol, :lanes] + product[npol:, :lanes]
        return energy * vector - (main + product[:npol, lanes:])

    def inner(left, right):
        return mean(left * right), mean(-sign * left * swap(right))

    def times(real, imag, vector):
        return real * vector + imag * (sign * swap(vector))

    start_image = hamiltonian(start)
    scale = 1.0 / norm(start)
    first = start * scale
    first_image = start_image * scale
    alpha_real, alpha_imag = inner(first, first_image)
    first_resid = first_image - times(alpha_real, alpha_imag, first)
    resid_image = hamiltonian(first_resid)
    beta_one = norm(first_resid)
    scale = 1.0 / beta_one
    second = first_resid * scale
    second_image = resid_image * scale
    gamma_real, gamma_imag = inner(second, second_image)
    second_resid = second_image - times(gamma_real, gamma_imag, second) - beta_one * first
    beta_two = norm(second_resid)

    coef_lane = iota(coef_out.shape, 1)
    coefs = jnp.zeros(coef_out.shape, jnp.float32)
    for at, value in enumerate((alpha_real, alpha_imag, gamma_real, gamma_imag, beta_one, beta_two)):
        coefs = jnp.where(coef_lane == at, value, coefs)
    coef_out[...] = coefs
    row = iota((2 * codes, lanes), 0)
    lane = iota((2 * codes, lanes), 1)
    here = (lane % mid // codes == lax.axis_index("ka")) & (lane // mid == row // codes)
    band = (row % codes).astype(jnp.float32)
    pick = jnp.where(here & (own[npol + 1 : npol + 2] == band), 1.0, 0.0).astype(jnp.bfloat16)
    picked = lax.dot_general(
        halves(second_resid), pick, (((1,), (1,)), ((), ())), preferred_element_type=jnp.float32
    )
    picked = (picked[:npol] + picked[npol:]) / beta_two
    next_out[0, :, 0, :] = picked[:, :codes]
    next_out[0, :, 1, :] = picked[:, codes:]


def haydock(ka, codes, scale_count, npol, pieces):
    lanes = pieces[0].shape[1]
    square = jax.ShapeDtypeStruct((lanes, lanes), jnp.float32)
    return pl.pallas_call(
        functools.partial(haydock_kernel, ka, codes, scale_count, npol),
        out_shape=[
            jax.ShapeDtypeStruct((1, npol, 2, codes), jnp.float32),
            jax.ShapeDtypeStruct((npol, 6), jnp.float32),
        ],
        in_specs=[vmem] * len(pieces),
        out_specs=[vmem, vmem],
        scratch_shapes=[pltpu.VMEM(square.shape, square.dtype)],
        compiler_params=limits(*pieces, square),
        name="haydock",
    )(*pieces)


def summed(value, axis):
    size = lax.axis_size(axis)
    if size & (size - 1):
        return value + sum(shifted(value, axis, step) for step in range(1, size))
    step = 1
    while step < size:
        value = value + exchanged(value, axis, lambda i, size: i ^ step)
        step *= 2
    return value


def local(
    ka,
    ga,
    ba,
    start_vector,
    valence_density,
    conduction_density,
    screening,
    qpoint_map,
    slot_owner,
    band_pairs,
    valence_energy,
    conduction_energy,
):
    npol = start_vector.shape[1]
    pair_count = start_vector.shape[3]
    kcount, vloc, val_count = qpoint_map.shape[0], valence_density.shape[3], valence_density.shape[4]
    cond_count = conduction_density.shape[3]
    pairs = vloc * val_count
    dims = (vloc, val_count, cond_count, npol)
    packed = pack(ka, ba, qpoint_map, slot_owner, valence_density, conduction_density)
    blocks = [packed[0]] + [shifted(packed[j], "ka", j) for j in range(1, ka)]
    early = ka // 2
    val_early = regroup(blocks[:early], 0, 2 * pairs)
    far_early = [shifted(val_early, "ga", r) for r in range(1, ga)]
    whole, near_table, far_table, extras = prepare(
        ka,
        dims,
        qpoint_map,
        slot_owner,
        band_pairs,
        valence_energy,
        conduction_energy,
        start_vector,
        screening,
        val_early,
    )
    val_late = regroup(blocks[early:], 0, 2 * pairs, (extras,))
    far_late = [shifted(val_late, "ga", r) for r in range(1, ga)]
    cond_half = regroup(blocks, 2 * pairs, blocks[0].shape[0], (val_late, *far_early))
    cond_all = [cond_half] + [handed(cond_half, r) for r in range(1, ba)]
    piece = near(ka, ba, dims, whole, near_table, extras, [val_early, val_late], cond_all)
    if ga > 1:
        coupled = couple(ka, ga, ba, dims, whole, cond_all)
        val_far = [half for both in zip(far_early, far_late) for half in both]
        piece = far(ka, ba, dims, far_table, piece, coupled, val_far)
    piece = piece + sum(handed(piece, r) for r in range(1, ba))
    piece = summed(piece, "ga")
    pieces = [piece] + [shifted(piece, "ka", j) for j in reversed(range(1, ka))]
    scale_count = float(kcount * pair_count)
    return tuple(haydock(ka, pair_count, scale_count, npol, pieces))


def solution(mesh):
    in_specs = (
        P(("grp", "ka"), None, None, None),
        P(("grp", "ka"), None, None, "ba", None, "ga"),
        P(("grp", "ka"), None, None, None, None, "ga"),
        P(("grp", "ka"), None, "ga", None),
        P(),
        P(),
        P(),
        P(("grp", "ka"), None),
        P(("grp", "ka"), None),
    )
    out_specs = (P(("grp", "ka"), None, None, None), P("grp", None))
    body = functools.partial(local, mesh.shape["ka"], mesh.shape["ga"], mesh.shape["ba"])
    return jax.shard_map(body, mesh=mesh, in_specs=in_specs, out_specs=out_specs, check_vma=False)
```

```python
import functools
import math

import jax
import jax.numpy as jnp
from jax import lax
from jax.experimental import pallas as pl
from jax.experimental.pallas import tpu as pltpu
from jax.sharding import PartitionSpec as P

EPSILON = 1e-06
EXACT = lax.Precision.HIGHEST
VMEM_LEAST = 8 * 1024 * 1024
VMEM_MOST = 56 * 1024 * 1024

vmem = pl.BlockSpec(memory_space=pltpu.VMEM)
anywhere = pl.BlockSpec(memory_space=pl.ANY)
EXTRA_ROWS = 8
LIGHT = pl.CostEstimate(flops=1, bytes_accessed=1, transcendentals=0)
CHUNKS = 3


def in_vmem(shape, dtype):
    return pltpu.VMEM(shape, dtype)


def placed(value, space):
    return pltpu.with_memory_space_constraint(value, space)


def iota(shape, axis):
    return lax.broadcasted_iota(jnp.int32, shape, axis)


def split(values):
    high = values.astype(jnp.bfloat16)
    low = (values - high.astype(jnp.float32)).astype(jnp.bfloat16)
    return high, low


def limits(*arrays):
    held = sum(math.prod(a.shape) * a.dtype.itemsize for a in arrays)
    return pltpu.CompilerParams(vmem_limit_bytes=min(VMEM_MOST, VMEM_LEAST + 4 * held))


def target(me, step, size):
    return lax.rem(me + step, size)


def origin(me, step, size):
    return lax.rem(me + size - step, size)


def exchanged(value, axis, move):
    size, cores = lax.axis_size(axis), lax.axis_size("ba")
    pairs = [
        (i * cores + h, move(i, size) * cores + (h + 1) % cores)
        for i in range(size)
        for h in range(cores)
    ]
    return lax.ppermute(value, (axis, "ba"), pairs)


def shifted(value, axis, step):
    return exchanged(value, axis, lambda i, size: (i + step) % size)


def handed(value, step):
    size = lax.axis_size("ba")
    return lax.ppermute(value, "ba", [(h, (h + step) % size) for h in range(size)])


def pack_kernel(ka, qmap_in, owner_in, valence_in, conduction_in, *rest):
    outs = rest[:ka]
    qmap, owner, partner, valence, conduction, sems = rest[ka:]
    copies = [
        pltpu.make_async_copy(src, dst, sems.at[at])
        for at, (src, dst) in enumerate(
            ((qmap_in, qmap), (owner_in, owner), (valence_in, valence), (conduction_in, conduction))
        )
    ]
    for copy in copies:
        copy.start()
    me = lax.axis_index("ka")
    half = lax.axis_index("ba")
    count, width = valence.shape[1], valence.shape[5]
    cond_count = conduction.shape[3]
    share = cond_count // lax.axis_size("ba")
    val_rows = 2 * valence.shape[3] * valence.shape[4]
    cond_rows = 2 * share * cond_count

    def note(k2, carry):
        partner[owner[qmap[me, k2]]] = k2
        return carry

    copies[0].wait()
    copies[1].wait()
    lax.fori_loop(0, count, note, 0)
    copies[2].wait()
    copies[3].wait()
    for at in range(ka):
        k2 = partner[target(me, at, ka)]
        block = valence[0, k2].astype(jnp.float32).reshape(val_rows, width)
        outs[at][:val_rows, :] = block.astype(jnp.bfloat16)
        to = lax.rem(half + min(at, 1), lax.axis_size("ba"))
        block = conduction[0, k2, :, pl.ds(to * share, share)].astype(jnp.float32)
        outs[at][val_rows:, :] = block.reshape(cond_rows, width).astype(jnp.bfloat16)


def pack(ka, ba, qmap, owner, valence, conduction):
    cond_count = conduction.shape[3]
    rows = 2 * valence.shape[3] * valence.shape[4] + 2 * cond_count // ba * cond_count
    shape = in_vmem((rows, valence.shape[5]), valence.dtype)
    operands = [placed(x, pltpu.HBM) for x in (qmap, owner, valence, conduction)]
    return pl.pallas_call(
        functools.partial(pack_kernel, ka),
        out_shape=[shape] * ka,
        in_specs=[anywhere] * 4,
        out_specs=[vmem] * ka,
        scratch_shapes=[
            pltpu.SMEM(qmap.shape, jnp.int32),
            pltpu.SMEM(owner.shape, jnp.int32),
            pltpu.SMEM(owner.shape, jnp.int32),
            pltpu.VMEM(valence.shape, valence.dtype),
            pltpu.VMEM(conduction.shape, conduction.dtype),
            pltpu.SemaphoreType.DMA((4,)),
        ],
        compiler_params=limits(valence, conduction),
        name="pack",
    )(*operands)


def prepare_kernel(ka, dims, *refs):
    vloc, val_count, cond_count, npol = dims
    ins, screening, (screen_out, near_table, far_table, extras), scratch = refs[:6], refs[6], refs[8:12], refs[12:]
    qmap, owner, band_pairs, val_energy, cond_energy, start, sems, screen_sem = scratch
    me = lax.axis_index("ka")
    half = lax.axis_index("ba")
    mine = lax.axis_index("ga")
    copies = [
        pltpu.make_async_copy(src, dst, sems.at[at])
        for at, (src, dst) in enumerate(
            zip(ins, (qmap, owner, band_pairs, val_energy, cond_energy, start))
        )
    ]
    load = pltpu.make_async_copy(screening.at[0, 0], screen_out, screen_sem)
    for copy in copies + [load]:
        copy.start()
    pairs = vloc * val_count
    block = 2 * pairs
    rows = ka * block
    codes = val_count * cond_count
    mid = ka * codes
    lanes = 2 * mid
    row = iota((2 * rows, lanes), 0)
    col = iota((2 * rows, lanes), 1)
    j_of_row = row % rows // block
    cores = lax.axis_size("ba")
    for moves, table in enumerate((near_table, far_table)):
        share = lax.rem(half + 2 * cores - moves - jnp.where(j_of_row == 0, 0, 1), cores)
        want = (
            (row % block // pairs) * mid
            + origin(me, j_of_row, ka) * codes
            + (share * vloc + row % pairs // val_count) * cond_count
        )
        joined = (col - want >= 0) & (col - want < cond_count)
        for v2 in range(val_count):
            pick = jnp.where(joined & (row % val_count == v2), 1.0, 0.0)
            table[:, v2 * lanes : (v2 + 1) * lanes] = pick.astype(jnp.bfloat16)

    for copy in copies:
        copy.wait()
    first = jnp.where((mine == 0) & (half == 0), 1.0, 0.0)
    lane = iota((1, lanes), 1)
    lane_k = lane % mid // codes
    band_row = iota((codes, lanes), 0)
    band_lane = iota((codes, lanes), 1)
    code = jnp.zeros((codes, lanes), jnp.int32)
    bands = jnp.full((1, lanes), -1.0, jnp.float32)
    for b in range(codes):
        code = jnp.where(band_row == b, band_pairs[b], code)
        bands = jnp.where(lane % codes == band_pairs[b], float(b), bands)
    vectors = jnp.zeros((npol, lanes), jnp.float32)
    for part in range(2):
        spot = part * mid + me * codes
        pick = jnp.where(band_lane == spot + code, first, 0.0)
        vectors = vectors + jnp.dot(start[0, :, part, :], pick, precision=EXACT)
    energy = jnp.zeros((1, lanes), jnp.float32)
    for c in range(cond_count):
        energy = jnp.where(lane % cond_count == c, cond_energy[0, c], energy)
    for v in range(val_count):
        energy = energy - jnp.where(lane % codes // cond_count == v, val_energy[0, v], 0.0)
    energy = jnp.where(lane_k == me, energy * first, 0.0)
    kcount = qmap.shape[0]

    def find(k2, found):
        return jnp.where(owner[qmap[0, k2]] == me, k2, found)

    back = lax.fori_loop(0, kcount, find, 0)
    second = lane_k + back
    second = jnp.where(second >= kcount, second - kcount, second).astype(jnp.float32) * first
    rest = jnp.zeros((EXTRA_ROWS - 3 - npol, lanes), jnp.float32)
    extras[...] = jnp.concatenate([vectors, energy, bands * first, second, rest], 0)
    load.wait()


def prepare(ka, dims, qmap, owner, band_pairs, val_energy, cond_energy, start, screening, after):
    vloc, val_count, cond_count, npol = dims
    rows = 4 * ka * vloc * val_count
    lanes = 2 * ka * val_count * cond_count
    operands = (qmap, owner, band_pairs, val_energy, cond_energy, start, screening)
    table = jax.ShapeDtypeStruct((rows, val_count * lanes), jnp.bfloat16)
    return pl.pallas_call(
        functools.partial(prepare_kernel, ka, dims),
        out_shape=[
            in_vmem(screening.shape[2:], screening.dtype),
            in_vmem(table.shape, table.dtype),
            in_vmem(table.shape, table.dtype),
            in_vmem((EXTRA_ROWS, lanes), jnp.float32),
        ],
        in_specs=[anywhere] * 8,
        out_specs=[vmem] * 4,
        scratch_shapes=[pltpu.SMEM(x.shape, x.dtype) for x in operands[:5]]
        + [
            pltpu.VMEM(start.shape, start.dtype),
            pltpu.SemaphoreType.DMA((6,)),
            pltpu.SemaphoreType.DMA,
        ],
        cost_estimate=pl.CostEstimate(
            flops=0, bytes_accessed=2 * screening.size, transcendentals=0
        ),
        compiler_params=limits(table),
        name="prepare",
    )(*[placed(x, pltpu.HBM) for x in operands], after)


def regroup_kernel(count, first, last, *refs):
    blocks, out = refs[:count], refs[-1]
    rows = last - first
    for at in range(count):
        out[at * rows : (at + 1) * rows, :] = blocks[at][first:last, :]


def regroup(blocks, first, last, after=()):
    shape = (len(blocks) * (last - first), blocks[0].shape[1])
    return pl.pallas_call(
        functools.partial(regroup_kernel, len(blocks), first, last),
        out_shape=in_vmem(shape, blocks[0].dtype),
        in_specs=[vmem] * len(blocks) + [anywhere] * len(after),
        out_specs=vmem,
        compiler_params=limits(*blocks),
        name="regroup",
    )(*blocks, *after)


def with_turned(halves, pairs):
    wide = jnp.concatenate([half[...].astype(jnp.float32) for half in halves], 0)
    parts = []
    for at in range(0, wide.shape[0], 2 * pairs):
        parts += [-wide[at + pairs : at + 2 * pairs], wide[at : at + pairs]]
    return wide, jnp.concatenate(parts, 0)


def columns_of(place, width):
    return pl.ds(pl.multiple_of(place * width, 128), width)


def placed_piece(kernel, table, dims, ba):
    vloc, val_count, cond_count, npol = dims
    half = lax.axis_index("ba")
    codes = val_count * cond_count
    lanes = table.shape[1] // val_count
    share = cond_count // ba
    cond_rows = cond_count * cond_count
    spread = jnp.dot(
        jnp.concatenate(split(kernel), 0), table[...], preferred_element_type=jnp.float32
    )
    spread = spread[:cond_rows] + spread[cond_rows:]
    crow = iota((cond_rows, lanes), 0)
    share_rows = share * cond_count
    c_of_row = origin(half, crow // share_rows, ba) * share + crow % share_rows // cond_count
    same_c = c_of_row == iota((cond_rows, lanes), 1) % cond_count
    spread = jnp.concatenate(
        [
            jnp.where(same_c, spread[:, v2 * lanes : (v2 + 1) * lanes], 0.0)
            for v2 in range(val_count)
        ],
        0,
    )
    out_row = iota((codes, val_count * cond_rows), 0)
    out_col = iota((codes, val_count * cond_rows), 1)
    fold = (out_row // cond_count == out_col // cond_rows) & (
        out_row % cond_count == out_col % cond_count
    )
    fold = jnp.where(fold, 1.0, 0.0).astype(jnp.bfloat16)
    piece = jnp.dot(fold, jnp.concatenate(split(spread), 1), preferred_element_type=jnp.float32)
    return piece[:, :lanes] + piece[:, lanes:]


def diagonal(crossed, ka, ba, share_rows):
    rows = crossed.shape[1] // 2
    lane = iota((share_rows, 2 * rows), 1)
    lane_j = lane % rows // (rows // ka)
    straight = lane < rows
    kernel = []
    for h in range(ba):
        total = jnp.zeros((share_rows, 2 * rows), jnp.float32)
        for j in range(ka):
            at = (h * ka + j) * 2 * share_rows
            real = crossed[at : at + share_rows]
            imag = crossed[at + share_rows : at + 2 * share_rows]
            total = jnp.where(lane_j == j, jnp.where(straight, real, imag), total)
        kernel.append(total)
    return jnp.concatenate(kernel, 0)


def couple_kernel(ka, ga, ba, share_rows, screen_real, screening, *refs):
    cond_in, outs, (screen_imag, sems) = refs[:ba], refs[ba:-2], refs[-2:]
    height = screen_imag.shape[0] // CHUNKS
    chunks = [pl.ds(c * height, height) for c in range(CHUNKS)]
    loads = [
        pltpu.make_async_copy(screening.at[0, 1, chunk], screen_imag.at[chunk], sems.at[c])
        for c, chunk in enumerate(chunks)
    ]
    for load in loads:
        load.start()
    mine = lax.axis_index("ga")
    wide = jnp.concatenate([ref[...].astype(jnp.float32) for ref in cond_in], 0)
    straight, turned = [], []
    for at in range(0, wide.shape[0], 2 * share_rows):
        real, imag = wide[at : at + share_rows], wide[at + share_rows : at + 2 * share_rows]
        straight += [real, -imag]
        turned += [imag, real]
    straight = jnp.concatenate(straight, 0).astype(jnp.bfloat16)
    turned = jnp.concatenate(turned, 0).astype(jnp.bfloat16)
    width = screen_imag.shape[1] // ga
    columns = [columns_of(origin(mine, r, ga), width) for r in range(ga)]
    coupled = [
        jnp.dot(straight, screen_real[:, block], preferred_element_type=jnp.float32) for block in columns
    ]
    for c, load in enumerate(loads):
        load.wait()
        part = turned[:, c * height : (c + 1) * height]
        for r, block in enumerate(columns):
            coupled[r] = coupled[r] + jnp.dot(
                part, screen_imag[chunks[c], block], preferred_element_type=jnp.float32
            )
    for out, value in zip(outs, coupled):
        high, low = split(value)
        out[: value.shape[0], :] = high
        out[value.shape[0] :, :] = low


def couple(ka, ga, ba, dims, screen_real, screening, cond_all):
    share_rows = dims[2] // ba * dims[2]
    rows = 2 * sum(x.shape[0] for x in cond_all)
    width = screen_real.shape[1] // ga
    operands = [screen_real, *cond_all]
    return pl.pallas_call(
        functools.partial(couple_kernel, ka, ga, ba, share_rows),
        out_shape=[in_vmem((rows, width), jnp.bfloat16)] * ga,
        in_specs=[vmem, anywhere] + [vmem] * len(cond_all),
        out_specs=[vmem] * ga,
        scratch_shapes=[
            pltpu.VMEM(screen_real.shape, screen_real.dtype),
            pltpu.SemaphoreType.DMA((CHUNKS,)),
        ],
        cost_estimate=LIGHT,
        compiler_params=limits(*operands),
        name="couple",
    )(screen_real, placed(screening, pltpu.HBM), *cond_all)


def contract_kernel(ka, ba, count, dims, *refs):
    vloc, val_count, cond_count, npol = dims
    table, held, out = refs[0], refs[1], refs[-1]
    each = (len(refs) - 3 - count) // count
    codes = val_count * cond_count
    crossed = None
    for r in range(count):
        coupled = refs[2 + r]
        halves = refs[2 + count + r * each : 2 + count + (r + 1) * each]
        rows = jnp.concatenate(with_turned(halves, vloc * val_count), 0).astype(jnp.bfloat16)
        term = lax.dot_general(
            coupled[...], rows, (((1,), (1,)), ((), ())), preferred_element_type=jnp.float32
        )
        crossed = term if crossed is None else crossed + term
    half = crossed.shape[0] // 2
    crossed = crossed[:half] + crossed[half:]
    kernel = diagonal(crossed, ka, ba, cond_count // ba * cond_count)
    piece = placed_piece(kernel, table, dims, ba)
    before = held.shape[0] - EXTRA_ROWS
    out[:codes, :] = piece + held[:codes, :] if before else piece
    out[codes:, :] = held[before:, :]


def contract(ka, ba, dims, table, held, coupled, valence, name):
    val_count, cond_count = dims[1:3]
    operands = [table, held, *coupled, *valence]
    shape = (val_count * cond_count + EXTRA_ROWS, held.shape[1])
    return pl.pallas_call(
        functools.partial(contract_kernel, ka, ba, len(coupled), dims),
        out_shape=in_vmem(shape, jnp.float32),
        in_specs=[vmem] * len(operands),
        out_specs=vmem,
        cost_estimate=LIGHT,
        compiler_params=limits(*operands),
        name=name,
    )(*operands)


def haydock_kernel(ka, codes, scale_count, npol, *refs):
    pieces = refs[:-3]
    next_out, coef_out, matrix = refs[-3:]
    lanes = pieces[0].shape[1]
    mid = lanes // 2
    height = codes + EXTRA_ROWS
    found = [(ref, at) for ref in pieces for at in range(0, ref.shape[0], height)]
    extras = None
    slots = []
    for ref, at in found:
        rows = ref[at + codes : at + height, :]
        extras = rows if extras is None else extras + rows
        slots.append((ref[at : at + codes, :], rows[npol + 2 : npol + 3]))
    own = pieces[0][codes:height, :]
    sign = jnp.where(iota((1, lanes), 1) < mid, -1.0, 1.0)
    for k2 in range(ka):
        block = jnp.zeros((codes, lanes), jnp.float32)
        for piece, second in slots:
            block = jnp.where(second == float(k2), piece, block)
        matrix[k2 * codes : (k2 + 1) * codes, :] = block
        matrix[mid + k2 * codes : mid + (k2 + 1) * codes, :] = sign * pltpu.roll(block, mid, 1)
    high, low = split(matrix[...])
    full = jnp.concatenate([high, low], 1)
    start = extras[:npol]
    energy = extras[npol : npol + 1]

    def halves(vector):
        top = vector.astype(jnp.bfloat16).astype(jnp.float32)
        return jnp.concatenate([top, vector - top], 0).astype(jnp.bfloat16)

    def mean(values):
        return jnp.sum(values, axis=1, keepdims=True) / scale_count

    def norm(vector):
        return jnp.sqrt(mean(vector * vector) + EPSILON)

    def swap(vector):
        return pltpu.roll(vector, mid, 1)

    def hamiltonian(vector):
        product = jnp.dot(halves(vector), full, preferred_element_type=jnp.float32)
        main = product[:npol, :lanes] + product[npol:, :lanes]
        return energy * vector - (main + product[:npol, lanes:])

    def inner(left, right):
        return mean(left * right), mean(-sign * left * swap(right))

    def times(real, imag, vector):
        return real * vector + imag * (sign * swap(vector))

    start_image = hamiltonian(start)
    scale = 1.0 / norm(start)
    first = start * scale
    first_image = start_image * scale
    alpha_real, alpha_imag = inner(first, first_image)
    first_resid = first_image - times(alpha_real, alpha_imag, first)
    resid_image = hamiltonian(first_resid)
    beta_one = norm(first_resid)
    scale = 1.0 / beta_one
    second = first_resid * scale
    second_image = resid_image * scale
    gamma_real, gamma_imag = inner(second, second_image)
    second_resid = second_image - times(gamma_real, gamma_imag, second) - beta_one * first
    beta_two = norm(second_resid)

    coef_lane = iota(coef_out.shape, 1)
    coefs = jnp.zeros(coef_out.shape, jnp.float32)
    for at, value in enumerate((alpha_real, alpha_imag, gamma_real, gamma_imag, beta_one, beta_two)):
        coefs = jnp.where(coef_lane == at, value, coefs)
    coef_out[...] = coefs
    row = iota((2 * codes, lanes), 0)
    lane = iota((2 * codes, lanes), 1)
    here = (lane % mid // codes == lax.axis_index("ka")) & (lane // mid == row // codes)
    band = (row % codes).astype(jnp.float32)
    pick = jnp.where(here & (own[npol + 1 : npol + 2] == band), 1.0, 0.0).astype(jnp.bfloat16)
    picked = lax.dot_general(
        halves(second_resid), pick, (((1,), (1,)), ((), ())), preferred_element_type=jnp.float32
    )
    picked = (picked[:npol] + picked[npol:]) / beta_two
    next_out[0, :, 0, :] = picked[:, :codes]
    next_out[0, :, 1, :] = picked[:, codes:]


def haydock(ka, codes, scale_count, npol, pieces):
    lanes = pieces[0].shape[1]
    square = jax.ShapeDtypeStruct((lanes, lanes), jnp.float32)
    return pl.pallas_call(
        functools.partial(haydock_kernel, ka, codes, scale_count, npol),
        out_shape=[
            jax.ShapeDtypeStruct((1, npol, 2, codes), jnp.float32),
            jax.ShapeDtypeStruct((npol, 6), jnp.float32),
        ],
        in_specs=[vmem] * len(pieces),
        out_specs=[vmem, vmem],
        scratch_shapes=[pltpu.VMEM(square.shape, square.dtype)],
        compiler_params=limits(*pieces, square),
        name="haydock",
    )(*pieces)


def summed(value, axis):
    size = lax.axis_size(axis)
    if size & (size - 1):
        return value + sum(shifted(value, axis, step) for step in range(1, size))
    step = 1
    while step < size:
        value = value + exchanged(value, axis, lambda i, size: i ^ step)
        step *= 2
    return value


def local(
    ka,
    ga,
    ba,
    start_vector,
    valence_density,
    conduction_density,
    screening,
    qpoint_map,
    slot_owner,
    band_pairs,
    valence_energy,
    conduction_energy,
):
    npol = start_vector.shape[1]
    pair_count = start_vector.shape[3]
    kcount, vloc, val_count = qpoint_map.shape[0], valence_density.shape[3], valence_density.shape[4]
    cond_count = conduction_density.shape[3]
    pairs = vloc * val_count
    dims = (vloc, val_count, cond_count, npol)
    packed = pack(ka, ba, qpoint_map, slot_owner, valence_density, conduction_density)
    blocks = [packed[0]] + [shifted(packed[j], "ka", j) for j in range(1, ka)]
    early = ka // 2
    val_early = regroup(blocks[:early], 0, 2 * pairs)
    far_early = [shifted(val_early, "ga", r) for r in range(1, ga)]
    real, near_table, far_table, extras = prepare(
        ka,
        dims,
        qpoint_map,
        slot_owner,
        band_pairs,
        valence_energy,
        conduction_energy,
        start_vector,
        screening,
        val_early,
    )
    val_late = regroup(blocks[early:], 0, 2 * pairs, (extras,))
    far_late = [shifted(val_late, "ga", r) for r in range(1, ga)]
    cond_half = regroup(blocks, 2 * pairs, blocks[0].shape[0], (val_late, *far_early))
    cond_all = [cond_half] + [handed(cond_half, r) for r in range(1, ba)]
    coupled = couple(ka, ga, ba, dims, real, screening, cond_all)
    near = [val_early, val_late]
    piece = contract(ka, ba, dims, near_table, extras, coupled[:1], near, "near")
    if ga > 1:
        far = [half for both in zip(far_early, far_late) for half in both]
        piece = contract(ka, ba, dims, far_table, piece, coupled[1:], far, "far")
    piece = piece + sum(handed(piece, r) for r in range(1, ba))
    piece = summed(piece, "ga")
    pieces = [piece] + [shifted(piece, "ka", j) for j in range(1, ka)]
    scale_count = float(kcount * pair_count)
    return tuple(haydock(ka, pair_count, scale_count, npol, pieces))


def solution(mesh):
    in_specs = (
        P(("grp", "ka"), None, None, None),
        P(("grp", "ka"), None, None, "ba", None, "ga"),
        P(("grp", "ka"), None, None, None, None, "ga"),
        P(("grp", "ka"), None, "ga", None),
        P(),
        P(),
        P(),
        P(("grp", "ka"), None),
        P(("grp", "ka"), None),
    )
    out_specs = (P(("grp", "ka"), None, None, None), P("grp", None))
    body = functools.partial(local, mesh.shape["ka"], mesh.shape["ga"], mesh.shape["ba"])
    return jax.shard_map(body, mesh=mesh, in_specs=in_specs, out_specs=out_specs, check_vma=False)
```

```python
import functools
import math

import jax
import jax.numpy as jnp
from jax import lax
from jax.experimental import pallas as pl
from jax.experimental.pallas import tpu as pltpu
from jax.sharding import PartitionSpec as P

EPSILON = 1e-06
EXACT = lax.Precision.HIGHEST
VMEM_LEAST = 8 * 1024 * 1024
VMEM_MOST = 56 * 1024 * 1024

vmem = pl.BlockSpec(memory_space=pltpu.VMEM)
anywhere = pl.BlockSpec(memory_space=pl.ANY)
EXTRA_ROWS = 8
LIGHT = pl.CostEstimate(flops=1, bytes_accessed=1, transcendentals=0)


def in_vmem(shape, dtype):
    return pltpu.VMEM(shape, dtype)


def placed(value, space):
    return pltpu.with_memory_space_constraint(value, space)


def iota(shape, axis):
    return lax.broadcasted_iota(jnp.int32, shape, axis)


def split(values):
    high = values.astype(jnp.bfloat16)
    low = (values - high.astype(jnp.float32)).astype(jnp.bfloat16)
    return high, low


def limits(*arrays):
    held = sum(math.prod(a.shape) * a.dtype.itemsize for a in arrays)
    return pltpu.CompilerParams(vmem_limit_bytes=min(VMEM_MOST, VMEM_LEAST + 4 * held))


def target(me, step, size):
    return lax.rem(me + step, size)


def origin(me, step, size):
    return lax.rem(me + size - step, size)


def exchanged(value, axis, move):
    size, cores = lax.axis_size(axis), lax.axis_size("ba")
    pairs = [
        (i * cores + h, move(i, size) * cores + (h + 1) % cores)
        for i in range(size)
        for h in range(cores)
    ]
    return lax.ppermute(value, (axis, "ba"), pairs)


def shifted(value, axis, step):
    return exchanged(value, axis, lambda i, size: (i + step) % size)


def handed(value, step):
    size = lax.axis_size("ba")
    return lax.ppermute(value, "ba", [(h, (h + step) % size) for h in range(size)])


def pack_kernel(ka, qmap_in, owner_in, valence_in, conduction_in, *rest):
    outs = rest[:ka]
    qmap, owner, partner, valence, conduction, sems = rest[ka:]
    copies = [
        pltpu.make_async_copy(src, dst, sems.at[at])
        for at, (src, dst) in enumerate(
            ((qmap_in, qmap), (owner_in, owner), (valence_in, valence), (conduction_in, conduction))
        )
    ]
    for copy in copies:
        copy.start()
    me = lax.axis_index("ka")
    half = lax.axis_index("ba")
    count, width = valence.shape[1], valence.shape[5]
    cond_count = conduction.shape[3]
    share = cond_count // lax.axis_size("ba")
    val_rows = 2 * valence.shape[3] * valence.shape[4]
    cond_rows = 2 * share * cond_count

    def note(k2, carry):
        partner[owner[qmap[me, k2]]] = k2
        return carry

    copies[0].wait()
    copies[1].wait()
    lax.fori_loop(0, count, note, 0)
    copies[2].wait()
    copies[3].wait()
    for at in range(ka):
        k2 = partner[target(me, at, ka)]
        block = valence[0, k2].astype(jnp.float32).reshape(val_rows, width)
        outs[at][:val_rows, :] = block.astype(jnp.bfloat16)
        to = lax.rem(half + min(at, 1), lax.axis_size("ba"))
        block = conduction[0, k2, :, pl.ds(to * share, share)].astype(jnp.float32)
        outs[at][val_rows:, :] = block.reshape(cond_rows, width).astype(jnp.bfloat16)


def pack(ka, ba, qmap, owner, valence, conduction):
    cond_count = conduction.shape[3]
    rows = 2 * valence.shape[3] * valence.shape[4] + 2 * cond_count // ba * cond_count
    shape = in_vmem((rows, valence.shape[5]), valence.dtype)
    operands = [placed(x, pltpu.HBM) for x in (qmap, owner, valence, conduction)]
    return pl.pallas_call(
        functools.partial(pack_kernel, ka),
        out_shape=[shape] * ka,
        in_specs=[anywhere] * 4,
        out_specs=[vmem] * ka,
        scratch_shapes=[
            pltpu.SMEM(qmap.shape, jnp.int32),
            pltpu.SMEM(owner.shape, jnp.int32),
            pltpu.SMEM(owner.shape, jnp.int32),
            pltpu.VMEM(valence.shape, valence.dtype),
            pltpu.VMEM(conduction.shape, conduction.dtype),
            pltpu.SemaphoreType.DMA((4,)),
        ],
        cost_estimate=pl.CostEstimate(
            flops=0, bytes_accessed=4 * (valence.size + conduction.size), transcendentals=0
        ),
        compiler_params=limits(valence, conduction),
        name="pack",
    )(*operands)


def prepare_kernel(ka, dims, *refs):
    vloc, val_count, cond_count, npol = dims
    ins, (near_table, far_table, extras), scratch = refs[:6], refs[7:10], refs[10:]
    qmap, owner, band_pairs, val_energy, cond_energy, start, sems = scratch
    me = lax.axis_index("ka")
    half = lax.axis_index("ba")
    mine = lax.axis_index("ga")
    copies = [
        pltpu.make_async_copy(src, dst, sems.at[at])
        for at, (src, dst) in enumerate(
            zip(ins, (qmap, owner, band_pairs, val_energy, cond_energy, start))
        )
    ]
    for copy in copies:
        copy.start()
    pairs = vloc * val_count
    block = 2 * pairs
    rows = ka * block
    codes = val_count * cond_count
    mid = ka * codes
    lanes = 2 * mid
    row = iota((2 * rows, lanes), 0)
    col = iota((2 * rows, lanes), 1)
    j_of_row = row % rows // block
    cores = lax.axis_size("ba")
    for moves, table in enumerate((near_table, far_table)):
        share = lax.rem(half + 2 * cores - moves - jnp.where(j_of_row == 0, 0, 1), cores)
        want = (
            (row % block // pairs) * mid
            + origin(me, j_of_row, ka) * codes
            + (share * vloc + row % pairs // val_count) * cond_count
        )
        joined = (col - want >= 0) & (col - want < cond_count)
        for v2 in range(val_count):
            pick = jnp.where(joined & (row % val_count == v2), 1.0, 0.0)
            table[:, v2 * lanes : (v2 + 1) * lanes] = pick.astype(jnp.bfloat16)

    for copy in copies:
        copy.wait()
    first = jnp.where((mine == 0) & (half == 0), 1.0, 0.0)
    lane = iota((1, lanes), 1)
    lane_k = lane % mid // codes
    band_row = iota((codes, lanes), 0)
    band_lane = iota((codes, lanes), 1)
    code = jnp.zeros((codes, lanes), jnp.int32)
    bands = jnp.full((1, lanes), -1.0, jnp.float32)
    for b in range(codes):
        code = jnp.where(band_row == b, band_pairs[b], code)
        bands = jnp.where(lane % codes == band_pairs[b], float(b), bands)
    vectors = jnp.zeros((npol, lanes), jnp.float32)
    for part in range(2):
        spot = part * mid + me * codes
        pick = jnp.where(band_lane == spot + code, first, 0.0)
        vectors = vectors + jnp.dot(start[0, :, part, :], pick, precision=EXACT)
    energy = jnp.zeros((1, lanes), jnp.float32)
    for c in range(cond_count):
        energy = jnp.where(lane % cond_count == c, cond_energy[0, c], energy)
    for v in range(val_count):
        energy = energy - jnp.where(lane % codes // cond_count == v, val_energy[0, v], 0.0)
    energy = jnp.where(lane_k == me, energy * first, 0.0)
    kcount = qmap.shape[0]

    def find(k2, found):
        return jnp.where(owner[qmap[0, k2]] == me, k2, found)

    back = lax.fori_loop(0, kcount, find, 0)
    second = lane_k + back
    second = jnp.where(second >= kcount, second - kcount, second).astype(jnp.float32) * first
    rest = jnp.zeros((EXTRA_ROWS - 3 - npol, lanes), jnp.float32)
    extras[...] = jnp.concatenate([vectors, energy, bands * first, second, rest], 0)


def prepare(ka, dims, qmap, owner, band_pairs, val_energy, cond_energy, start, after):
    vloc, val_count, cond_count, npol = dims
    rows = 4 * ka * vloc * val_count
    lanes = 2 * ka * val_count * cond_count
    operands = (qmap, owner, band_pairs, val_energy, cond_energy, start)
    table = jax.ShapeDtypeStruct((rows, val_count * lanes), jnp.bfloat16)
    return pl.pallas_call(
        functools.partial(prepare_kernel, ka, dims),
        out_shape=[
            in_vmem(table.shape, table.dtype),
            in_vmem(table.shape, table.dtype),
            in_vmem((EXTRA_ROWS, lanes), jnp.float32),
        ],
        in_specs=[anywhere] * 7,
        out_specs=[vmem] * 3,
        scratch_shapes=[pltpu.SMEM(x.shape, x.dtype) for x in operands[:5]]
        + [
            pltpu.VMEM(start.shape, start.dtype),
            pltpu.SemaphoreType.DMA((6,)),
        ],
        cost_estimate=pl.CostEstimate(
            flops=0, bytes_accessed=4 * math.prod(table.shape), transcendentals=0
        ),
        compiler_params=limits(table),
        name="prepare",
    )(*[placed(x, pltpu.HBM) for x in operands], after)


def regroup_kernel(count, first, last, *refs):
    blocks, out = refs[:count], refs[-1]
    rows = last - first
    for at in range(count):
        out[at * rows : (at + 1) * rows, :] = blocks[at][first:last, :]


def regroup(blocks, first, last, after=()):
    shape = (len(blocks) * (last - first), blocks[0].shape[1])
    return pl.pallas_call(
        functools.partial(regroup_kernel, len(blocks), first, last),
        out_shape=in_vmem(shape, blocks[0].dtype),
        in_specs=[vmem] * len(blocks) + [anywhere] * len(after),
        out_specs=vmem,
        compiler_params=limits(*blocks),
        name="regroup",
    )(*blocks, *after)


def with_turned(halves, pairs):
    wide = jnp.concatenate([half[...].astype(jnp.float32) for half in halves], 0)
    parts = []
    for at in range(0, wide.shape[0], 2 * pairs):
        parts += [-wide[at + pairs : at + 2 * pairs], wide[at : at + pairs]]
    return wide, jnp.concatenate(parts, 0)


def columns_of(place, width):
    return pl.ds(pl.multiple_of(place * width, 128), width)


def placed_piece(kernel, table, dims, ba):
    vloc, val_count, cond_count, npol = dims
    half = lax.axis_index("ba")
    codes = val_count * cond_count
    lanes = table.shape[1] // val_count
    share = cond_count // ba
    cond_rows = cond_count * cond_count
    spread = jnp.dot(
        jnp.concatenate(split(kernel), 0), table[...], preferred_element_type=jnp.float32
    )
    spread = spread[:cond_rows] + spread[cond_rows:]
    crow = iota((cond_rows, lanes), 0)
    share_rows = share * cond_count
    c_of_row = origin(half, crow // share_rows, ba) * share + crow % share_rows // cond_count
    same_c = c_of_row == iota((cond_rows, lanes), 1) % cond_count
    spread = jnp.concatenate(
        [
            jnp.where(same_c, spread[:, v2 * lanes : (v2 + 1) * lanes], 0.0)
            for v2 in range(val_count)
        ],
        0,
    )
    out_row = iota((codes, val_count * cond_rows), 0)
    out_col = iota((codes, val_count * cond_rows), 1)
    fold = (out_row // cond_count == out_col // cond_rows) & (
        out_row % cond_count == out_col % cond_count
    )
    fold = jnp.where(fold, 1.0, 0.0).astype(jnp.bfloat16)
    piece = jnp.dot(fold, jnp.concatenate(split(spread), 1), preferred_element_type=jnp.float32)
    return piece[:, :lanes] + piece[:, lanes:]


def diagonal(crossed, ka, ba, share_rows):
    rows = crossed.shape[1] // 2
    lane = iota((share_rows, 2 * rows), 1)
    lane_j = lane % rows // (rows // ka)
    straight = lane < rows
    kernel = []
    for h in range(ba):
        total = jnp.zeros((share_rows, 2 * rows), jnp.float32)
        for j in range(ka):
            at = (h * ka + j) * 2 * share_rows
            real = crossed[at : at + share_rows]
            imag = crossed[at + share_rows : at + 2 * share_rows]
            total = jnp.where(lane_j == j, jnp.where(straight, real, imag), total)
        kernel.append(total)
    return jnp.concatenate(kernel, 0)


def couple_kernel(ka, ga, ba, share_rows, screening, *refs):
    cond_in, outs = refs[:ba], refs[ba:]
    mine = lax.axis_index("ga")
    wide = jnp.concatenate([ref[...].astype(jnp.float32) for ref in cond_in], 0)
    straight, turned = [], []
    for at in range(0, wide.shape[0], 2 * share_rows):
        real, imag = wide[at : at + share_rows], wide[at + share_rows : at + 2 * share_rows]
        straight += [real, -imag]
        turned += [imag, real]
    straight = jnp.concatenate(straight, 0).astype(jnp.bfloat16)
    turned = jnp.concatenate(turned, 0).astype(jnp.bfloat16)
    width = screening.shape[3] // ga
    columns = [columns_of(origin(mine, r, ga), width) for r in range(ga)]
    coupled = [
        jnp.dot(straight, screening[0, 0, :, block], preferred_element_type=jnp.float32)
        + jnp.dot(turned, screening[0, 1, :, block], preferred_element_type=jnp.float32)
        for block in columns
    ]
    for out, value in zip(outs, coupled):
        high, low = split(value)
        out[: value.shape[0], :] = high
        out[value.shape[0] :, :] = low


def couple(ka, ga, ba, dims, screening, cond_all):
    share_rows = dims[2] // ba * dims[2]
    rows = 2 * sum(x.shape[0] for x in cond_all)
    width = screening.shape[3] // ga
    return pl.pallas_call(
        functools.partial(couple_kernel, ka, ga, ba, share_rows),
        out_shape=[in_vmem((rows, width), jnp.bfloat16)] * ga,
        in_specs=[vmem] * (1 + len(cond_all)),
        out_specs=[vmem] * ga,
        cost_estimate=LIGHT,
        compiler_params=limits(*cond_all),
        name="couple",
    )(placed(screening, pltpu.VMEM), *cond_all)


def contract_kernel(ka, ba, count, dims, *refs):
    vloc, val_count, cond_count, npol = dims
    table, held, out = refs[0], refs[1], refs[-1]
    each = (len(refs) - 3 - count) // count
    codes = val_count * cond_count
    crossed = None
    for r in range(count):
        coupled = refs[2 + r]
        halves = refs[2 + count + r * each : 2 + count + (r + 1) * each]
        rows = jnp.concatenate(with_turned(halves, vloc * val_count), 0).astype(jnp.bfloat16)
        term = lax.dot_general(
            coupled[...], rows, (((1,), (1,)), ((), ())), preferred_element_type=jnp.float32
        )
        crossed = term if crossed is None else crossed + term
    half = crossed.shape[0] // 2
    crossed = crossed[:half] + crossed[half:]
    kernel = diagonal(crossed, ka, ba, cond_count // ba * cond_count)
    piece = placed_piece(kernel, table, dims, ba)
    before = held.shape[0] - EXTRA_ROWS
    out[:codes, :] = piece + held[:codes, :] if before else piece
    out[codes:, :] = held[before:, :]


def contract(ka, ba, dims, table, held, coupled, valence, name):
    val_count, cond_count = dims[1:3]
    operands = [table, held, *coupled, *valence]
    shape = (val_count * cond_count + EXTRA_ROWS, held.shape[1])
    return pl.pallas_call(
        functools.partial(contract_kernel, ka, ba, len(coupled), dims),
        out_shape=in_vmem(shape, jnp.float32),
        in_specs=[vmem] * len(operands),
        out_specs=vmem,
        cost_estimate=LIGHT,
        compiler_params=limits(*operands),
        name=name,
    )(*operands)


def haydock_kernel(ka, codes, scale_count, npol, *refs):
    pieces = refs[:-3]
    next_out, coef_out, matrix = refs[-3:]
    lanes = pieces[0].shape[1]
    mid = lanes // 2
    height = codes + EXTRA_ROWS
    found = [(ref, at) for ref in pieces for at in range(0, ref.shape[0], height)]
    extras = None
    slots = []
    for ref, at in found:
        rows = ref[at + codes : at + height, :]
        extras = rows if extras is None else extras + rows
        slots.append((ref[at : at + codes, :], rows[npol + 2 : npol + 3]))
    own = pieces[0][codes:height, :]
    sign = jnp.where(iota((1, lanes), 1) < mid, -1.0, 1.0)
    for k2 in range(ka):
        block = jnp.zeros((codes, lanes), jnp.float32)
        for piece, second in slots:
            block = jnp.where(second == float(k2), piece, block)
        matrix[k2 * codes : (k2 + 1) * codes, :] = block
        matrix[mid + k2 * codes : mid + (k2 + 1) * codes, :] = sign * pltpu.roll(block, mid, 1)
    high, low = split(matrix[...])
    full = jnp.concatenate([high, low], 1)
    start = extras[:npol]
    energy = extras[npol : npol + 1]

    def halves(vector):
        top = vector.astype(jnp.bfloat16).astype(jnp.float32)
        return jnp.concatenate([top, vector - top], 0).astype(jnp.bfloat16)

    def mean(values):
        return jnp.sum(values, axis=1, keepdims=True) / scale_count

    def norm(vector):
        return jnp.sqrt(mean(vector * vector) + EPSILON)

    def swap(vector):
        return pltpu.roll(vector, mid, 1)

    def hamiltonian(vector):
        product = jnp.dot(halves(vector), full, preferred_element_type=jnp.float32)
        main = product[:npol, :lanes] + product[npol:, :lanes]
        return energy * vector - (main + product[:npol, lanes:])

    def inner(left, right):
        return mean(left * right), mean(-sign * left * swap(right))

    def times(real, imag, vector):
        return real * vector + imag * (sign * swap(vector))

    start_image = hamiltonian(start)
    scale = 1.0 / norm(start)
    first = start * scale
    first_image = start_image * scale
    alpha_real, alpha_imag = inner(first, first_image)
    first_resid = first_image - times(alpha_real, alpha_imag, first)
    resid_image = hamiltonian(first_resid)
    beta_one = norm(first_resid)
    scale = 1.0 / beta_one
    second = first_resid * scale
    second_image = resid_image * scale
    gamma_real, gamma_imag = inner(second, second_image)
    second_resid = second_image - times(gamma_real, gamma_imag, second) - beta_one * first
    beta_two = norm(second_resid)

    coef_lane = iota(coef_out.shape, 1)
    coefs = jnp.zeros(coef_out.shape, jnp.float32)
    for at, value in enumerate((alpha_real, alpha_imag, gamma_real, gamma_imag, beta_one, beta_two)):
        coefs = jnp.where(coef_lane == at, value, coefs)
    coef_out[...] = coefs
    row = iota((2 * codes, lanes), 0)
    lane = iota((2 * codes, lanes), 1)
    here = (lane % mid // codes == lax.axis_index("ka")) & (lane // mid == row // codes)
    band = (row % codes).astype(jnp.float32)
    pick = jnp.where(here & (own[npol + 1 : npol + 2] == band), 1.0, 0.0).astype(jnp.bfloat16)
    picked = lax.dot_general(
        halves(second_resid), pick, (((1,), (1,)), ((), ())), preferred_element_type=jnp.float32
    )
    picked = (picked[:npol] + picked[npol:]) / beta_two
    next_out[0, :, 0, :] = picked[:, :codes]
    next_out[0, :, 1, :] = picked[:, codes:]


def haydock(ka, codes, scale_count, npol, pieces):
    lanes = pieces[0].shape[1]
    square = jax.ShapeDtypeStruct((lanes, lanes), jnp.float32)
    return pl.pallas_call(
        functools.partial(haydock_kernel, ka, codes, scale_count, npol),
        out_shape=[
            jax.ShapeDtypeStruct((1, npol, 2, codes), jnp.float32),
            jax.ShapeDtypeStruct((npol, 6), jnp.float32),
        ],
        in_specs=[vmem] * len(pieces),
        out_specs=[vmem, vmem],
        scratch_shapes=[pltpu.VMEM(square.shape, square.dtype)],
        compiler_params=limits(*pieces, square),
        name="haydock",
    )(*pieces)


def summed(value, axis):
    size = lax.axis_size(axis)
    if size & (size - 1):
        return value + sum(shifted(value, axis, step) for step in range(1, size))
    step = 1
    while step < size:
        value = value + exchanged(value, axis, lambda i, size: i ^ step)
        step *= 2
    return value


def local(
    ka,
    ga,
    ba,
    start_vector,
    valence_density,
    conduction_density,
    screening,
    qpoint_map,
    slot_owner,
    band_pairs,
    valence_energy,
    conduction_energy,
):
    npol = start_vector.shape[1]
    pair_count = start_vector.shape[3]
    kcount, vloc, val_count = qpoint_map.shape[0], valence_density.shape[3], valence_density.shape[4]
    cond_count = conduction_density.shape[3]
    pairs = vloc * val_count
    dims = (vloc, val_count, cond_count, npol)
    screening = lax.ppermute(screening, "ba", [(h, h) for h in range(ba)])
    packed = pack(ka, ba, qpoint_map, slot_owner, valence_density, conduction_density)
    blocks = [packed[0]] + [shifted(packed[j], "ka", j) for j in range(1, ka)]
    early = ka // 2
    val_early = regroup(blocks[:early], 0, 2 * pairs)
    far_early = [shifted(val_early, "ga", r) for r in range(1, ga)]
    near_table, far_table, extras = prepare(
        ka,
        dims,
        qpoint_map,
        slot_owner,
        band_pairs,
        valence_energy,
        conduction_energy,
        start_vector,
        val_early,
    )
    val_late = regroup(blocks[early:], 0, 2 * pairs, (extras,))
    far_late = [shifted(val_late, "ga", r) for r in range(1, ga)]
    cond_half = regroup(blocks, 2 * pairs, blocks[0].shape[0], (val_late, *far_early))
    cond_all = [cond_half] + [handed(cond_half, r) for r in range(1, ba)]
    coupled = couple(ka, ga, ba, dims, screening, cond_all)
    near = [val_early, val_late]
    piece = contract(ka, ba, dims, near_table, extras, coupled[:1], near, "near")
    if ga > 1:
        far = [half for both in zip(far_early, far_late) for half in both]
        piece = contract(ka, ba, dims, far_table, piece, coupled[1:], far, "far")
    piece = piece + sum(handed(piece, r) for r in range(1, ba))
    piece = summed(piece, "ga")
    pieces = [piece] + [shifted(piece, "ka", j) for j in range(1, ka)]
    scale_count = float(kcount * pair_count)
    return tuple(haydock(ka, pair_count, scale_count, npol, pieces))


def solution(mesh):
    in_specs = (
        P(("grp", "ka"), None, None, None),
        P(("grp", "ka"), None, None, "ba", None, "ga"),
        P(("grp", "ka"), None, None, None, None, "ga"),
        P(("grp", "ka"), None, "ga", None),
        P(),
        P(),
        P(),
        P(("grp", "ka"), None),
        P(("grp", "ka"), None),
    )
    out_specs = (P(("grp", "ka"), None, None, None), P("grp", None))
    body = functools.partial(local, mesh.shape["ka"], mesh.shape["ga"], mesh.shape["ba"])
    return jax.shard_map(body, mesh=mesh, in_specs=in_specs, out_specs=out_specs, check_vma=False)
```

```python
import functools
import math

import jax
import jax.numpy as jnp
from jax import lax
from jax.experimental import pallas as pl
from jax.experimental.pallas import tpu as pltpu
from jax.sharding import PartitionSpec as P

EPSILON = 1e-06
EXACT = lax.Precision.HIGHEST
VMEM_LEAST = 8 * 1024 * 1024
VMEM_MOST = 56 * 1024 * 1024

vmem = pl.BlockSpec(memory_space=pltpu.VMEM)
anywhere = pl.BlockSpec(memory_space=pl.ANY)
EXTRA_ROWS = 8
LIGHT = pl.CostEstimate(flops=1, bytes_accessed=1, transcendentals=0)
CHUNKS = 4
PARTS = 2


def in_vmem(shape, dtype):
    return pltpu.VMEM(shape, dtype)


def placed(value, space):
    return pltpu.with_memory_space_constraint(value, space)


def iota(shape, axis):
    return lax.broadcasted_iota(jnp.int32, shape, axis)


def split(values):
    high = values.astype(jnp.bfloat16)
    low = (values - high.astype(jnp.float32)).astype(jnp.bfloat16)
    return high, low


def limits(*arrays):
    held = sum(math.prod(a.shape) * a.dtype.itemsize for a in arrays)
    return pltpu.CompilerParams(vmem_limit_bytes=min(VMEM_MOST, VMEM_LEAST + 4 * held))


def target(me, step, size):
    return lax.rem(me + step, size)


def origin(me, step, size):
    return lax.rem(me + size - step, size)


def exchanged(value, axis, move):
    size, cores = lax.axis_size(axis), lax.axis_size("ba")
    pairs = [
        (i * cores + h, move(i, size) * cores + (h + 1) % cores)
        for i in range(size)
        for h in range(cores)
    ]
    return lax.ppermute(value, (axis, "ba"), pairs)


def shifted(value, axis, step):
    return exchanged(value, axis, lambda i, size: (i + step) % size)


def handed(value, step):
    size = lax.axis_size("ba")
    return lax.ppermute(value, "ba", [(h, (h + step) % size) for h in range(size)])


def pack_kernel(ka, qmap_in, owner_in, valence_in, conduction_in, *rest):
    outs = rest[:ka]
    qmap, owner, partner, valence, conduction, sems = rest[ka:]
    copies = [
        pltpu.make_async_copy(src, dst, sems.at[at])
        for at, (src, dst) in enumerate(
            ((qmap_in, qmap), (owner_in, owner), (valence_in, valence), (conduction_in, conduction))
        )
    ]
    for copy in copies:
        copy.start()
    me = lax.axis_index("ka")
    half = lax.axis_index("ba")
    count, width = valence.shape[1], valence.shape[5]
    cond_count = conduction.shape[3]
    share = cond_count // lax.axis_size("ba")
    val_rows = 2 * valence.shape[3] * valence.shape[4]
    cond_rows = 2 * share * cond_count

    def note(k2, carry):
        partner[owner[qmap[me, k2]]] = k2
        return carry

    copies[0].wait()
    copies[1].wait()
    lax.fori_loop(0, count, note, 0)
    copies[2].wait()
    copies[3].wait()
    for at in range(ka):
        k2 = partner[target(me, at, ka)]
        block = valence[0, k2].astype(jnp.float32).reshape(val_rows, width)
        outs[at][:val_rows, :] = block.astype(jnp.bfloat16)
        to = lax.rem(half + min(at, 1), lax.axis_size("ba"))
        block = conduction[0, k2, :, pl.ds(to * share, share)].astype(jnp.float32)
        outs[at][val_rows : val_rows + cond_rows, :] = block.reshape(cond_rows, width).astype(jnp.bfloat16)
    cores = lax.axis_size("ba")
    for h in range(1, cores):
        part = lax.rem(half + cores - h, cores)
        block = conduction[0, partner[me], :, pl.ds(part * share, share)].astype(jnp.float32)
        rows = slice(val_rows + h * cond_rows, val_rows + (h + 1) * cond_rows)
        outs[0][rows, :] = block.reshape(cond_rows, width).astype(jnp.bfloat16)


def pack(ka, ba, qmap, owner, valence, conduction):
    cond_count = conduction.shape[3]
    val_rows, cond_rows = 2 * valence.shape[3] * valence.shape[4], 2 * cond_count // ba * cond_count
    own = in_vmem((val_rows + ba * cond_rows, valence.shape[5]), valence.dtype)
    shape = in_vmem((val_rows + cond_rows, valence.shape[5]), valence.dtype)
    operands = [placed(x, pltpu.HBM) for x in (qmap, owner, valence, conduction)]
    return pl.pallas_call(
        functools.partial(pack_kernel, ka),
        out_shape=[own] + [shape] * (ka - 1),
        in_specs=[anywhere] * 4,
        out_specs=[vmem] * ka,
        scratch_shapes=[
            pltpu.SMEM(qmap.shape, jnp.int32),
            pltpu.SMEM(owner.shape, jnp.int32),
            pltpu.SMEM(owner.shape, jnp.int32),
            pltpu.VMEM(valence.shape, valence.dtype),
            pltpu.VMEM(conduction.shape, conduction.dtype),
            pltpu.SemaphoreType.DMA((4,)),
        ],
        compiler_params=limits(valence, conduction),
        name="pack",
    )(*operands)


def prepare_kernel(ka, dims, *refs):
    vloc, val_count, cond_count, npol = dims
    ins, screening, (screen_out, near_table, far_table, extras), scratch = refs[:6], refs[6], refs[8:12], refs[12:]
    qmap, owner, band_pairs, val_energy, cond_energy, start, sems, screen_sems = scratch
    me = lax.axis_index("ka")
    half = lax.axis_index("ba")
    mine = lax.axis_index("ga")
    copies = [
        pltpu.make_async_copy(src, dst, sems.at[at])
        for at, (src, dst) in enumerate(
            zip(ins, (qmap, owner, band_pairs, val_energy, cond_energy, start))
        )
    ]
    height = screening.shape[2] // CHUNKS
    chunks = [
        pltpu.make_async_copy(
            screening.at[0, part, pl.ds(c * height, height)],
            screen_out.at[part, pl.ds(c * height, height)],
            screen_sems.at[part, c],
        )
        for part in range(2)
        for c in range(CHUNKS)
    ]
    for copy in copies + chunks:
        copy.start()
    pairs = vloc * val_count
    block = 2 * pairs
    rows = ka * block
    codes = val_count * cond_count
    mid = ka * codes
    lanes = 2 * mid
    row = iota((2 * rows, lanes), 0)
    col = iota((2 * rows, lanes), 1)
    j_of_row = row % rows // block
    cores = lax.axis_size("ba")
    for moves, table in enumerate((near_table, far_table)):
        share = lax.rem(half + 2 * cores - moves - jnp.where(j_of_row == 0, 0, 1), cores)
        want = (
            (row % block // pairs) * mid
            + origin(me, j_of_row, ka) * codes
            + (share * vloc + row % pairs // val_count) * cond_count
        )
        joined = (col - want >= 0) & (col - want < cond_count)
        for v2 in range(val_count):
            pick = jnp.where(joined & (row % val_count == v2), 1.0, 0.0)
            table[:, v2 * lanes : (v2 + 1) * lanes] = pick.astype(jnp.bfloat16)

    for copy in copies:
        copy.wait()
    first = jnp.where((mine == 0) & (half == 0), 1.0, 0.0)
    lane = iota((1, lanes), 1)
    lane_k = lane % mid // codes
    band_row = iota((codes, lanes), 0)
    band_lane = iota((codes, lanes), 1)
    code = jnp.zeros((codes, lanes), jnp.int32)
    bands = jnp.full((1, lanes), -1.0, jnp.float32)
    for b in range(codes):
        code = jnp.where(band_row == b, band_pairs[b], code)
        bands = jnp.where(lane % codes == band_pairs[b], float(b), bands)
    vectors = jnp.zeros((npol, lanes), jnp.float32)
    for part in range(2):
        spot = part * mid + me * codes
        pick = jnp.where(band_lane == spot + code, first, 0.0)
        vectors = vectors + jnp.dot(start[0, :, part, :], pick, precision=EXACT)
    energy = jnp.zeros((1, lanes), jnp.float32)
    for c in range(cond_count):
        energy = jnp.where(lane % cond_count == c, cond_energy[0, c], energy)
    for v in range(val_count):
        energy = energy - jnp.where(lane % codes // cond_count == v, val_energy[0, v], 0.0)
    energy = jnp.where(lane_k == me, energy * first, 0.0)
    kcount = qmap.shape[0]

    def find(k2, found):
        return jnp.where(owner[qmap[0, k2]] == me, k2, found)

    back = lax.fori_loop(0, kcount, find, 0)
    second = lane_k + back
    second = jnp.where(second >= kcount, second - kcount, second).astype(jnp.float32) * first
    rest = jnp.zeros((EXTRA_ROWS - 3 - npol, lanes), jnp.float32)
    extras[...] = jnp.concatenate([vectors, energy, bands * first, second, rest], 0)
    for copy in chunks:
        copy.wait()


def prepare(ka, dims, qmap, owner, band_pairs, val_energy, cond_energy, start, screening, after):
    vloc, val_count, cond_count, npol = dims
    rows = 4 * ka * vloc * val_count
    lanes = 2 * ka * val_count * cond_count
    operands = (qmap, owner, band_pairs, val_energy, cond_energy, start, screening)
    table = jax.ShapeDtypeStruct((rows, val_count * lanes), jnp.bfloat16)
    return pl.pallas_call(
        functools.partial(prepare_kernel, ka, dims),
        out_shape=[
            in_vmem(screening.shape[1:], screening.dtype),
            in_vmem(table.shape, table.dtype),
            in_vmem(table.shape, table.dtype),
            in_vmem((EXTRA_ROWS, lanes), jnp.float32),
        ],
        in_specs=[anywhere] * 8,
        out_specs=[vmem] * 4,
        scratch_shapes=[pltpu.SMEM(x.shape, x.dtype) for x in operands[:5]]
        + [
            pltpu.VMEM(start.shape, start.dtype),
            pltpu.SemaphoreType.DMA((6,)),
            pltpu.SemaphoreType.DMA((2, CHUNKS)),
        ],
        cost_estimate=pl.CostEstimate(
            flops=0, bytes_accessed=4 * screening.size, transcendentals=0
        ),
        compiler_params=limits(table),
        name="prepare",
    )(*[placed(x, pltpu.HBM) for x in operands], after)


def regroup_kernel(count, rows, columns, *refs):
    blocks, out = refs[:count], refs[-1]
    height = rows.stop - rows.start
    for at in range(count):
        out[at * height : (at + 1) * height, :] = blocks[at][rows, columns]


def regroup(blocks, rows, after=(), columns=None):
    columns = columns or slice(0, blocks[0].shape[1])
    shape = (len(blocks) * (rows.stop - rows.start), columns.stop - columns.start)
    return pl.pallas_call(
        functools.partial(regroup_kernel, len(blocks), rows, columns),
        out_shape=in_vmem(shape, blocks[0].dtype),
        in_specs=[vmem] * len(blocks) + [anywhere] * len(after),
        out_specs=vmem,
        compiler_params=limits(*blocks),
        name="regroup",
    )(*blocks, *after)


def assemble_kernel(rows, own, *refs):
    parts, out = refs[:-1], refs[-1]
    height = rows.stop - rows.start
    out[:height, :] = own[rows, :]
    width = parts[0].shape[1]
    for c, part in enumerate(parts):
        out[height:, c * width : (c + 1) * width] = part[...]


def assemble(rows, own, parts):
    height = rows.stop - rows.start + parts[0].shape[0]
    return pl.pallas_call(
        functools.partial(assemble_kernel, rows),
        out_shape=in_vmem((height, own.shape[1]), own.dtype),
        in_specs=[vmem] * (1 + len(parts)),
        out_specs=vmem,
        compiler_params=limits(own, *parts),
        name="assemble",
    )(own, *parts)


def with_turned(halves, pairs):
    wide = jnp.concatenate([half[...].astype(jnp.float32) for half in halves], 0)
    parts = []
    for at in range(0, wide.shape[0], 2 * pairs):
        parts += [-wide[at + pairs : at + 2 * pairs], wide[at : at + pairs]]
    return wide, jnp.concatenate(parts, 0)


def columns_of(place, width):
    return pl.ds(pl.multiple_of(place * width, 128), width)


def placed_piece(kernel, table, dims, ba):
    vloc, val_count, cond_count, npol = dims
    half = lax.axis_index("ba")
    codes = val_count * cond_count
    lanes = table.shape[1] // val_count
    share = cond_count // ba
    cond_rows = cond_count * cond_count
    spread = jnp.dot(
        jnp.concatenate(split(kernel), 0), table[...], preferred_element_type=jnp.float32
    )
    spread = spread[:cond_rows] + spread[cond_rows:]
    crow = iota((cond_rows, lanes), 0)
    share_rows = share * cond_count
    c_of_row = origin(half, crow // share_rows, ba) * share + crow % share_rows // cond_count
    same_c = c_of_row == iota((cond_rows, lanes), 1) % cond_count
    spread = jnp.concatenate(
        [
            jnp.where(same_c, spread[:, v2 * lanes : (v2 + 1) * lanes], 0.0)
            for v2 in range(val_count)
        ],
        0,
    )
    out_row = iota((codes, val_count * cond_rows), 0)
    out_col = iota((codes, val_count * cond_rows), 1)
    fold = (out_row // cond_count == out_col // cond_rows) & (
        out_row % cond_count == out_col % cond_count
    )
    fold = jnp.where(fold, 1.0, 0.0).astype(jnp.bfloat16)
    piece = jnp.dot(fold, jnp.concatenate(split(spread), 1), preferred_element_type=jnp.float32)
    return piece[:, :lanes] + piece[:, lanes:]


def diagonal(crossed, ka, ba, share_rows):
    rows = crossed.shape[1] // 2
    lane = iota((share_rows, 2 * rows), 1)
    lane_j = lane % rows // (rows // ka)
    straight = lane < rows
    kernel = []
    for h in range(ba):
        total = jnp.zeros((share_rows, 2 * rows), jnp.float32)
        for j in range(ka):
            at = (h * ka + j) * 2 * share_rows
            real = crossed[at : at + share_rows]
            imag = crossed[at + share_rows : at + 2 * share_rows]
            total = jnp.where(lane_j == j, jnp.where(straight, real, imag), total)
        kernel.append(total)
    return jnp.concatenate(kernel, 0)


def couple_kernel(ka, ga, ba, share_rows, screening, *refs):
    cond_in, outs = refs[:ba], refs[ba:]
    mine = lax.axis_index("ga")
    wide = jnp.concatenate([ref[...].astype(jnp.float32) for ref in cond_in], 0)
    straight, turned = [], []
    for at in range(0, wide.shape[0], 2 * share_rows):
        real, imag = wide[at : at + share_rows], wide[at + share_rows : at + 2 * share_rows]
        straight += [real, -imag]
        turned += [imag, real]
    straight = jnp.concatenate(straight, 0).astype(jnp.bfloat16)
    turned = jnp.concatenate(turned, 0).astype(jnp.bfloat16)
    width = screening.shape[2] // ga
    columns = [columns_of(origin(mine, r, ga), width) for r in range(ga)]
    coupled = [
        jnp.dot(straight, screening[0, :, block], preferred_element_type=jnp.float32)
        + jnp.dot(turned, screening[1, :, block], preferred_element_type=jnp.float32)
        for block in columns
    ]
    for out, value in zip(outs, coupled):
        high, low = split(value)
        out[: value.shape[0], :] = high
        out[value.shape[0] :, :] = low


def couple(ka, ga, ba, dims, screening, cond_all):
    share_rows = dims[2] // ba * dims[2]
    rows = 2 * sum(x.shape[0] for x in cond_all)
    width = screening.shape[2] // ga
    operands = [screening, *cond_all]
    return pl.pallas_call(
        functools.partial(couple_kernel, ka, ga, ba, share_rows),
        out_shape=[in_vmem((rows, width), jnp.bfloat16)] * ga,
        in_specs=[vmem] * len(operands),
        out_specs=[vmem] * ga,
        cost_estimate=LIGHT,
        compiler_params=limits(*operands),
        name="couple",
    )(*operands)


def contract_kernel(ka, ba, count, dims, *refs):
    vloc, val_count, cond_count, npol = dims
    table, held, out = refs[0], refs[1], refs[-1]
    each = (len(refs) - 3 - count) // count
    codes = val_count * cond_count
    crossed = None
    for r in range(count):
        coupled = refs[2 + r]
        halves = refs[2 + count + r * each : 2 + count + (r + 1) * each]
        rows = jnp.concatenate(with_turned(halves, vloc * val_count), 0).astype(jnp.bfloat16)
        term = lax.dot_general(
            coupled[...], rows, (((1,), (1,)), ((), ())), preferred_element_type=jnp.float32
        )
        crossed = term if crossed is None else crossed + term
    half = crossed.shape[0] // 2
    crossed = crossed[:half] + crossed[half:]
    kernel = diagonal(crossed, ka, ba, cond_count // ba * cond_count)
    piece = placed_piece(kernel, table, dims, ba)
    before = held.shape[0] - EXTRA_ROWS
    out[:codes, :] = piece + held[:codes, :] if before else piece
    out[codes:, :] = held[before:, :]


def contract(ka, ba, dims, table, held, coupled, valence, name):
    val_count, cond_count = dims[1:3]
    operands = [table, held, *coupled, *valence]
    shape = (val_count * cond_count + EXTRA_ROWS, held.shape[1])
    return pl.pallas_call(
        functools.partial(contract_kernel, ka, ba, len(coupled), dims),
        out_shape=in_vmem(shape, jnp.float32),
        in_specs=[vmem] * len(operands),
        out_specs=vmem,
        cost_estimate=LIGHT,
        compiler_params=limits(*operands),
        name=name,
    )(*operands)


def haydock_kernel(ka, codes, scale_count, npol, *refs):
    pieces = refs[:-3]
    next_out, coef_out, matrix = refs[-3:]
    lanes = pieces[0].shape[1]
    mid = lanes // 2
    height = codes + EXTRA_ROWS
    found = [(ref, at) for ref in pieces for at in range(0, ref.shape[0], height)]
    extras = None
    slots = []
    for ref, at in found:
        rows = ref[at + codes : at + height, :]
        extras = rows if extras is None else extras + rows
        slots.append((ref[at : at + codes, :], rows[npol + 2 : npol + 3]))
    own = pieces[0][codes:height, :]
    sign = jnp.where(iota((1, lanes), 1) < mid, -1.0, 1.0)
    for k2 in range(ka):
        block = jnp.zeros((codes, lanes), jnp.float32)
        for piece, second in slots:
            block = jnp.where(second == float(k2), piece, block)
        matrix[k2 * codes : (k2 + 1) * codes, :] = block
        matrix[mid + k2 * codes : mid + (k2 + 1) * codes, :] = sign * pltpu.roll(block, mid, 1)
    high, low = split(matrix[...])
    full = jnp.concatenate([high, low], 1)
    start = extras[:npol]
    energy = extras[npol : npol + 1]

    def halves(vector):
        top = vector.astype(jnp.bfloat16).astype(jnp.float32)
        return jnp.concatenate([top, vector - top], 0).astype(jnp.bfloat16)

    def mean(values):
        return jnp.sum(values, axis=1, keepdims=True) / scale_count

    def norm(vector):
        return jnp.sqrt(mean(vector * vector) + EPSILON)

    def swap(vector):
        return pltpu.roll(vector, mid, 1)

    def hamiltonian(vector):
        product = jnp.dot(halves(vector), full, preferred_element_type=jnp.float32)
        main = product[:npol, :lanes] + product[npol:, :lanes]
        return energy * vector - (main + product[:npol, lanes:])

    def inner(left, right):
        return mean(left * right), mean(-sign * left * swap(right))

    def times(real, imag, vector):
        return real * vector + imag * (sign * swap(vector))

    start_image = hamiltonian(start)
    scale = 1.0 / norm(start)
    first = start * scale
    first_image = start_image * scale
    alpha_real, alpha_imag = inner(first, first_image)
    first_resid = first_image - times(alpha_real, alpha_imag, first)
    resid_image = hamiltonian(first_resid)
    beta_one = norm(first_resid)
    scale = 1.0 / beta_one
    second = first_resid * scale
    second_image = resid_image * scale
    gamma_real, gamma_imag = inner(second, second_image)
    second_resid = second_image - times(gamma_real, gamma_imag, second) - beta_one * first
    beta_two = norm(second_resid)

    coef_lane = iota(coef_out.shape, 1)
    coefs = jnp.zeros(coef_out.shape, jnp.float32)
    for at, value in enumerate((alpha_real, alpha_imag, gamma_real, gamma_imag, beta_one, beta_two)):
        coefs = jnp.where(coef_lane == at, value, coefs)
    coef_out[...] = coefs
    row = iota((2 * codes, lanes), 0)
    lane = iota((2 * codes, lanes), 1)
    here = (lane % mid // codes == lax.axis_index("ka")) & (lane // mid == row // codes)
    band = (row % codes).astype(jnp.float32)
    pick = jnp.where(here & (own[npol + 1 : npol + 2] == band), 1.0, 0.0).astype(jnp.bfloat16)
    picked = lax.dot_general(
        halves(second_resid), pick, (((1,), (1,)), ((), ())), preferred_element_type=jnp.float32
    )
    picked = (picked[:npol] + picked[npol:]) / beta_two
    next_out[0, :, 0, :] = picked[:, :codes]
    next_out[0, :, 1, :] = picked[:, codes:]


def haydock(ka, codes, scale_count, npol, pieces):
    lanes = pieces[0].shape[1]
    square = jax.ShapeDtypeStruct((lanes, lanes), jnp.float32)
    return pl.pallas_call(
        functools.partial(haydock_kernel, ka, codes, scale_count, npol),
        out_shape=[
            jax.ShapeDtypeStruct((1, npol, 2, codes), jnp.float32),
            jax.ShapeDtypeStruct((npol, 6), jnp.float32),
        ],
        in_specs=[vmem] * len(pieces),
        out_specs=[vmem, vmem],
        scratch_shapes=[pltpu.VMEM(square.shape, square.dtype)],
        compiler_params=limits(*pieces, square),
        name="haydock",
    )(*pieces)


def summed(value, axis):
    size = lax.axis_size(axis)
    if size & (size - 1):
        return value + sum(shifted(value, axis, step) for step in range(1, size))
    step = 1
    while step < size:
        value = value + exchanged(value, axis, lambda i, size: i ^ step)
        step *= 2
    return value


def local(
    ka,
    ga,
    ba,
    start_vector,
    valence_density,
    conduction_density,
    screening,
    qpoint_map,
    slot_owner,
    band_pairs,
    valence_energy,
    conduction_energy,
):
    npol = start_vector.shape[1]
    pair_count = start_vector.shape[3]
    kcount, vloc, val_count = qpoint_map.shape[0], valence_density.shape[3], valence_density.shape[4]
    cond_count = conduction_density.shape[3]
    pairs = vloc * val_count
    dims = (vloc, val_count, cond_count, npol)
    packed = pack(ka, ba, qpoint_map, slot_owner, valence_density, conduction_density)
    blocks = [packed[0]] + [shifted(packed[j], "ka", j) for j in range(1, ka)]
    early = ka // 2
    val_rows = slice(0, 2 * pairs)
    val_early = regroup(blocks[:early], val_rows)
    far_early = [shifted(val_early, "ga", r) for r in range(1, ga)]
    whole, near_table, far_table, extras = prepare(
        ka,
        dims,
        qpoint_map,
        slot_owner,
        band_pairs,
        valence_energy,
        conduction_energy,
        start_vector,
        screening,
        val_early,
    )
    val_late = regroup(blocks[early:], val_rows, (extras,))
    far_late = [shifted(val_late, "ga", r) for r in range(1, ga)]
    height = 2 * cond_count // ba * cond_count
    width = blocks[0].shape[1] // PARTS
    cond_rows = slice(2 * pairs, 2 * pairs + height)
    cond_parts = [
        regroup(blocks[1:], cond_rows, (val_late, *far_early), slice(c * width, (c + 1) * width))
        for c in range(PARTS)
    ]
    cond_all = [regroup(blocks, cond_rows)]
    for r in range(1, ba):
        own_rows = slice(2 * pairs + r * height, 2 * pairs + (r + 1) * height)
        came = [handed(part, r) for part in cond_parts]
        cond_all.append(assemble(own_rows, blocks[0], came))
    coupled = couple(ka, ga, ba, dims, whole, cond_all)
    near = [val_early, val_late]
    piece = contract(ka, ba, dims, near_table, extras, coupled[:1], near, "near")
    if ga > 1:
        far = [half for both in zip(far_early, far_late) for half in both]
        piece = contract(ka, ba, dims, far_table, piece, coupled[1:], far, "far")
    piece = piece + sum(handed(piece, r) for r in range(1, ba))
    piece = summed(piece, "ga")
    pieces = [piece] + [shifted(piece, "ka", j) for j in reversed(range(1, ka))]
    scale_count = float(kcount * pair_count)
    return tuple(haydock(ka, pair_count, scale_count, npol, pieces))


def solution(mesh):
    in_specs = (
        P(("grp", "ka"), None, None, None),
        P(("grp", "ka"), None, None, "ba", None, "ga"),
        P(("grp", "ka"), None, None, None, None, "ga"),
        P(("grp", "ka"), None, "ga", None),
        P(),
        P(),
        P(),
        P(("grp", "ka"), None),
        P(("grp", "ka"), None),
    )
    out_specs = (P(("grp", "ka"), None, None, None), P("grp", None))
    body = functools.partial(local, mesh.shape["ka"], mesh.shape["ga"], mesh.shape["ba"])
    return jax.shard_map(body, mesh=mesh, in_specs=in_specs, out_specs=out_specs, check_vma=False)
```

```python
import functools
import math

import jax
import jax.numpy as jnp
from jax import lax
from jax.experimental import pallas as pl
from jax.experimental.pallas import tpu as pltpu
from jax.sharding import PartitionSpec as P

EPSILON = 1e-06
EXACT = lax.Precision.HIGHEST
VMEM_LEAST = 8 * 1024 * 1024
VMEM_MOST = 56 * 1024 * 1024

vmem = pl.BlockSpec(memory_space=pltpu.VMEM)
anywhere = pl.BlockSpec(memory_space=pl.ANY)
EXTRA_ROWS = 8
LIGHT = pl.CostEstimate(flops=1, bytes_accessed=1, transcendentals=0)
CHUNKS = 4
PARTS = 2


def in_vmem(shape, dtype):
    return pltpu.VMEM(shape, dtype)


def placed(value, space):
    return pltpu.with_memory_space_constraint(value, space)


def iota(shape, axis):
    return lax.broadcasted_iota(jnp.int32, shape, axis)


def split(values):
    high = values.astype(jnp.bfloat16)
    low = (values - high.astype(jnp.float32)).astype(jnp.bfloat16)
    return high, low


def limits(*arrays):
    held = sum(math.prod(a.shape) * a.dtype.itemsize for a in arrays)
    return pltpu.CompilerParams(vmem_limit_bytes=min(VMEM_MOST, VMEM_LEAST + 4 * held))


def target(me, step, size):
    return lax.rem(me + step, size)


def origin(me, step, size):
    return lax.rem(me + size - step, size)


def exchanged(value, axis, move):
    size, cores = lax.axis_size(axis), lax.axis_size("ba")
    pairs = [
        (i * cores + h, move(i, size) * cores + (h + 1) % cores)
        for i in range(size)
        for h in range(cores)
    ]
    return lax.ppermute(value, (axis, "ba"), pairs)


def shifted(value, axis, step):
    return exchanged(value, axis, lambda i, size: (i + step) % size)


def handed(value, step):
    size = lax.axis_size("ba")
    return lax.ppermute(value, "ba", [(h, (h + step) % size) for h in range(size)])


def pack_kernel(ka, qmap_in, owner_in, valence_in, conduction_in, *rest):
    outs = rest[:ka]
    qmap, owner, partner, valence, conduction, sems = rest[ka:]
    copies = [
        pltpu.make_async_copy(src, dst, sems.at[at])
        for at, (src, dst) in enumerate(
            ((qmap_in, qmap), (owner_in, owner), (valence_in, valence), (conduction_in, conduction))
        )
    ]
    for copy in copies:
        copy.start()
    me = lax.axis_index("ka")
    half = lax.axis_index("ba")
    count, width = valence.shape[1], valence.shape[5]
    cond_count = conduction.shape[3]
    share = cond_count // lax.axis_size("ba")
    val_rows = 2 * valence.shape[3] * valence.shape[4]
    cond_rows = 2 * share * cond_count

    def note(k2, carry):
        partner[owner[qmap[me, k2]]] = k2
        return carry

    copies[0].wait()
    copies[1].wait()
    lax.fori_loop(0, count, note, 0)
    copies[2].wait()
    copies[3].wait()
    for at in range(ka):
        k2 = partner[target(me, at, ka)]
        block = valence[0, k2].astype(jnp.float32).reshape(val_rows, width)
        outs[at][:val_rows, :] = block.astype(jnp.bfloat16)
        to = lax.rem(half + min(at, 1), lax.axis_size("ba"))
        block = conduction[0, k2, :, pl.ds(to * share, share)].astype(jnp.float32)
        outs[at][val_rows : val_rows + cond_rows, :] = block.reshape(cond_rows, width).astype(jnp.bfloat16)
    cores = lax.axis_size("ba")
    for h in range(1, cores):
        part = lax.rem(half + cores - h, cores)
        block = conduction[0, partner[me], :, pl.ds(part * share, share)].astype(jnp.float32)
        rows = slice(val_rows + h * cond_rows, val_rows + (h + 1) * cond_rows)
        outs[0][rows, :] = block.reshape(cond_rows, width).astype(jnp.bfloat16)


def pack(ka, ba, qmap, owner, valence, conduction):
    cond_count = conduction.shape[3]
    val_rows, cond_rows = 2 * valence.shape[3] * valence.shape[4], 2 * cond_count // ba * cond_count
    own = in_vmem((val_rows + ba * cond_rows, valence.shape[5]), valence.dtype)
    shape = in_vmem((val_rows + cond_rows, valence.shape[5]), valence.dtype)
    operands = [placed(x, pltpu.HBM) for x in (qmap, owner, valence, conduction)]
    return pl.pallas_call(
        functools.partial(pack_kernel, ka),
        out_shape=[own] + [shape] * (ka - 1),
        in_specs=[anywhere] * 4,
        out_specs=[vmem] * ka,
        scratch_shapes=[
            pltpu.SMEM(qmap.shape, jnp.int32),
            pltpu.SMEM(owner.shape, jnp.int32),
            pltpu.SMEM(owner.shape, jnp.int32),
            pltpu.VMEM(valence.shape, valence.dtype),
            pltpu.VMEM(conduction.shape, conduction.dtype),
            pltpu.SemaphoreType.DMA((4,)),
        ],
        compiler_params=limits(valence, conduction),
        name="pack",
    )(*operands)


def prepare_kernel(ka, dims, *refs):
    vloc, val_count, cond_count, npol = dims
    ins, screening, (screen_out, near_table, far_table, extras), scratch = refs[:6], refs[6], refs[8:12], refs[12:]
    qmap, owner, band_pairs, val_energy, cond_energy, start, sems, screen_sems = scratch
    me = lax.axis_index("ka")
    half = lax.axis_index("ba")
    mine = lax.axis_index("ga")
    copies = [
        pltpu.make_async_copy(src, dst, sems.at[at])
        for at, (src, dst) in enumerate(
            zip(ins, (qmap, owner, band_pairs, val_energy, cond_energy, start))
        )
    ]
    height = screening.shape[2] // CHUNKS
    chunks = [
        pltpu.make_async_copy(
            screening.at[0, part, pl.ds(c * height, height)],
            screen_out.at[part, pl.ds(c * height, height)],
            screen_sems.at[part, c],
        )
        for part in range(2)
        for c in range(CHUNKS)
    ]
    for copy in copies + chunks:
        copy.start()
    pairs = vloc * val_count
    block = 2 * pairs
    rows = ka * block
    codes = val_count * cond_count
    mid = ka * codes
    lanes = 2 * mid
    row = iota((2 * rows, lanes), 0)
    col = iota((2 * rows, lanes), 1)
    j_of_row = row % rows // block
    cores = lax.axis_size("ba")
    for moves, table in enumerate((near_table, far_table)):
        share = lax.rem(half + 2 * cores - moves - jnp.where(j_of_row == 0, 0, 1), cores)
        want = (
            (row % block // pairs) * mid
            + origin(me, j_of_row, ka) * codes
            + (share * vloc + row % pairs // val_count) * cond_count
        )
        joined = (col - want >= 0) & (col - want < cond_count)
        for v2 in range(val_count):
            pick = jnp.where(joined & (row % val_count == v2), 1.0, 0.0)
            table[:, v2 * lanes : (v2 + 1) * lanes] = pick.astype(jnp.bfloat16)

    for copy in copies:
        copy.wait()
    first = jnp.where((mine == 0) & (half == 0), 1.0, 0.0)
    lane = iota((1, lanes), 1)
    lane_k = lane % mid // codes
    band_row = iota((codes, lanes), 0)
    band_lane = iota((codes, lanes), 1)
    code = jnp.zeros((codes, lanes), jnp.int32)
    bands = jnp.full((1, lanes), -1.0, jnp.float32)
    for b in range(codes):
        code = jnp.where(band_row == b, band_pairs[b], code)
        bands = jnp.where(lane % codes == band_pairs[b], float(b), bands)
    vectors = jnp.zeros((npol, lanes), jnp.float32)
    for part in range(2):
        spot = part * mid + me * codes
        pick = jnp.where(band_lane == spot + code, first, 0.0)
        vectors = vectors + jnp.dot(start[0, :, part, :], pick, precision=EXACT)
    energy = jnp.zeros((1, lanes), jnp.float32)
    for c in range(cond_count):
        energy = jnp.where(lane % cond_count == c, cond_energy[0, c], energy)
    for v in range(val_count):
        energy = energy - jnp.where(lane % codes // cond_count == v, val_energy[0, v], 0.0)
    energy = jnp.where(lane_k == me, energy * first, 0.0)
    kcount = qmap.shape[0]

    def find(k2, found):
        return jnp.where(owner[qmap[0, k2]] == me, k2, found)

    back = lax.fori_loop(0, kcount, find, 0)
    second = lane_k + back
    second = jnp.where(second >= kcount, second - kcount, second).astype(jnp.float32) * first
    rest = jnp.zeros((EXTRA_ROWS - 3 - npol, lanes), jnp.float32)
    extras[...] = jnp.concatenate([vectors, energy, bands * first, second, rest], 0)
    for copy in chunks:
        copy.wait()


def prepare(ka, dims, qmap, owner, band_pairs, val_energy, cond_energy, start, screening, after):
    vloc, val_count, cond_count, npol = dims
    rows = 4 * ka * vloc * val_count
    lanes = 2 * ka * val_count * cond_count
    operands = (qmap, owner, band_pairs, val_energy, cond_energy, start, screening)
    table = jax.ShapeDtypeStruct((rows, val_count * lanes), jnp.bfloat16)
    return pl.pallas_call(
        functools.partial(prepare_kernel, ka, dims),
        out_shape=[
            in_vmem(screening.shape[1:], screening.dtype),
            in_vmem(table.shape, table.dtype),
            in_vmem(table.shape, table.dtype),
            in_vmem((EXTRA_ROWS, lanes), jnp.float32),
        ],
        in_specs=[anywhere] * 8,
        out_specs=[vmem] * 4,
        scratch_shapes=[pltpu.SMEM(x.shape, x.dtype) for x in operands[:5]]
        + [
            pltpu.VMEM(start.shape, start.dtype),
            pltpu.SemaphoreType.DMA((6,)),
            pltpu.SemaphoreType.DMA((2, CHUNKS)),
        ],
        cost_estimate=pl.CostEstimate(
            flops=0, bytes_accessed=4 * screening.size, transcendentals=0
        ),
        compiler_params=limits(table),
        name="prepare",
    )(*[placed(x, pltpu.HBM) for x in operands], after)


def regroup_kernel(count, rows, columns, *refs):
    blocks, out = refs[:count], refs[-1]
    height = rows.stop - rows.start
    for at in range(count):
        out[at * height : (at + 1) * height, :] = blocks[at][rows, columns]


def regroup(blocks, rows, after=(), columns=None):
    columns = columns or slice(0, blocks[0].shape[1])
    shape = (len(blocks) * (rows.stop - rows.start), columns.stop - columns.start)
    return pl.pallas_call(
        functools.partial(regroup_kernel, len(blocks), rows, columns),
        out_shape=in_vmem(shape, blocks[0].dtype),
        in_specs=[vmem] * len(blocks) + [anywhere] * len(after),
        out_specs=vmem,
        compiler_params=limits(*blocks),
        name="regroup",
    )(*blocks, *after)


def assemble_kernel(rows, own, *refs):
    parts, out = refs[:PARTS], refs[-1]
    height = rows.stop - rows.start
    out[:height, :] = own[rows, :]
    width = parts[0].shape[1]
    for c, part in enumerate(parts):
        out[height:, c * width : (c + 1) * width] = part[...]


def assemble(rows, own, parts, after):
    height = rows.stop - rows.start + parts[0].shape[0]
    return pl.pallas_call(
        functools.partial(assemble_kernel, rows),
        out_shape=in_vmem((height, own.shape[1]), own.dtype),
        in_specs=[vmem] * (1 + len(parts)) + [anywhere],
        out_specs=vmem,
        compiler_params=limits(own, *parts),
        name="assemble",
    )(own, *parts, after)


def with_turned(halves, pairs):
    wide = jnp.concatenate([half[...].astype(jnp.float32) for half in halves], 0)
    parts = []
    for at in range(0, wide.shape[0], 2 * pairs):
        parts += [-wide[at + pairs : at + 2 * pairs], wide[at : at + pairs]]
    return wide, jnp.concatenate(parts, 0)


def columns_of(place, width):
    return pl.ds(pl.multiple_of(place * width, 128), width)


def placed_piece(kernel, table, dims, ba):
    vloc, val_count, cond_count, npol = dims
    half = lax.axis_index("ba")
    codes = val_count * cond_count
    lanes = table.shape[1] // val_count
    share = cond_count // ba
    cond_rows = cond_count * cond_count
    spread = jnp.dot(
        jnp.concatenate(split(kernel), 0), table[...], preferred_element_type=jnp.float32
    )
    spread = spread[:cond_rows] + spread[cond_rows:]
    crow = iota((cond_rows, lanes), 0)
    share_rows = share * cond_count
    c_of_row = origin(half, crow // share_rows, ba) * share + crow % share_rows // cond_count
    same_c = c_of_row == iota((cond_rows, lanes), 1) % cond_count
    spread = jnp.concatenate(
        [
            jnp.where(same_c, spread[:, v2 * lanes : (v2 + 1) * lanes], 0.0)
            for v2 in range(val_count)
        ],
        0,
    )
    out_row = iota((codes, val_count * cond_rows), 0)
    out_col = iota((codes, val_count * cond_rows), 1)
    fold = (out_row // cond_count == out_col // cond_rows) & (
        out_row % cond_count == out_col % cond_count
    )
    fold = jnp.where(fold, 1.0, 0.0).astype(jnp.bfloat16)
    piece = jnp.dot(fold, jnp.concatenate(split(spread), 1), preferred_element_type=jnp.float32)
    return piece[:, :lanes] + piece[:, lanes:]


def diagonal(crossed, ka, ba, share_rows, sign):
    rows = crossed.shape[1] // 2
    lane = iota((share_rows, 2 * rows), 1)
    lane_j = lane % rows // (rows // ka)
    straight = lane < rows
    kernel = []
    for h in range(ba):
        total = jnp.zeros((share_rows, 2 * rows), jnp.float32)
        for j in range(ka):
            at = (h * ka + j) * 2 * share_rows
            real = crossed[at : at + share_rows]
            imag = crossed[at + share_rows : at + 2 * share_rows]
            total = jnp.where(lane_j == j, jnp.where(straight, real, sign * imag), total)
        kernel.append(total)
    return jnp.concatenate(kernel, 0)


def field_kernel(pairs, screening, *refs):
    halves, out = refs[:-1], refs[-1]
    columns = columns_of(lax.axis_index("ga"), halves[0].shape[1])
    wide, turned = with_turned(halves, pairs)
    real = jnp.concatenate([wide, turned], 0).astype(jnp.bfloat16)
    imag = jnp.concatenate([turned, -wide], 0).astype(jnp.bfloat16)
    form = (((1,), (1,)), ((), ()))
    fields = lax.dot_general(
        screening[0, :, columns], real, form, preferred_element_type=jnp.float32
    ) + lax.dot_general(screening[1, :, columns], imag, form, preferred_element_type=jnp.float32)
    lanes = fields.shape[1]
    high, low = split(fields)
    out[:, :lanes] = high
    out[:, lanes:] = low


def field(pairs, screening, halves):
    operands = [screening, *halves]
    rows = sum(half.shape[0] for half in halves)
    return pl.pallas_call(
        functools.partial(field_kernel, pairs),
        out_shape=in_vmem((screening.shape[1], 4 * rows), jnp.bfloat16),
        in_specs=[vmem] * len(operands),
        out_specs=vmem,
        cost_estimate=LIGHT,
        compiler_params=limits(*operands),
        name="field",
    )(*operands)


def near_kernel(ka, ba, dims, *refs):
    vloc, val_count, cond_count, npol = dims
    fields, table, extras = refs[:3]
    cond_in, out = refs[3:-1], refs[-1]
    codes = val_count * cond_count
    cond = jnp.concatenate([ref[...] for ref in cond_in], 0)
    crossed = jnp.dot(cond, fields[...], preferred_element_type=jnp.float32)
    half = crossed.shape[1] // 2
    crossed = crossed[:, :half] + crossed[:, half:]
    kernel = diagonal(crossed, ka, ba, cond_count // ba * cond_count, -1.0)
    out[:codes, :] = placed_piece(kernel, table, dims, ba)
    out[codes:, :] = extras[...]


def near(ka, ba, dims, fields, table, extras, cond_all):
    vloc, val_count, cond_count, npol = dims
    operands = [fields, table, extras, *cond_all]
    shape = (val_count * cond_count + EXTRA_ROWS, extras.shape[1])
    return pl.pallas_call(
        functools.partial(near_kernel, ka, ba, dims),
        out_shape=in_vmem(shape, jnp.float32),
        in_specs=[vmem] * len(operands),
        out_specs=vmem,
        cost_estimate=LIGHT,
        compiler_params=limits(*operands),
        name="near",
    )(*operands)


def couple_kernel(ka, ga, ba, share_rows, screening, *refs):
    cond_in, outs = refs[:ba], refs[ba:]
    mine = lax.axis_index("ga")
    wide = jnp.concatenate([ref[...].astype(jnp.float32) for ref in cond_in], 0)
    straight, turned = [], []
    for at in range(0, wide.shape[0], 2 * share_rows):
        real, imag = wide[at : at + share_rows], wide[at + share_rows : at + 2 * share_rows]
        straight += [real, -imag]
        turned += [imag, real]
    straight = jnp.concatenate(straight, 0).astype(jnp.bfloat16)
    turned = jnp.concatenate(turned, 0).astype(jnp.bfloat16)
    width = screening.shape[2] // ga
    columns = [columns_of(origin(mine, r, ga), width) for r in range(1, ga)]
    coupled = [
        jnp.dot(straight, screening[0, :, block], preferred_element_type=jnp.float32)
        + jnp.dot(turned, screening[1, :, block], preferred_element_type=jnp.float32)
        for block in columns
    ]
    for out, value in zip(outs, coupled):
        high, low = split(value)
        out[: value.shape[0], :] = high
        out[value.shape[0] :, :] = low


def couple(ka, ga, ba, dims, screening, cond_all):
    share_rows = dims[2] // ba * dims[2]
    rows = 2 * sum(x.shape[0] for x in cond_all)
    width = screening.shape[2] // ga
    operands = [screening, *cond_all]
    return pl.pallas_call(
        functools.partial(couple_kernel, ka, ga, ba, share_rows),
        out_shape=[in_vmem((rows, width), jnp.bfloat16)] * (ga - 1),
        in_specs=[vmem] * len(operands),
        out_specs=[vmem] * (ga - 1),
        cost_estimate=LIGHT,
        compiler_params=limits(*operands),
        name="couple",
    )(*operands)


def contract_kernel(ka, ba, count, dims, *refs):
    vloc, val_count, cond_count, npol = dims
    table, held, out = refs[0], refs[1], refs[-1]
    each = (len(refs) - 3 - count) // count
    codes = val_count * cond_count
    crossed = None
    for r in range(count):
        coupled = refs[2 + r]
        halves = refs[2 + count + r * each : 2 + count + (r + 1) * each]
        rows = jnp.concatenate(with_turned(halves, vloc * val_count), 0).astype(jnp.bfloat16)
        term = lax.dot_general(
            coupled[...], rows, (((1,), (1,)), ((), ())), preferred_element_type=jnp.float32
        )
        crossed = term if crossed is None else crossed + term
    half = crossed.shape[0] // 2
    crossed = crossed[:half] + crossed[half:]
    kernel = diagonal(crossed, ka, ba, cond_count // ba * cond_count, 1.0)
    piece = placed_piece(kernel, table, dims, ba)
    before = held.shape[0] - EXTRA_ROWS
    out[:codes, :] = piece + held[:codes, :] if before else piece
    out[codes:, :] = held[before:, :]


def contract(ka, ba, dims, table, held, coupled, valence, name):
    val_count, cond_count = dims[1:3]
    operands = [table, held, *coupled, *valence]
    shape = (val_count * cond_count + EXTRA_ROWS, held.shape[1])
    return pl.pallas_call(
        functools.partial(contract_kernel, ka, ba, len(coupled), dims),
        out_shape=in_vmem(shape, jnp.float32),
        in_specs=[vmem] * len(operands),
        out_specs=vmem,
        cost_estimate=LIGHT,
        compiler_params=limits(*operands),
        name=name,
    )(*operands)


def haydock_kernel(ka, codes, scale_count, npol, *refs):
    pieces = refs[:-3]
    next_out, coef_out, matrix = refs[-3:]
    lanes = pieces[0].shape[1]
    mid = lanes // 2
    height = codes + EXTRA_ROWS
    found = [(ref, at) for ref in pieces for at in range(0, ref.shape[0], height)]
    extras = None
    slots = []
    for ref, at in found:
        rows = ref[at + codes : at + height, :]
        extras = rows if extras is None else extras + rows
        slots.append((ref[at : at + codes, :], rows[npol + 2 : npol + 3]))
    own = pieces[0][codes:height, :]
    sign = jnp.where(iota((1, lanes), 1) < mid, -1.0, 1.0)
    for k2 in range(ka):
        block = jnp.zeros((codes, lanes), jnp.float32)
        for piece, second in slots:
            block = jnp.where(second == float(k2), piece, block)
        matrix[k2 * codes : (k2 + 1) * codes, :] = block
        matrix[mid + k2 * codes : mid + (k2 + 1) * codes, :] = sign * pltpu.roll(block, mid, 1)
    high, low = split(matrix[...])
    full = jnp.concatenate([high, low], 1)
    start = extras[:npol]
    energy = extras[npol : npol + 1]

    def halves(vector):
        top = vector.astype(jnp.bfloat16).astype(jnp.float32)
        return jnp.concatenate([top, vector - top], 0).astype(jnp.bfloat16)

    def mean(values):
        return jnp.sum(values, axis=1, keepdims=True) / scale_count

    def norm(vector):
        return jnp.sqrt(mean(vector * vector) + EPSILON)

    def swap(vector):
        return pltpu.roll(vector, mid, 1)

    def hamiltonian(vector):
        product = jnp.dot(halves(vector), full, preferred_element_type=jnp.float32)
        main = product[:npol, :lanes] + product[npol:, :lanes]
        return energy * vector - (main + product[:npol, lanes:])

    def inner(left, right):
        return mean(left * right), mean(-sign * left * swap(right))

    def times(real, imag, vector):
        return real * vector + imag * (sign * swap(vector))

    start_image = hamiltonian(start)
    scale = 1.0 / norm(start)
    first = start * scale
    first_image = start_image * scale
    alpha_real, alpha_imag = inner(first, first_image)
    first_resid = first_image - times(alpha_real, alpha_imag, first)
    resid_image = hamiltonian(first_resid)
    beta_one = norm(first_resid)
    scale = 1.0 / beta_one
    second = first_resid * scale
    second_image = resid_image * scale
    gamma_real, gamma_imag = inner(second, second_image)
    second_resid = second_image - times(gamma_real, gamma_imag, second) - beta_one * first
    beta_two = norm(second_resid)

    coef_lane = iota(coef_out.shape, 1)
    coefs = jnp.zeros(coef_out.shape, jnp.float32)
    for at, value in enumerate((alpha_real, alpha_imag, gamma_real, gamma_imag, beta_one, beta_two)):
        coefs = jnp.where(coef_lane == at, value, coefs)
    coef_out[...] = coefs
    row = iota((2 * codes, lanes), 0)
    lane = iota((2 * codes, lanes), 1)
    here = (lane % mid // codes == lax.axis_index("ka")) & (lane // mid == row // codes)
    band = (row % codes).astype(jnp.float32)
    pick = jnp.where(here & (own[npol + 1 : npol + 2] == band), 1.0, 0.0).astype(jnp.bfloat16)
    picked = lax.dot_general(
        halves(second_resid), pick, (((1,), (1,)), ((), ())), preferred_element_type=jnp.float32
    )
    picked = (picked[:npol] + picked[npol:]) / beta_two
    next_out[0, :, 0, :] = picked[:, :codes]
    next_out[0, :, 1, :] = picked[:, codes:]


def haydock(ka, codes, scale_count, npol, pieces):
    lanes = pieces[0].shape[1]
    square = jax.ShapeDtypeStruct((lanes, lanes), jnp.float32)
    return pl.pallas_call(
        functools.partial(haydock_kernel, ka, codes, scale_count, npol),
        out_shape=[
            jax.ShapeDtypeStruct((1, npol, 2, codes), jnp.float32),
            jax.ShapeDtypeStruct((npol, 6), jnp.float32),
        ],
        in_specs=[vmem] * len(pieces),
        out_specs=[vmem, vmem],
        scratch_shapes=[pltpu.VMEM(square.shape, square.dtype)],
        compiler_params=limits(*pieces, square),
        name="haydock",
    )(*pieces)


def summed(value, axis):
    size = lax.axis_size(axis)
    if size & (size - 1):
        return value + sum(shifted(value, axis, step) for step in range(1, size))
    step = 1
    while step < size:
        value = value + exchanged(value, axis, lambda i, size: i ^ step)
        step *= 2
    return value


def local(
    ka,
    ga,
    ba,
    start_vector,
    valence_density,
    conduction_density,
    screening,
    qpoint_map,
    slot_owner,
    band_pairs,
    valence_energy,
    conduction_energy,
):
    npol = start_vector.shape[1]
    pair_count = start_vector.shape[3]
    kcount, vloc, val_count = qpoint_map.shape[0], valence_density.shape[3], valence_density.shape[4]
    cond_count = conduction_density.shape[3]
    pairs = vloc * val_count
    dims = (vloc, val_count, cond_count, npol)
    packed = pack(ka, ba, qpoint_map, slot_owner, valence_density, conduction_density)
    blocks = [packed[0]] + [shifted(packed[j], "ka", j) for j in range(1, ka)]
    early = ka // 2
    val_rows = slice(0, 2 * pairs)
    val_early = regroup(blocks[:early], val_rows)
    far_early = [shifted(val_early, "ga", r) for r in range(1, ga)]
    whole, near_table, far_table, extras = prepare(
        ka,
        dims,
        qpoint_map,
        slot_owner,
        band_pairs,
        valence_energy,
        conduction_energy,
        start_vector,
        screening,
        val_early,
    )
    val_late = regroup(blocks[early:], val_rows, (extras,))
    far_late = [shifted(val_late, "ga", r) for r in range(1, ga)]
    height = 2 * cond_count // ba * cond_count
    width = blocks[0].shape[1] // PARTS
    cond_rows = slice(2 * pairs, 2 * pairs + height)
    cond_parts = [
        regroup(blocks[1:], cond_rows, (val_late, *far_early), slice(c * width, (c + 1) * width))
        for c in range(PARTS)
    ]
    fields = field(pairs, whole, [val_early, val_late])
    cond_all = [regroup(blocks, cond_rows)]
    for r in range(1, ba):
        own_rows = slice(2 * pairs + r * height, 2 * pairs + (r + 1) * height)
        came = [handed(part, r) for part in cond_parts]
        cond_all.append(assemble(own_rows, blocks[0], came, fields))
    piece = near(ka, ba, dims, fields, near_table, extras, cond_all)
    if ga > 1:
        coupled = couple(ka, ga, ba, dims, whole, cond_all)
        far = [half for both in zip(far_early, far_late) for half in both]
        piece = contract(ka, ba, dims, far_table, piece, coupled, far, "far")
    piece = piece + sum(handed(piece, r) for r in range(1, ba))
    piece = summed(piece, "ga")
    pieces = [piece] + [shifted(piece, "ka", j) for j in range(1, ka)]
    scale_count = float(kcount * pair_count)
    return tuple(haydock(ka, pair_count, scale_count, npol, pieces))


def solution(mesh):
    in_specs = (
        P(("grp", "ka"), None, None, None),
        P(("grp", "ka"), None, None, "ba", None, "ga"),
        P(("grp", "ka"), None, None, None, None, "ga"),
        P(("grp", "ka"), None, "ga", None),
        P(),
        P(),
        P(),
        P(("grp", "ka"), None),
        P(("grp", "ka"), None),
    )
    out_specs = (P(("grp", "ka"), None, None, None), P("grp", None))
    body = functools.partial(local, mesh.shape["ka"], mesh.shape["ga"], mesh.shape["ba"])
    return jax.shard_map(body, mesh=mesh, in_specs=in_specs, out_specs=out_specs, check_vma=False)
```

```python
import functools
import math

import jax
import jax.numpy as jnp
from jax import lax
from jax.experimental import pallas as pl
from jax.experimental.pallas import tpu as pltpu
from jax.sharding import PartitionSpec as P

EPSILON = 1e-06
EXACT = lax.Precision.HIGHEST
VMEM_LEAST = 8 * 1024 * 1024
VMEM_MOST = 56 * 1024 * 1024

vmem = pl.BlockSpec(memory_space=pltpu.VMEM)
anywhere = pl.BlockSpec(memory_space=pl.ANY)
EXTRA_ROWS = 8
LIGHT = pl.CostEstimate(flops=1, bytes_accessed=1, transcendentals=0)
CHUNKS = 4
PARTS = 2


def in_vmem(shape, dtype):
    return pltpu.VMEM(shape, dtype)


def placed(value, space):
    return pltpu.with_memory_space_constraint(value, space)


def iota(shape, axis):
    return lax.broadcasted_iota(jnp.int32, shape, axis)


def split(values):
    high = values.astype(jnp.bfloat16)
    low = (values - high.astype(jnp.float32)).astype(jnp.bfloat16)
    return high, low


def limits(*arrays):
    held = sum(math.prod(a.shape) * a.dtype.itemsize for a in arrays)
    return pltpu.CompilerParams(vmem_limit_bytes=min(VMEM_MOST, VMEM_LEAST + 4 * held))


def target(me, step, size):
    return lax.rem(me + step, size)


def origin(me, step, size):
    return lax.rem(me + size - step, size)


def exchanged(value, axis, move):
    size, cores = lax.axis_size(axis), lax.axis_size("ba")
    pairs = [
        (i * cores + h, move(i, size) * cores + (h + 1) % cores)
        for i in range(size)
        for h in range(cores)
    ]
    return lax.ppermute(value, (axis, "ba"), pairs)


def shifted(value, axis, step):
    return exchanged(value, axis, lambda i, size: (i + step) % size)


def handed(value, step):
    size = lax.axis_size("ba")
    return lax.ppermute(value, "ba", [(h, (h + step) % size) for h in range(size)])


def pack_kernel(ka, qmap_in, owner_in, valence_in, conduction_in, *rest):
    outs = rest[:ka]
    qmap, owner, partner, valence, conduction, sems = rest[ka:]
    copies = [
        pltpu.make_async_copy(src, dst, sems.at[at])
        for at, (src, dst) in enumerate(
            ((qmap_in, qmap), (owner_in, owner), (valence_in, valence), (conduction_in, conduction))
        )
    ]
    for copy in copies:
        copy.start()
    me = lax.axis_index("ka")
    half = lax.axis_index("ba")
    count, width = valence.shape[1], valence.shape[5]
    cond_count = conduction.shape[3]
    share = cond_count // lax.axis_size("ba")
    val_rows = 2 * valence.shape[3] * valence.shape[4]
    cond_rows = 2 * share * cond_count

    def note(k2, carry):
        partner[owner[qmap[me, k2]]] = k2
        return carry

    copies[0].wait()
    copies[1].wait()
    lax.fori_loop(0, count, note, 0)
    copies[2].wait()
    copies[3].wait()
    for at in range(ka):
        k2 = partner[target(me, at, ka)]
        block = valence[0, k2].astype(jnp.float32).reshape(val_rows, width)
        outs[at][:val_rows, :] = block.astype(jnp.bfloat16)
        to = lax.rem(half + min(at, 1), lax.axis_size("ba"))
        block = conduction[0, k2, :, pl.ds(to * share, share)].astype(jnp.float32)
        outs[at][val_rows : val_rows + cond_rows, :] = block.reshape(cond_rows, width).astype(jnp.bfloat16)
    cores = lax.axis_size("ba")
    for h in range(1, cores):
        part = lax.rem(half + cores - h, cores)
        block = conduction[0, partner[me], :, pl.ds(part * share, share)].astype(jnp.float32)
        rows = slice(val_rows + h * cond_rows, val_rows + (h + 1) * cond_rows)
        outs[0][rows, :] = block.reshape(cond_rows, width).astype(jnp.bfloat16)


def pack(ka, ba, qmap, owner, valence, conduction):
    cond_count = conduction.shape[3]
    val_rows, cond_rows = 2 * valence.shape[3] * valence.shape[4], 2 * cond_count // ba * cond_count
    own = in_vmem((val_rows + ba * cond_rows, valence.shape[5]), valence.dtype)
    shape = in_vmem((val_rows + cond_rows, valence.shape[5]), valence.dtype)
    operands = [placed(x, pltpu.HBM) for x in (qmap, owner, valence, conduction)]
    return pl.pallas_call(
        functools.partial(pack_kernel, ka),
        out_shape=[own] + [shape] * (ka - 1),
        in_specs=[anywhere] * 4,
        out_specs=[vmem] * ka,
        scratch_shapes=[
            pltpu.SMEM(qmap.shape, jnp.int32),
            pltpu.SMEM(owner.shape, jnp.int32),
            pltpu.SMEM(owner.shape, jnp.int32),
            pltpu.VMEM(valence.shape, valence.dtype),
            pltpu.VMEM(conduction.shape, conduction.dtype),
            pltpu.SemaphoreType.DMA((4,)),
        ],
        compiler_params=limits(valence, conduction),
        name="pack",
    )(*operands)


def prepare_kernel(ka, dims, *refs):
    vloc, val_count, cond_count, npol = dims
    ins, screening, (screen_out, near_table, far_table, extras), scratch = refs[:6], refs[6], refs[8:12], refs[12:]
    qmap, owner, band_pairs, val_energy, cond_energy, start, sems, screen_sems = scratch
    me = lax.axis_index("ka")
    half = lax.axis_index("ba")
    mine = lax.axis_index("ga")
    copies = [
        pltpu.make_async_copy(src, dst, sems.at[at])
        for at, (src, dst) in enumerate(
            zip(ins, (qmap, owner, band_pairs, val_energy, cond_energy, start))
        )
    ]
    height = screening.shape[2] // CHUNKS
    chunks = [
        pltpu.make_async_copy(
            screening.at[0, part, pl.ds(c * height, height)],
            screen_out.at[part, pl.ds(c * height, height)],
            screen_sems.at[part, c],
        )
        for part in range(2)
        for c in range(CHUNKS)
    ]
    for copy in copies + chunks:
        copy.start()
    pairs = vloc * val_count
    block = 2 * pairs
    rows = ka * block
    codes = val_count * cond_count
    mid = ka * codes
    lanes = 2 * mid
    row = iota((2 * rows, lanes), 0)
    col = iota((2 * rows, lanes), 1)
    j_of_row = row % rows // block
    cores = lax.axis_size("ba")
    for moves, table in enumerate((near_table, far_table)):
        share = lax.rem(half + 2 * cores - moves - jnp.where(j_of_row == 0, 0, 1), cores)
        want = (
            (row % block // pairs) * mid
            + origin(me, j_of_row, ka) * codes
            + (share * vloc + row % pairs // val_count) * cond_count
        )
        joined = (col - want >= 0) & (col - want < cond_count)
        for v2 in range(val_count):
            pick = jnp.where(joined & (row % val_count == v2), 1.0, 0.0)
            table[:, v2 * lanes : (v2 + 1) * lanes] = pick.astype(jnp.bfloat16)

    for copy in copies:
        copy.wait()
    first = jnp.where((mine == 0) & (half == 0), 1.0, 0.0)
    lane = iota((1, lanes), 1)
    lane_k = lane % mid // codes
    band_row = iota((codes, lanes), 0)
    band_lane = iota((codes, lanes), 1)
    code = jnp.zeros((codes, lanes), jnp.int32)
    bands = jnp.full((1, lanes), -1.0, jnp.float32)
    for b in range(codes):
        code = jnp.where(band_row == b, band_pairs[b], code)
        bands = jnp.where(lane % codes == band_pairs[b], float(b), bands)
    vectors = jnp.zeros((npol, lanes), jnp.float32)
    for part in range(2):
        spot = part * mid + me * codes
        pick = jnp.where(band_lane == spot + code, first, 0.0)
        vectors = vectors + jnp.dot(start[0, :, part, :], pick, precision=EXACT)
    energy = jnp.zeros((1, lanes), jnp.float32)
    for c in range(cond_count):
        energy = jnp.where(lane % cond_count == c, cond_energy[0, c], energy)
    for v in range(val_count):
        energy = energy - jnp.where(lane % codes // cond_count == v, val_energy[0, v], 0.0)
    energy = jnp.where(lane_k == me, energy * first, 0.0)
    kcount = qmap.shape[0]

    def find(k2, found):
        return jnp.where(owner[qmap[0, k2]] == me, k2, found)

    back = lax.fori_loop(0, kcount, find, 0)
    second = lane_k + back
    second = jnp.where(second >= kcount, second - kcount, second).astype(jnp.float32) * first
    rest = jnp.zeros((EXTRA_ROWS - 3 - npol, lanes), jnp.float32)
    extras[...] = jnp.concatenate([vectors, energy, bands * first, second, rest], 0)
    for copy in chunks:
        copy.wait()


def prepare(ka, dims, qmap, owner, band_pairs, val_energy, cond_energy, start, screening, after):
    vloc, val_count, cond_count, npol = dims
    rows = 4 * ka * vloc * val_count
    lanes = 2 * ka * val_count * cond_count
    operands = (qmap, owner, band_pairs, val_energy, cond_energy, start, screening)
    table = jax.ShapeDtypeStruct((rows, val_count * lanes), jnp.bfloat16)
    return pl.pallas_call(
        functools.partial(prepare_kernel, ka, dims),
        out_shape=[
            in_vmem(screening.shape[1:], screening.dtype),
            in_vmem(table.shape, table.dtype),
            in_vmem(table.shape, table.dtype),
            in_vmem((EXTRA_ROWS, lanes), jnp.float32),
        ],
        in_specs=[anywhere] * 8,
        out_specs=[vmem] * 4,
        scratch_shapes=[pltpu.SMEM(x.shape, x.dtype) for x in operands[:5]]
        + [
            pltpu.VMEM(start.shape, start.dtype),
            pltpu.SemaphoreType.DMA((6,)),
            pltpu.SemaphoreType.DMA((2, CHUNKS)),
        ],
        cost_estimate=pl.CostEstimate(
            flops=0, bytes_accessed=4 * screening.size, transcendentals=0
        ),
        compiler_params=limits(table),
        name="prepare",
    )(*[placed(x, pltpu.HBM) for x in operands], after)


def regroup_kernel(count, rows, columns, *refs):
    blocks, out = refs[:count], refs[-1]
    height = rows.stop - rows.start
    for at in range(count):
        out[at * height : (at + 1) * height, :] = blocks[at][rows, columns]


def regroup(blocks, rows, after=(), columns=None):
    columns = columns or slice(0, blocks[0].shape[1])
    shape = (len(blocks) * (rows.stop - rows.start), columns.stop - columns.start)
    return pl.pallas_call(
        functools.partial(regroup_kernel, len(blocks), rows, columns),
        out_shape=in_vmem(shape, blocks[0].dtype),
        in_specs=[vmem] * len(blocks) + [anywhere] * len(after),
        out_specs=vmem,
        compiler_params=limits(*blocks),
        name="regroup",
    )(*blocks, *after)


def assemble_kernel(rows, own, *refs):
    parts, out = refs[:PARTS], refs[-1]
    height = rows.stop - rows.start
    out[:height, :] = own[rows, :]
    width = parts[0].shape[1]
    for c, part in enumerate(parts):
        out[height:, c * width : (c + 1) * width] = part[...]


def assemble(rows, own, parts, after):
    height = rows.stop - rows.start + parts[0].shape[0]
    return pl.pallas_call(
        functools.partial(assemble_kernel, rows),
        out_shape=in_vmem((height, own.shape[1]), own.dtype),
        in_specs=[vmem] * (1 + len(parts)) + [anywhere],
        out_specs=vmem,
        compiler_params=limits(own, *parts),
        name="assemble",
    )(own, *parts, after)


def with_turned(halves, pairs):
    wide = jnp.concatenate([half[...].astype(jnp.float32) for half in halves], 0)
    parts = []
    for at in range(0, wide.shape[0], 2 * pairs):
        parts += [-wide[at + pairs : at + 2 * pairs], wide[at : at + pairs]]
    return wide, jnp.concatenate(parts, 0)


def columns_of(place, width):
    return pl.ds(pl.multiple_of(place * width, 128), width)


def placed_piece(kernel, table, dims, ba):
    vloc, val_count, cond_count, npol = dims
    half = lax.axis_index("ba")
    codes = val_count * cond_count
    lanes = table.shape[1] // val_count
    share = cond_count // ba
    cond_rows = cond_count * cond_count
    spread = jnp.dot(
        jnp.concatenate(split(kernel), 0), table[...], preferred_element_type=jnp.float32
    )
    spread = spread[:cond_rows] + spread[cond_rows:]
    crow = iota((cond_rows, lanes), 0)
    share_rows = share * cond_count
    c_of_row = origin(half, crow // share_rows, ba) * share + crow % share_rows // cond_count
    same_c = c_of_row == iota((cond_rows, lanes), 1) % cond_count
    rows = []
    for v2 in range(val_count):
        kept = jnp.where(same_c, spread[:, v2 * lanes : (v2 + 1) * lanes], 0.0)
        parts = [kept[c * cond_count : (c + 1) * cond_count] for c in range(cond_count)]
        while len(parts) > 1:
            parts = [x + y for x, y in zip(parts[::2], parts[1::2])] + parts[len(parts) // 2 * 2 :]
        rows.append(parts[0])
    return jnp.concatenate(rows, 0)


def diagonal(crossed, ka, ba, share_rows, sign):
    rows = crossed.shape[1] // 2
    lane = iota((share_rows, 2 * rows), 1)
    lane_j = lane % rows // (rows // ka)
    straight = lane < rows
    kernel = []
    for h in range(ba):
        total = jnp.zeros((share_rows, 2 * rows), jnp.float32)
        for j in range(ka):
            at = (h * ka + j) * 2 * share_rows
            real = crossed[at : at + share_rows]
            imag = crossed[at + share_rows : at + 2 * share_rows]
            total = jnp.where(lane_j == j, jnp.where(straight, real, sign * imag), total)
        kernel.append(total)
    return jnp.concatenate(kernel, 0)


def field_kernel(pairs, screening, *refs):
    halves, out = refs[:-1], refs[-1]
    columns = columns_of(lax.axis_index("ga"), halves[0].shape[1])
    wide, turned = with_turned(halves, pairs)
    real = jnp.concatenate([wide, turned], 0).astype(jnp.bfloat16)
    imag = jnp.concatenate([turned, -wide], 0).astype(jnp.bfloat16)
    form = (((1,), (1,)), ((), ()))
    fields = lax.dot_general(
        screening[0, :, columns], real, form, preferred_element_type=jnp.float32
    ) + lax.dot_general(screening[1, :, columns], imag, form, preferred_element_type=jnp.float32)
    lanes = fields.shape[1]
    high, low = split(fields)
    out[:, :lanes] = high
    out[:, lanes:] = low


def field(pairs, screening, halves):
    operands = [screening, *halves]
    rows = sum(half.shape[0] for half in halves)
    return pl.pallas_call(
        functools.partial(field_kernel, pairs),
        out_shape=in_vmem((screening.shape[1], 4 * rows), jnp.bfloat16),
        in_specs=[vmem] * len(operands),
        out_specs=vmem,
        cost_estimate=LIGHT,
        compiler_params=limits(*operands),
        name="field",
    )(*operands)


def near_kernel(ka, ba, dims, *refs):
    vloc, val_count, cond_count, npol = dims
    fields, table, extras = refs[:3]
    cond_in, out = refs[3:-1], refs[-1]
    codes = val_count * cond_count
    cond = jnp.concatenate([ref[...] for ref in cond_in], 0)
    crossed = jnp.dot(cond, fields[...], preferred_element_type=jnp.float32)
    half = crossed.shape[1] // 2
    crossed = crossed[:, :half] + crossed[:, half:]
    kernel = diagonal(crossed, ka, ba, cond_count // ba * cond_count, -1.0)
    out[:codes, :] = placed_piece(kernel, table, dims, ba)
    out[codes:, :] = extras[...]


def near(ka, ba, dims, fields, table, extras, cond_all):
    vloc, val_count, cond_count, npol = dims
    operands = [fields, table, extras, *cond_all]
    shape = (val_count * cond_count + EXTRA_ROWS, extras.shape[1])
    return pl.pallas_call(
        functools.partial(near_kernel, ka, ba, dims),
        out_shape=in_vmem(shape, jnp.float32),
        in_specs=[vmem] * len(operands),
        out_specs=vmem,
        cost_estimate=LIGHT,
        compiler_params=limits(*operands),
        name="near",
    )(*operands)


def couple_kernel(ka, ga, ba, share_rows, screening, *refs):
    cond_in, outs = refs[:ba], refs[ba:]
    mine = lax.axis_index("ga")
    wide = jnp.concatenate([ref[...].astype(jnp.float32) for ref in cond_in], 0)
    straight, turned = [], []
    for at in range(0, wide.shape[0], 2 * share_rows):
        real, imag = wide[at : at + share_rows], wide[at + share_rows : at + 2 * share_rows]
        straight += [real, -imag]
        turned += [imag, real]
    straight = jnp.concatenate(straight, 0).astype(jnp.bfloat16)
    turned = jnp.concatenate(turned, 0).astype(jnp.bfloat16)
    width = screening.shape[2] // ga
    columns = [columns_of(origin(mine, r, ga), width) for r in range(1, ga)]
    coupled = [
        jnp.dot(straight, screening[0, :, block], preferred_element_type=jnp.float32)
        + jnp.dot(turned, screening[1, :, block], preferred_element_type=jnp.float32)
        for block in columns
    ]
    for out, value in zip(outs, coupled):
        high, low = split(value)
        out[: value.shape[0], :] = high
        out[value.shape[0] :, :] = low


def couple(ka, ga, ba, dims, screening, cond_all):
    share_rows = dims[2] // ba * dims[2]
    rows = 2 * sum(x.shape[0] for x in cond_all)
    width = screening.shape[2] // ga
    operands = [screening, *cond_all]
    return pl.pallas_call(
        functools.partial(couple_kernel, ka, ga, ba, share_rows),
        out_shape=[in_vmem((rows, width), jnp.bfloat16)] * (ga - 1),
        in_specs=[vmem] * len(operands),
        out_specs=[vmem] * (ga - 1),
        cost_estimate=LIGHT,
        compiler_params=limits(*operands),
        name="couple",
    )(*operands)


def contract_kernel(ka, ba, count, dims, *refs):
    vloc, val_count, cond_count, npol = dims
    table, held, out = refs[0], refs[1], refs[-1]
    each = (len(refs) - 3 - count) // count
    codes = val_count * cond_count
    crossed = None
    for r in range(count):
        coupled = refs[2 + r]
        halves = refs[2 + count + r * each : 2 + count + (r + 1) * each]
        rows = jnp.concatenate(with_turned(halves, vloc * val_count), 0).astype(jnp.bfloat16)
        term = lax.dot_general(
            coupled[...], rows, (((1,), (1,)), ((), ())), preferred_element_type=jnp.float32
        )
        crossed = term if crossed is None else crossed + term
    half = crossed.shape[0] // 2
    crossed = crossed[:half] + crossed[half:]
    kernel = diagonal(crossed, ka, ba, cond_count // ba * cond_count, 1.0)
    piece = placed_piece(kernel, table, dims, ba)
    before = held.shape[0] - EXTRA_ROWS
    out[:codes, :] = piece + held[:codes, :] if before else piece
    out[codes:, :] = held[before:, :]


def contract(ka, ba, dims, table, held, coupled, valence, name):
    val_count, cond_count = dims[1:3]
    operands = [table, held, *coupled, *valence]
    shape = (val_count * cond_count + EXTRA_ROWS, held.shape[1])
    return pl.pallas_call(
        functools.partial(contract_kernel, ka, ba, len(coupled), dims),
        out_shape=in_vmem(shape, jnp.float32),
        in_specs=[vmem] * len(operands),
        out_specs=vmem,
        cost_estimate=LIGHT,
        compiler_params=limits(*operands),
        name=name,
    )(*operands)


def haydock_kernel(ka, codes, scale_count, npol, *refs):
    pieces = refs[:-2]
    next_out, coef_out = refs[-2:]
    lanes = pieces[0].shape[1]
    mid = lanes // 2
    height = codes + EXTRA_ROWS
    found = [(ref, at) for ref in pieces for at in range(0, ref.shape[0], height)]
    extras = None
    slots = []
    for ref, at in found:
        rows = ref[at + codes : at + height, :]
        extras = rows if extras is None else extras + rows
        slots.append((ref[at : at + codes, :], rows[npol + 2 : npol + 3]))
    own = pieces[0][codes:height, :]
    sign = jnp.where(iota((1, lanes), 1) < mid, -1.0, 1.0)
    top = []
    for k2 in range(ka):
        block = jnp.zeros((codes, lanes), jnp.float32)
        for piece, second in slots:
            block = jnp.where(second == float(k2), piece, block)
        top.append(block)
    top = jnp.concatenate(top, 0)
    matrix = jnp.concatenate([top, sign * pltpu.roll(top, mid, 1)], 0)
    full = jnp.concatenate(split(matrix), 1)
    start = extras[:npol]
    energy = extras[npol : npol + 1]

    def halves(vector):
        top = vector.astype(jnp.bfloat16).astype(jnp.float32)
        return jnp.concatenate([top, vector - top], 0).astype(jnp.bfloat16)

    def mean(values):
        return jnp.sum(values, axis=1, keepdims=True) / scale_count

    def norm(vector):
        return jnp.sqrt(mean(vector * vector) + EPSILON)

    def swap(vector):
        return pltpu.roll(vector, mid, 1)

    def hamiltonian(vector):
        product = jnp.dot(halves(vector), full, preferred_element_type=jnp.float32)
        main = product[:npol, :lanes] + product[npol:, :lanes]
        return energy * vector - (main + product[:npol, lanes:])

    def inner(left, right):
        return mean(left * right), mean(-sign * left * swap(right))

    def times(real, imag, vector):
        return real * vector + imag * (sign * swap(vector))

    start_image = hamiltonian(start)
    scale = 1.0 / norm(start)
    first = start * scale
    first_image = start_image * scale
    alpha_real, alpha_imag = inner(first, first_image)
    first_resid = first_image - times(alpha_real, alpha_imag, first)
    resid_image = hamiltonian(first_resid)
    beta_one = norm(first_resid)
    scale = 1.0 / beta_one
    second = first_resid * scale
    second_image = resid_image * scale
    gamma_real, gamma_imag = inner(second, second_image)
    second_resid = second_image - times(gamma_real, gamma_imag, second) - beta_one * first
    beta_two = norm(second_resid)

    coef_lane = iota(coef_out.shape, 1)
    coefs = jnp.zeros(coef_out.shape, jnp.float32)
    for at, value in enumerate((alpha_real, alpha_imag, gamma_real, gamma_imag, beta_one, beta_two)):
        coefs = jnp.where(coef_lane == at, value, coefs)
    coef_out[...] = coefs
    row = iota((2 * codes, lanes), 0)
    lane = iota((2 * codes, lanes), 1)
    here = (lane % mid // codes == lax.axis_index("ka")) & (lane // mid == row // codes)
    band = (row % codes).astype(jnp.float32)
    pick = jnp.where(here & (own[npol + 1 : npol + 2] == band), 1.0, 0.0).astype(jnp.bfloat16)
    picked = lax.dot_general(
        halves(second_resid), pick, (((1,), (1,)), ((), ())), preferred_element_type=jnp.float32
    )
    picked = (picked[:npol] + picked[npol:]) / beta_two
    next_out[0, :, 0, :] = picked[:, :codes]
    next_out[0, :, 1, :] = picked[:, codes:]


def haydock(ka, codes, scale_count, npol, pieces):
    lanes = pieces[0].shape[1]
    square = jax.ShapeDtypeStruct((lanes, lanes), jnp.float32)
    return pl.pallas_call(
        functools.partial(haydock_kernel, ka, codes, scale_count, npol),
        out_shape=[
            jax.ShapeDtypeStruct((1, npol, 2, codes), jnp.float32),
            jax.ShapeDtypeStruct((npol, 6), jnp.float32),
        ],
        in_specs=[vmem] * len(pieces),
        out_specs=[vmem, vmem],
        compiler_params=limits(*pieces, square),
        name="haydock",
    )(*pieces)


def summed(value, axis):
    size = lax.axis_size(axis)
    if size & (size - 1):
        return value + sum(shifted(value, axis, step) for step in range(1, size))
    step = 1
    while step < size:
        value = value + exchanged(value, axis, lambda i, size: i ^ step)
        step *= 2
    return value


def local(
    ka,
    ga,
    ba,
    start_vector,
    valence_density,
    conduction_density,
    screening,
    qpoint_map,
    slot_owner,
    band_pairs,
    valence_energy,
    conduction_energy,
):
    npol = start_vector.shape[1]
    pair_count = start_vector.shape[3]
    kcount, vloc, val_count = qpoint_map.shape[0], valence_density.shape[3], valence_density.shape[4]
    cond_count = conduction_density.shape[3]
    pairs = vloc * val_count
    dims = (vloc, val_count, cond_count, npol)
    packed = pack(ka, ba, qpoint_map, slot_owner, valence_density, conduction_density)
    blocks = [packed[0]] + [shifted(packed[j], "ka", j) for j in range(1, ka)]
    early = ka // 2
    val_rows = slice(0, 2 * pairs)
    val_early = regroup(blocks[:early], val_rows)
    far_early = [shifted(val_early, "ga", r) for r in range(1, ga)]
    whole, near_table, far_table, extras = prepare(
        ka,
        dims,
        qpoint_map,
        slot_owner,
        band_pairs,
        valence_energy,
        conduction_energy,
        start_vector,
        screening,
        val_early,
    )
    val_late = regroup(blocks[early:], val_rows, (extras,))
    far_late = [shifted(val_late, "ga", r) for r in range(1, ga)]
    height = 2 * cond_count // ba * cond_count
    width = blocks[0].shape[1] // PARTS
    cond_rows = slice(2 * pairs, 2 * pairs + height)
    cond_parts = [
        regroup(blocks[1:], cond_rows, (val_late, *far_early), slice(c * width, (c + 1) * width))
        for c in range(PARTS)
    ]
    fields = field(pairs, whole, [val_early, val_late])
    cond_all = [regroup(blocks, cond_rows)]
    for r in range(1, ba):
        own_rows = slice(2 * pairs + r * height, 2 * pairs + (r + 1) * height)
        came = [handed(part, r) for part in cond_parts]
        cond_all.append(assemble(own_rows, blocks[0], came, fields))
    piece = near(ka, ba, dims, fields, near_table, extras, cond_all)
    if ga > 1:
        coupled = couple(ka, ga, ba, dims, whole, cond_all)
        far = [half for both in zip(far_early, far_late) for half in both]
        piece = contract(ka, ba, dims, far_table, piece, coupled, far, "far")
    piece = piece + sum(handed(piece, r) for r in range(1, ba))
    piece = summed(piece, "ga")
    pieces = [piece] + [shifted(piece, "ka", j) for j in range(1, ka)]
    scale_count = float(kcount * pair_count)
    return tuple(haydock(ka, pair_count, scale_count, npol, pieces))


def solution(mesh):
    in_specs = (
        P(("grp", "ka"), None, None, None),
        P(("grp", "ka"), None, None, "ba", None, "ga"),
        P(("grp", "ka"), None, None, None, None, "ga"),
        P(("grp", "ka"), None, "ga", None),
        P(),
        P(),
        P(),
        P(("grp", "ka"), None),
        P(("grp", "ka"), None),
    )
    out_specs = (P(("grp", "ka"), None, None, None), P("grp", None))
    body = functools.partial(local, mesh.shape["ka"], mesh.shape["ga"], mesh.shape["ba"])
    return jax.shard_map(body, mesh=mesh, in_specs=in_specs, out_specs=out_specs, check_vma=False)
```

```python
import functools
import math

import jax
import jax.numpy as jnp
from jax import lax
from jax.experimental import pallas as pl
from jax.experimental.pallas import tpu as pltpu
from jax.sharding import PartitionSpec as P

EPSILON = 1e-06
EXACT = lax.Precision.HIGHEST
VMEM_LEAST = 8 * 1024 * 1024
VMEM_MOST = 56 * 1024 * 1024

vmem = pl.BlockSpec(memory_space=pltpu.VMEM)
anywhere = pl.BlockSpec(memory_space=pl.ANY)
EXTRA_ROWS = 8
LIGHT = pl.CostEstimate(flops=1, bytes_accessed=1, transcendentals=0)
CHUNKS = 4
PARTS = 2


def in_vmem(shape, dtype):
    return pltpu.VMEM(shape, dtype)


def placed(value, space):
    return pltpu.with_memory_space_constraint(value, space)


def iota(shape, axis):
    return lax.broadcasted_iota(jnp.int32, shape, axis)


def split(values):
    high = values.astype(jnp.bfloat16)
    low = (values - high.astype(jnp.float32)).astype(jnp.bfloat16)
    return high, low


def limits(*arrays):
    held = sum(math.prod(a.shape) * a.dtype.itemsize for a in arrays)
    return pltpu.CompilerParams(vmem_limit_bytes=min(VMEM_MOST, VMEM_LEAST + 4 * held))


def target(me, step, size):
    return lax.rem(me + step, size)


def origin(me, step, size):
    return lax.rem(me + size - step, size)


def exchanged(value, axis, move):
    size, cores = lax.axis_size(axis), lax.axis_size("ba")
    pairs = [
        (i * cores + h, move(i, size) * cores + (h + 1) % cores)
        for i in range(size)
        for h in range(cores)
    ]
    return lax.ppermute(value, (axis, "ba"), pairs)


def shifted(value, axis, step):
    return exchanged(value, axis, lambda i, size: (i + step) % size)


def handed(value, step):
    size = lax.axis_size("ba")
    return lax.ppermute(value, "ba", [(h, (h + step) % size) for h in range(size)])


def pack_kernel(ka, qmap_in, owner_in, valence_in, conduction_in, *rest):
    outs = rest[:ka]
    qmap, owner, partner, valence, conduction, sems = rest[ka:]
    copies = [
        pltpu.make_async_copy(src, dst, sems.at[at])
        for at, (src, dst) in enumerate(
            ((qmap_in, qmap), (owner_in, owner), (valence_in, valence), (conduction_in, conduction))
        )
    ]
    for copy in copies:
        copy.start()
    me = lax.axis_index("ka")
    half = lax.axis_index("ba")
    count, width = valence.shape[1], valence.shape[5]
    cond_count = conduction.shape[3]
    share = cond_count // lax.axis_size("ba")
    val_rows = 2 * valence.shape[3] * valence.shape[4]
    cond_rows = 2 * share * cond_count

    def note(k2, carry):
        partner[owner[qmap[me, k2]]] = k2
        return carry

    copies[0].wait()
    copies[1].wait()
    lax.fori_loop(0, count, note, 0)
    copies[2].wait()
    copies[3].wait()
    for at in range(ka):
        k2 = partner[target(me, at, ka)]
        block = valence[0, k2].astype(jnp.float32).reshape(val_rows, width)
        outs[at][:val_rows, :] = block.astype(jnp.bfloat16)
        to = lax.rem(half + min(at, 1), lax.axis_size("ba"))
        block = conduction[0, k2, :, pl.ds(to * share, share)].astype(jnp.float32)
        outs[at][val_rows : val_rows + cond_rows, :] = block.reshape(cond_rows, width).astype(jnp.bfloat16)
    cores = lax.axis_size("ba")
    for h in range(1, cores):
        part = lax.rem(half + cores - h, cores)
        block = conduction[0, partner[me], :, pl.ds(part * share, share)].astype(jnp.float32)
        rows = slice(val_rows + h * cond_rows, val_rows + (h + 1) * cond_rows)
        outs[0][rows, :] = block.reshape(cond_rows, width).astype(jnp.bfloat16)


def pack(ka, ba, qmap, owner, valence, conduction):
    cond_count = conduction.shape[3]
    val_rows, cond_rows = 2 * valence.shape[3] * valence.shape[4], 2 * cond_count // ba * cond_count
    own = in_vmem((val_rows + ba * cond_rows, valence.shape[5]), valence.dtype)
    shape = in_vmem((val_rows + cond_rows, valence.shape[5]), valence.dtype)
    operands = [placed(x, pltpu.HBM) for x in (qmap, owner, valence, conduction)]
    return pl.pallas_call(
        functools.partial(pack_kernel, ka),
        out_shape=[own] + [shape] * (ka - 1),
        in_specs=[anywhere] * 4,
        out_specs=[vmem] * ka,
        scratch_shapes=[
            pltpu.SMEM(qmap.shape, jnp.int32),
            pltpu.SMEM(owner.shape, jnp.int32),
            pltpu.SMEM(owner.shape, jnp.int32),
            pltpu.VMEM(valence.shape, valence.dtype),
            pltpu.VMEM(conduction.shape, conduction.dtype),
            pltpu.SemaphoreType.DMA((4,)),
        ],
        compiler_params=limits(valence, conduction),
        name="pack",
    )(*operands)


def prepare_kernel(ka, dims, *refs):
    vloc, val_count, cond_count, npol = dims
    ins, screening, (screen_out, near_table, far_table, extras), scratch = refs[:6], refs[6], refs[8:12], refs[12:]
    qmap, owner, band_pairs, val_energy, cond_energy, start, sems, screen_sems = scratch
    me = lax.axis_index("ka")
    half = lax.axis_index("ba")
    mine = lax.axis_index("ga")
    copies = [
        pltpu.make_async_copy(src, dst, sems.at[at])
        for at, (src, dst) in enumerate(
            zip(ins, (qmap, owner, band_pairs, val_energy, cond_energy, start))
        )
    ]
    height = screening.shape[2] // CHUNKS
    chunks = [
        pltpu.make_async_copy(
            screening.at[0, part, pl.ds(c * height, height)],
            screen_out.at[part, pl.ds(c * height, height)],
            screen_sems.at[part, c],
        )
        for part in range(2)
        for c in range(CHUNKS)
    ]
    for copy in copies + chunks:
        copy.start()
    pairs = vloc * val_count
    block = 2 * pairs
    rows = ka * block
    codes = val_count * cond_count
    mid = ka * codes
    lanes = 2 * mid
    row = iota((2 * rows, lanes), 0)
    col = iota((2 * rows, lanes), 1)
    j_of_row = row % rows // block
    cores = lax.axis_size("ba")
    for moves, table in enumerate((near_table, far_table)):
        share = lax.rem(half + 2 * cores - moves - jnp.where(j_of_row == 0, 0, 1), cores)
        want = (
            (row % block // pairs) * mid
            + origin(me, j_of_row, ka) * codes
            + (share * vloc + row % pairs // val_count) * cond_count
        )
        joined = (col - want >= 0) & (col - want < cond_count)
        for v2 in range(val_count):
            pick = jnp.where(joined & (row % val_count == v2), 1.0, 0.0)
            table[:, v2 * lanes : (v2 + 1) * lanes] = pick.astype(jnp.bfloat16)

    for copy in copies:
        copy.wait()
    first = jnp.where((mine == 0) & (half == 0), 1.0, 0.0)
    lane = iota((1, lanes), 1)
    lane_k = lane % mid // codes
    band_row = iota((codes, lanes), 0)
    band_lane = iota((codes, lanes), 1)
    code = jnp.zeros((codes, lanes), jnp.int32)
    bands = jnp.full((1, lanes), -1.0, jnp.float32)
    for b in range(codes):
        code = jnp.where(band_row == b, band_pairs[b], code)
        bands = jnp.where(lane % codes == band_pairs[b], float(b), bands)
    vectors = jnp.zeros((npol, lanes), jnp.float32)
    for part in range(2):
        spot = part * mid + me * codes
        pick = jnp.where(band_lane == spot + code, first, 0.0)
        vectors = vectors + jnp.dot(start[0, :, part, :], pick, precision=EXACT)
    energy = jnp.zeros((1, lanes), jnp.float32)
    for c in range(cond_count):
        energy = jnp.where(lane % cond_count == c, cond_energy[0, c], energy)
    for v in range(val_count):
        energy = energy - jnp.where(lane % codes // cond_count == v, val_energy[0, v], 0.0)
    energy = jnp.where(lane_k == me, energy * first, 0.0)
    kcount = qmap.shape[0]

    def find(k2, found):
        return jnp.where(owner[qmap[0, k2]] == me, k2, found)

    back = lax.fori_loop(0, kcount, find, 0)
    second = lane_k + back
    second = jnp.where(second >= kcount, second - kcount, second).astype(jnp.float32) * first
    rest = jnp.zeros((EXTRA_ROWS - 3 - npol, lanes), jnp.float32)
    extras[...] = jnp.concatenate([vectors, energy, bands * first, second, rest], 0)
    for copy in chunks:
        copy.wait()


def prepare(ka, dims, qmap, owner, band_pairs, val_energy, cond_energy, start, screening, after):
    vloc, val_count, cond_count, npol = dims
    rows = 4 * ka * vloc * val_count
    lanes = 2 * ka * val_count * cond_count
    operands = (qmap, owner, band_pairs, val_energy, cond_energy, start, screening)
    table = jax.ShapeDtypeStruct((rows, val_count * lanes), jnp.bfloat16)
    return pl.pallas_call(
        functools.partial(prepare_kernel, ka, dims),
        out_shape=[
            in_vmem(screening.shape[1:], screening.dtype),
            in_vmem(table.shape, table.dtype),
            in_vmem(table.shape, table.dtype),
            in_vmem((EXTRA_ROWS, lanes), jnp.float32),
        ],
        in_specs=[anywhere] * 8,
        out_specs=[vmem] * 4,
        scratch_shapes=[pltpu.SMEM(x.shape, x.dtype) for x in operands[:5]]
        + [
            pltpu.VMEM(start.shape, start.dtype),
            pltpu.SemaphoreType.DMA((6,)),
            pltpu.SemaphoreType.DMA((2, CHUNKS)),
        ],
        cost_estimate=pl.CostEstimate(
            flops=0, bytes_accessed=4 * screening.size, transcendentals=0
        ),
        compiler_params=limits(table),
        name="prepare",
    )(*[placed(x, pltpu.HBM) for x in operands], after)


def regroup_kernel(count, rows, columns, *refs):
    blocks, out = refs[:count], refs[-1]
    height = rows.stop - rows.start
    for at in range(count):
        out[at * height : (at + 1) * height, :] = blocks[at][rows, columns]


def regroup(blocks, rows, after=(), columns=None):
    columns = columns or slice(0, blocks[0].shape[1])
    shape = (len(blocks) * (rows.stop - rows.start), columns.stop - columns.start)
    return pl.pallas_call(
        functools.partial(regroup_kernel, len(blocks), rows, columns),
        out_shape=in_vmem(shape, blocks[0].dtype),
        in_specs=[vmem] * len(blocks) + [anywhere] * len(after),
        out_specs=vmem,
        compiler_params=limits(*blocks),
        name="regroup",
    )(*blocks, *after)


def assemble_kernel(rows, own, *refs):
    parts, out = refs[:PARTS], refs[-1]
    height = rows.stop - rows.start
    out[:height, :] = own[rows, :]
    width = parts[0].shape[1]
    for c, part in enumerate(parts):
        out[height:, c * width : (c + 1) * width] = part[...]


def assemble(rows, own, parts, after):
    height = rows.stop - rows.start + parts[0].shape[0]
    return pl.pallas_call(
        functools.partial(assemble_kernel, rows),
        out_shape=in_vmem((height, own.shape[1]), own.dtype),
        in_specs=[vmem] * (1 + len(parts)) + [anywhere] * len(after),
        out_specs=vmem,
        compiler_params=limits(own, *parts),
        name="assemble",
    )(own, *parts, *after)


def with_turned(halves, pairs):
    wide = jnp.concatenate([half[...].astype(jnp.float32) for half in halves], 0)
    parts = []
    for at in range(0, wide.shape[0], 2 * pairs):
        parts += [-wide[at + pairs : at + 2 * pairs], wide[at : at + pairs]]
    return wide, jnp.concatenate(parts, 0)


def columns_of(place, width):
    return pl.ds(pl.multiple_of(place * width, 128), width)


def placed_piece(kernel, table, dims, ba):
    vloc, val_count, cond_count, npol = dims
    half = lax.axis_index("ba")
    codes = val_count * cond_count
    lanes = table.shape[1] // val_count
    share = cond_count // ba
    cond_rows = cond_count * cond_count
    spread = jnp.dot(
        jnp.concatenate(split(kernel), 0), table[...], preferred_element_type=jnp.float32
    )
    spread = spread[:cond_rows] + spread[cond_rows:]
    crow = iota((cond_rows, lanes), 0)
    share_rows = share * cond_count
    c_of_row = origin(half, crow // share_rows, ba) * share + crow % share_rows // cond_count
    same_c = c_of_row == iota((cond_rows, lanes), 1) % cond_count
    rows = []
    for v2 in range(val_count):
        kept = jnp.where(same_c, spread[:, v2 * lanes : (v2 + 1) * lanes], 0.0)
        parts = [kept[c * cond_count : (c + 1) * cond_count] for c in range(cond_count)]
        while len(parts) > 1:
            parts = [x + y for x, y in zip(parts[::2], parts[1::2])] + parts[len(parts) // 2 * 2 :]
        rows.append(parts[0])
    return jnp.concatenate(rows, 0)


def diagonal(crossed, ka, ba, share_rows, sign):
    rows = crossed.shape[1] // 2
    lane = iota((share_rows, 2 * rows), 1)
    lane_j = lane % rows // (rows // ka)
    straight = lane < rows
    kernel = []
    for h in range(ba):
        total = jnp.zeros((share_rows, 2 * rows), jnp.float32)
        for j in range(ka):
            at = (h * ka + j) * 2 * share_rows
            real = crossed[at : at + share_rows]
            imag = crossed[at + share_rows : at + 2 * share_rows]
            total = jnp.where(lane_j == j, jnp.where(straight, real, sign * imag), total)
        kernel.append(total)
    return jnp.concatenate(kernel, 0)


def field_kernel(pairs, screening, *refs):
    halves, out = refs[:-1], refs[-1]
    columns = columns_of(lax.axis_index("ga"), halves[0].shape[1])
    wide, turned = with_turned(halves, pairs)
    real = jnp.concatenate([wide, turned], 0).astype(jnp.bfloat16)
    imag = jnp.concatenate([turned, -wide], 0).astype(jnp.bfloat16)
    form = (((1,), (1,)), ((), ()))
    fields = lax.dot_general(
        screening[0, :, columns], real, form, preferred_element_type=jnp.float32
    ) + lax.dot_general(screening[1, :, columns], imag, form, preferred_element_type=jnp.float32)
    lanes = fields.shape[1]
    high, low = split(fields)
    out[:, :lanes] = high
    out[:, lanes:] = low


def field(pairs, screening, halves):
    operands = [screening, *halves]
    rows = sum(half.shape[0] for half in halves)
    return pl.pallas_call(
        functools.partial(field_kernel, pairs),
        out_shape=in_vmem((screening.shape[1], 4 * rows), jnp.bfloat16),
        in_specs=[vmem] * len(operands),
        out_specs=vmem,
        cost_estimate=LIGHT,
        compiler_params=limits(*operands),
        name="field",
    )(*operands)


def near_kernel(ka, ba, dims, *refs):
    vloc, val_count, cond_count, npol = dims
    fields, table, extras = refs[:3]
    cond_in, out = refs[3 : 3 + ba], refs[-1]
    codes = val_count * cond_count
    cond = jnp.concatenate([ref[...] for ref in cond_in], 0)
    crossed = jnp.dot(cond, fields[...], preferred_element_type=jnp.float32)
    half = crossed.shape[1] // 2
    crossed = crossed[:, :half] + crossed[:, half:]
    kernel = diagonal(crossed, ka, ba, cond_count // ba * cond_count, -1.0)
    out[:codes, :] = placed_piece(kernel, table, dims, ba)
    out[codes:, :] = extras[...]


def near(ka, ba, dims, fields, table, extras, cond_all, after):
    vloc, val_count, cond_count, npol = dims
    operands = [fields, table, extras, *cond_all]
    shape = (val_count * cond_count + EXTRA_ROWS, extras.shape[1])
    return pl.pallas_call(
        functools.partial(near_kernel, ka, ba, dims),
        out_shape=in_vmem(shape, jnp.float32),
        in_specs=[vmem] * len(operands) + [anywhere] * len(after),
        out_specs=vmem,
        cost_estimate=LIGHT,
        compiler_params=limits(*operands),
        name="near",
    )(*operands, *after)


def couple_kernel(ka, ga, ba, share_rows, screening, *refs):
    cond_in, outs = refs[:ba], refs[ba:]
    mine = lax.axis_index("ga")
    wide = jnp.concatenate([ref[...].astype(jnp.float32) for ref in cond_in], 0)
    straight, turned = [], []
    for at in range(0, wide.shape[0], 2 * share_rows):
        real, imag = wide[at : at + share_rows], wide[at + share_rows : at + 2 * share_rows]
        straight += [real, -imag]
        turned += [imag, real]
    straight = jnp.concatenate(straight, 0).astype(jnp.bfloat16)
    turned = jnp.concatenate(turned, 0).astype(jnp.bfloat16)
    width = screening.shape[2] // ga
    columns = [columns_of(origin(mine, r, ga), width) for r in range(1, ga)]
    coupled = [
        jnp.dot(straight, screening[0, :, block], preferred_element_type=jnp.float32)
        + jnp.dot(turned, screening[1, :, block], preferred_element_type=jnp.float32)
        for block in columns
    ]
    for out, value in zip(outs, coupled):
        high, low = split(value)
        out[: value.shape[0], :] = high
        out[value.shape[0] :, :] = low


def couple(ka, ga, ba, dims, screening, cond_all):
    share_rows = dims[2] // ba * dims[2]
    rows = 2 * sum(x.shape[0] for x in cond_all)
    width = screening.shape[2] // ga
    operands = [screening, *cond_all]
    return pl.pallas_call(
        functools.partial(couple_kernel, ka, ga, ba, share_rows),
        out_shape=[in_vmem((rows, width), jnp.bfloat16)] * (ga - 1),
        in_specs=[vmem] * len(operands),
        out_specs=[vmem] * (ga - 1),
        cost_estimate=LIGHT,
        compiler_params=limits(*operands),
        name="couple",
    )(*operands)


def contract_kernel(ka, ba, count, dims, *refs):
    vloc, val_count, cond_count, npol = dims
    table, held, out = refs[0], refs[1], refs[-1]
    each = (len(refs) - 3 - count) // count
    codes = val_count * cond_count
    crossed = None
    for r in range(count):
        coupled = refs[2 + r]
        halves = refs[2 + count + r * each : 2 + count + (r + 1) * each]
        rows = jnp.concatenate(with_turned(halves, vloc * val_count), 0).astype(jnp.bfloat16)
        term = lax.dot_general(
            coupled[...], rows, (((1,), (1,)), ((), ())), preferred_element_type=jnp.float32
        )
        crossed = term if crossed is None else crossed + term
    half = crossed.shape[0] // 2
    crossed = crossed[:half] + crossed[half:]
    kernel = diagonal(crossed, ka, ba, cond_count // ba * cond_count, 1.0)
    piece = placed_piece(kernel, table, dims, ba)
    before = held.shape[0] - EXTRA_ROWS
    out[:codes, :] = piece + held[:codes, :] if before else piece
    out[codes:, :] = held[before:, :]


def contract(ka, ba, dims, table, held, coupled, valence, name):
    val_count, cond_count = dims[1:3]
    operands = [table, held, *coupled, *valence]
    shape = (val_count * cond_count + EXTRA_ROWS, held.shape[1])
    return pl.pallas_call(
        functools.partial(contract_kernel, ka, ba, len(coupled), dims),
        out_shape=in_vmem(shape, jnp.float32),
        in_specs=[vmem] * len(operands),
        out_specs=vmem,
        cost_estimate=LIGHT,
        compiler_params=limits(*operands),
        name=name,
    )(*operands)


def haydock_kernel(ka, codes, scale_count, npol, *refs):
    pieces = refs[:-2]
    next_out, coef_out = refs[-2:]
    lanes = pieces[0].shape[1]
    mid = lanes // 2
    height = codes + EXTRA_ROWS
    found = [(ref, at) for ref in pieces for at in range(0, ref.shape[0], height)]
    extras = None
    slots = []
    for ref, at in found:
        rows = ref[at + codes : at + height, :]
        extras = rows if extras is None else extras + rows
        slots.append((ref[at : at + codes, :], rows[npol + 2 : npol + 3]))
    own = pieces[0][codes:height, :]
    sign = jnp.where(iota((1, lanes), 1) < mid, -1.0, 1.0)
    top = []
    for k2 in range(ka):
        block = jnp.zeros((codes, lanes), jnp.float32)
        for piece, second in slots:
            block = jnp.where(second == float(k2), piece, block)
        top.append(block)
    top = jnp.concatenate(top, 0)
    matrix = jnp.concatenate([top, sign * pltpu.roll(top, mid, 1)], 0)
    full = jnp.concatenate(split(matrix), 1)
    start = extras[:npol]
    energy = extras[npol : npol + 1]

    def halves(vector):
        top = vector.astype(jnp.bfloat16).astype(jnp.float32)
        return jnp.concatenate([top, vector - top], 0).astype(jnp.bfloat16)

    def mean(values):
        return jnp.sum(values, axis=1, keepdims=True) / scale_count

    def norm(vector):
        return jnp.sqrt(mean(vector * vector) + EPSILON)

    def swap(vector):
        return pltpu.roll(vector, mid, 1)

    def hamiltonian(vector):
        product = jnp.dot(halves(vector), full, preferred_element_type=jnp.float32)
        main = product[:npol, :lanes] + product[npol:, :lanes]
        return energy * vector - (main + product[:npol, lanes:])

    def inner(left, right):
        return mean(left * right), mean(-sign * left * swap(right))

    def times(real, imag, vector):
        return real * vector + imag * (sign * swap(vector))

    start_image = hamiltonian(start)
    scale = 1.0 / norm(start)
    first = start * scale
    first_image = start_image * scale
    alpha_real, alpha_imag = inner(first, first_image)
    first_resid = first_image - times(alpha_real, alpha_imag, first)
    resid_image = hamiltonian(first_resid)
    beta_one = norm(first_resid)
    scale = 1.0 / beta_one
    second = first_resid * scale
    second_image = resid_image * scale
    gamma_real, gamma_imag = inner(second, second_image)
    second_resid = second_image - times(gamma_real, gamma_imag, second) - beta_one * first
    beta_two = norm(second_resid)

    coef_lane = iota(coef_out.shape, 1)
    coefs = jnp.zeros(coef_out.shape, jnp.float32)
    for at, value in enumerate((alpha_real, alpha_imag, gamma_real, gamma_imag, beta_one, beta_two)):
        coefs = jnp.where(coef_lane == at, value, coefs)
    coef_out[...] = coefs
    row = iota((2 * codes, lanes), 0)
    lane = iota((2 * codes, lanes), 1)
    here = (lane % mid // codes == lax.axis_index("ka")) & (lane // mid == row // codes)
    band = (row % codes).astype(jnp.float32)
    pick = jnp.where(here & (own[npol + 1 : npol + 2] == band), 1.0, 0.0).astype(jnp.bfloat16)
    picked = lax.dot_general(
        halves(second_resid), pick, (((1,), (1,)), ((), ())), preferred_element_type=jnp.float32
    )
    picked = (picked[:npol] + picked[npol:]) / beta_two
    next_out[0, :, 0, :] = picked[:, :codes]
    next_out[0, :, 1, :] = picked[:, codes:]


def haydock(ka, codes, scale_count, npol, pieces):
    lanes = pieces[0].shape[1]
    square = jax.ShapeDtypeStruct((lanes, lanes), jnp.float32)
    return pl.pallas_call(
        functools.partial(haydock_kernel, ka, codes, scale_count, npol),
        out_shape=[
            jax.ShapeDtypeStruct((1, npol, 2, codes), jnp.float32),
            jax.ShapeDtypeStruct((npol, 6), jnp.float32),
        ],
        in_specs=[vmem] * len(pieces),
        out_specs=[vmem, vmem],
        compiler_params=limits(*pieces, square),
        name="haydock",
    )(*pieces)


def summed(value, axis):
    size = lax.axis_size(axis)
    if size & (size - 1):
        return value + sum(shifted(value, axis, step) for step in range(1, size))
    step = 1
    while step < size:
        value = value + exchanged(value, axis, lambda i, size: i ^ step)
        step *= 2
    return value


def local(
    ka,
    ga,
    ba,
    start_vector,
    valence_density,
    conduction_density,
    screening,
    qpoint_map,
    slot_owner,
    band_pairs,
    valence_energy,
    conduction_energy,
):
    npol = start_vector.shape[1]
    pair_count = start_vector.shape[3]
    kcount, vloc, val_count = qpoint_map.shape[0], valence_density.shape[3], valence_density.shape[4]
    cond_count = conduction_density.shape[3]
    pairs = vloc * val_count
    dims = (vloc, val_count, cond_count, npol)
    packed = pack(ka, ba, qpoint_map, slot_owner, valence_density, conduction_density)
    blocks = [packed[0]] + [shifted(packed[j], "ka", j) for j in range(1, ka)]
    whole, near_table, far_table, extras = prepare(
        ka,
        dims,
        qpoint_map,
        slot_owner,
        band_pairs,
        valence_energy,
        conduction_energy,
        start_vector,
        screening,
        packed[0],
    )
    early = ka // 2
    val_rows = slice(0, 2 * pairs)
    val_early = regroup(blocks[:early], val_rows, (extras,))
    far_early = [shifted(val_early, "ga", r) for r in range(1, ga)]
    val_late = regroup(blocks[early:], val_rows)
    far_late = [shifted(val_late, "ga", r) for r in range(1, ga)]
    height = 2 * cond_count // ba * cond_count
    width = blocks[0].shape[1] // PARTS
    cond_rows = slice(2 * pairs, 2 * pairs + height)
    cond_parts = [
        regroup(blocks[1:], cond_rows, (val_late,), slice(c * width, (c + 1) * width))
        for c in range(PARTS)
    ]
    fields = field(pairs, whole, [val_early, val_late])
    cond_all = [regroup(blocks, cond_rows)]
    for r in range(1, ba):
        own_rows = slice(2 * pairs + r * height, 2 * pairs + (r + 1) * height)
        came = [handed(part, r) for part in cond_parts]
        cond_all.append(assemble(own_rows, blocks[0], came, (fields,)))
    piece = near(ka, ba, dims, fields, near_table, extras, cond_all, far_early)
    if ga > 1:
        coupled = couple(ka, ga, ba, dims, whole, cond_all)
        far = [half for both in zip(far_early, far_late) for half in both]
        piece = contract(ka, ba, dims, far_table, piece, coupled, far, "far")
    piece = piece + sum(handed(piece, r) for r in range(1, ba))
    piece = summed(piece, "ga")
    pieces = [piece] + [shifted(piece, "ka", j) for j in range(1, ka)]
    scale_count = float(kcount * pair_count)
    return tuple(haydock(ka, pair_count, scale_count, npol, pieces))


def solution(mesh):
    in_specs = (
        P(("grp", "ka"), None, None, None),
        P(("grp", "ka"), None, None, "ba", None, "ga"),
        P(("grp", "ka"), None, None, None, None, "ga"),
        P(("grp", "ka"), None, "ga", None),
        P(),
        P(),
        P(),
        P(("grp", "ka"), None),
        P(("grp", "ka"), None),
    )
    out_specs = (P(("grp", "ka"), None, None, None), P("grp", None))
    body = functools.partial(local, mesh.shape["ka"], mesh.shape["ga"], mesh.shape["ba"])
    return jax.shard_map(body, mesh=mesh, in_specs=in_specs, out_specs=out_specs, check_vma=False)
```

```python
import functools
import math

import jax
import jax.numpy as jnp
from jax import lax
from jax.experimental import pallas as pl
from jax.experimental.pallas import tpu as pltpu
from jax.sharding import PartitionSpec as P

EPSILON = 1e-06
EXACT = lax.Precision.HIGHEST
VMEM_LEAST = 8 * 1024 * 1024
VMEM_MOST = 56 * 1024 * 1024

vmem = pl.BlockSpec(memory_space=pltpu.VMEM)
anywhere = pl.BlockSpec(memory_space=pl.ANY)
EXTRA_ROWS = 8
LIGHT = pl.CostEstimate(flops=1, bytes_accessed=1, transcendentals=0)
CHUNKS = 4
PARTS = 2


def in_vmem(shape, dtype):
    return pltpu.VMEM(shape, dtype)


def placed(value, space):
    return pltpu.with_memory_space_constraint(value, space)


def iota(shape, axis):
    return lax.broadcasted_iota(jnp.int32, shape, axis)


def split(values):
    high = values.astype(jnp.bfloat16)
    low = (values - high.astype(jnp.float32)).astype(jnp.bfloat16)
    return high, low


def limits(*arrays):
    held = sum(math.prod(a.shape) * a.dtype.itemsize for a in arrays)
    return pltpu.CompilerParams(vmem_limit_bytes=min(VMEM_MOST, VMEM_LEAST + 4 * held))


def target(me, step, size):
    return lax.rem(me + step, size)


def origin(me, step, size):
    return lax.rem(me + size - step, size)


def exchanged(value, axis, move):
    size, cores = lax.axis_size(axis), lax.axis_size("ba")
    pairs = [
        (i * cores + h, move(i, size) * cores + (h + 1) % cores)
        for i in range(size)
        for h in range(cores)
    ]
    return lax.ppermute(value, (axis, "ba"), pairs)


def shifted(value, axis, step):
    return exchanged(value, axis, lambda i, size: (i + step) % size)


def handed(value, step):
    size = lax.axis_size("ba")
    return lax.ppermute(value, "ba", [(h, (h + step) % size) for h in range(size)])


def pack_kernel(ka, qmap_in, owner_in, valence_in, conduction_in, *rest):
    outs = rest[:ka]
    qmap, owner, partner, valence, conduction, sems = rest[ka:]
    copies = [
        pltpu.make_async_copy(src, dst, sems.at[at])
        for at, (src, dst) in enumerate(
            ((qmap_in, qmap), (owner_in, owner), (valence_in, valence), (conduction_in, conduction))
        )
    ]
    for copy in copies:
        copy.start()
    me = lax.axis_index("ka")
    half = lax.axis_index("ba")
    count, width = valence.shape[1], valence.shape[5]
    cond_count = conduction.shape[3]
    share = cond_count // lax.axis_size("ba")
    val_rows = 2 * valence.shape[3] * valence.shape[4]
    cond_rows = 2 * share * cond_count

    def note(k2, carry):
        partner[owner[qmap[me, k2]]] = k2
        return carry

    copies[0].wait()
    copies[1].wait()
    lax.fori_loop(0, count, note, 0)
    copies[2].wait()
    copies[3].wait()
    for at in range(ka):
        k2 = partner[target(me, at, ka)]
        block = valence[0, k2].astype(jnp.float32).reshape(val_rows, width)
        outs[at][:val_rows, :] = block.astype(jnp.bfloat16)
        to = lax.rem(half + min(at, 1), lax.axis_size("ba"))
        block = conduction[0, k2, :, pl.ds(to * share, share)].astype(jnp.float32)
        outs[at][val_rows : val_rows + cond_rows, :] = block.reshape(cond_rows, width).astype(jnp.bfloat16)
    cores = lax.axis_size("ba")
    for h in range(1, cores):
        part = lax.rem(half + cores - h, cores)
        block = conduction[0, partner[me], :, pl.ds(part * share, share)].astype(jnp.float32)
        rows = slice(val_rows + h * cond_rows, val_rows + (h + 1) * cond_rows)
        outs[0][rows, :] = block.reshape(cond_rows, width).astype(jnp.bfloat16)


def pack(ka, ba, qmap, owner, valence, conduction):
    cond_count = conduction.shape[3]
    val_rows, cond_rows = 2 * valence.shape[3] * valence.shape[4], 2 * cond_count // ba * cond_count
    own = in_vmem((val_rows + ba * cond_rows, valence.shape[5]), valence.dtype)
    shape = in_vmem((val_rows + cond_rows, valence.shape[5]), valence.dtype)
    operands = [placed(x, pltpu.HBM) for x in (qmap, owner, valence, conduction)]
    return pl.pallas_call(
        functools.partial(pack_kernel, ka),
        out_shape=[own] + [shape] * (ka - 1),
        in_specs=[anywhere] * 4,
        out_specs=[vmem] * ka,
        scratch_shapes=[
            pltpu.SMEM(qmap.shape, jnp.int32),
            pltpu.SMEM(owner.shape, jnp.int32),
            pltpu.SMEM(owner.shape, jnp.int32),
            pltpu.VMEM(valence.shape, valence.dtype),
            pltpu.VMEM(conduction.shape, conduction.dtype),
            pltpu.SemaphoreType.DMA((4,)),
        ],
        compiler_params=limits(valence, conduction),
        name="pack",
    )(*operands)


def prepare_kernel(ka, dims, *refs):
    vloc, val_count, cond_count, npol = dims
    ins, screening, (screen_out, near_table, far_table, extras), scratch = refs[:6], refs[6], refs[8:12], refs[12:]
    qmap, owner, band_pairs, val_energy, cond_energy, start, sems, screen_sems = scratch
    me = lax.axis_index("ka")
    half = lax.axis_index("ba")
    mine = lax.axis_index("ga")
    copies = [
        pltpu.make_async_copy(src, dst, sems.at[at])
        for at, (src, dst) in enumerate(
            zip(ins, (qmap, owner, band_pairs, val_energy, cond_energy, start))
        )
    ]
    height = screening.shape[2] // CHUNKS
    chunks = [
        pltpu.make_async_copy(
            screening.at[0, part, pl.ds(c * height, height)],
            screen_out.at[part, pl.ds(c * height, height)],
            screen_sems.at[part, c],
        )
        for part in range(2)
        for c in range(CHUNKS)
    ]
    for copy in copies + chunks:
        copy.start()
    pairs = vloc * val_count
    block = 2 * pairs
    rows = ka * block
    codes = val_count * cond_count
    mid = ka * codes
    lanes = 2 * mid
    row = iota((2 * rows, lanes), 0)
    col = iota((2 * rows, lanes), 1)
    j_of_row = row % rows // block
    cores = lax.axis_size("ba")
    for moves, table in enumerate((near_table, far_table)):
        share = lax.rem(half + 2 * cores - moves - jnp.where(j_of_row == 0, 0, 1), cores)
        want = (
            (row % block // pairs) * mid
            + origin(me, j_of_row, ka) * codes
            + (share * vloc + row % pairs // val_count) * cond_count
        )
        joined = (col - want >= 0) & (col - want < cond_count)
        for v2 in range(val_count):
            pick = jnp.where(joined & (row % val_count == v2), 1.0, 0.0)
            table[:, v2 * lanes : (v2 + 1) * lanes] = pick.astype(jnp.bfloat16)

    for copy in copies:
        copy.wait()
    first = jnp.where((mine == 0) & (half == 0), 1.0, 0.0)
    lane = iota((1, lanes), 1)
    lane_k = lane % mid // codes
    band_row = iota((codes, lanes), 0)
    band_lane = iota((codes, lanes), 1)
    code = jnp.zeros((codes, lanes), jnp.int32)
    bands = jnp.full((1, lanes), -1.0, jnp.float32)
    for b in range(codes):
        code = jnp.where(band_row == b, band_pairs[b], code)
        bands = jnp.where(lane % codes == band_pairs[b], float(b), bands)
    vectors = jnp.zeros((npol, lanes), jnp.float32)
    for part in range(2):
        spot = part * mid + me * codes
        pick = jnp.where(band_lane == spot + code, first, 0.0)
        vectors = vectors + jnp.dot(start[0, :, part, :], pick, precision=EXACT)
    energy = jnp.zeros((1, lanes), jnp.float32)
    for c in range(cond_count):
        energy = jnp.where(lane % cond_count == c, cond_energy[0, c], energy)
    for v in range(val_count):
        energy = energy - jnp.where(lane % codes // cond_count == v, val_energy[0, v], 0.0)
    energy = jnp.where(lane_k == me, energy * first, 0.0)
    kcount = qmap.shape[0]

    def find(k2, found):
        return jnp.where(owner[qmap[0, k2]] == me, k2, found)

    back = lax.fori_loop(0, kcount, find, 0)
    second = lane_k + back
    second = jnp.where(second >= kcount, second - kcount, second).astype(jnp.float32) * first
    rest = jnp.zeros((EXTRA_ROWS - 3 - npol, lanes), jnp.float32)
    extras[...] = jnp.concatenate([vectors, energy, bands * first, second, rest], 0)
    for copy in chunks:
        copy.wait()


def prepare(ka, dims, qmap, owner, band_pairs, val_energy, cond_energy, start, screening, after):
    vloc, val_count, cond_count, npol = dims
    rows = 4 * ka * vloc * val_count
    lanes = 2 * ka * val_count * cond_count
    operands = (qmap, owner, band_pairs, val_energy, cond_energy, start, screening)
    table = jax.ShapeDtypeStruct((rows, val_count * lanes), jnp.bfloat16)
    return pl.pallas_call(
        functools.partial(prepare_kernel, ka, dims),
        out_shape=[
            in_vmem(screening.shape[1:], screening.dtype),
            in_vmem(table.shape, table.dtype),
            in_vmem(table.shape, table.dtype),
            in_vmem((EXTRA_ROWS, lanes), jnp.float32),
        ],
        in_specs=[anywhere] * 8,
        out_specs=[vmem] * 4,
        scratch_shapes=[pltpu.SMEM(x.shape, x.dtype) for x in operands[:5]]
        + [
            pltpu.VMEM(start.shape, start.dtype),
            pltpu.SemaphoreType.DMA((6,)),
            pltpu.SemaphoreType.DMA((2, CHUNKS)),
        ],
        cost_estimate=pl.CostEstimate(
            flops=0, bytes_accessed=4 * screening.size, transcendentals=0
        ),
        compiler_params=limits(table),
        name="prepare",
    )(*[placed(x, pltpu.HBM) for x in operands], after)


def regroup_kernel(count, rows, columns, *refs):
    blocks, out = refs[:count], refs[-1]
    height = rows.stop - rows.start
    for at in range(count):
        out[at * height : (at + 1) * height, :] = blocks[at][rows, columns]


def regroup(blocks, rows, after=(), columns=None):
    columns = columns or slice(0, blocks[0].shape[1])
    shape = (len(blocks) * (rows.stop - rows.start), columns.stop - columns.start)
    return pl.pallas_call(
        functools.partial(regroup_kernel, len(blocks), rows, columns),
        out_shape=in_vmem(shape, blocks[0].dtype),
        in_specs=[vmem] * len(blocks) + [anywhere] * len(after),
        out_specs=vmem,
        compiler_params=limits(*blocks),
        name="regroup",
    )(*blocks, *after)


def assemble_kernel(rows, own, *refs):
    parts, out = refs[:PARTS], refs[-1]
    height = rows.stop - rows.start
    out[:height, :] = own[rows, :]
    width = parts[0].shape[1]
    for c, part in enumerate(parts):
        out[height:, c * width : (c + 1) * width] = part[...]


def assemble(rows, own, parts, after):
    height = rows.stop - rows.start + parts[0].shape[0]
    return pl.pallas_call(
        functools.partial(assemble_kernel, rows),
        out_shape=in_vmem((height, own.shape[1]), own.dtype),
        in_specs=[vmem] * (1 + len(parts)) + [anywhere],
        out_specs=vmem,
        compiler_params=limits(own, *parts),
        name="assemble",
    )(own, *parts, after)


def with_turned(halves, pairs):
    wide = jnp.concatenate([half[...].astype(jnp.float32) for half in halves], 0)
    parts = []
    for at in range(0, wide.shape[0], 2 * pairs):
        parts += [-wide[at + pairs : at + 2 * pairs], wide[at : at + pairs]]
    return wide, jnp.concatenate(parts, 0)


def columns_of(place, width):
    return pl.ds(pl.multiple_of(place * width, 128), width)


def placed_piece(kernel, table, dims, ba):
    vloc, val_count, cond_count, npol = dims
    half = lax.axis_index("ba")
    codes = val_count * cond_count
    lanes = table.shape[1] // val_count
    share = cond_count // ba
    cond_rows = cond_count * cond_count
    spread = jnp.dot(
        jnp.concatenate(split(kernel), 0), table[...], preferred_element_type=jnp.float32
    )
    spread = spread[:cond_rows] + spread[cond_rows:]
    crow = iota((cond_rows, lanes), 0)
    share_rows = share * cond_count
    c_of_row = origin(half, crow // share_rows, ba) * share + crow % share_rows // cond_count
    same_c = c_of_row == iota((cond_rows, lanes), 1) % cond_count
    rows = []
    for v2 in range(val_count):
        kept = jnp.where(same_c, spread[:, v2 * lanes : (v2 + 1) * lanes], 0.0)
        parts = [kept[c * cond_count : (c + 1) * cond_count] for c in range(cond_count)]
        while len(parts) > 1:
            parts = [x + y for x, y in zip(parts[::2], parts[1::2])] + parts[len(parts) // 2 * 2 :]
        rows.append(parts[0])
    return jnp.concatenate(rows, 0)


def diagonal(crossed, ka, ba, share_rows, sign):
    rows = crossed.shape[1] // 2
    lane = iota((share_rows, 2 * rows), 1)
    lane_j = lane % rows // (rows // ka)
    straight = lane < rows
    kernel = []
    for h in range(ba):
        total = jnp.zeros((share_rows, 2 * rows), jnp.float32)
        for j in range(ka):
            at = (h * ka + j) * 2 * share_rows
            real = crossed[at : at + share_rows]
            imag = crossed[at + share_rows : at + 2 * share_rows]
            total = jnp.where(lane_j == j, jnp.where(straight, real, sign * imag), total)
        kernel.append(total)
    return jnp.concatenate(kernel, 0)


def field_kernel(pairs, screening, *refs):
    halves, out = refs[:-1], refs[-1]
    columns = columns_of(lax.axis_index("ga"), halves[0].shape[1])
    wide, turned = with_turned(halves, pairs)
    real = jnp.concatenate([wide, turned], 0).astype(jnp.bfloat16)
    imag = jnp.concatenate([turned, -wide], 0).astype(jnp.bfloat16)
    form = (((1,), (1,)), ((), ()))
    fields = lax.dot_general(
        screening[0, :, columns], real, form, preferred_element_type=jnp.float32
    ) + lax.dot_general(screening[1, :, columns], imag, form, preferred_element_type=jnp.float32)
    lanes = fields.shape[1]
    high, low = split(fields)
    out[:, :lanes] = high
    out[:, lanes:] = low


def field(pairs, screening, halves):
    operands = [screening, *halves]
    rows = sum(half.shape[0] for half in halves)
    return pl.pallas_call(
        functools.partial(field_kernel, pairs),
        out_shape=in_vmem((screening.shape[1], 4 * rows), jnp.bfloat16),
        in_specs=[vmem] * len(operands),
        out_specs=vmem,
        cost_estimate=LIGHT,
        compiler_params=limits(*operands),
        name="field",
    )(*operands)


def near_kernel(ka, ba, dims, *refs):
    vloc, val_count, cond_count, npol = dims
    fields, table, extras = refs[:3]
    cond_in, out = refs[3:-1], refs[-1]
    codes = val_count * cond_count
    cond = jnp.concatenate([ref[...] for ref in cond_in], 0)
    crossed = jnp.dot(cond, fields[...], preferred_element_type=jnp.float32)
    half = crossed.shape[1] // 2
    crossed = crossed[:, :half] + crossed[:, half:]
    kernel = diagonal(crossed, ka, ba, cond_count // ba * cond_count, -1.0)
    out[:codes, :] = placed_piece(kernel, table, dims, ba)
    out[codes:, :] = extras[...]


def near(ka, ba, dims, fields, table, extras, cond_all):
    vloc, val_count, cond_count, npol = dims
    operands = [fields, table, extras, *cond_all]
    shape = (val_count * cond_count + EXTRA_ROWS, extras.shape[1])
    return pl.pallas_call(
        functools.partial(near_kernel, ka, ba, dims),
        out_shape=in_vmem(shape, jnp.float32),
        in_specs=[vmem] * len(operands),
        out_specs=vmem,
        cost_estimate=LIGHT,
        compiler_params=limits(*operands),
        name="near",
    )(*operands)


def couple_kernel(ka, ga, ba, share_rows, screening, *refs):
    cond_in, outs = refs[:ba], refs[ba:]
    mine = lax.axis_index("ga")
    wide = jnp.concatenate([ref[...].astype(jnp.float32) for ref in cond_in], 0)
    straight, turned = [], []
    for at in range(0, wide.shape[0], 2 * share_rows):
        real, imag = wide[at : at + share_rows], wide[at + share_rows : at + 2 * share_rows]
        straight += [real, -imag]
        turned += [imag, real]
    straight = jnp.concatenate(straight, 0).astype(jnp.bfloat16)
    turned = jnp.concatenate(turned, 0).astype(jnp.bfloat16)
    width = screening.shape[2] // ga
    columns = [columns_of(origin(mine, r, ga), width) for r in range(1, ga)]
    coupled = [
        jnp.dot(straight, screening[0, :, block], preferred_element_type=jnp.float32)
        + jnp.dot(turned, screening[1, :, block], preferred_element_type=jnp.float32)
        for block in columns
    ]
    for out, value in zip(outs, coupled):
        high, low = split(value)
        out[: value.shape[0], :] = high
        out[value.shape[0] :, :] = low


def couple(ka, ga, ba, dims, screening, cond_all):
    share_rows = dims[2] // ba * dims[2]
    rows = 2 * sum(x.shape[0] for x in cond_all)
    width = screening.shape[2] // ga
    operands = [screening, *cond_all]
    return pl.pallas_call(
        functools.partial(couple_kernel, ka, ga, ba, share_rows),
        out_shape=[in_vmem((rows, width), jnp.bfloat16)] * (ga - 1),
        in_specs=[vmem] * len(operands),
        out_specs=[vmem] * (ga - 1),
        cost_estimate=LIGHT,
        compiler_params=limits(*operands),
        name="couple",
    )(*operands)


def contract_kernel(ka, ba, count, dims, *refs):
    vloc, val_count, cond_count, npol = dims
    table, held, out = refs[0], refs[1], refs[-1]
    each = (len(refs) - 3 - count) // count
    codes = val_count * cond_count
    crossed = None
    for r in range(count):
        coupled = refs[2 + r]
        halves = refs[2 + count + r * each : 2 + count + (r + 1) * each]
        rows = jnp.concatenate(with_turned(halves, vloc * val_count), 0).astype(jnp.bfloat16)
        term = lax.dot_general(
            coupled[...], rows, (((1,), (1,)), ((), ())), preferred_element_type=jnp.float32
        )
        crossed = term if crossed is None else crossed + term
    half = crossed.shape[0] // 2
    crossed = crossed[:half] + crossed[half:]
    kernel = diagonal(crossed, ka, ba, cond_count // ba * cond_count, 1.0)
    piece = placed_piece(kernel, table, dims, ba)
    before = held.shape[0] - EXTRA_ROWS
    out[:codes, :] = piece + held[:codes, :] if before else piece
    out[codes:, :] = held[before:, :]


def contract(ka, ba, dims, table, held, coupled, valence, name):
    val_count, cond_count = dims[1:3]
    operands = [table, held, *coupled, *valence]
    shape = (val_count * cond_count + EXTRA_ROWS, held.shape[1])
    return pl.pallas_call(
        functools.partial(contract_kernel, ka, ba, len(coupled), dims),
        out_shape=in_vmem(shape, jnp.float32),
        in_specs=[vmem] * len(operands),
        out_specs=vmem,
        cost_estimate=LIGHT,
        compiler_params=limits(*operands),
        name=name,
    )(*operands)


def haydock_kernel(ka, codes, scale_count, npol, *refs):
    pieces = refs[:-2]
    next_out, coef_out = refs[-2:]
    lanes = pieces[0].shape[1]
    mid = lanes // 2
    height = codes + EXTRA_ROWS
    found = [(ref, at) for ref in pieces for at in range(0, ref.shape[0], height)]
    extras = None
    slots = []
    for ref, at in found:
        rows = ref[at + codes : at + height, :]
        extras = rows if extras is None else extras + rows
        slots.append((ref[at : at + codes, :], rows[npol + 2 : npol + 3]))
    own = pieces[0][codes:height, :]
    sign = jnp.where(iota((1, lanes), 1) < mid, -1.0, 1.0)
    top = []
    for k2 in range(ka):
        block = jnp.zeros((codes, lanes), jnp.float32)
        for piece, second in slots:
            block = jnp.where(second == float(k2), piece, block)
        top.append(block)
    top = jnp.concatenate(top, 0)
    matrix = jnp.concatenate([top, sign * pltpu.roll(top, mid, 1)], 0)
    full = jnp.concatenate(split(matrix), 1)
    start = extras[:npol]
    energy = extras[npol : npol + 1]

    def halves(vector):
        top = vector.astype(jnp.bfloat16).astype(jnp.float32)
        return jnp.concatenate([top, vector - top], 0).astype(jnp.bfloat16)

    def mean(values):
        return jnp.sum(values, axis=1, keepdims=True) * (1.0 / scale_count)

    def square_norm(vector):
        return mean(vector * vector) + EPSILON

    def swap(vector):
        return pltpu.roll(vector, mid, 1)

    def hamiltonian(vector):
        product = jnp.dot(halves(vector), full, preferred_element_type=jnp.float32)
        main = product[:npol, :lanes] + product[npol:, :lanes]
        return energy * vector - (main + product[:npol, lanes:])

    def inner(left, right):
        return mean(left * right), mean(-sign * left * swap(right))

    def times(real, imag, vector):
        return real * vector + imag * (sign * swap(vector))

    start_image = hamiltonian(start)
    scale = lax.rsqrt(square_norm(start))
    first = start * scale
    alpha_real, alpha_imag = (value * (scale * scale) for value in inner(start, start_image))
    first_resid = start_image * scale - times(alpha_real, alpha_imag, first)
    resid_image = hamiltonian(first_resid)
    square_one = square_norm(first_resid)
    scale, beta_one = lax.rsqrt(square_one), jnp.sqrt(square_one)
    second = first_resid * scale
    gamma_real, gamma_imag = (value * (scale * scale) for value in inner(first_resid, resid_image))
    second_resid = resid_image * scale - beta_one * first - times(gamma_real, gamma_imag, second)
    square_two = square_norm(second_resid)
    beta_two = jnp.sqrt(square_two)

    coef_lane = iota(coef_out.shape, 1)
    coefs = jnp.zeros(coef_out.shape, jnp.float32)
    for at, value in enumerate((alpha_real, alpha_imag, gamma_real, gamma_imag, beta_one, beta_two)):
        coefs = jnp.where(coef_lane == at, value, coefs)
    coef_out[...] = coefs
    row = iota((2 * codes, lanes), 0)
    lane = iota((2 * codes, lanes), 1)
    here = (lane % mid // codes == lax.axis_index("ka")) & (lane // mid == row // codes)
    band = (row % codes).astype(jnp.float32)
    pick = jnp.where(here & (own[npol + 1 : npol + 2] == band), 1.0, 0.0).astype(jnp.bfloat16)
    picked = lax.dot_general(
        halves(second_resid), pick, (((1,), (1,)), ((), ())), preferred_element_type=jnp.float32
    )
    picked = (picked[:npol] + picked[npol:]) * lax.rsqrt(square_two)
    next_out[0, :, 0, :] = picked[:, :codes]
    next_out[0, :, 1, :] = picked[:, codes:]


def haydock(ka, codes, scale_count, npol, pieces):
    lanes = pieces[0].shape[1]
    square = jax.ShapeDtypeStruct((lanes, lanes), jnp.float32)
    return pl.pallas_call(
        functools.partial(haydock_kernel, ka, codes, scale_count, npol),
        out_shape=[
            jax.ShapeDtypeStruct((1, npol, 2, codes), jnp.float32),
            jax.ShapeDtypeStruct((npol, 6), jnp.float32),
        ],
        in_specs=[vmem] * len(pieces),
        out_specs=[vmem, vmem],
        compiler_params=limits(*pieces, square),
        name="haydock",
    )(*pieces)


def summed(value, axis):
    size = lax.axis_size(axis)
    if size & (size - 1):
        return value + sum(shifted(value, axis, step) for step in range(1, size))
    step = 1
    while step < size:
        value = value + exchanged(value, axis, lambda i, size: i ^ step)
        step *= 2
    return value


def local(
    ka,
    ga,
    ba,
    start_vector,
    valence_density,
    conduction_density,
    screening,
    qpoint_map,
    slot_owner,
    band_pairs,
    valence_energy,
    conduction_energy,
):
    npol = start_vector.shape[1]
    pair_count = start_vector.shape[3]
    kcount, vloc, val_count = qpoint_map.shape[0], valence_density.shape[3], valence_density.shape[4]
    cond_count = conduction_density.shape[3]
    pairs = vloc * val_count
    dims = (vloc, val_count, cond_count, npol)
    packed = pack(ka, ba, qpoint_map, slot_owner, valence_density, conduction_density)
    blocks = [packed[0]] + [shifted(packed[j], "ka", j) for j in range(1, ka)]
    early = ka // 2
    val_rows = slice(0, 2 * pairs)
    val_early = regroup(blocks[:early], val_rows)
    far_early = [shifted(val_early, "ga", r) for r in range(1, ga)]
    whole, near_table, far_table, extras = prepare(
        ka,
        dims,
        qpoint_map,
        slot_owner,
        band_pairs,
        valence_energy,
        conduction_energy,
        start_vector,
        screening,
        val_early,
    )
    val_late = regroup(blocks[early:], val_rows, (extras,))
    far_late = [shifted(val_late, "ga", r) for r in range(1, ga)]
    height = 2 * cond_count // ba * cond_count
    width = blocks[0].shape[1] // PARTS
    cond_rows = slice(2 * pairs, 2 * pairs + height)
    cond_parts = [
        regroup(blocks[1:], cond_rows, (val_late, *far_early), slice(c * width, (c + 1) * width))
        for c in range(PARTS)
    ]
    fields = field(pairs, whole, [val_early, val_late])
    cond_all = [regroup(blocks, cond_rows)]
    for r in range(1, ba):
        own_rows = slice(2 * pairs + r * height, 2 * pairs + (r + 1) * height)
        came = [handed(part, r) for part in cond_parts]
        cond_all.append(assemble(own_rows, blocks[0], came, fields))
    piece = near(ka, ba, dims, fields, near_table, extras, cond_all)
    if ga > 1:
        coupled = couple(ka, ga, ba, dims, whole, cond_all)
        far = [half for both in zip(far_early, far_late) for half in both]
        piece = contract(ka, ba, dims, far_table, piece, coupled, far, "far")
    piece = piece + sum(handed(piece, r) for r in range(1, ba))
    piece = summed(piece, "ga")
    pieces = [piece] + [shifted(piece, "ka", j) for j in range(1, ka)]
    scale_count = float(kcount * pair_count)
    return tuple(haydock(ka, pair_count, scale_count, npol, pieces))


def solution(mesh):
    in_specs = (
        P(("grp", "ka"), None, None, None),
        P(("grp", "ka"), None, None, "ba", None, "ga"),
        P(("grp", "ka"), None, None, None, None, "ga"),
        P(("grp", "ka"), None, "ga", None),
        P(),
        P(),
        P(),
        P(("grp", "ka"), None),
        P(("grp", "ka"), None),
    )
    out_specs = (P(("grp", "ka"), None, None, None), P("grp", None))
    body = functools.partial(local, mesh.shape["ka"], mesh.shape["ga"], mesh.shape["ba"])
    return jax.shard_map(body, mesh=mesh, in_specs=in_specs, out_specs=out_specs, check_vma=False)
```

```python
import functools
import math

import jax
import jax.numpy as jnp
from jax import lax
from jax.experimental import pallas as pl
from jax.experimental.pallas import tpu as pltpu
from jax.sharding import PartitionSpec as P

EPSILON = 1e-06
EXACT = lax.Precision.HIGHEST
VMEM_LEAST = 8 * 1024 * 1024
VMEM_MOST = 56 * 1024 * 1024

vmem = pl.BlockSpec(memory_space=pltpu.VMEM)
anywhere = pl.BlockSpec(memory_space=pl.ANY)
EXTRA_ROWS = 8
LIGHT = pl.CostEstimate(flops=1, bytes_accessed=1, transcendentals=0)
CHUNKS = 4
PARTS = 2


def in_vmem(shape, dtype):
    return pltpu.VMEM(shape, dtype)


def placed(value, space):
    return pltpu.with_memory_space_constraint(value, space)


def iota(shape, axis):
    return lax.broadcasted_iota(jnp.int32, shape, axis)


def split(values):
    high = values.astype(jnp.bfloat16)
    low = (values - high.astype(jnp.float32)).astype(jnp.bfloat16)
    return high, low


def limits(*arrays):
    held = sum(math.prod(a.shape) * a.dtype.itemsize for a in arrays)
    return pltpu.CompilerParams(vmem_limit_bytes=min(VMEM_MOST, VMEM_LEAST + 4 * held))


def target(me, step, size):
    return lax.rem(me + step, size)


def origin(me, step, size):
    return lax.rem(me + size - step, size)


def exchanged(value, axis, move):
    size, cores = lax.axis_size(axis), lax.axis_size("ba")
    pairs = [
        (i * cores + h, move(i, size) * cores + (h + 1) % cores)
        for i in range(size)
        for h in range(cores)
    ]
    return lax.ppermute(value, (axis, "ba"), pairs)


def shifted(value, axis, step):
    return exchanged(value, axis, lambda i, size: (i + step) % size)


def handed(value, step):
    size = lax.axis_size("ba")
    return lax.ppermute(value, "ba", [(h, (h + step) % size) for h in range(size)])


def pack_kernel(ka, qmap_in, owner_in, valence_in, conduction_in, *rest):
    outs = rest[:ka]
    qmap, owner, partner, valence, conduction, sems = rest[ka:]
    copies = [
        pltpu.make_async_copy(src, dst, sems.at[at])
        for at, (src, dst) in enumerate(
            ((qmap_in, qmap), (owner_in, owner), (valence_in, valence), (conduction_in, conduction))
        )
    ]
    for copy in copies:
        copy.start()
    me = lax.axis_index("ka")
    half = lax.axis_index("ba")
    count, width = valence.shape[1], valence.shape[5]
    cond_count = conduction.shape[3]
    share = cond_count // lax.axis_size("ba")
    val_rows = 2 * valence.shape[3] * valence.shape[4]
    cond_rows = 2 * share * cond_count

    def note(k2, carry):
        partner[owner[qmap[me, k2]]] = k2
        return carry

    copies[0].wait()
    copies[1].wait()
    lax.fori_loop(0, count, note, 0)
    copies[2].wait()
    copies[3].wait()
    for at in range(ka):
        k2 = partner[target(me, at, ka)]
        block = valence[0, k2].astype(jnp.float32).reshape(val_rows, width)
        outs[at][:val_rows, :] = block.astype(jnp.bfloat16)
        to = lax.rem(half + min(at, 1), lax.axis_size("ba"))
        block = conduction[0, k2, :, pl.ds(to * share, share)].astype(jnp.float32)
        outs[at][val_rows : val_rows + cond_rows, :] = block.reshape(cond_rows, width).astype(jnp.bfloat16)
    cores = lax.axis_size("ba")
    for h in range(1, cores):
        part = lax.rem(half + cores - h, cores)
        block = conduction[0, partner[me], :, pl.ds(part * share, share)].astype(jnp.float32)
        rows = slice(val_rows + h * cond_rows, val_rows + (h + 1) * cond_rows)
        outs[0][rows, :] = block.reshape(cond_rows, width).astype(jnp.bfloat16)


def pack(ka, ba, qmap, owner, valence, conduction):
    cond_count = conduction.shape[3]
    val_rows, cond_rows = 2 * valence.shape[3] * valence.shape[4], 2 * cond_count // ba * cond_count
    own = in_vmem((val_rows + ba * cond_rows, valence.shape[5]), valence.dtype)
    shape = in_vmem((val_rows + cond_rows, valence.shape[5]), valence.dtype)
    operands = [placed(x, pltpu.HBM) for x in (qmap, owner, valence, conduction)]
    return pl.pallas_call(
        functools.partial(pack_kernel, ka),
        out_shape=[own] + [shape] * (ka - 1),
        in_specs=[anywhere] * 4,
        out_specs=[vmem] * ka,
        scratch_shapes=[
            pltpu.SMEM(qmap.shape, jnp.int32),
            pltpu.SMEM(owner.shape, jnp.int32),
            pltpu.SMEM(owner.shape, jnp.int32),
            pltpu.VMEM(valence.shape, valence.dtype),
            pltpu.VMEM(conduction.shape, conduction.dtype),
            pltpu.SemaphoreType.DMA((4,)),
        ],
        compiler_params=limits(valence, conduction),
        name="pack",
    )(*operands)


def prepare_kernel(ka, dims, *refs):
    vloc, val_count, cond_count, npol = dims
    ins, screening, (screen_out, near_table, far_table, extras), scratch = refs[:6], refs[6], refs[8:12], refs[12:]
    qmap, owner, band_pairs, val_energy, cond_energy, start, sems, screen_sems = scratch
    me = lax.axis_index("ka")
    half = lax.axis_index("ba")
    mine = lax.axis_index("ga")
    copies = [
        pltpu.make_async_copy(src, dst, sems.at[at])
        for at, (src, dst) in enumerate(
            zip(ins, (qmap, owner, band_pairs, val_energy, cond_energy, start))
        )
    ]
    height = screening.shape[2] // CHUNKS
    chunks = [
        pltpu.make_async_copy(
            screening.at[0, part, pl.ds(c * height, height)],
            screen_out.at[part, pl.ds(c * height, height)],
            screen_sems.at[part, c],
        )
        for part in range(2)
        for c in range(CHUNKS)
    ]
    for copy in copies + chunks:
        copy.start()
    pairs = vloc * val_count
    block = 2 * pairs
    rows = ka * block
    codes = val_count * cond_count
    mid = ka * codes
    lanes = 2 * mid
    row = iota((2 * rows, lanes), 0)
    col = iota((2 * rows, lanes), 1)
    j_of_row = row % rows // block
    cores = lax.axis_size("ba")
    for moves, table in enumerate((near_table, far_table)):
        share = lax.rem(half + 2 * cores - moves - jnp.where(j_of_row == 0, 0, 1), cores)
        want = (
            (row % block // pairs) * mid
            + origin(me, j_of_row, ka) * codes
            + (share * vloc + row % pairs // val_count) * cond_count
        )
        joined = (col - want >= 0) & (col - want < cond_count)
        for v2 in range(val_count):
            pick = jnp.where(joined & (row % val_count == v2), 1.0, 0.0)
            table[:, v2 * lanes : (v2 + 1) * lanes] = pick.astype(jnp.bfloat16)

    for copy in copies:
        copy.wait()
    first = jnp.where((mine == 0) & (half == 0), 1.0, 0.0)
    lane = iota((1, lanes), 1)
    lane_k = lane % mid // codes
    band_row = iota((codes, lanes), 0)
    band_lane = iota((codes, lanes), 1)
    code = jnp.zeros((codes, lanes), jnp.int32)
    bands = jnp.full((1, lanes), -1.0, jnp.float32)
    for b in range(codes):
        code = jnp.where(band_row == b, band_pairs[b], code)
        bands = jnp.where(lane % codes == band_pairs[b], float(b), bands)
    vectors = jnp.zeros((npol, lanes), jnp.float32)
    for part in range(2):
        spot = part * mid + me * codes
        pick = jnp.where(band_lane == spot + code, first, 0.0)
        vectors = vectors + jnp.dot(start[0, :, part, :], pick, precision=EXACT)
    energy = jnp.zeros((1, lanes), jnp.float32)
    for c in range(cond_count):
        energy = jnp.where(lane % cond_count == c, cond_energy[0, c], energy)
    for v in range(val_count):
        energy = energy - jnp.where(lane % codes // cond_count == v, val_energy[0, v], 0.0)
    energy = jnp.where(lane_k == me, energy * first, 0.0)
    kcount = qmap.shape[0]

    def find(k2, found):
        return jnp.where(owner[qmap[0, k2]] == me, k2, found)

    back = lax.fori_loop(0, kcount, find, 0)
    second = lane_k + back
    second = jnp.where(second >= kcount, second - kcount, second).astype(jnp.float32) * first
    rest = jnp.zeros((EXTRA_ROWS - 3 - npol, lanes), jnp.float32)
    extras[...] = jnp.concatenate([vectors, energy, bands * first, second, rest], 0)
    for copy in chunks:
        copy.wait()


def prepare(ka, dims, qmap, owner, band_pairs, val_energy, cond_energy, start, screening, after):
    vloc, val_count, cond_count, npol = dims
    rows = 4 * ka * vloc * val_count
    lanes = 2 * ka * val_count * cond_count
    operands = (qmap, owner, band_pairs, val_energy, cond_energy, start, screening)
    table = jax.ShapeDtypeStruct((rows, val_count * lanes), jnp.bfloat16)
    return pl.pallas_call(
        functools.partial(prepare_kernel, ka, dims),
        out_shape=[
            in_vmem(screening.shape[1:], screening.dtype),
            in_vmem(table.shape, table.dtype),
            in_vmem(table.shape, table.dtype),
            in_vmem((EXTRA_ROWS, lanes), jnp.float32),
        ],
        in_specs=[anywhere] * 8,
        out_specs=[vmem] * 4,
        scratch_shapes=[pltpu.SMEM(x.shape, x.dtype) for x in operands[:5]]
        + [
            pltpu.VMEM(start.shape, start.dtype),
            pltpu.SemaphoreType.DMA((6,)),
            pltpu.SemaphoreType.DMA((2, CHUNKS)),
        ],
        cost_estimate=pl.CostEstimate(
            flops=0, bytes_accessed=4 * screening.size, transcendentals=0
        ),
        compiler_params=limits(table),
        name="prepare",
    )(*[placed(x, pltpu.HBM) for x in operands], after)


def regroup_kernel(count, rows, columns, *refs):
    blocks, out = refs[:count], refs[-1]
    height = rows.stop - rows.start
    for at in range(count):
        out[at * height : (at + 1) * height, :] = blocks[at][rows, columns]


def regroup(blocks, rows, after=(), columns=None):
    columns = columns or slice(0, blocks[0].shape[1])
    shape = (len(blocks) * (rows.stop - rows.start), columns.stop - columns.start)
    return pl.pallas_call(
        functools.partial(regroup_kernel, len(blocks), rows, columns),
        out_shape=in_vmem(shape, blocks[0].dtype),
        in_specs=[vmem] * len(blocks) + [anywhere] * len(after),
        out_specs=vmem,
        compiler_params=limits(*blocks),
        name="regroup",
    )(*blocks, *after)


def assemble_kernel(rows, own, *refs):
    parts, out = refs[:PARTS], refs[-1]
    height = rows.stop - rows.start
    out[:height, :] = own[rows, :]
    width = parts[0].shape[1]
    for c, part in enumerate(parts):
        out[height:, c * width : (c + 1) * width] = part[...]


def assemble(rows, own, parts, after):
    height = rows.stop - rows.start + parts[0].shape[0]
    return pl.pallas_call(
        functools.partial(assemble_kernel, rows),
        out_shape=in_vmem((height, own.shape[1]), own.dtype),
        in_specs=[vmem] * (1 + len(parts)) + [anywhere],
        out_specs=vmem,
        compiler_params=limits(own, *parts),
        name="assemble",
    )(own, *parts, after)


def with_turned(halves, pairs):
    wide = jnp.concatenate([half[...].astype(jnp.float32) for half in halves], 0)
    parts = []
    for at in range(0, wide.shape[0], 2 * pairs):
        parts += [-wide[at + pairs : at + 2 * pairs], wide[at : at + pairs]]
    return wide, jnp.concatenate(parts, 0)


def columns_of(place, width):
    return pl.ds(pl.multiple_of(place * width, 128), width)


def placed_piece(kernel, table, dims, ba):
    vloc, val_count, cond_count, npol = dims
    half = lax.axis_index("ba")
    codes = val_count * cond_count
    lanes = table.shape[1] // val_count
    share = cond_count // ba
    cond_rows = cond_count * cond_count
    spread = jnp.dot(
        jnp.concatenate(split(kernel), 0), table[...], preferred_element_type=jnp.float32
    )
    spread = spread[:cond_rows] + spread[cond_rows:]
    crow = iota((cond_rows, lanes), 0)
    share_rows = share * cond_count
    c_of_row = origin(half, crow // share_rows, ba) * share + crow % share_rows // cond_count
    same_c = c_of_row == iota((cond_rows, lanes), 1) % cond_count
    rows = []
    for v2 in range(val_count):
        kept = jnp.where(same_c, spread[:, v2 * lanes : (v2 + 1) * lanes], 0.0)
        parts = [kept[c * cond_count : (c + 1) * cond_count] for c in range(cond_count)]
        while len(parts) > 1:
            parts = [x + y for x, y in zip(parts[::2], parts[1::2])] + parts[len(parts) // 2 * 2 :]
        rows.append(parts[0])
    return jnp.concatenate(rows, 0)


def diagonal(crossed, ka, ba, share_rows, sign):
    rows = crossed.shape[1] // 2
    lane = iota((share_rows, 2 * rows), 1)
    lane_j = lane % rows // (rows // ka)
    straight = lane < rows
    kernel = []
    for h in range(ba):
        total = jnp.zeros((share_rows, 2 * rows), jnp.float32)
        for j in range(ka):
            at = (h * ka + j) * 2 * share_rows
            real = crossed[at : at + share_rows]
            imag = crossed[at + share_rows : at + 2 * share_rows]
            total = jnp.where(lane_j == j, jnp.where(straight, real, sign * imag), total)
        kernel.append(total)
    return jnp.concatenate(kernel, 0)


def field_kernel(pairs, screening, *refs):
    halves, out = refs[:-1], refs[-1]
    columns = columns_of(lax.axis_index("ga"), halves[0].shape[1])
    wide, turned = with_turned(halves, pairs)
    real = jnp.concatenate([wide, turned], 0).astype(jnp.bfloat16)
    imag = jnp.concatenate([turned, -wide], 0).astype(jnp.bfloat16)
    form = (((1,), (1,)), ((), ()))
    fields = lax.dot_general(
        screening[0, :, columns], real, form, preferred_element_type=jnp.float32
    ) + lax.dot_general(screening[1, :, columns], imag, form, preferred_element_type=jnp.float32)
    lanes = fields.shape[1]
    high, low = split(fields)
    out[:, :lanes] = high
    out[:, lanes:] = low


def field(pairs, screening, halves):
    operands = [screening, *halves]
    rows = sum(half.shape[0] for half in halves)
    return pl.pallas_call(
        functools.partial(field_kernel, pairs),
        out_shape=in_vmem((screening.shape[1], 4 * rows), jnp.bfloat16),
        in_specs=[vmem] * len(operands),
        out_specs=vmem,
        cost_estimate=LIGHT,
        compiler_params=limits(*operands),
        name="field",
    )(*operands)


def near_kernel(ka, ba, dims, *refs):
    vloc, val_count, cond_count, npol = dims
    fields, table, extras = refs[:3]
    cond_in, out = refs[3:-1], refs[-1]
    codes = val_count * cond_count
    cond = jnp.concatenate([ref[...] for ref in cond_in], 0)
    crossed = jnp.dot(cond, fields[...], preferred_element_type=jnp.float32)
    half = crossed.shape[1] // 2
    crossed = crossed[:, :half] + crossed[:, half:]
    kernel = diagonal(crossed, ka, ba, cond_count // ba * cond_count, -1.0)
    out[:codes, :] = placed_piece(kernel, table, dims, ba)
    out[codes:, :] = extras[...]


def near(ka, ba, dims, fields, table, extras, cond_all):
    vloc, val_count, cond_count, npol = dims
    operands = [fields, table, extras, *cond_all]
    shape = (val_count * cond_count + EXTRA_ROWS, extras.shape[1])
    return pl.pallas_call(
        functools.partial(near_kernel, ka, ba, dims),
        out_shape=in_vmem(shape, jnp.float32),
        in_specs=[vmem] * len(operands),
        out_specs=vmem,
        cost_estimate=LIGHT,
        compiler_params=limits(*operands),
        name="near",
    )(*operands)


def couple_kernel(ka, ga, ba, share_rows, screening, *refs):
    cond_in, outs = refs[:ba], refs[ba:]
    mine = lax.axis_index("ga")
    wide = jnp.concatenate([ref[...].astype(jnp.float32) for ref in cond_in], 0)
    straight, turned = [], []
    for at in range(0, wide.shape[0], 2 * share_rows):
        real, imag = wide[at : at + share_rows], wide[at + share_rows : at + 2 * share_rows]
        straight += [real, -imag]
        turned += [imag, real]
    straight = jnp.concatenate(straight, 0).astype(jnp.bfloat16)
    turned = jnp.concatenate(turned, 0).astype(jnp.bfloat16)
    width = screening.shape[2] // ga
    columns = [columns_of(origin(mine, r, ga), width) for r in range(1, ga)]
    coupled = [
        jnp.dot(straight, screening[0, :, block], preferred_element_type=jnp.float32)
        + jnp.dot(turned, screening[1, :, block], preferred_element_type=jnp.float32)
        for block in columns
    ]
    for out, value in zip(outs, coupled):
        high, low = split(value)
        out[: value.shape[0], :] = high
        out[value.shape[0] :, :] = low


def couple(ka, ga, ba, dims, screening, cond_all):
    share_rows = dims[2] // ba * dims[2]
    rows = 2 * sum(x.shape[0] for x in cond_all)
    width = screening.shape[2] // ga
    operands = [screening, *cond_all]
    return pl.pallas_call(
        functools.partial(couple_kernel, ka, ga, ba, share_rows),
        out_shape=[in_vmem((rows, width), jnp.bfloat16)] * (ga - 1),
        in_specs=[vmem] * len(operands),
        out_specs=[vmem] * (ga - 1),
        cost_estimate=LIGHT,
        compiler_params=limits(*operands),
        name="couple",
    )(*operands)


def contract_kernel(ka, ba, count, dims, *refs):
    vloc, val_count, cond_count, npol = dims
    table, held, out = refs[0], refs[1], refs[-1]
    each = (len(refs) - 3 - count) // count
    codes = val_count * cond_count
    crossed = None
    for r in range(count):
        coupled = refs[2 + r]
        halves = refs[2 + count + r * each : 2 + count + (r + 1) * each]
        rows = jnp.concatenate(with_turned(halves, vloc * val_count), 0).astype(jnp.bfloat16)
        term = lax.dot_general(
            coupled[...], rows, (((1,), (1,)), ((), ())), preferred_element_type=jnp.float32
        )
        crossed = term if crossed is None else crossed + term
    half = crossed.shape[0] // 2
    crossed = crossed[:half] + crossed[half:]
    kernel = diagonal(crossed, ka, ba, cond_count // ba * cond_count, 1.0)
    piece = placed_piece(kernel, table, dims, ba)
    before = held.shape[0] - EXTRA_ROWS
    out[:codes, :] = piece + held[:codes, :] if before else piece
    out[codes:, :] = held[before:, :]


def contract(ka, ba, dims, table, held, coupled, valence, name):
    val_count, cond_count = dims[1:3]
    operands = [table, held, *coupled, *valence]
    shape = (val_count * cond_count + EXTRA_ROWS, held.shape[1])
    return pl.pallas_call(
        functools.partial(contract_kernel, ka, ba, len(coupled), dims),
        out_shape=in_vmem(shape, jnp.float32),
        in_specs=[vmem] * len(operands),
        out_specs=vmem,
        cost_estimate=LIGHT,
        compiler_params=limits(*operands),
        name=name,
    )(*operands)


def haydock_kernel(ka, codes, scale_count, npol, *refs):
    pieces = refs[:-2]
    next_out, coef_out = refs[-2:]
    lanes = pieces[0].shape[1]
    mid = lanes // 2
    height = codes + EXTRA_ROWS
    found = [(ref, at) for ref in pieces for at in range(0, ref.shape[0], height)]
    extras = None
    slots = []
    for ref, at in found:
        rows = ref[at + codes : at + height, :]
        extras = rows if extras is None else extras + rows
        slots.append((ref[at : at + codes, :], rows[npol + 2 : npol + 3]))
    own = pieces[0][codes:height, :]
    sign = jnp.where(iota((1, lanes), 1) < mid, -1.0, 1.0)
    top = []
    for k2 in range(ka):
        block = jnp.zeros((codes, lanes), jnp.float32)
        for piece, second in slots:
            block = jnp.where(second == float(k2), piece, block)
        top.append(block)
    top = jnp.concatenate(top, 0)
    matrix = jnp.concatenate([top, sign * pltpu.roll(top, mid, 1)], 0)
    full = jnp.concatenate(split(matrix), 1)
    start = extras[:npol]
    energy = extras[npol : npol + 1]

    def halves(vector):
        top = vector.astype(jnp.bfloat16).astype(jnp.float32)
        return jnp.concatenate([top, vector - top], 0).astype(jnp.bfloat16)

    def mean(values):
        return jnp.sum(values, axis=1, keepdims=True) * (1.0 / scale_count)

    def square_norm(vector):
        return mean(vector * vector) + EPSILON

    def swap(vector):
        return pltpu.roll(vector, mid, 1)

    def hamiltonian(vector):
        product = jnp.dot(halves(vector), full, preferred_element_type=jnp.float32)
        main = product[:npol, :lanes] + product[npol:, :lanes]
        return energy * vector - (main + product[:npol, lanes:])

    def inner(left, right):
        return mean(left * right), mean(-sign * left * swap(right))

    def times(real, imag, vector):
        return real * vector + imag * (sign * swap(vector))

    start_image = hamiltonian(start)
    scale = lax.rsqrt(square_norm(start))
    first = start * scale
    alpha_real, alpha_imag = (value * (scale * scale) for value in inner(start, start_image))
    first_resid = start_image * scale - times(alpha_real, alpha_imag, first)
    resid_image = hamiltonian(first_resid)
    square_one = square_norm(first_resid)
    scale, beta_one = lax.rsqrt(square_one), jnp.sqrt(square_one)
    second = first_resid * scale
    gamma_real, gamma_imag = (value * (scale * scale) for value in inner(first_resid, resid_image))
    second_resid = resid_image * scale - beta_one * first - times(gamma_real, gamma_imag, second)
    square_two = square_norm(second_resid)
    beta_two = jnp.sqrt(square_two)

    coef_lane = iota(coef_out.shape, 1)
    coefs = jnp.zeros(coef_out.shape, jnp.float32)
    for at, value in enumerate((alpha_real, alpha_imag, gamma_real, gamma_imag, beta_one, beta_two)):
        coefs = jnp.where(coef_lane == at, value, coefs)
    coef_out[...] = coefs
    row = iota((2 * codes, lanes), 0)
    lane = iota((2 * codes, lanes), 1)
    here = (lane % mid // codes == lax.axis_index("ka")) & (lane // mid == row // codes)
    band = (row % codes).astype(jnp.float32)
    pick = jnp.where(here & (own[npol + 1 : npol + 2] == band), 1.0, 0.0).astype(jnp.bfloat16)
    picked = lax.dot_general(
        halves(second_resid), pick, (((1,), (1,)), ((), ())), preferred_element_type=jnp.float32
    )
    picked = (picked[:npol] + picked[npol:]) * lax.rsqrt(square_two)
    next_out[0, :, 0, :] = picked[:, :codes]
    next_out[0, :, 1, :] = picked[:, codes:]


def haydock(ka, codes, scale_count, npol, pieces):
    lanes = pieces[0].shape[1]
    square = jax.ShapeDtypeStruct((lanes, lanes), jnp.float32)
    return pl.pallas_call(
        functools.partial(haydock_kernel, ka, codes, scale_count, npol),
        out_shape=[
            jax.ShapeDtypeStruct((1, npol, 2, codes), jnp.float32),
            jax.ShapeDtypeStruct((npol, 6), jnp.float32),
        ],
        in_specs=[vmem] * len(pieces),
        out_specs=[vmem, vmem],
        compiler_params=limits(*pieces, square),
        name="haydock",
    )(*pieces)


def summed(value, axis):
    size = lax.axis_size(axis)
    if size & (size - 1):
        return value + sum(shifted(value, axis, step) for step in range(1, size))
    step = 1
    while step < size:
        value = value + exchanged(value, axis, lambda i, size: i ^ step)
        step *= 2
    return value


def local(
    ka,
    ga,
    ba,
    start_vector,
    valence_density,
    conduction_density,
    screening,
    qpoint_map,
    slot_owner,
    band_pairs,
    valence_energy,
    conduction_energy,
):
    npol = start_vector.shape[1]
    pair_count = start_vector.shape[3]
    kcount, vloc, val_count = qpoint_map.shape[0], valence_density.shape[3], valence_density.shape[4]
    cond_count = conduction_density.shape[3]
    pairs = vloc * val_count
    dims = (vloc, val_count, cond_count, npol)
    packed = pack(ka, ba, qpoint_map, slot_owner, valence_density, conduction_density)
    blocks = [packed[0]] + [shifted(packed[j], "ka", j) for j in range(1, ka)]
    early = ka // 2
    val_rows = slice(0, 2 * pairs)
    val_early = regroup(blocks[:early], val_rows)
    far_early = [shifted(val_early, "ga", r) for r in range(1, ga)]
    whole, near_table, far_table, extras = prepare(
        ka,
        dims,
        qpoint_map,
        slot_owner,
        band_pairs,
        valence_energy,
        conduction_energy,
        start_vector,
        screening,
        val_early,
    )
    val_late = regroup(blocks[early:], val_rows, (extras,))
    far_late = [shifted(val_late, "ga", r) for r in range(1, ga)]
    height = 2 * cond_count // ba * cond_count
    width = blocks[0].shape[1] // PARTS
    cond_rows = slice(2 * pairs, 2 * pairs + height)
    cond_parts = [
        regroup(blocks[1:], cond_rows, (val_late, *far_early), slice(c * width, (c + 1) * width))
        for c in range(PARTS)
    ]
    fields = field(pairs, whole, [val_early, val_late])
    cond_all = [regroup(blocks, cond_rows)]
    for r in range(1, ba):
        own_rows = slice(2 * pairs + r * height, 2 * pairs + (r + 1) * height)
        came = [handed(part, r) for part in cond_parts]
        cond_all.append(assemble(own_rows, blocks[0], came, fields))
    piece = near(ka, ba, dims, fields, near_table, extras, cond_all)
    if ga > 1:
        coupled = couple(ka, ga, ba, dims, whole, cond_all)
        far = [half for both in zip(far_early, far_late) for half in both]
        piece = contract(ka, ba, dims, far_table, piece, coupled, far, "far")
    piece = piece + sum(handed(piece, r) for r in range(1, ba))
    piece = summed(piece, "ga")
    order = sorted(range(1, ka), key=lambda j: (-min(j, ka - j), j))
    pieces = [piece] + [shifted(piece, "ka", j) for j in order]
    scale_count = float(kcount * pair_count)
    return tuple(haydock(ka, pair_count, scale_count, npol, pieces))


def solution(mesh):
    in_specs = (
        P(("grp", "ka"), None, None, None),
        P(("grp", "ka"), None, None, "ba", None, "ga"),
        P(("grp", "ka"), None, None, None, None, "ga"),
        P(("grp", "ka"), None, "ga", None),
        P(),
        P(),
        P(),
        P(("grp", "ka"), None),
        P(("grp", "ka"), None),
    )
    out_specs = (P(("grp", "ka"), None, None, None), P("grp", None))
    body = functools.partial(local, mesh.shape["ka"], mesh.shape["ga"], mesh.shape["ba"])
    return jax.shard_map(body, mesh=mesh, in_specs=in_specs, out_specs=out_specs, check_vma=False)
```

```python
import functools
import math

import jax
import jax.numpy as jnp
from jax import lax
from jax.experimental import pallas as pl
from jax.experimental.pallas import tpu as pltpu
from jax.sharding import PartitionSpec as P

EPSILON = 1e-06
EXACT = lax.Precision.HIGHEST
VMEM_LEAST = 8 * 1024 * 1024
VMEM_MOST = 56 * 1024 * 1024

vmem = pl.BlockSpec(memory_space=pltpu.VMEM)
anywhere = pl.BlockSpec(memory_space=pl.ANY)
EXTRA_ROWS = 8
LIGHT = pl.CostEstimate(flops=1, bytes_accessed=1, transcendentals=0)
CHUNKS = 4
PARTS = 2


def in_vmem(shape, dtype):
    return pltpu.VMEM(shape, dtype)


def placed(value, space):
    return pltpu.with_memory_space_constraint(value, space)


def iota(shape, axis):
    return lax.broadcasted_iota(jnp.int32, shape, axis)


def split(values):
    high = values.astype(jnp.bfloat16)
    low = (values - high.astype(jnp.float32)).astype(jnp.bfloat16)
    return high, low


def limits(*arrays):
    held = sum(math.prod(a.shape) * a.dtype.itemsize for a in arrays)
    return pltpu.CompilerParams(vmem_limit_bytes=min(VMEM_MOST, VMEM_LEAST + 4 * held))


def order(size):
    return [0] + sorted(range(1, size), key=lambda j: (-min(j, size - j), j))


def target(me, step, size):
    return lax.rem(me + step, size)


def origin(me, step, size):
    return lax.rem(me + size - step, size)


def exchanged(value, axis, move):
    size, cores = lax.axis_size(axis), lax.axis_size("ba")
    pairs = [
        (i * cores + h, move(i, size) * cores + (h + 1) % cores)
        for i in range(size)
        for h in range(cores)
    ]
    return lax.ppermute(value, (axis, "ba"), pairs)


def shifted(value, axis, step):
    return exchanged(value, axis, lambda i, size: (i + step) % size)


def handed(value, step):
    size = lax.axis_size("ba")
    return lax.ppermute(value, "ba", [(h, (h + step) % size) for h in range(size)])


def pack_kernel(ka, qmap_in, owner_in, valence_in, conduction_in, *rest):
    outs = rest[:ka]
    qmap, owner, partner, valence, conduction, sems = rest[ka:]
    copies = [
        pltpu.make_async_copy(src, dst, sems.at[at])
        for at, (src, dst) in enumerate(
            ((qmap_in, qmap), (owner_in, owner), (valence_in, valence), (conduction_in, conduction))
        )
    ]
    for copy in copies:
        copy.start()
    me = lax.axis_index("ka")
    half = lax.axis_index("ba")
    count, width = valence.shape[1], valence.shape[5]
    cond_count = conduction.shape[3]
    share = cond_count // lax.axis_size("ba")
    val_rows = 2 * valence.shape[3] * valence.shape[4]
    cond_rows = 2 * share * cond_count

    def note(k2, carry):
        partner[owner[qmap[me, k2]]] = k2
        return carry

    copies[0].wait()
    copies[1].wait()
    lax.fori_loop(0, count, note, 0)
    copies[2].wait()
    copies[3].wait()
    for at in range(ka):
        k2 = partner[target(me, order(ka)[at], ka)]
        block = valence[0, k2].astype(jnp.float32).reshape(val_rows, width)
        outs[at][:val_rows, :] = block.astype(jnp.bfloat16)
        to = lax.rem(half + min(at, 1), lax.axis_size("ba"))
        block = conduction[0, k2, :, pl.ds(to * share, share)].astype(jnp.float32)
        outs[at][val_rows : val_rows + cond_rows, :] = block.reshape(cond_rows, width).astype(jnp.bfloat16)
    cores = lax.axis_size("ba")
    for h in range(1, cores):
        part = lax.rem(half + cores - h, cores)
        block = conduction[0, partner[me], :, pl.ds(part * share, share)].astype(jnp.float32)
        rows = slice(val_rows + h * cond_rows, val_rows + (h + 1) * cond_rows)
        outs[0][rows, :] = block.reshape(cond_rows, width).astype(jnp.bfloat16)


def pack(ka, ba, qmap, owner, valence, conduction):
    cond_count = conduction.shape[3]
    val_rows, cond_rows = 2 * valence.shape[3] * valence.shape[4], 2 * cond_count // ba * cond_count
    own = in_vmem((val_rows + ba * cond_rows, valence.shape[5]), valence.dtype)
    shape = in_vmem((val_rows + cond_rows, valence.shape[5]), valence.dtype)
    operands = [placed(x, pltpu.HBM) for x in (qmap, owner, valence, conduction)]
    return pl.pallas_call(
        functools.partial(pack_kernel, ka),
        out_shape=[own] + [shape] * (ka - 1),
        in_specs=[anywhere] * 4,
        out_specs=[vmem] * ka,
        scratch_shapes=[
            pltpu.SMEM(qmap.shape, jnp.int32),
            pltpu.SMEM(owner.shape, jnp.int32),
            pltpu.SMEM(owner.shape, jnp.int32),
            pltpu.VMEM(valence.shape, valence.dtype),
            pltpu.VMEM(conduction.shape, conduction.dtype),
            pltpu.SemaphoreType.DMA((4,)),
        ],
        compiler_params=limits(valence, conduction),
        name="pack",
    )(*operands)


def prepare_kernel(ka, dims, *refs):
    vloc, val_count, cond_count, npol = dims
    ins, screening, (screen_out, near_table, far_table, extras), scratch = refs[:6], refs[6], refs[8:12], refs[12:]
    qmap, owner, band_pairs, val_energy, cond_energy, start, sems, screen_sems = scratch
    me = lax.axis_index("ka")
    half = lax.axis_index("ba")
    mine = lax.axis_index("ga")
    copies = [
        pltpu.make_async_copy(src, dst, sems.at[at])
        for at, (src, dst) in enumerate(
            zip(ins, (qmap, owner, band_pairs, val_energy, cond_energy, start))
        )
    ]
    height = screening.shape[2] // CHUNKS
    chunks = [
        pltpu.make_async_copy(
            screening.at[0, part, pl.ds(c * height, height)],
            screen_out.at[part, pl.ds(c * height, height)],
            screen_sems.at[part, c],
        )
        for part in range(2)
        for c in range(CHUNKS)
    ]
    for copy in copies + chunks:
        copy.start()
    pairs = vloc * val_count
    block = 2 * pairs
    rows = ka * block
    codes = val_count * cond_count
    mid = ka * codes
    lanes = 2 * mid
    row = iota((2 * rows, lanes), 0)
    col = iota((2 * rows, lanes), 1)
    j_of_row = row % rows // block
    position = iota((2 * rows, 1), 0) % rows // block
    step = jnp.zeros((2 * rows, 1), jnp.int32)
    for at, j in enumerate(order(ka)):
        step = jnp.where(position == at, j, step)
    cores = lax.axis_size("ba")
    for moves, table in enumerate((near_table, far_table)):
        share = lax.rem(half + 2 * cores - moves - jnp.where(j_of_row == 0, 0, 1), cores)
        want = (
            (row % block // pairs) * mid
            + origin(me, step, ka) * codes
            + (share * vloc + row % pairs // val_count) * cond_count
        )
        joined = (col - want >= 0) & (col - want < cond_count)
        for v2 in range(val_count):
            pick = jnp.where(joined & (row % val_count == v2), 1.0, 0.0)
            table[:, v2 * lanes : (v2 + 1) * lanes] = pick.astype(jnp.bfloat16)

    for copy in copies:
        copy.wait()
    first = jnp.where((mine == 0) & (half == 0), 1.0, 0.0)
    lane = iota((1, lanes), 1)
    lane_k = lane % mid // codes
    band_row = iota((codes, lanes), 0)
    band_lane = iota((codes, lanes), 1)
    code = jnp.zeros((codes, lanes), jnp.int32)
    bands = jnp.full((1, lanes), -1.0, jnp.float32)
    for b in range(codes):
        code = jnp.where(band_row == b, band_pairs[b], code)
        bands = jnp.where(lane % codes == band_pairs[b], float(b), bands)
    vectors = jnp.zeros((npol, lanes), jnp.float32)
    for part in range(2):
        spot = part * mid + me * codes
        pick = jnp.where(band_lane == spot + code, first, 0.0)
        vectors = vectors + jnp.dot(start[0, :, part, :], pick, precision=EXACT)
    energy = jnp.zeros((1, lanes), jnp.float32)
    for c in range(cond_count):
        energy = jnp.where(lane % cond_count == c, cond_energy[0, c], energy)
    for v in range(val_count):
        energy = energy - jnp.where(lane % codes // cond_count == v, val_energy[0, v], 0.0)
    energy = jnp.where(lane_k == me, energy * first, 0.0)
    kcount = qmap.shape[0]

    def find(k2, found):
        return jnp.where(owner[qmap[0, k2]] == me, k2, found)

    back = lax.fori_loop(0, kcount, find, 0)
    second = lane_k + back
    second = jnp.where(second >= kcount, second - kcount, second).astype(jnp.float32) * first
    rest = jnp.zeros((EXTRA_ROWS - 3 - npol, lanes), jnp.float32)
    extras[...] = jnp.concatenate([vectors, energy, bands * first, second, rest], 0)
    for copy in chunks:
        copy.wait()


def prepare(ka, dims, qmap, owner, band_pairs, val_energy, cond_energy, start, screening, after):
    vloc, val_count, cond_count, npol = dims
    rows = 4 * ka * vloc * val_count
    lanes = 2 * ka * val_count * cond_count
    operands = (qmap, owner, band_pairs, val_energy, cond_energy, start, screening)
    table = jax.ShapeDtypeStruct((rows, val_count * lanes), jnp.bfloat16)
    return pl.pallas_call(
        functools.partial(prepare_kernel, ka, dims),
        out_shape=[
            in_vmem(screening.shape[1:], screening.dtype),
            in_vmem(table.shape, table.dtype),
            in_vmem(table.shape, table.dtype),
            in_vmem((EXTRA_ROWS, lanes), jnp.float32),
        ],
        in_specs=[anywhere] * 8,
        out_specs=[vmem] * 4,
        scratch_shapes=[pltpu.SMEM(x.shape, x.dtype) for x in operands[:5]]
        + [
            pltpu.VMEM(start.shape, start.dtype),
            pltpu.SemaphoreType.DMA((6,)),
            pltpu.SemaphoreType.DMA((2, CHUNKS)),
        ],
        cost_estimate=pl.CostEstimate(
            flops=0, bytes_accessed=4 * screening.size, transcendentals=0
        ),
        compiler_params=limits(table),
        name="prepare",
    )(*[placed(x, pltpu.HBM) for x in operands], after)


def regroup_kernel(count, rows, columns, *refs):
    blocks, out = refs[:count], refs[-1]
    height = rows.stop - rows.start
    for at in range(count):
        out[at * height : (at + 1) * height, :] = blocks[at][rows, columns]


def regroup(blocks, rows, after=(), columns=None):
    columns = columns or slice(0, blocks[0].shape[1])
    shape = (len(blocks) * (rows.stop - rows.start), columns.stop - columns.start)
    return pl.pallas_call(
        functools.partial(regroup_kernel, len(blocks), rows, columns),
        out_shape=in_vmem(shape, blocks[0].dtype),
        in_specs=[vmem] * len(blocks) + [anywhere] * len(after),
        out_specs=vmem,
        compiler_params=limits(*blocks),
        name="regroup",
    )(*blocks, *after)


def assemble_kernel(rows, own, *refs):
    parts, out = refs[:PARTS], refs[-1]
    height = rows.stop - rows.start
    out[:height, :] = own[rows, :]
    width = parts[0].shape[1]
    for c, part in enumerate(parts):
        out[height:, c * width : (c + 1) * width] = part[...]


def assemble(rows, own, parts, after):
    height = rows.stop - rows.start + parts[0].shape[0]
    return pl.pallas_call(
        functools.partial(assemble_kernel, rows),
        out_shape=in_vmem((height, own.shape[1]), own.dtype),
        in_specs=[vmem] * (1 + len(parts)) + [anywhere],
        out_specs=vmem,
        compiler_params=limits(own, *parts),
        name="assemble",
    )(own, *parts, after)


def with_turned(halves, pairs):
    wide = jnp.concatenate([half[...].astype(jnp.float32) for half in halves], 0)
    parts = []
    for at in range(0, wide.shape[0], 2 * pairs):
        parts += [-wide[at + pairs : at + 2 * pairs], wide[at : at + pairs]]
    return wide, jnp.concatenate(parts, 0)


def columns_of(place, width):
    return pl.ds(pl.multiple_of(place * width, 128), width)


def placed_piece(kernel, table, dims, ba):
    vloc, val_count, cond_count, npol = dims
    half = lax.axis_index("ba")
    codes = val_count * cond_count
    lanes = table.shape[1] // val_count
    share = cond_count // ba
    cond_rows = cond_count * cond_count
    spread = jnp.dot(
        jnp.concatenate(split(kernel), 0), table[...], preferred_element_type=jnp.float32
    )
    spread = spread[:cond_rows] + spread[cond_rows:]
    crow = iota((cond_rows, lanes), 0)
    share_rows = share * cond_count
    c_of_row = origin(half, crow // share_rows, ba) * share + crow % share_rows // cond_count
    same_c = c_of_row == iota((cond_rows, lanes), 1) % cond_count
    rows = []
    for v2 in range(val_count):
        kept = jnp.where(same_c, spread[:, v2 * lanes : (v2 + 1) * lanes], 0.0)
        parts = [kept[c * cond_count : (c + 1) * cond_count] for c in range(cond_count)]
        while len(parts) > 1:
            parts = [x + y for x, y in zip(parts[::2], parts[1::2])] + parts[len(parts) // 2 * 2 :]
        rows.append(parts[0])
    return jnp.concatenate(rows, 0)


def diagonal(crossed, ka, ba, share_rows, sign):
    rows = crossed.shape[1] // 2
    lane = iota((share_rows, 2 * rows), 1)
    lane_j = lane % rows // (rows // ka)
    straight = lane < rows
    kernel = []
    for h in range(ba):
        total = jnp.zeros((share_rows, 2 * rows), jnp.float32)
        for j in range(ka):
            at = (h * ka + j) * 2 * share_rows
            real = crossed[at : at + share_rows]
            imag = crossed[at + share_rows : at + 2 * share_rows]
            total = jnp.where(lane_j == j, jnp.where(straight, real, sign * imag), total)
        kernel.append(total)
    return jnp.concatenate(kernel, 0)


def field_kernel(pairs, screening, *refs):
    halves, out = refs[:-1], refs[-1]
    columns = columns_of(lax.axis_index("ga"), halves[0].shape[1])
    wide, turned = with_turned(halves, pairs)
    real = jnp.concatenate([wide, turned], 0).astype(jnp.bfloat16)
    imag = jnp.concatenate([turned, -wide], 0).astype(jnp.bfloat16)
    form = (((1,), (1,)), ((), ()))
    fields = lax.dot_general(
        screening[0, :, columns], real, form, preferred_element_type=jnp.float32
    ) + lax.dot_general(screening[1, :, columns], imag, form, preferred_element_type=jnp.float32)
    lanes = fields.shape[1]
    high, low = split(fields)
    out[:, :lanes] = high
    out[:, lanes:] = low


def field(pairs, screening, halves):
    operands = [screening, *halves]
    rows = sum(half.shape[0] for half in halves)
    return pl.pallas_call(
        functools.partial(field_kernel, pairs),
        out_shape=in_vmem((screening.shape[1], 4 * rows), jnp.bfloat16),
        in_specs=[vmem] * len(operands),
        out_specs=vmem,
        cost_estimate=LIGHT,
        compiler_params=limits(*operands),
        name="field",
    )(*operands)


def near_kernel(ka, ba, dims, *refs):
    vloc, val_count, cond_count, npol = dims
    fields, table, extras = refs[:3]
    cond_in, out = refs[3:-1], refs[-1]
    codes = val_count * cond_count
    cond = jnp.concatenate([ref[...] for ref in cond_in], 0)
    crossed = jnp.dot(cond, fields[...], preferred_element_type=jnp.float32)
    half = crossed.shape[1] // 2
    crossed = crossed[:, :half] + crossed[:, half:]
    kernel = diagonal(crossed, ka, ba, cond_count // ba * cond_count, -1.0)
    out[:codes, :] = placed_piece(kernel, table, dims, ba)
    out[codes:, :] = extras[...]


def near(ka, ba, dims, fields, table, extras, cond_all):
    vloc, val_count, cond_count, npol = dims
    operands = [fields, table, extras, *cond_all]
    shape = (val_count * cond_count + EXTRA_ROWS, extras.shape[1])
    return pl.pallas_call(
        functools.partial(near_kernel, ka, ba, dims),
        out_shape=in_vmem(shape, jnp.float32),
        in_specs=[vmem] * len(operands),
        out_specs=vmem,
        cost_estimate=LIGHT,
        compiler_params=limits(*operands),
        name="near",
    )(*operands)


def couple_kernel(ka, ga, ba, share_rows, screening, *refs):
    cond_in, outs = refs[:ba], refs[ba:]
    mine = lax.axis_index("ga")
    wide = jnp.concatenate([ref[...].astype(jnp.float32) for ref in cond_in], 0)
    straight, turned = [], []
    for at in range(0, wide.shape[0], 2 * share_rows):
        real, imag = wide[at : at + share_rows], wide[at + share_rows : at + 2 * share_rows]
        straight += [real, -imag]
        turned += [imag, real]
    straight = jnp.concatenate(straight, 0).astype(jnp.bfloat16)
    turned = jnp.concatenate(turned, 0).astype(jnp.bfloat16)
    width = screening.shape[2] // ga
    columns = [columns_of(origin(mine, r, ga), width) for r in range(1, ga)]
    coupled = [
        jnp.dot(straight, screening[0, :, block], preferred_element_type=jnp.float32)
        + jnp.dot(turned, screening[1, :, block], preferred_element_type=jnp.float32)
        for block in columns
    ]
    for out, value in zip(outs, coupled):
        high, low = split(value)
        out[: value.shape[0], :] = high
        out[value.shape[0] :, :] = low


def couple(ka, ga, ba, dims, screening, cond_all):
    share_rows = dims[2] // ba * dims[2]
    rows = 2 * sum(x.shape[0] for x in cond_all)
    width = screening.shape[2] // ga
    operands = [screening, *cond_all]
    return pl.pallas_call(
        functools.partial(couple_kernel, ka, ga, ba, share_rows),
        out_shape=[in_vmem((rows, width), jnp.bfloat16)] * (ga - 1),
        in_specs=[vmem] * len(operands),
        out_specs=[vmem] * (ga - 1),
        cost_estimate=LIGHT,
        compiler_params=limits(*operands),
        name="couple",
    )(*operands)


def contract_kernel(ka, ba, count, dims, *refs):
    vloc, val_count, cond_count, npol = dims
    table, held, out = refs[0], refs[1], refs[-1]
    each = (len(refs) - 3 - count) // count
    codes = val_count * cond_count
    crossed = None
    for r in range(count):
        coupled = refs[2 + r]
        halves = refs[2 + count + r * each : 2 + count + (r + 1) * each]
        rows = jnp.concatenate(with_turned(halves, vloc * val_count), 0).astype(jnp.bfloat16)
        term = lax.dot_general(
            coupled[...], rows, (((1,), (1,)), ((), ())), preferred_element_type=jnp.float32
        )
        crossed = term if crossed is None else crossed + term
    half = crossed.shape[0] // 2
    crossed = crossed[:half] + crossed[half:]
    kernel = diagonal(crossed, ka, ba, cond_count // ba * cond_count, 1.0)
    piece = placed_piece(kernel, table, dims, ba)
    before = held.shape[0] - EXTRA_ROWS
    out[:codes, :] = piece + held[:codes, :] if before else piece
    out[codes:, :] = held[before:, :]


def contract(ka, ba, dims, table, held, coupled, valence, name):
    val_count, cond_count = dims[1:3]
    operands = [table, held, *coupled, *valence]
    shape = (val_count * cond_count + EXTRA_ROWS, held.shape[1])
    return pl.pallas_call(
        functools.partial(contract_kernel, ka, ba, len(coupled), dims),
        out_shape=in_vmem(shape, jnp.float32),
        in_specs=[vmem] * len(operands),
        out_specs=vmem,
        cost_estimate=LIGHT,
        compiler_params=limits(*operands),
        name=name,
    )(*operands)


def haydock_kernel(ka, codes, scale_count, npol, *refs):
    pieces = refs[:-2]
    next_out, coef_out = refs[-2:]
    lanes = pieces[0].shape[1]
    mid = lanes // 2
    height = codes + EXTRA_ROWS
    found = [(ref, at) for ref in pieces for at in range(0, ref.shape[0], height)]
    extras = None
    slots = []
    for ref, at in found:
        rows = ref[at + codes : at + height, :]
        extras = rows if extras is None else extras + rows
        slots.append((ref[at : at + codes, :], rows[npol + 2 : npol + 3]))
    own = pieces[0][codes:height, :]
    sign = jnp.where(iota((1, lanes), 1) < mid, -1.0, 1.0)
    top = []
    for k2 in range(ka):
        block = jnp.zeros((codes, lanes), jnp.float32)
        for piece, second in slots:
            block = jnp.where(second == float(k2), piece, block)
        top.append(block)
    top = jnp.concatenate(top, 0)
    matrix = jnp.concatenate([top, sign * pltpu.roll(top, mid, 1)], 0)
    full = jnp.concatenate(split(matrix), 1)
    start = extras[:npol]
    energy = extras[npol : npol + 1]

    def halves(vector):
        top = vector.astype(jnp.bfloat16).astype(jnp.float32)
        return jnp.concatenate([top, vector - top], 0).astype(jnp.bfloat16)

    def mean(values):
        return jnp.sum(values, axis=1, keepdims=True) * (1.0 / scale_count)

    def square_norm(vector):
        return mean(vector * vector) + EPSILON

    def swap(vector):
        return pltpu.roll(vector, mid, 1)

    def hamiltonian(vector):
        product = jnp.dot(halves(vector), full, preferred_element_type=jnp.float32)
        main = product[:npol, :lanes] + product[npol:, :lanes]
        return energy * vector - (main + product[:npol, lanes:])

    def inner(left, right):
        return mean(left * right), mean(-sign * left * swap(right))

    def times(real, imag, vector):
        return real * vector + imag * (sign * swap(vector))

    start_image = hamiltonian(start)
    scale = lax.rsqrt(square_norm(start))
    first = start * scale
    alpha_real, alpha_imag = (value * (scale * scale) for value in inner(start, start_image))
    first_resid = start_image * scale - times(alpha_real, alpha_imag, first)
    resid_image = hamiltonian(first_resid)
    square_one = square_norm(first_resid)
    scale, beta_one = lax.rsqrt(square_one), jnp.sqrt(square_one)
    second = first_resid * scale
    gamma_real, gamma_imag = (value * (scale * scale) for value in inner(first_resid, resid_image))
    second_resid = resid_image * scale - beta_one * first - times(gamma_real, gamma_imag, second)
    square_two = square_norm(second_resid)
    beta_two = jnp.sqrt(square_two)

    coef_lane = iota(coef_out.shape, 1)
    coefs = jnp.zeros(coef_out.shape, jnp.float32)
    for at, value in enumerate((alpha_real, alpha_imag, gamma_real, gamma_imag, beta_one, beta_two)):
        coefs = jnp.where(coef_lane == at, value, coefs)
    coef_out[...] = coefs
    row = iota((2 * codes, lanes), 0)
    lane = iota((2 * codes, lanes), 1)
    here = (lane % mid // codes == lax.axis_index("ka")) & (lane // mid == row // codes)
    band = (row % codes).astype(jnp.float32)
    pick = jnp.where(here & (own[npol + 1 : npol + 2] == band), 1.0, 0.0).astype(jnp.bfloat16)
    picked = lax.dot_general(
        halves(second_resid), pick, (((1,), (1,)), ((), ())), preferred_element_type=jnp.float32
    )
    picked = (picked[:npol] + picked[npol:]) * lax.rsqrt(square_two)
    next_out[0, :, 0, :] = picked[:, :codes]
    next_out[0, :, 1, :] = picked[:, codes:]


def haydock(ka, codes, scale_count, npol, pieces):
    lanes = pieces[0].shape[1]
    square = jax.ShapeDtypeStruct((lanes, lanes), jnp.float32)
    return pl.pallas_call(
        functools.partial(haydock_kernel, ka, codes, scale_count, npol),
        out_shape=[
            jax.ShapeDtypeStruct((1, npol, 2, codes), jnp.float32),
            jax.ShapeDtypeStruct((npol, 6), jnp.float32),
        ],
        in_specs=[vmem] * len(pieces),
        out_specs=[vmem, vmem],
        compiler_params=limits(*pieces, square),
        name="haydock",
    )(*pieces)


def summed(value, axis):
    size = lax.axis_size(axis)
    if size & (size - 1):
        return value + sum(shifted(value, axis, step) for step in range(1, size))
    step = 1
    while step < size:
        value = value + exchanged(value, axis, lambda i, size: i ^ step)
        step *= 2
    return value


def local(
    ka,
    ga,
    ba,
    start_vector,
    valence_density,
    conduction_density,
    screening,
    qpoint_map,
    slot_owner,
    band_pairs,
    valence_energy,
    conduction_energy,
):
    npol = start_vector.shape[1]
    pair_count = start_vector.shape[3]
    kcount, vloc, val_count = qpoint_map.shape[0], valence_density.shape[3], valence_density.shape[4]
    cond_count = conduction_density.shape[3]
    pairs = vloc * val_count
    dims = (vloc, val_count, cond_count, npol)
    packed = pack(ka, ba, qpoint_map, slot_owner, valence_density, conduction_density)
    blocks = [packed[0]] + [shifted(packed[at], "ka", j) for at, j in enumerate(order(ka)) if at]
    early = ka // 2
    val_rows = slice(0, 2 * pairs)
    val_early = regroup(blocks[:early], val_rows)
    far_early = [shifted(val_early, "ga", r) for r in range(1, ga)]
    whole, near_table, far_table, extras = prepare(
        ka,
        dims,
        qpoint_map,
        slot_owner,
        band_pairs,
        valence_energy,
        conduction_energy,
        start_vector,
        screening,
        val_early,
    )
    val_late = regroup(blocks[early:], val_rows, (extras,))
    far_late = [shifted(val_late, "ga", r) for r in range(1, ga)]
    height = 2 * cond_count // ba * cond_count
    width = blocks[0].shape[1] // PARTS
    cond_rows = slice(2 * pairs, 2 * pairs + height)
    cond_parts = [
        regroup(blocks[1:], cond_rows, (val_late, *far_early), slice(c * width, (c + 1) * width))
        for c in range(PARTS)
    ]
    fields = field(pairs, whole, [val_early, val_late])
    cond_all = [regroup(blocks, cond_rows)]
    for r in range(1, ba):
        own_rows = slice(2 * pairs + r * height, 2 * pairs + (r + 1) * height)
        came = [handed(part, r) for part in cond_parts]
        cond_all.append(assemble(own_rows, blocks[0], came, fields))
    piece = near(ka, ba, dims, fields, near_table, extras, cond_all)
    if ga > 1:
        coupled = couple(ka, ga, ba, dims, whole, cond_all)
        far = [half for both in zip(far_early, far_late) for half in both]
        piece = contract(ka, ba, dims, far_table, piece, coupled, far, "far")
    piece = piece + sum(handed(piece, r) for r in range(1, ba))
    piece = summed(piece, "ga")
    pieces = [piece] + [shifted(piece, "ka", j) for j in range(1, ka)]
    scale_count = float(kcount * pair_count)
    return tuple(haydock(ka, pair_count, scale_count, npol, pieces))


def solution(mesh):
    in_specs = (
        P(("grp", "ka"), None, None, None),
        P(("grp", "ka"), None, None, "ba", None, "ga"),
        P(("grp", "ka"), None, None, None, None, "ga"),
        P(("grp", "ka"), None, "ga", None),
        P(),
        P(),
        P(),
        P(("grp", "ka"), None),
        P(("grp", "ka"), None),
    )
    out_specs = (P(("grp", "ka"), None, None, None), P("grp", None))
    body = functools.partial(local, mesh.shape["ka"], mesh.shape["ga"], mesh.shape["ba"])
    return jax.shard_map(body, mesh=mesh, in_specs=in_specs, out_specs=out_specs, check_vma=False)
```
